32 devices in a mesh: groups: 2 (over x), section: 8 (over z, y), tp: 2 (over core).
Axes of the slice: x: 2, y: 2, z: 4, core: 2. Of those that a mesh axis runs over, the one named last changes fastest.
Arguments:
- prompts: bfloat16 [12288, 12288], P(('groups', 'section'), 'tp'), parts along dimension 0, may hold values from -6 to 6
- decode_hidden: bfloat16 [2048, 12288], P(('groups', 'section'), 'tp'), parts along dimension 0, may hold values from -6 to 6
- queries: bfloat16 [2048, 6144], P(('groups', 'section'), 'tp'), parts along dimension 0, may hold values from -12 to 12
- kv_cache: bfloat16 [2048, 32, 1024], P(('groups', 'section'), None, 'tp'), parts along dimension 0, may hold values from -12 to 12
- cache_len: int32 [2048], P(('groups', 'section')), parts along dimension 0, may hold values from 2 to 32, as said below
- span_len: int32 [16, 12], P('groups'), parts along dimension 0, may hold values from 1 to 64, 576 in all within a row
- target_row: int32 [16, 12], P('groups'), parts along dimension 0, may hold values from 0 to 1023, as said below
- w_kv: bfloat16 [12288, 1024], P('tp'), may hold values from -0.0546875 to 0.0546875
- kv_scale: float32 [1024], replicated, may hold values from 0.5 to 2
Outputs:
- attended: bfloat16 [2048, 6144], P(('groups', 'section'), 'tp'), parts along dimension 0
The draws below stay inside these ranges and needn't reach their ends.
There are 2 independent parts, one for each index of `groups`. The reference program is written for one: setup_inputs(seed, part) draws one part's arguments, and reference() takes and returns one part's arrays. A program takes and returns all parts, laid end to end along the dimension named above; an argument that names none is the same for every part. Nothing has to cross between parts.
Inputs may be any that keep to these rules, and one draw needn't show every extreme that they name: target_row[s, r] // 128 is the decode section of section s's r-th request and target_row[s, r] % 128 its row there. No two requests name the same decode row. A section sends at most 2 of its requests to one decode section, and exactly 2 to some decode section. `cache_len`: every section has a decode row with exactly 32 valid positions.
All inputs are finite; a program needn't handle non-finite values.
Results may differ from the reference program's by a relative error of at most 0.0059.
Values may be sent and summed in bfloat16 or wider, within the bound.
No kernel may reach another device: no remote copies, remote signals or barrier semaphores. Data moves between devices by JAX's collectives and lax.ppermute only.
A program may use at most 128 MiB of HBM per device.

```python
import math
import jax
import jax.numpy as jnp
import numpy as np
from jax import lax

D = 12288
HD = 128
QH = 48
KVH = 4
REQ_DEV = 12
SPAN = 64
CAP = 2
ROWS = 128
CACHE = 32
PROMPT_ROWS = 6144
DEC_ROWS = 1024
N_SECTION = 8
N_TP = 2


def draw_queries(key, part):
    key = jax.random.fold_in(key, 3)
    total_rows = N_SECTION * ROWS
    values = jnp.clip(jax.random.normal(key, (total_rows, QH, HD), jnp.float32), -6.0, 6.0)
    return values.reshape(total_rows, QH * HD).astype(jnp.bfloat16)


def draw_kv_cache(key, part):
    key = jax.random.fold_in(key, 5)
    total_rows = N_SECTION * ROWS
    values = jnp.clip(jax.random.normal(key, (total_rows, CACHE, KVH, 2, HD), jnp.float32), -6.0, 6.0)
    return values.reshape(total_rows, CACHE, KVH * 2 * HD).astype(jnp.bfloat16)


def draw_cache_len(key, part):
    key = jax.random.fold_in(key, 7)
    length_key, full_key = jax.random.split(key)
    lengths = jax.random.randint(length_key, (N_SECTION, ROWS), 2, CACHE + 1)
    full_row = jax.random.randint(full_key, (N_SECTION, 1), 0, ROWS)
    lengths = jnp.where(jnp.arange(ROWS)[None, :] == full_row, CACHE, lengths)
    return lengths.reshape(N_SECTION * ROWS).astype(jnp.int32)


def draw_target_row(key, part):
    key = jax.random.fold_in(key, 11)
    score_key, hot_key, order_key, rows_key = jax.random.split(key, 4)
    sections = jnp.arange(N_SECTION)
    hot_start = jax.random.randint(hot_key, (), 0, 4)
    hot = (sections + hot_start) % 4 == 0
    scores = jax.random.randint(score_key, (N_SECTION, N_SECTION), 0, N_SECTION) + jnp.where(hot, N_SECTION, 0)[None, :]
    scores = (scores * N_SECTION + sections[None, :]).astype(jnp.int32)
    group_total = (REQ_DEV - CAP) // CAP + CAP
    top_values, chosen_sections = lax.top_k(scores, group_total)
    position = jnp.arange(REQ_DEV)
    paired = position < REQ_DEV - CAP
    group_of = jnp.where(paired, position // CAP, (REQ_DEV - CAP) // CAP + position - (REQ_DEV - CAP))
    member = jnp.where(paired, position % CAP, 0)
    random_ints = jax.random.randint(order_key, (N_SECTION, REQ_DEV), 0, 1 << 20)
    shuffled = jnp.argsort(random_ints * REQ_DEV + position[None, :], axis=1)
    destination = jnp.take_along_axis(chosen_sections, group_of[shuffled], axis=1)
    slot_number = sections[:, None] * CAP + member[shuffled]
    row_perm = jax.random.permutation(rows_key, ROWS)
    local_row = row_perm[slot_number]
    return (destination * ROWS + local_row).astype(jnp.int32)


def steps_of(own_key, extent, pieces, low, high):
    loudness = 1.0
    for dim, parts in pieces:
        heights = jax.random.uniform(jax.random.fold_in(jax.random.fold_in(own_key, 6), dim), (parts,), jnp.float32, low / len(pieces), high / len(pieces))
        loudness = loudness * jnp.repeat(jnp.exp(heights), extent[dim] // parts).reshape((-1,) + (1,) * (len(extent) - 1 - dim))
    return loudness


def length_profile(amount, total, limit, skew):
    loads = [(1 << 20) // math.isqrt(rank ** skew) + 1 for rank in range(2, amount + 1)]
    rest, given = total - limit - (amount - 1), [1] * (amount - 1)
    while rest > 0:
        movable = [i for i in range(amount - 1) if given[i] < limit]
        mass, left = sum([loads[i] for i in movable]), rest
        for i in movable:
            extra = min(limit - given[i], max(1, left * loads[i] // mass), rest)
            given[i] = given[i] + extra
            rest = rest - extra
    return np.array([limit] + given)


def ragged_sizes(rng, amount, total, bound, lean):
    if amount == 2:
        one = jax.random.randint(rng, (), max(1, total - bound), min(bound, total - 1) + 1)
        return jnp.stack([one, total - one])
    sizes = jnp.asarray(length_profile(amount, total, bound, lean), jnp.int32)
    twos = (amount - 1) // 2
    source_of, receiver = sizes[1:1 + 2 * twos:2], sizes[2:2 + 2 * twos:2]
    slack = jnp.minimum(source_of - 1, bound - receiver)
    moved = jax.random.randint(jax.random.fold_in(rng, 1), (twos,), 0, 1 << 20) % (slack + 1)
    sizes = sizes.at[1:1 + 2 * twos:2].set(source_of - moved).at[2:2 + 2 * twos:2].set(receiver + moved)
    return sizes[jax.random.permutation(jax.random.fold_in(rng, 2), amount)]


def normal_values(own_key, dims, spread, bound, shards=(), kind=jnp.bfloat16):
    values = jax.random.normal(own_key, dims, jnp.float32) * spread
    if len(shards) > 0:
        values = steps_of(own_key, dims, shards, -0.22, 0.18) * values
    return jnp.clip(values, min=-bound, max=bound).astype(kind)


def setup_inputs(seed: int = 0, part: int = 0) -> dict:
    arg_keys = jax.random.split(jax.random.key(seed), 10)
    own_keys = jax.random.split(jax.random.fold_in(arg_keys[9], part), 10)
    return {
        "prompts": normal_values(own_keys[0], (PROMPT_ROWS, D), 1.0, 6.0, ((0, 8), (1, 2))),
        "decode_hidden": normal_values(own_keys[1], (DEC_ROWS, D), 1.0, 6.0, ((0, 8), (1, 2))),
        "queries": draw_queries(jax.random.fold_in(jax.random.fold_in(arg_keys[9], part), 71), part),
        "kv_cache": draw_kv_cache(jax.random.fold_in(jax.random.fold_in(arg_keys[9], part), 71), part),
        "cache_len": draw_cache_len(jax.random.fold_in(jax.random.fold_in(arg_keys[9], part), 71), part),
        "span_len": jax.vmap(lambda own: ragged_sizes(own, REQ_DEV, REQ_DEV * SPAN * 3 // 4, SPAN, 1))(jax.random.split(own_keys[5], N_SECTION)).reshape((N_SECTION, REQ_DEV)).astype(jnp.int32),
        "target_row": draw_target_row(jax.random.fold_in(jax.random.fold_in(arg_keys[9], part), 71), part),
        "w_kv": normal_values(arg_keys[7], (D, 2 * KVH * HD), D ** -0.5, 0.0546875, ((0, 2),)),
        "kv_scale": jnp.clip(jnp.exp(jax.random.uniform(arg_keys[8], (2 * KVH * HD,), jnp.float32, math.log(0.5), math.log(2.0))), 0.5, 2.0),
    }


masked_score = -1e30


def project(rows_in, w_kv, kv_scale):
    feature_block = D // N_TP
    running_sum = jnp.zeros((rows_in.shape[0], w_kv.shape[1]), jnp.float32)
    for tp_index in range(N_TP):
        lower = tp_index * feature_block
        partial_term = jnp.dot(rows_in[:, lower:lower + feature_block], w_kv[lower:lower + feature_block], preferred_element_type=jnp.float32) * kv_scale
        partial_term = lax.optimization_barrier(partial_term.astype(jnp.bfloat16)).astype(jnp.float32)
        running_sum = running_sum + partial_term
    return running_sum.astype(jnp.bfloat16)


def attend(queries, cache_rows, own_kv, arrived, cache_len, new_len):
    row_count = queries.shape[0]
    kv_heads = own_kv.shape[1] // (2 * HD)
    group_size = queries.shape[1] // (kv_heads * HD)
    query_heads = queries.reshape(row_count, kv_heads, group_size, HD).astype(jnp.float32)
    cache_rows = cache_rows.reshape(row_count, cache_rows.shape[1], kv_heads, 2, HD).astype(jnp.float32)
    arrived = arrived.reshape(row_count, arrived.shape[1], kv_heads, 2, HD).astype(jnp.float32)
    own_kv = own_kv.reshape(row_count, kv_heads, 2, HD).astype(jnp.float32)
    score_scale = HD ** -0.5
    cache_scores = jnp.einsum("bhgd,bthd->bhgt", query_heads, cache_rows[:, :, :, 0]) * score_scale
    new_scores = jnp.einsum("bhgd,bthd->bhgt", query_heads, arrived[:, :, :, 0]) * score_scale
    own_scores = jnp.einsum("bhgd,bhd->bhg", query_heads, own_kv[:, :, 0]) * score_scale
    cache_valid = (jnp.arange(cache_rows.shape[1], dtype=jnp.int32)[None, :] < cache_len[:, None])[:, None, None, :]
    new_valid = (jnp.arange(arrived.shape[1], dtype=jnp.int32)[None, :] < new_len[:, None])[:, None, None, :]
    cache_scores = jnp.where(cache_valid, cache_scores, masked_score)
    new_scores = jnp.where(new_valid, new_scores, masked_score)
    largest = jnp.maximum(jnp.maximum(jnp.max(cache_scores, axis=3), jnp.max(new_scores, axis=3)), own_scores)
    cache_exp = jnp.exp(cache_scores - largest[..., None])
    new_exp = jnp.exp(new_scores - largest[..., None])
    own_exp = jnp.exp(own_scores - largest)
    denominator = jnp.sum(cache_exp, axis=3) + jnp.sum(new_exp, axis=3) + own_exp
    cache_weights = (cache_exp / denominator[..., None]).astype(jnp.bfloat16).astype(jnp.float32)
    new_weights = (new_exp / denominator[..., None]).astype(jnp.bfloat16).astype(jnp.float32)
    own_weights = (own_exp / denominator).astype(jnp.bfloat16).astype(jnp.float32)
    combined = jnp.einsum("bhgt,bthd->bhgd", cache_weights, cache_rows[:, :, :, 1])
    combined = combined + jnp.einsum("bhgt,bthd->bhgd", new_weights, arrived[:, :, :, 1])
    combined = combined + own_weights[..., None] * own_kv[:, :, 1][:, :, None, :]
    return combined.astype(jnp.bfloat16).reshape(row_count, kv_heads * group_size * HD)


def reference(prompts, decode_hidden, queries, kv_cache, cache_len, span_len, target_row, w_kv, kv_scale):
    prompt_kv = project(prompts, w_kv, kv_scale)
    own_all = project(decode_hidden, w_kv, kv_scale)
    request_total = N_SECTION * REQ_DEV
    packed = prompt_kv.reshape(request_total, SPAN * 2 * KVH * HD)
    targets = target_row.reshape(request_total)
    lengths = span_len.reshape(request_total)

    def one_section(section_index):
        row_ids = section_index * ROWS + jnp.arange(ROWS, dtype=jnp.int32)
        matches = targets[None, :] == row_ids[:, None]
        arrived = jnp.dot(matches.astype(jnp.bfloat16), packed, preferred_element_type=jnp.float32).astype(jnp.bfloat16)
        new_len = jnp.sum(jnp.where(matches, lengths[None, :], 0), axis=1).astype(jnp.int32)
        row_start = (section_index * ROWS).astype(jnp.int32)
        query_rows = lax.dynamic_slice_in_dim(queries, row_start, ROWS, 0)
        cache_rows = lax.dynamic_slice_in_dim(kv_cache, row_start, ROWS, 0)
        own_rows = lax.dynamic_slice_in_dim(own_all, row_start, ROWS, 0)
        length_rows = lax.dynamic_slice_in_dim(cache_len, row_start, ROWS, 0)
        return attend(query_rows, cache_rows, own_rows, arrived.reshape(ROWS, SPAN, 2 * KVH * HD), length_rows, new_len)

    result = lax.map(one_section, jnp.arange(N_SECTION, dtype=jnp.int32))
    return result.reshape(N_SECTION * ROWS, QH * HD)
```

```python
import functools
import math

import jax
import jax.numpy as jnp
from jax import lax
from jax.experimental import pallas as pl
from jax.experimental.pallas import tpu as pltpu
from jax.sharding import PartitionSpec as P

HD = 128
CAP = 2
STATS = 128
MASKED = -1e30
LOG2_SCALE = HD ** (-0.5) * math.log2(math.e)
F32 = jnp.float32
BF16 = jnp.bfloat16
VMEM_LIMIT = 56 * 1024 * 1024


def iota(shape, dim):
    return lax.broadcasted_iota(jnp.int32, shape, dim)


def decode_slots(target_ref, first_section, position, row_count):
    sections, requests = target_ref.shape
    slots = sections * CAP
    slot_id = iota((slots, requests), 0)
    table = jnp.zeros((slots, requests), jnp.int32)
    for step in range(sections):
        row = target_ref[pl.ds(lax.rem(first_section + step, sections), 1), :]
        table = jnp.where((slot_id >= step * CAP) & (slot_id < (step + 1) * CAP), row, table)
    local = table - position * row_count
    here = ((local >= 0) & (local < row_count)).astype(jnp.int32)
    member = lax.rem(iota((slots, 1), 0), CAP)
    earlier = jnp.zeros((slots, 1), jnp.int32)
    found = jnp.full((slots, 1), -1, jnp.int32)
    for r in range(requests):
        named = here[:, r : r + 1]
        found = jnp.where((named == 1) & (earlier == member), local[:, r : r + 1], found)
        earlier = earlier + named
    return found


def request_slots(target_ref, span_ref, position, row_count, padded):
    sections, requests = target_ref.shape
    target = target_ref[pl.ds(position, 1), :].astype(F32)
    span = span_ref[pl.ds(position, 1), :].astype(F32)
    section = jnp.zeros_like(target)
    for s in range(1, sections):
        section = section + (target >= s * row_count).astype(F32)
    diagonal = iota((padded, requests), 0) == iota((padded, requests), 1)
    section_col = jnp.sum(jnp.where(diagonal, section, 0.0), axis=1, keepdims=True)
    span_col = jnp.sum(jnp.where(diagonal, span, 0.0), axis=1, keepdims=True)
    real = iota((padded, 1), 0) < requests
    section_col = jnp.where(real, section_col, -1.0)
    square_0, square_1 = iota((padded, padded), 0), iota((padded, padded), 1)
    section_row = jnp.sum(jnp.where(square_0 == square_1, section_col, 0.0), axis=0, keepdims=True)
    before = (section_row == section_col) & (square_1 < square_0)
    rank_col = jnp.sum(before.astype(F32), axis=1, keepdims=True)
    slot_col = jnp.where(real, section_col * CAP + rank_col, -1.0)
    slot_row = jnp.sum(jnp.where(square_0 == square_1, slot_col, 0.0), axis=0, keepdims=True)
    return slot_col.astype(jnp.int32), slot_row.astype(jnp.int32), span_col.astype(jnp.int32)


def select_queries(place_ref, target_ref, queries_ref, out_ref):
    row_count = queries_ref.shape[0]
    rows = decode_slots(target_ref, 0, place_ref[0], row_count)
    pick = (iota((rows.shape[0], row_count), 1) == rows).astype(BF16)
    out_ref[...] = jnp.dot(pick, queries_ref[...], preferred_element_type=F32).astype(BF16)


def project(place_ref, prompts_ref, hidden_ref, w_ref, scale_ref, out_ref, total_ref):
    step = pl.program_id(0)
    prompt_rows = prompts_ref.shape[0]
    w = w_ref[...]
    prompt_part = jnp.dot(prompts_ref[...], w, preferred_element_type=F32)
    hidden_part = jnp.dot(hidden_ref[...], w, preferred_element_type=F32)

    @pl.when(step == 0)
    def _():
        total_ref[:prompt_rows] = prompt_part
        total_ref[prompt_rows:] = hidden_part

    @pl.when(step > 0)
    def _():
        total_ref[:prompt_rows] += prompt_part
        total_ref[prompt_rows:] += hidden_part

    @pl.when(step == pl.num_programs(0) - 1)
    def _():
        out_ref[...] = (total_ref[...] * scale_ref[...]).astype(BF16)


def split_bf16(x):
    high = x.astype(BF16).astype(F32)
    middle = (x - high).astype(BF16).astype(F32)
    return high, middle, (x - high - middle).astype(BF16).astype(F32)


def attend_arrived(place_ref, target_ref, span_ref, mine_ref, other_ref, queries_ref, out_ref):
    sections, requests = target_ref.shape
    padded = -(-requests // 16) * 16
    prompt_rows = mine_ref.shape[0]
    span_rows = prompt_rows // requests
    slots, width = queries_ref.shape
    group = width // HD
    slot_col, slot_row, span_col = request_slots(
        target_ref, span_ref, place_ref[0], place_ref[2], padded
    )
    from_slot = (iota((padded, slots), 1) == slot_col).astype(BF16)
    to_slot = (iota((slots, padded), 0) == slot_row).astype(BF16)
    rows = jnp.dot(from_slot, queries_ref[...], preferred_element_type=F32).astype(BF16)
    stacked = jnp.concatenate([rows[:, i * HD : (i + 1) * HD] for i in range(group)], axis=0)
    kv = (mine_ref[...].astype(F32) + other_ref[...].astype(F32)).astype(BF16)
    scores = lax.dot_general(
        stacked, kv[:, :HD], (((1,), (1,)), ((), ())), preferred_element_type=F32
    )
    key = iota((padded, prompt_rows), 1) - iota((padded, prompt_rows), 0) * span_rows
    valid = (key >= 0) & (key < span_col)
    bias = jnp.where(valid, 0.0, MASKED)
    scores = scores.reshape(group, padded, prompt_rows) * LOG2_SCALE + bias[None]
    largest = jnp.max(scores, axis=2, keepdims=True)
    weights = jnp.exp2(scores - largest)
    total = jnp.sum(weights, axis=2, keepdims=True)
    values = jnp.dot(
        weights.reshape(group * padded, prompt_rows).astype(BF16),
        kv[:, HD:],
        preferred_element_type=F32,
    ).reshape(group, padded, HD)
    values = values / total
    lse = largest + jnp.log2(total)
    lane = iota((padded, STATS), 1)
    stats = jnp.zeros((padded, STATS), F32)
    for i in range(group):
        for part, piece in enumerate(split_bf16(lse[i])):
            stats = jnp.where(lane == part * group + i, piece, stats)
    result = jnp.concatenate([values[i] for i in range(group)] + [stats], axis=1)
    out_ref[...] = jnp.dot(to_slot, result.astype(BF16), preferred_element_type=F32).astype(BF16)


def attend_cache(
    queries_ref, cache_ref, len_ref, mine_ref, other_ref, out_ref, stats_ref
):
    block_rows, cache_rows, width = cache_ref.shape
    kv_heads = width // (2 * HD)
    group = queries_ref.shape[1] // (kv_heads * HD)
    unit = 8
    queries = queries_ref[...].astype(F32)
    own = (mine_ref[...].astype(F32) + other_ref[...].astype(F32)).astype(BF16).astype(F32)
    shape = (unit, unit * cache_rows)
    key = iota(shape, 1) - iota(shape, 0) * cache_rows
    lane = iota((unit, STATS), 1)
    outs, all_stats = [], []
    for u in range(block_rows // unit):
        at = slice(u * unit, (u + 1) * unit)
        valid = (key >= 0) & (key < len_ref[at, :])
        bias = jnp.where(valid, 0.0, MASKED)
        stats = jnp.zeros((unit, STATS), F32)
        pieces = []
        for h in range(kv_heads):
            first = h * group
            q = jnp.stack(
                [queries[at, (first + i) * HD : (first + i + 1) * HD] for i in range(group)], axis=0
            )
            base = h * 2 * HD
            keys = cache_ref[at, :, base : base + HD].reshape(unit * cache_rows, HD)
            values = cache_ref[at, :, base + HD : base + 2 * HD].reshape(unit * cache_rows, HD)
            scores = lax.dot_general(
                q.reshape(group * unit, HD).astype(BF16),
                keys,
                (((1,), (1,)), ((), ())),
                preferred_element_type=F32,
            ).reshape(group, unit, unit * cache_rows)
            scores = scores * LOG2_SCALE + bias[None]
            own_key = own[at, base : base + HD]
            own_value = own[at, base + HD : base + 2 * HD]
            own_score = jnp.sum(q * own_key[None], axis=2, keepdims=True) * LOG2_SCALE
            largest = jnp.maximum(jnp.max(scores, axis=2, keepdims=True), own_score)
            weights = jnp.exp2(scores - largest)
            own_weight = jnp.exp2(own_score - largest)
            total = jnp.sum(weights, axis=2, keepdims=True) + own_weight
            result = jnp.dot(
                weights.reshape(group * unit, unit * cache_rows).astype(BF16),
                values,
                preferred_element_type=F32,
            ).reshape(group, unit, HD)
            result = (result + own_weight * own_value[None]) / total
            lse = largest + jnp.log2(total)
            pieces += [result[i] for i in range(group)]
            for i in range(group):
                stats = jnp.where(lane == first + i, lse[i], stats)
        outs.append(jnp.concatenate(pieces, axis=1))
        all_stats.append(stats)
    out_ref[...] = jnp.concatenate(outs, axis=0).astype(out_ref.dtype)
    stats_ref[...] = jnp.concatenate(all_stats, axis=0)


def merge(place_ref, target_ref, arrived_ref, cache_ref, stats_ref, out_ref, *, group):
    row_count = cache_ref.shape[0]
    head = pl.program_id(0)
    slots = arrived_ref.shape[0]
    rows = decode_slots(target_ref, 0, place_ref[0], row_count)
    pick = (iota((slots, row_count), 1) == rows).astype(BF16)
    has = lax.dot_general(
        pick, jnp.ones((slots, STATS), BF16), (((0,), (0,)), ((), ())), preferred_element_type=F32
    )
    arrived = lax.dot_general(
        pick, arrived_ref[...], (((0,), (0,)), ((), ())), preferred_element_type=F32
    )
    stats = stats_ref[...]
    first = arrived[:, group * HD :]
    for i in range(group):
        cache_lse = jnp.where(
            head == 0, stats[:, i : i + 1], stats[:, group + i : group + i + 1]
        )
        new_lse = (
            first[:, i : i + 1]
            + first[:, group + i : group + i + 1]
            + first[:, 2 * group + i : 2 * group + i + 1]
        )
        new_lse = jnp.where(has[:, :1] > 0.5, new_lse, MASKED)
        largest = jnp.maximum(cache_lse, new_lse)
        cache_weight = jnp.exp2(cache_lse - largest)
        new_weight = jnp.exp2(new_lse - largest)
        total = cache_weight + new_weight
        at = slice(i * HD, (i + 1) * HD)
        out_ref[:, at] = (
            cache_ref[:, at].astype(F32) * (cache_weight / total)
            + arrived[:, at] * (new_weight / total)
        ).astype(BF16)


def compiler_params():
    return pltpu.CompilerParams(vmem_limit_bytes=VMEM_LIMIT)


def whole(array):
    return pl.BlockSpec(array.shape, lambda *_: (0,) * array.ndim)


def shards(
    prompts, decode_hidden, queries, kv_cache, cache_len, span_len, target_row, w_kv, kv_scale
):
    row_count = decode_hidden.shape[0]
    prompt_rows, features = prompts.shape
    sections = lax.axis_size("section")
    tensor_parts = lax.axis_size("tp")
    local_width = kv_cache.shape[2]
    cache_rows = kv_cache.shape[1]
    kv_heads = local_width // (2 * HD)
    query_width = queries.shape[1]
    group = query_width // (kv_heads * HD)
    slots = sections * CAP
    all_rows = prompt_rows + row_count
    tp = lax.axis_index("tp")
    place = jnp.stack(
        [lax.axis_index("section"), tp, jnp.int32(row_count), tensor_parts - 1 - tp]
    ).astype(jnp.int32)
    scale = kv_scale.reshape(1, -1)
    lengths = cache_len.reshape(-1, 1)

    asked = pl.pallas_call(
        select_queries,
        grid_spec=pltpu.PrefetchScalarGridSpec(
            num_scalar_prefetch=1,
            grid=(1,),
            in_specs=[whole(target_row), whole(queries)],
            out_specs=pl.BlockSpec((slots, query_width), lambda *_: (0, 0)),
        ),
        out_shape=jax.ShapeDtypeStruct((slots, query_width), BF16),
        compiler_params=compiler_params(),
        name="select_queries",
    )(place, target_row, queries)
    asked = lax.all_to_all(asked, "section", 0, 0, tiled=True)

    depth = 1024

    def projected(which):
        return pl.pallas_call(
            project,
            grid_spec=pltpu.PrefetchScalarGridSpec(
                num_scalar_prefetch=1,
                grid=(features // depth,),
                in_specs=[
                    pl.BlockSpec((prompt_rows, depth), lambda k, place: (0, k)),
                    pl.BlockSpec((row_count, depth), lambda k, place: (0, k)),
                    pl.BlockSpec((depth, local_width), lambda k, place: (k, place[which])),
                    pl.BlockSpec((1, local_width), lambda k, place: (0, place[which])),
                ],
                out_specs=pl.BlockSpec((all_rows, local_width), lambda k, place: (0, 0)),
                scratch_shapes=[pltpu.VMEM((all_rows, local_width), F32)],
            ),
            out_shape=jax.ShapeDtypeStruct((all_rows, local_width), BF16),
            compiler_params=compiler_params(),
            name="project",
        )(place, prompts, decode_hidden, w_kv, scale)

    theirs = projected(3)
    other = lax.ppermute(theirs, "tp", [(0, 1), (1, 0)])
    mine = projected(1)

    head_width = group * HD
    answer_width = head_width + STATS
    answers = pl.pallas_call(
        attend_arrived,
        grid_spec=pltpu.PrefetchScalarGridSpec(
            num_scalar_prefetch=1,
            grid=(kv_heads,),
            in_specs=[
                whole(target_row),
                whole(span_len),
                pl.BlockSpec((prompt_rows, 2 * HD), lambda h, place: (0, h)),
                pl.BlockSpec((prompt_rows, 2 * HD), lambda h, place: (0, h)),
                pl.BlockSpec((slots, head_width), lambda h, place: (0, h)),
            ],
            out_specs=pl.BlockSpec((slots, answer_width), lambda h, place: (0, h)),
        ),
        out_shape=jax.ShapeDtypeStruct((slots, kv_heads * answer_width), BF16),
        compiler_params=compiler_params(),
        name="attend_arrived",
    )(place, target_row, span_len, mine, other, asked)
    answers = lax.all_to_all(answers, "section", 0, 0, tiled=True)

    block = 16
    own_block = prompt_rows // block
    cached, stats = pl.pallas_call(
        attend_cache,
        grid=(row_count // block,),
        in_specs=[
            pl.BlockSpec((block, query_width), lambda b: (b, 0)),
            pl.BlockSpec((block, cache_rows, local_width), lambda b: (b, 0, 0)),
            pl.BlockSpec((block, 1), lambda b: (b, 0)),
            pl.BlockSpec((block, local_width), lambda b: (own_block + b, 0)),
            pl.BlockSpec((block, local_width), lambda b: (own_block + b, 0)),
        ],
        out_specs=[
            pl.BlockSpec((block, query_width), lambda b: (b, 0)),
            pl.BlockSpec((block, STATS), lambda b: (b, 0)),
        ],
        out_shape=[
            jax.ShapeDtypeStruct((row_count, query_width), F32),
            jax.ShapeDtypeStruct((row_count, STATS), F32),
        ],
        compiler_params=compiler_params(),
        name="attend_cache",
    )(queries, kv_cache, lengths, mine, other)

    return pl.pallas_call(
        functools.partial(merge, group=group),
        grid_spec=pltpu.PrefetchScalarGridSpec(
            num_scalar_prefetch=1,
            grid=(kv_heads,),
            in_specs=[
                whole(target_row),
                pl.BlockSpec((slots, answer_width), lambda h, place: (0, h)),
                pl.BlockSpec((row_count, head_width), lambda h, place: (0, h)),
                whole(stats),
            ],
            out_specs=pl.BlockSpec((row_count, head_width), lambda h, place: (0, h)),
        ),
        out_shape=jax.ShapeDtypeStruct((row_count, query_width), BF16),
        compiler_params=compiler_params(),
        name="merge",
    )(place, target_row, answers, cached, stats)


def solution(mesh):
    in_specs = (
        P(("groups", "section"), "tp"),
        P(("groups", "section"), "tp"),
        P(("groups", "section"), "tp"),
        P(("groups", "section"), None, "tp"),
        P(("groups", "section")),
        P("groups", None),
        P("groups", None),
        P("tp", None),
        P(),
    )
    out_specs = P(("groups", "section"), "tp")
    return jax.shard_map(shards, mesh=mesh, in_specs=in_specs, out_specs=out_specs, check_vma=False)
```

```python
import functools
import math

import jax
import jax.numpy as jnp
from jax import lax
from jax.experimental import pallas as pl
from jax.experimental.pallas import tpu as pltpu
from jax.sharding import PartitionSpec as P

HD = 128
CAP = 2
STATS = 128
MASKED = -1e30
LOG2_SCALE = HD ** (-0.5) * math.log2(math.e)
F32 = jnp.float32
BF16 = jnp.bfloat16


def iota(shape, dim):
    return lax.broadcasted_iota(jnp.int32, shape, dim)


def decode_slots(target_ref, position, row_count, section_major):
    sections, requests = target_ref.shape
    slots = sections * CAP
    slot = iota((slots, 1), 0)
    if section_major:
        table = jnp.zeros((slots, requests), jnp.int32)
        slot_id = iota((slots, requests), 0)
        for s in range(sections):
            mine = (slot_id >= s * CAP) & (slot_id < (s + 1) * CAP)
            table = jnp.where(mine, target_ref[s : s + 1, :], table)
        member = lax.rem(slot, CAP)
    else:
        table = jnp.concatenate([target_ref[...]] * CAP, axis=0)
        member = sum((slot >= j * sections).astype(jnp.int32) for j in range(1, CAP))
    local = table - position * row_count
    here = (local >= 0) & (local < row_count)
    square = (requests, requests)
    earlier = jnp.dot(
        here.astype(F32).astype(BF16),
        (iota(square, 0) < iota(square, 1)).astype(F32).astype(BF16),
        preferred_element_type=F32,
    )
    chosen = here & (earlier == member.astype(F32))
    return jnp.max(jnp.where(chosen, local.astype(F32), -1.0), axis=1, keepdims=True).astype(
        jnp.int32
    )


def request_slots(target_ref, span_ref, position, row_count, padded):
    sections, requests = target_ref.shape
    target = target_ref[pl.ds(position, 1), :].astype(F32)
    span = span_ref[pl.ds(position, 1), :].astype(F32)
    diagonal = iota((padded, requests), 0) == iota((padded, requests), 1)
    target_col = jnp.sum(jnp.where(diagonal, target, 0.0), axis=1, keepdims=True)
    span_col = jnp.sum(jnp.where(diagonal, span, 0.0), axis=1, keepdims=True)
    section_row = jnp.zeros_like(target)
    section_col = jnp.zeros_like(target_col)
    for s in range(1, sections):
        section_row = section_row + (target >= s * row_count).astype(F32)
        section_col = section_col + (target_col >= s * row_count).astype(F32)
    before = (section_row == section_col) & (
        iota((padded, requests), 1) < iota((padded, requests), 0)
    )
    rank_col = jnp.sum(before.astype(F32), axis=1, keepdims=True)
    section_col = jnp.where(iota((padded, 1), 0) < requests, section_col, -1.0)
    return section_col.astype(jnp.int32), rank_col.astype(jnp.int32), span_col.astype(jnp.int32)


def select_queries(place_ref, target_ref, queries_ref, out_ref):
    row_count = queries_ref.shape[0]
    rows = decode_slots(target_ref, place_ref[0], row_count, False)
    pick = (iota((rows.shape[0], row_count), 1) == rows).astype(F32).astype(BF16)
    out_ref[...] = jnp.dot(pick, queries_ref[...], preferred_element_type=F32).astype(BF16)


def project_first(
    place_ref,
    prompts_ref,
    hidden_ref,
    w_ref,
    scale_ref,
    out_ref,
    rows_ref,
    w_mine_ref,
    w_theirs_ref,
    total_ref,
    row_sems,
    hidden_sems,
    theirs_sems,
    mine_sems,
    *,
    edges,
):
    prompt_rows = prompts_ref.shape[0]
    width = out_ref.shape[1]
    theirs = pl.ds(pl.multiple_of(place_ref[2] * width, width), width)
    mine = pl.ds(pl.multiple_of(place_ref[1] * width, width), width)
    chunks = [slice(a, b) for a, b in zip(edges[:-1], edges[1:])]
    waits = []
    for c, at in enumerate(chunks):
        copies = [
            pltpu.make_async_copy(
                w_ref.at[at, theirs], w_theirs_ref.at[at, :], theirs_sems.at[c]
            ),
            pltpu.make_async_copy(
                prompts_ref.at[:, at], rows_ref.at[:prompt_rows, at], row_sems.at[c]
            ),
            pltpu.make_async_copy(
                hidden_ref.at[:, at], rows_ref.at[prompt_rows:, at], hidden_sems.at[c]
            ),
        ]
        for copy in copies:
            copy.start()
        waits.append(copies)
    later = []
    for c, at in enumerate(chunks):
        copy = pltpu.make_async_copy(w_ref.at[at, mine], w_mine_ref.at[at, :], mine_sems.at[c])
        copy.start()
        later.append(copy)
    for c, at in enumerate(chunks):
        for copy in waits[c]:
            copy.wait()
        part = jnp.dot(rows_ref[:, at], w_theirs_ref[at, :], preferred_element_type=F32)
        if c == 0:
            total_ref[...] = part
        elif c < len(chunks) - 1:
            total_ref[...] += part
        else:
            out_ref[...] = ((total_ref[...] + part) * scale_ref[...]).astype(BF16)
    for copy in later:
        copy.wait()


def project_second(place_ref, rows_ref, w_ref, scale_ref, out_ref, *, block):
    for m in range(0, rows_ref.shape[0], block):
        at = slice(m, m + block)
        total = jnp.dot(rows_ref[at, :], w_ref[...], preferred_element_type=F32)
        out_ref[at, :] = (total * scale_ref[...]).astype(BF16)


def split_bf16(x):
    high = x.astype(BF16).astype(F32)
    middle = (x - high).astype(BF16).astype(F32)
    return high, middle, (x - high - middle).astype(BF16).astype(F32)


def attend_arrived(
    place_ref, target_ref, span_ref, mine_ref, other_ref, asked_ref, out_ref, *, row_count
):
    sections, requests = target_ref.shape
    slots = sections * CAP
    padded = -(-requests // 16) * 16
    position = place_ref[0]
    prompt_rows = mine_ref.shape[0] - row_count
    span_rows = prompt_rows // requests
    kv_heads = mine_ref.shape[1] // (2 * HD)
    group = asked_ref.shape[1] // (kv_heads * HD)
    section_col, rank_col, span_col = request_slots(
        target_ref, span_ref, position, row_count, padded
    )
    asked_at = jnp.where(
        section_col >= 0, section_col * slots + rank_col * sections + position, -1
    )
    from_asked = (iota((padded, asked_ref.shape[0]), 1) == asked_at).astype(F32).astype(BF16)
    answer_at = jnp.where(section_col >= 0, section_col * CAP + rank_col, -1)
    to_slot = (iota((padded, slots), 1) == answer_at).astype(F32).astype(BF16)
    key = iota((padded, prompt_rows), 1) - iota((padded, prompt_rows), 0) * span_rows
    bias = jnp.where((key >= 0) & (key < span_col), 0.0, MASKED)
    rows = jnp.dot(from_asked, asked_ref[...], preferred_element_type=F32).astype(BF16)
    kv = (
        mine_ref[:prompt_rows, :].astype(F32) + other_ref[:prompt_rows, :].astype(F32)
    ).astype(BF16)
    scores = []
    for h in range(kv_heads):
        stacked = jnp.concatenate(
            [rows[:, (h * group + i) * HD : (h * group + i + 1) * HD] for i in range(group)],
            axis=0,
        )
        keys = kv[:, h * 2 * HD : (h * 2 + 1) * HD]
        scores.append(
            lax.dot_general(
                stacked, keys, (((1,), (1,)), ((), ())), preferred_element_type=F32
            )
        )
    scores = [
        x.reshape(group, padded, prompt_rows) * LOG2_SCALE + bias[None] for x in scores
    ]
    largest = [jnp.max(x, axis=2, keepdims=True) for x in scores]
    weights = [jnp.exp2(x - y) for x, y in zip(scores, largest)]
    totals = [jnp.sum(x, axis=2, keepdims=True) for x in weights]
    lane = iota((padded, STATS), 1)
    lse = jnp.zeros((padded, STATS), F32)
    pieces = []
    for h in range(kv_heads):
        values = jnp.dot(
            weights[h].reshape(group * padded, prompt_rows).astype(BF16),
            kv[:, (h * 2 + 1) * HD : (h * 2 + 2) * HD],
            preferred_element_type=F32,
        ).reshape(group, padded, HD)
        values = values / totals[h]
        head_lse = largest[h] + jnp.log2(totals[h])
        for i in range(group):
            pieces.append(values[i])
            lse = jnp.where(lane == h * group + i, head_lse[i], lse)
    result = jnp.concatenate(pieces + list(split_bf16(lse)), axis=1).astype(BF16)
    answers = lax.dot_general(
        to_slot, result, (((0,), (0,)), ((), ())), preferred_element_type=F32
    ).astype(BF16)
    for s in range(sections):
        out_ref[s] = answers[s * CAP : (s + 1) * CAP]


def attend_cache(queries_ref, cache_ref, len_ref, mine_ref, other_ref, out_ref, stats_ref):
    block_rows, cache_rows, width = cache_ref.shape
    kv_heads = width // (2 * HD)
    group = queries_ref.shape[1] // (kv_heads * HD)
    unit = 8
    keys_of = unit * cache_rows
    queries = queries_ref[...].astype(F32)
    own = (mine_ref[...].astype(F32) + other_ref[...].astype(F32)).astype(BF16).astype(F32)
    key = iota((unit, keys_of), 1) - iota((unit, keys_of), 0) * cache_rows
    lengths = len_ref[...].astype(F32)
    row_count = lengths.shape[1]
    first_row = pl.program_id(0) * block_rows
    lane = iota((unit, STATS), 1)
    ones = jnp.ones((keys_of, HD), BF16)
    units = range(block_rows // unit)
    pairs = [(u, h) for u in units for h in range(kv_heads)]
    bias = []
    for u in units:
        row = iota((unit, row_count), 0) + (first_row + u * unit)
        length = jnp.sum(
            jnp.where(iota((unit, row_count), 1) == row, lengths, 0.0), axis=1, keepdims=True
        ).astype(jnp.int32)
        bias.append(jnp.where((key >= 0) & (key < length), 0.0, MASKED))
    q, scores, own_scores = [], [], []
    for u, h in pairs:
        at = slice(u * unit, (u + 1) * unit)
        q.append(
            jnp.stack(
                [
                    queries[at, (h * group + i) * HD : (h * group + i + 1) * HD]
                    for i in range(group)
                ],
                axis=0,
            )
        )
        keys = cache_ref[at, :, h * 2 * HD : (h * 2 + 1) * HD].reshape(keys_of, HD)
        scores.append(
            lax.dot_general(
                q[-1].reshape(group * unit, HD).astype(BF16),
                keys,
                (((1,), (1,)), ((), ())),
                preferred_element_type=F32,
            ).reshape(group, unit, keys_of)
        )
    for n, (u, h) in enumerate(pairs):
        at = slice(u * unit, (u + 1) * unit)
        own_key = own[at, h * 2 * HD : (h * 2 + 1) * HD]
        own_scores.append(jnp.sum(q[n] * own_key[None], axis=2, keepdims=True) * LOG2_SCALE)
    scores = [scores[n] * LOG2_SCALE + bias[u][None] for n, (u, h) in enumerate(pairs)]
    largest = [
        jnp.maximum(jnp.max(x, axis=2, keepdims=True), y) for x, y in zip(scores, own_scores)
    ]
    weights = [jnp.exp2(x - y).astype(BF16) for x, y in zip(scores, largest)]
    own_weights = [jnp.exp2(x - y) for x, y in zip(own_scores, largest)]
    sums = []
    for n, (u, h) in enumerate(pairs):
        at = slice(u * unit, (u + 1) * unit)
        values = cache_ref[at, :, (h * 2 + 1) * HD : (h * 2 + 2) * HD].reshape(keys_of, HD)
        sums.append(
            jnp.dot(
                weights[n].reshape(group * unit, keys_of),
                jnp.concatenate([values, ones], axis=1),
                preferred_element_type=F32,
            ).reshape(group, unit, 2 * HD)
        )
    pieces = [[] for _ in units]
    stats = [jnp.zeros((unit, STATS), F32) for _ in units]
    for n, (u, h) in enumerate(pairs):
        at = slice(u * unit, (u + 1) * unit)
        own_value = own[at, (h * 2 + 1) * HD : (h * 2 + 2) * HD]
        total = sums[n][:, :, HD:] + own_weights[n]
        result = (sums[n][:, :, :HD] + own_weights[n] * own_value[None]) / total
        lse = largest[n] + jnp.log2(total)
        for i in range(group):
            pieces[u].append(result[i])
            stats[u] = jnp.where(lane == h * group + i, lse[i], stats[u])
    out_ref[...] = jnp.concatenate(
        [jnp.concatenate(x, axis=1) for x in pieces], axis=0
    ).astype(out_ref.dtype)
    stats_ref[...] = jnp.concatenate(stats, axis=0)


def merge(place_ref, target_ref, arrived_ref, cached_ref, stats_ref, out_ref):
    row_count, width = cached_ref.shape
    heads = width // HD
    sections = arrived_ref.shape[0]
    slots = sections * CAP
    rows = decode_slots(target_ref, place_ref[0], row_count, True)
    pick_f32 = (iota((slots, row_count), 1) == rows).astype(F32)
    pick = pick_f32.astype(BF16)
    transposed = (((0,), (0,)), ((), ()))
    has = lax.dot_general(
        pick, jnp.ones((slots, HD), BF16), transposed, preferred_element_type=F32
    )
    cached = jnp.dot(pick, cached_ref[...], preferred_element_type=F32)
    cached_lse = jnp.dot(
        pick_f32, stats_ref[...], preferred_element_type=F32, precision=lax.Precision.HIGHEST
    )
    arrived = jnp.concatenate([arrived_ref[s].astype(F32) for s in range(sections)], axis=0)
    arrived_lse = (
        arrived[:, width : width + STATS]
        + arrived[:, width + STATS : width + 2 * STATS]
        + arrived[:, width + 2 * STATS :]
    )
    largest = jnp.maximum(cached_lse, arrived_lse)
    cached_weight = jnp.exp2(cached_lse - largest)
    arrived_weight = jnp.exp2(arrived_lse - largest)
    total = cached_weight + arrived_weight
    cached_weight = cached_weight / total
    arrived_weight = arrived_weight / total
    merged = jnp.concatenate(
        [
            cached[:, i * HD : (i + 1) * HD] * cached_weight[:, i : i + 1]
            + arrived[:, i * HD : (i + 1) * HD] * arrived_weight[:, i : i + 1]
            for i in range(heads)
        ],
        axis=1,
    ).astype(BF16)
    placed = lax.dot_general(pick, merged, transposed, preferred_element_type=F32)
    for i in range(heads):
        at = slice(i * HD, (i + 1) * HD)
        out_ref[:, at] = jnp.where(
            has > 0.5, placed[:, at], cached_ref[:, at].astype(F32)
        ).astype(BF16)


def compiler_params(megabytes):
    return pltpu.CompilerParams(vmem_limit_bytes=megabytes * 1024 * 1024)


SCALARS = pl.BlockSpec(memory_space=pltpu.SMEM)
RESIDENT = pl.BlockSpec(memory_space=pltpu.VMEM)
REMAINS = pl.BlockSpec(memory_space=pl.ANY)


def in_vmem(x):
    return pltpu.with_memory_space_constraint(x, pltpu.VMEM)


def shards(
    prompts, decode_hidden, queries, kv_cache, cache_len, span_len, target_row, w_kv, kv_scale
):
    row_count = decode_hidden.shape[0]
    prompt_rows, features = prompts.shape
    sections = lax.axis_size("section")
    local_width = kv_cache.shape[2]
    cache_rows = kv_cache.shape[1]
    kv_heads = local_width // (2 * HD)
    query_width = queries.shape[1]
    slots = sections * CAP
    all_rows = prompt_rows + row_count
    tp = lax.axis_index("tp")
    place = jnp.stack([lax.axis_index("section"), tp, 1 - tp]).astype(jnp.int32)
    scale = kv_scale.reshape(1, -1)
    lengths = cache_len.reshape(1, -1)

    asked = pl.pallas_call(
        select_queries,
        in_specs=[SCALARS, RESIDENT, RESIDENT],
        out_specs=RESIDENT,
        out_shape=jax.ShapeDtypeStruct((slots, query_width), BF16),
        compiler_params=compiler_params(16),
        name="select_queries",
    )(place, target_row, queries)
    asked = lax.all_gather(asked, "section", axis=0, tiled=True)

    depth = 512
    edges = tuple(range(0, features + 1, depth))
    count = len(edges) - 1
    theirs, rows, w_mine = pl.pallas_call(
        functools.partial(project_first, edges=edges),
        grid_spec=pltpu.PrefetchScalarGridSpec(
            num_scalar_prefetch=1,
            grid=(1,),
            in_specs=[
                REMAINS,
                REMAINS,
                REMAINS,
                pl.BlockSpec((1, local_width), lambda k, place: (0, place[2])),
            ],
            out_specs=[RESIDENT, RESIDENT, RESIDENT],
            scratch_shapes=[
                pltpu.VMEM((features, local_width), BF16),
                pltpu.VMEM((all_rows, local_width), F32),
                pltpu.SemaphoreType.DMA((count,)),
                pltpu.SemaphoreType.DMA((count,)),
                pltpu.SemaphoreType.DMA((count,)),
                pltpu.SemaphoreType.DMA((count,)),
            ],
        ),
        out_shape=[
            jax.ShapeDtypeStruct((all_rows, local_width), BF16),
            pltpu.VMEM((all_rows, features), BF16),
            pltpu.VMEM((features, local_width), BF16),
        ],
        compiler_params=compiler_params(16),
        name="project_first",
    )(place, prompts, decode_hidden, w_kv, scale)
    other = lax.ppermute(theirs, "tp", [(0, 1), (1, 0)])
    mine = pl.pallas_call(
        functools.partial(project_second, block=all_rows // 2),
        grid_spec=pltpu.PrefetchScalarGridSpec(
            num_scalar_prefetch=1,
            grid=(1,),
            in_specs=[
                RESIDENT,
                RESIDENT,
                pl.BlockSpec((1, local_width), lambda k, place: (0, place[1])),
            ],
            out_specs=RESIDENT,
        ),
        out_shape=pltpu.VMEM((all_rows, local_width), BF16),
        compiler_params=compiler_params(16),
        name="project_second",
    )(place, in_vmem(rows), in_vmem(w_mine), scale)

    answer_width = query_width + 3 * STATS
    answers = pl.pallas_call(
        functools.partial(attend_arrived, row_count=row_count),
        in_specs=[SCALARS] + [RESIDENT] * 5,
        out_specs=RESIDENT,
        out_shape=jax.ShapeDtypeStruct((sections, CAP, answer_width), BF16),
        compiler_params=compiler_params(24),
        name="attend_arrived",
    )(place, target_row, span_len, in_vmem(mine), in_vmem(other), asked)
    answers = lax.all_to_all(answers, "section", 0, 0)

    block = 32
    own_block = prompt_rows // block
    cached, stats = pl.pallas_call(
        attend_cache,
        grid=(row_count // block,),
        in_specs=[
            pl.BlockSpec((block, query_width), lambda b: (b, 0)),
            pl.BlockSpec((block, cache_rows, local_width), lambda b: (b, 0, 0)),
            pl.BlockSpec((1, row_count), lambda b: (0, 0)),
            pl.BlockSpec((block, local_width), lambda b: (own_block + b, 0)),
            pl.BlockSpec((block, local_width), lambda b: (own_block + b, 0)),
        ],
        out_specs=[
            pl.BlockSpec((block, query_width), lambda b: (b, 0)),
            pl.BlockSpec((block, STATS), lambda b: (b, 0)),
        ],
        out_shape=[
            jax.ShapeDtypeStruct((row_count, query_width), BF16),
            jax.ShapeDtypeStruct((row_count, STATS), F32),
        ],
        compiler_params=compiler_params(24),
        name="attend_cache",
    )(queries, kv_cache, lengths, mine, other)

    return pl.pallas_call(
        merge,
        in_specs=[SCALARS] + [RESIDENT] * 4,
        out_specs=RESIDENT,
        out_shape=jax.ShapeDtypeStruct((row_count, query_width), BF16),
        compiler_params=compiler_params(24),
        name="merge",
    )(place, target_row, in_vmem(answers), cached, stats)


def solution(mesh):
    in_specs = (
        P(("groups", "section"), "tp"),
        P(("groups", "section"), "tp"),
        P(("groups", "section"), "tp"),
        P(("groups", "section"), None, "tp"),
        P(("groups", "section")),
        P("groups", None),
        P("groups", None),
        P("tp", None),
        P(),
    )
    out_specs = P(("groups", "section"), "tp")
    return jax.shard_map(shards, mesh=mesh, in_specs=in_specs, out_specs=out_specs, check_vma=False)
```

```python
import functools
import math

import jax
import jax.numpy as jnp
from jax import lax
from jax.experimental import pallas as pl
from jax.experimental.pallas import tpu as pltpu
from jax.sharding import PartitionSpec as P

HD = 128
CAP = 2
STATS = 128
MASKED = -1e30
LOG2_SCALE = HD ** (-0.5) * math.log2(math.e)
F32 = jnp.float32
BF16 = jnp.bfloat16
TRANSPOSED = (((0,), (0,)), ((), ()))


def iota(shape, dim):
    return lax.broadcasted_iota(jnp.int32, shape, dim)


def one_hot(shape, dim, index):
    return (iota(shape, dim) == index).astype(F32).astype(BF16)


def select_queries(target_ref, queries_ref, pick_ref, *asked_refs):
    sections, requests = target_ref.shape
    row_count = queries_ref.shape[0]
    slots = sections * CAP
    position = lax.axis_index("section")
    slot_id = iota((slots, requests), 0)
    table = jnp.zeros((slots, requests), jnp.int32)
    for k in range(sections):
        row = target_ref[pl.ds(lax.rem(position + k, sections), 1), :]
        table = jnp.where((slot_id >= k * CAP) & (slot_id < (k + 1) * CAP), row, table)
    local = table - position * row_count
    here = (local >= 0) & (local < row_count)
    square = (requests, requests)
    earlier = jnp.dot(
        here.astype(F32).astype(BF16),
        (iota(square, 0) < iota(square, 1)).astype(F32).astype(BF16),
        preferred_element_type=F32,
    )
    chosen = here & (earlier == lax.rem(slot_id, CAP).astype(F32))
    row = jnp.max(jnp.where(chosen, local.astype(F32), -1.0), axis=1, keepdims=True)
    pick = one_hot((slots, row_count), 1, row.astype(jnp.int32))
    pick_ref[...] = pick
    asked = jnp.dot(pick, queries_ref[...], preferred_element_type=F32).astype(BF16)
    for k in range(sections):
        asked_refs[k][...] = asked[k * CAP : (k + 1) * CAP]


def project_first(
    prompts_ref,
    hidden_ref,
    w_ref,
    scale_ref,
    after_ref,
    out_ref,
    rows_ref,
    w_mine_ref,
    w_theirs_ref,
    total_ref,
    scale_here_ref,
    row_sems,
    hidden_sems,
    theirs_sems,
    mine_sems,
    scale_sem,
    *,
    edges,
):
    prompt_rows = prompts_ref.shape[0]
    width = out_ref.shape[1]
    tp = lax.axis_index("tp")
    theirs = pl.ds(pl.multiple_of((1 - tp) * width, width), width)
    mine = pl.ds(pl.multiple_of(tp * width, width), width)
    chunks = [slice(a, b) for a, b in zip(edges[:-1], edges[1:])]
    waits = []
    for c, at in enumerate(chunks):
        copies = [
            pltpu.make_async_copy(
                w_ref.at[at, theirs], w_theirs_ref.at[at, :], theirs_sems.at[c]
            ),
            pltpu.make_async_copy(
                prompts_ref.at[:, at], rows_ref.at[:prompt_rows, at], row_sems.at[c]
            ),
            pltpu.make_async_copy(
                hidden_ref.at[:, at], rows_ref.at[prompt_rows:, at], hidden_sems.at[c]
            ),
        ]
        for copy in copies:
            copy.start()
        waits.append(copies)
    later = [
        pltpu.make_async_copy(w_ref.at[at, mine], w_mine_ref.at[at, :], mine_sems.at[c])
        for c, at in enumerate(chunks)
    ]
    later.append(pltpu.make_async_copy(scale_ref.at[:, theirs], scale_here_ref, scale_sem))
    for copy in later:
        copy.start()
    for c, at in enumerate(chunks):
        for copy in waits[c]:
            copy.wait()
        part = jnp.dot(rows_ref[:, at], w_theirs_ref[at, :], preferred_element_type=F32)
        if c == 0:
            total_ref[...] = part
        elif c < len(chunks) - 1:
            total_ref[...] += part
        else:
            later[-1].wait()
            out_ref[...] = ((total_ref[...] + part) * scale_here_ref[...]).astype(BF16)
    for copy in later[:-1]:
        copy.wait()


def project_second(
    rows_ref,
    w_ref,
    scale_ref,
    cache_ref,
    queries_ref,
    out_ref,
    cache_here_ref,
    queries_here_ref,
    scale_here_ref,
    scale_sem,
    cache_sem,
    queries_sem,
    *,
    block,
):
    width = out_ref.shape[1]
    mine = pl.ds(pl.multiple_of(lax.axis_index("tp") * width, width), width)
    copies = [
        pltpu.make_async_copy(scale_ref.at[:, mine], scale_here_ref, scale_sem),
        pltpu.make_async_copy(queries_ref, queries_here_ref, queries_sem),
        pltpu.make_async_copy(cache_ref, cache_here_ref, cache_sem),
    ]
    for copy in copies:
        copy.start()
    for m in range(0, rows_ref.shape[0], block):
        at = slice(m, m + block)
        total = jnp.dot(rows_ref[at, :], w_ref[...], preferred_element_type=F32)
        if m == 0:
            copies[0].wait()
        out_ref[at, :] = (total * scale_here_ref[...]).astype(BF16)
    for copy in copies[1:]:
        copy.wait()


def split_bf16(x):
    high = x.astype(BF16).astype(F32)
    middle = (x - high).astype(BF16).astype(F32)
    return high, middle, (x - high - middle).astype(BF16).astype(F32)


def request_slots(target_ref, span_ref, row_count, padded):
    sections, requests = target_ref.shape
    position = lax.axis_index("section")
    target = target_ref[pl.ds(position, 1), :].astype(F32)
    span = span_ref[pl.ds(position, 1), :].astype(F32)
    diagonal = iota((padded, requests), 0) == iota((padded, requests), 1)
    target_col = jnp.sum(jnp.where(diagonal, target, 0.0), axis=1, keepdims=True)
    span_col = jnp.sum(jnp.where(diagonal, span, 0.0), axis=1, keepdims=True)
    section_row = jnp.zeros_like(target)
    section_col = jnp.zeros_like(target_col)
    for s in range(1, sections):
        section_row = section_row + (target >= s * row_count).astype(F32)
        section_col = section_col + (target_col >= s * row_count).astype(F32)
    before = (section_row == section_col) & (
        iota((padded, requests), 1) < iota((padded, requests), 0)
    )
    rank_col = jnp.sum(before.astype(F32), axis=1, keepdims=True).astype(jnp.int32)
    back = position - section_col.astype(jnp.int32)
    back = jnp.where(back < 0, back + sections, back)
    real = iota((padded, 1), 0) < requests
    return jnp.where(real, back * CAP + rank_col, -1), span_col.astype(jnp.int32)


def attend_arrived(target_ref, span_ref, mine_ref, other_ref, *refs, row_count):
    sections, requests = target_ref.shape
    asked_refs, out_refs = refs[:sections], refs[sections:]
    slots = sections * CAP
    padded = -(-requests // 16) * 16
    prompt_rows = mine_ref.shape[0] - row_count
    span_rows = prompt_rows // requests
    kv_heads = mine_ref.shape[1] // (2 * HD)
    group = asked_refs[0].shape[1] // (kv_heads * HD)
    slot_col, span_col = request_slots(target_ref, span_ref, row_count, padded)
    slot_of = one_hot((padded, slots), 1, slot_col)
    key = iota((padded, prompt_rows), 1) - iota((padded, prompt_rows), 0) * span_rows
    bias = jnp.where((key >= 0) & (key < span_col), 0.0, MASKED)
    asked = jnp.concatenate([ref[...].astype(F32) for ref in asked_refs], axis=0).astype(BF16)
    rows = jnp.dot(slot_of, asked, preferred_element_type=F32).astype(BF16)
    kv = (
        mine_ref[:prompt_rows, :].astype(F32) + other_ref[:prompt_rows, :].astype(F32)
    ).astype(BF16)
    scores = []
    for h in range(kv_heads):
        stacked = jnp.concatenate(
            [rows[:, (h * group + i) * HD : (h * group + i + 1) * HD] for i in range(group)],
            axis=0,
        )
        keys = kv[:, h * 2 * HD : (h * 2 + 1) * HD]
        scores.append(
            lax.dot_general(
                stacked, keys, (((1,), (1,)), ((), ())), preferred_element_type=F32
            )
        )
    scores = [
        x.reshape(group, padded, prompt_rows) * LOG2_SCALE + bias[None] for x in scores
    ]
    largest = [jnp.max(x, axis=2, keepdims=True) for x in scores]
    weights = [jnp.exp2(x - y) for x, y in zip(scores, largest)]
    totals = [jnp.sum(x, axis=2, keepdims=True) for x in weights]
    lane = iota((padded, STATS), 1)
    lse = jnp.zeros((padded, STATS), F32)
    pieces = []
    for h in range(kv_heads):
        values = jnp.dot(
            weights[h].reshape(group * padded, prompt_rows).astype(BF16),
            kv[:, (h * 2 + 1) * HD : (h * 2 + 2) * HD],
            preferred_element_type=F32,
        ).reshape(group, padded, HD)
        values = values / totals[h]
        head_lse = largest[h] + jnp.log2(totals[h])
        for i in range(group):
            pieces.append(values[i])
            lse = jnp.where(lane == h * group + i, head_lse[i], lse)
    result = jnp.concatenate(pieces + list(split_bf16(lse)), axis=1).astype(BF16)
    answers = lax.dot_general(slot_of, result, TRANSPOSED, preferred_element_type=F32).astype(BF16)
    for k in range(sections):
        out_refs[k][...] = answers[k * CAP : (k + 1) * CAP]


def attend_cache(
    queries_ref,
    cache_ref,
    len_ref,
    mine_ref,
    other_ref,
    pick_ref,
    after_ref,
    out_ref,
    slot_out_ref,
    slot_lse_ref,
    *,
    block_rows,
):
    row_count, cache_rows, width = cache_ref.shape
    kv_heads = width // (2 * HD)
    group = queries_ref.shape[1] // (kv_heads * HD)
    unit = 8
    keys_of = unit * cache_rows
    first_row = pl.multiple_of(pl.program_id(0) * block_rows, block_rows)
    block = pl.ds(first_row, block_rows)
    own_block = pl.ds(first_row + (mine_ref.shape[0] - row_count), block_rows)
    queries = queries_ref[block, :].astype(F32)
    own = mine_ref[own_block, :].astype(F32) + other_ref[own_block, :].astype(F32)
    own = own.astype(BF16).astype(F32)
    key = iota((unit, keys_of), 1) - iota((unit, keys_of), 0) * cache_rows
    lengths = len_ref[...].astype(F32)
    lane = iota((unit, STATS), 1)
    ones = jnp.ones((keys_of, HD), BF16)
    units = range(block_rows // unit)

    def rows_of(u):
        return pl.ds(first_row + u * unit, unit)

    pairs = [(u, h) for u in units for h in range(kv_heads)]
    bias = []
    for u in units:
        row = iota((unit, row_count), 0) + (first_row + u * unit)
        length = jnp.sum(
            jnp.where(iota((unit, row_count), 1) == row, lengths, 0.0), axis=1, keepdims=True
        ).astype(jnp.int32)
        bias.append(jnp.where((key >= 0) & (key < length), 0.0, MASKED))
    q, scores, own_scores = [], [], []
    for u, h in pairs:
        at = slice(u * unit, (u + 1) * unit)
        q.append(
            jnp.stack(
                [
                    queries[at, (h * group + i) * HD : (h * group + i + 1) * HD]
                    for i in range(group)
                ],
                axis=0,
            )
        )
        keys = cache_ref[rows_of(u), :, h * 2 * HD : (h * 2 + 1) * HD].reshape(keys_of, HD)
        scores.append(
            lax.dot_general(
                q[-1].reshape(group * unit, HD).astype(BF16),
                keys,
                (((1,), (1,)), ((), ())),
                preferred_element_type=F32,
            ).reshape(group, unit, keys_of)
        )
    for n, (u, h) in enumerate(pairs):
        at = slice(u * unit, (u + 1) * unit)
        own_key = own[at, h * 2 * HD : (h * 2 + 1) * HD]
        own_scores.append(jnp.sum(q[n] * own_key[None], axis=2, keepdims=True) * LOG2_SCALE)
    scores = [scores[n] * LOG2_SCALE + bias[u][None] for n, (u, h) in enumerate(pairs)]
    largest = [
        jnp.maximum(jnp.max(x, axis=2, keepdims=True), y) for x, y in zip(scores, own_scores)
    ]
    weights = [jnp.exp2(x - y).astype(BF16) for x, y in zip(scores, largest)]
    own_weights = [jnp.exp2(x - y) for x, y in zip(own_scores, largest)]
    sums = []
    for n, (u, h) in enumerate(pairs):
        at = slice(u * unit, (u + 1) * unit)
        values = cache_ref[rows_of(u), :, (h * 2 + 1) * HD : (h * 2 + 2) * HD].reshape(keys_of, HD)
        sums.append(
            jnp.dot(
                weights[n].reshape(group * unit, keys_of),
                jnp.concatenate([values, ones], axis=1),
                preferred_element_type=F32,
            ).reshape(group, unit, 2 * HD)
        )
    pieces = [[] for _ in units]
    stats = [jnp.zeros((unit, STATS), F32) for _ in units]
    for n, (u, h) in enumerate(pairs):
        at = slice(u * unit, (u + 1) * unit)
        own_value = own[at, (h * 2 + 1) * HD : (h * 2 + 2) * HD]
        total = sums[n][:, :, HD:] + own_weights[n]
        result = (sums[n][:, :, :HD] + own_weights[n] * own_value[None]) / total
        lse = largest[n] + jnp.log2(total)
        for i in range(group):
            pieces[u].append(result[i])
            stats[u] = jnp.where(lane == h * group + i, lse[i], stats[u])
    out = jnp.concatenate([jnp.concatenate(x, axis=1) for x in pieces], axis=0).astype(BF16)
    out_ref[block, :] = out
    pick = pick_ref[...]
    here = iota((row_count, block_rows), 0) == iota((row_count, block_rows), 1) + first_row
    pick = jnp.dot(pick, here.astype(F32).astype(BF16), preferred_element_type=F32).astype(BF16)
    slot_out = jnp.dot(pick, out, preferred_element_type=F32)
    lse = jnp.concatenate(stats, axis=0)
    slot_lse = sum(
        jnp.dot(pick, part.astype(BF16), preferred_element_type=F32) for part in split_bf16(lse)
    )

    @pl.when(pl.program_id(0) == 0)
    def _():
        slot_out_ref[...] = slot_out
        slot_lse_ref[...] = slot_lse

    @pl.when(pl.program_id(0) > 0)
    def _():
        slot_out_ref[...] += slot_out
        slot_lse_ref[...] += slot_lse


def merge(pick_ref, cached_ref, slot_out_ref, slot_lse_ref, *refs):
    arrived_refs, out_ref = refs[:-1], refs[-1]
    width = cached_ref.shape[1]
    pick = pick_ref[...]
    arrived = jnp.concatenate([ref[...].astype(F32) for ref in arrived_refs], axis=0)
    arrived_lse = (
        arrived[:, width : width + STATS]
        + arrived[:, width + STATS : width + 2 * STATS]
        + arrived[:, width + 2 * STATS :]
    )
    cached_lse = slot_lse_ref[...]
    largest = jnp.maximum(cached_lse, arrived_lse)
    cached_weight = jnp.exp2(cached_lse - largest)
    arrived_weight = jnp.exp2(arrived_lse - largest)
    total = cached_weight + arrived_weight
    cached_weight = cached_weight / total
    arrived_weight = arrived_weight / total
    has = lax.dot_general(
        pick, jnp.ones((pick.shape[0], HD), BF16), TRANSPOSED, preferred_element_type=F32
    )
    for i in range(width // HD):
        at = slice(i * HD, (i + 1) * HD)
        merged = (
            slot_out_ref[:, at] * cached_weight[:, i : i + 1]
            + arrived[:, at] * arrived_weight[:, i : i + 1]
        )
        placed = lax.dot_general(
            pick, merged.astype(BF16), TRANSPOSED, preferred_element_type=F32
        )
        out_ref[:, at] = jnp.where(has > 0.5, placed, cached_ref[:, at].astype(F32)).astype(BF16)


def compiler_params(megabytes):
    return pltpu.CompilerParams(vmem_limit_bytes=megabytes * 1024 * 1024)


RESIDENT = pl.BlockSpec(memory_space=pltpu.VMEM)
REMAINS = pl.BlockSpec(memory_space=pl.ANY)


def in_vmem(x):
    return pltpu.with_memory_space_constraint(x, pltpu.VMEM)


def in_hbm(x):
    return pltpu.with_memory_space_constraint(x, pltpu.HBM)


def shards(
    prompts, decode_hidden, queries, kv_cache, cache_len, span_len, target_row, w_kv, kv_scale
):
    row_count = decode_hidden.shape[0]
    prompt_rows, features = prompts.shape
    sections = lax.axis_size("section")
    local_width = kv_cache.shape[2]
    query_width = queries.shape[1]
    slots = sections * CAP
    all_rows = prompt_rows + row_count
    scale = kv_scale.reshape(1, -1)
    lengths = cache_len.reshape(1, -1)

    def moved(arrays, sign):
        return [arrays[0]] + [
            lax.ppermute(
                arrays[k], "section", [(i, (i + sign * k) % sections) for i in range(sections)]
            )
            for k in range(1, sections)
        ]

    pick, *asked = pl.pallas_call(
        select_queries,
        in_specs=[RESIDENT, RESIDENT],
        out_specs=[RESIDENT] * (1 + sections),
        out_shape=[pltpu.VMEM((slots, row_count), BF16)]
        + [pltpu.VMEM((CAP, query_width), BF16)] * sections,
        compiler_params=compiler_params(16),
        name="select_queries",
    )(in_hbm(target_row), in_hbm(queries))
    asked = moved(asked, 1)

    depth = 512
    edges = tuple(range(0, features + 1, depth))
    count = len(edges) - 1
    theirs, rows, w_mine = pl.pallas_call(
        functools.partial(project_first, edges=edges),
        in_specs=[REMAINS] * 5,
        out_specs=[RESIDENT, RESIDENT, RESIDENT],
        scratch_shapes=[
            pltpu.VMEM((features, local_width), BF16),
            pltpu.VMEM((all_rows, local_width), F32),
            pltpu.VMEM((1, local_width), F32),
            pltpu.SemaphoreType.DMA((count,)),
            pltpu.SemaphoreType.DMA((count,)),
            pltpu.SemaphoreType.DMA((count,)),
            pltpu.SemaphoreType.DMA((count,)),
            pltpu.SemaphoreType.DMA(()),
        ],
        out_shape=[
            pltpu.VMEM((all_rows, local_width), BF16),
            pltpu.VMEM((all_rows, features), BF16),
            pltpu.VMEM((features, local_width), BF16),
        ],
        compiler_params=compiler_params(16),
        name="project_first",
    )(in_hbm(prompts), in_hbm(decode_hidden), in_hbm(w_kv), in_hbm(scale), in_vmem(pick))
    other = lax.ppermute(theirs, "tp", [(0, 1), (1, 0)])
    mine, cache_here, queries_here = pl.pallas_call(
        functools.partial(project_second, block=all_rows // 2),
        in_specs=[RESIDENT, RESIDENT, REMAINS, REMAINS, REMAINS],
        out_specs=[RESIDENT, RESIDENT, RESIDENT],
        scratch_shapes=[
            pltpu.VMEM((1, local_width), F32),
            pltpu.SemaphoreType.DMA(()),
            pltpu.SemaphoreType.DMA(()),
            pltpu.SemaphoreType.DMA(()),
        ],
        out_shape=[
            pltpu.VMEM((all_rows, local_width), BF16),
            pltpu.VMEM(kv_cache.shape, BF16),
            pltpu.VMEM(queries.shape, BF16),
        ],
        compiler_params=compiler_params(16),
        name="project_second",
    )(in_vmem(rows), in_vmem(w_mine), in_hbm(scale), in_hbm(kv_cache), in_hbm(queries))

    answer_width = query_width + 3 * STATS
    answers = pl.pallas_call(
        functools.partial(attend_arrived, row_count=row_count),
        in_specs=[RESIDENT] * (4 + sections),
        out_specs=[RESIDENT] * sections,
        out_shape=[pltpu.VMEM((CAP, answer_width), BF16)] * sections,
        compiler_params=compiler_params(24),
        name="attend_arrived",
    )(in_hbm(target_row), in_hbm(span_len), in_vmem(mine), in_vmem(other), *map(in_vmem, asked))
    after = answers[0]
    answers = moved(answers, -1)

    block = 32
    cached, slot_out, slot_lse = pl.pallas_call(
        functools.partial(attend_cache, block_rows=block),
        grid=(row_count // block,),
        in_specs=[RESIDENT] * 6 + [REMAINS],
        out_specs=[RESIDENT] * 3,
        out_shape=[
            pltpu.VMEM((row_count, query_width), BF16),
            pltpu.VMEM((slots, query_width), F32),
            pltpu.VMEM((slots, STATS), F32),
        ],
        compiler_params=compiler_params(24),
        name="attend_cache",
    )(
        in_vmem(queries_here),
        in_vmem(cache_here),
        in_hbm(lengths),
        in_vmem(mine),
        in_vmem(other),
        in_vmem(pick),
        in_vmem(after),
    )

    return pl.pallas_call(
        merge,
        in_specs=[RESIDENT] * (4 + sections),
        out_specs=RESIDENT,
        out_shape=jax.ShapeDtypeStruct((row_count, query_width), BF16),
        compiler_params=compiler_params(24),
        name="merge",
    )(*map(in_vmem, (pick, cached, slot_out, slot_lse, *answers)))


def solution(mesh):
    in_specs = (
        P(("groups", "section"), "tp"),
        P(("groups", "section"), "tp"),
        P(("groups", "section"), "tp"),
        P(("groups", "section"), None, "tp"),
        P(("groups", "section")),
        P("groups", None),
        P("groups", None),
        P("tp", None),
        P(),
    )
    out_specs = P(("groups", "section"), "tp")
    return jax.shard_map(shards, mesh=mesh, in_specs=in_specs, out_specs=out_specs, check_vma=False)
```

```python
import functools
import math

import jax
import jax.numpy as jnp
from jax import lax
from jax.experimental import pallas as pl
from jax.experimental.pallas import tpu as pltpu
from jax.sharding import PartitionSpec as P

HD = 128
CAP = 2
STATS = 128
MASKED = -1e30
LOG2_SCALE = HD ** (-0.5) * math.log2(math.e)
F32 = jnp.float32
BF16 = jnp.bfloat16
TRANSPOSED = (((0,), (0,)), ((), ()))


def iota(shape, dim):
    return lax.broadcasted_iota(jnp.int32, shape, dim)


def one_hot(shape, dim, index):
    return (iota(shape, dim) == index).astype(F32).astype(BF16)


def select_queries(target_ref, queries_ref, pick_ref, asked_ref):
    sections, requests = target_ref.shape
    row_count = queries_ref.shape[0]
    slots = sections * CAP
    position = lax.axis_index("section")
    slot_id = iota((slots, requests), 0)
    table = jnp.zeros((slots, requests), jnp.int32)
    for k in range(sections):
        mine = (slot_id >= k * CAP) & (slot_id < (k + 1) * CAP)
        table = jnp.where(mine, target_ref[k : k + 1, :], table)
    local = table - position * row_count
    here = (local >= 0) & (local < row_count)
    square = (requests, requests)
    earlier = jnp.dot(
        here.astype(F32).astype(BF16),
        (iota(square, 0) < iota(square, 1)).astype(F32).astype(BF16),
        preferred_element_type=F32,
    )
    chosen = here & (earlier == lax.rem(slot_id, CAP).astype(F32))
    row = jnp.max(jnp.where(chosen, local.astype(F32), -1.0), axis=1, keepdims=True)
    pick = one_hot((slots, row_count), 1, row.astype(jnp.int32))
    pick_ref[...] = pick
    asked = jnp.dot(pick, queries_ref[...], preferred_element_type=F32).astype(BF16)
    for k in range(sections):
        asked_ref[k] = asked[k * CAP : (k + 1) * CAP]


def spans(edges):
    return [slice(a, b) for a, b in zip(edges[:-1], edges[1:])]


def accumulate(rows_ref, w_ref, total_ref, out_ref, scale_ref, chunks, waits, scale_copy):
    for c, at in enumerate(chunks):
        for copy in waits[c]:
            copy.wait()
        part = jnp.dot(rows_ref[:, at], w_ref[at, :], preferred_element_type=F32)
        if c == 0:
            total_ref[...] = part
        elif c < len(chunks) - 1:
            total_ref[...] += part
        else:
            scale_copy.wait()
            out_ref[...] = ((total_ref[...] + part) * scale_ref[...]).astype(BF16)


def project_first(
    prompts_ref,
    hidden_ref,
    w_ref,
    scale_ref,
    after_ref,
    out_ref,
    rows_ref,
    w_mine_ref,
    w_theirs_ref,
    total_ref,
    scale_here_ref,
    row_sems,
    hidden_sems,
    theirs_sems,
    mine_sem,
    scale_sem,
    *,
    edges,
):
    prompt_rows = prompts_ref.shape[0]
    width = out_ref.shape[1]
    tp = lax.axis_index("tp")
    theirs = pl.ds(pl.multiple_of((1 - tp) * width, width), width)
    mine = pl.ds(pl.multiple_of(tp * width, width), width)
    chunks = spans(edges)
    waits = []
    for c, at in enumerate(chunks):
        copies = [
            pltpu.make_async_copy(
                w_ref.at[at, theirs], w_theirs_ref.at[at, :], theirs_sems.at[c]
            ),
            pltpu.make_async_copy(
                prompts_ref.at[:, at], rows_ref.at[:prompt_rows, at], row_sems.at[c]
            ),
            pltpu.make_async_copy(
                hidden_ref.at[:, at], rows_ref.at[prompt_rows:, at], hidden_sems.at[c]
            ),
        ]
        for copy in copies:
            copy.start()
        waits.append(copies)
    scale_copy = pltpu.make_async_copy(scale_ref.at[:, theirs], scale_here_ref, scale_sem)
    head = pl.ds(0, w_mine_ref.shape[0])
    mine_copy = pltpu.make_async_copy(w_ref.at[head, mine], w_mine_ref, mine_sem)
    scale_copy.start()
    mine_copy.start()
    accumulate(
        rows_ref, w_theirs_ref, total_ref, out_ref, scale_here_ref, chunks, waits, scale_copy
    )
    mine_copy.wait()


def project_second(
    rows_ref,
    w_head_ref,
    w_ref,
    scale_ref,
    cache_ref,
    queries_ref,
    out_ref,
    cache_here_ref,
    queries_here_ref,
    w_tail_ref,
    total_ref,
    scale_here_ref,
    tail_sem,
    scale_sem,
    cache_sem,
    queries_sem,
):
    width = out_ref.shape[1]
    mine = pl.ds(pl.multiple_of(lax.axis_index("tp") * width, width), width)
    head = w_head_ref.shape[0]
    tail = pl.ds(head, w_tail_ref.shape[0])
    copies = [
        pltpu.make_async_copy(w_ref.at[tail, mine], w_tail_ref, tail_sem),
        pltpu.make_async_copy(scale_ref.at[:, mine], scale_here_ref, scale_sem),
        pltpu.make_async_copy(queries_ref, queries_here_ref, queries_sem),
        pltpu.make_async_copy(cache_ref, cache_here_ref, cache_sem),
    ]
    for copy in copies:
        copy.start()
    total_ref[...] = jnp.dot(rows_ref[:, :head], w_head_ref[...], preferred_element_type=F32)
    copies[0].wait()
    copies[1].wait()
    part = jnp.dot(rows_ref[:, head:], w_tail_ref[...], preferred_element_type=F32)
    out_ref[...] = ((total_ref[...] + part) * scale_here_ref[...]).astype(BF16)
    for copy in copies[2:]:
        copy.wait()


def split_bf16(x):
    high = x.astype(BF16).astype(F32)
    middle = (x - high).astype(BF16).astype(F32)
    return high, middle, (x - high - middle).astype(BF16).astype(F32)


def request_slots(target_ref, span_ref, row_count, padded):
    sections, requests = target_ref.shape
    position = lax.axis_index("section")
    target = target_ref[pl.ds(position, 1), :].astype(F32)
    span = span_ref[pl.ds(position, 1), :].astype(F32)
    diagonal = iota((padded, requests), 0) == iota((padded, requests), 1)
    target_col = jnp.sum(jnp.where(diagonal, target, 0.0), axis=1, keepdims=True)
    span_col = jnp.sum(jnp.where(diagonal, span, 0.0), axis=1, keepdims=True)
    section_row = jnp.zeros_like(target)
    section_col = jnp.zeros_like(target_col)
    for s in range(1, sections):
        section_row = section_row + (target >= s * row_count).astype(F32)
        section_col = section_col + (target_col >= s * row_count).astype(F32)
    before = (section_row == section_col) & (
        iota((padded, requests), 1) < iota((padded, requests), 0)
    )
    rank_col = jnp.sum(before.astype(F32), axis=1, keepdims=True).astype(jnp.int32)
    real = iota((padded, 1), 0) < requests
    slot_col = jnp.where(real, section_col.astype(jnp.int32) * CAP + rank_col, -1)
    return slot_col, span_col.astype(jnp.int32)


def attend_arrived(
    target_ref, span_ref, mine_ref, other_ref, asked_ref, out_ref, *, row_count
):
    sections, requests = target_ref.shape
    slots = sections * CAP
    padded = -(-requests // 16) * 16
    prompt_rows = mine_ref.shape[0] - row_count
    span_rows = prompt_rows // requests
    kv_heads = mine_ref.shape[1] // (2 * HD)
    group = asked_ref.shape[2] // (kv_heads * HD)
    slot_col, span_col = request_slots(target_ref, span_ref, row_count, padded)
    slot_of = one_hot((padded, slots), 1, slot_col)
    key = iota((padded, prompt_rows), 1) - iota((padded, prompt_rows), 0) * span_rows
    bias = jnp.where((key >= 0) & (key < span_col), 0.0, MASKED)
    asked = jnp.concatenate([asked_ref[s].astype(F32) for s in range(sections)], axis=0).astype(BF16)
    rows = jnp.dot(slot_of, asked, preferred_element_type=F32).astype(BF16)
    kv = (
        mine_ref[:prompt_rows, :].astype(F32) + other_ref[:prompt_rows, :].astype(F32)
    ).astype(BF16)
    scores = []
    for h in range(kv_heads):
        stacked = jnp.concatenate(
            [rows[:, (h * group + i) * HD : (h * group + i + 1) * HD] for i in range(group)],
            axis=0,
        )
        keys = kv[:, h * 2 * HD : (h * 2 + 1) * HD]
        scores.append(
            lax.dot_general(
                stacked, keys, (((1,), (1,)), ((), ())), preferred_element_type=F32
            )
        )
    scores = [
        x.reshape(group, padded, prompt_rows) * LOG2_SCALE + bias[None] for x in scores
    ]
    largest = [jnp.max(x, axis=2, keepdims=True) for x in scores]
    weights = [jnp.exp2(x - y) for x, y in zip(scores, largest)]
    totals = [jnp.sum(x, axis=2, keepdims=True) for x in weights]
    lane = iota((padded, STATS), 1)
    lse = jnp.zeros((padded, STATS), F32)
    pieces = []
    for h in range(kv_heads):
        values = jnp.dot(
            weights[h].reshape(group * padded, prompt_rows).astype(BF16),
            kv[:, (h * 2 + 1) * HD : (h * 2 + 2) * HD],
            preferred_element_type=F32,
        ).reshape(group, padded, HD)
        values = values / totals[h]
        head_lse = largest[h] + jnp.log2(totals[h])
        for i in range(group):
            pieces.append(values[i])
            lse = jnp.where(lane == h * group + i, head_lse[i], lse)
    result = jnp.concatenate(pieces + list(split_bf16(lse)), axis=1).astype(BF16)
    answers = lax.dot_general(slot_of, result, TRANSPOSED, preferred_element_type=F32).astype(BF16)
    for s in range(sections):
        out_ref[s] = answers[s * CAP : (s + 1) * CAP]


def attend_cache(
    queries_ref,
    cache_ref,
    len_ref,
    mine_ref,
    other_ref,
    pick_ref,
    after_ref,
    out_ref,
    slot_out_ref,
    slot_lse_ref,
    *,
    block_rows,
):
    row_count, cache_rows, width = cache_ref.shape
    kv_heads = width // (2 * HD)
    group = queries_ref.shape[1] // (kv_heads * HD)
    unit = 8
    keys_of = unit * cache_rows
    first_row = pl.multiple_of(pl.program_id(0) * block_rows, block_rows)
    block = pl.ds(first_row, block_rows)
    own_block = pl.ds(first_row + (mine_ref.shape[0] - row_count), block_rows)
    queries = queries_ref[block, :].astype(F32)
    own = mine_ref[own_block, :].astype(F32) + other_ref[own_block, :].astype(F32)
    own = own.astype(BF16).astype(F32)
    key = iota((unit, keys_of), 1) - iota((unit, keys_of), 0) * cache_rows
    lengths = len_ref[...].astype(F32)
    lane = iota((unit, STATS), 1)
    ones = jnp.ones((keys_of, HD), BF16)
    units = range(block_rows // unit)

    def rows_of(u):
        return pl.ds(first_row + u * unit, unit)

    pairs = [(u, h) for u in units for h in range(kv_heads)]
    bias = []
    for u in units:
        row = iota((unit, row_count), 0) + (first_row + u * unit)
        length = jnp.sum(
            jnp.where(iota((unit, row_count), 1) == row, lengths, 0.0), axis=1, keepdims=True
        ).astype(jnp.int32)
        bias.append(jnp.where((key >= 0) & (key < length), 0.0, MASKED))
    q, scores, own_scores = [], [], []
    for u, h in pairs:
        at = slice(u * unit, (u + 1) * unit)
        q.append(
            jnp.stack(
                [
                    queries[at, (h * group + i) * HD : (h * group + i + 1) * HD]
                    for i in range(group)
                ],
                axis=0,
            )
        )
        keys = cache_ref[rows_of(u), :, h * 2 * HD : (h * 2 + 1) * HD].reshape(keys_of, HD)
        scores.append(
            lax.dot_general(
                q[-1].reshape(group * unit, HD).astype(BF16),
                keys,
                (((1,), (1,)), ((), ())),
                preferred_element_type=F32,
            ).reshape(group, unit, keys_of)
        )
    for n, (u, h) in enumerate(pairs):
        at = slice(u * unit, (u + 1) * unit)
        own_key = own[at, h * 2 * HD : (h * 2 + 1) * HD]
        own_scores.append(jnp.sum(q[n] * own_key[None], axis=2, keepdims=True) * LOG2_SCALE)
    scores = [scores[n] * LOG2_SCALE + bias[u][None] for n, (u, h) in enumerate(pairs)]
    largest = [
        jnp.maximum(jnp.max(x, axis=2, keepdims=True), y) for x, y in zip(scores, own_scores)
    ]
    weights = [jnp.exp2(x - y).astype(BF16) for x, y in zip(scores, largest)]
    own_weights = [jnp.exp2(x - y) for x, y in zip(own_scores, largest)]
    sums = []
    for n, (u, h) in enumerate(pairs):
        at = slice(u * unit, (u + 1) * unit)
        values = cache_ref[rows_of(u), :, (h * 2 + 1) * HD : (h * 2 + 2) * HD].reshape(keys_of, HD)
        sums.append(
            jnp.dot(
                weights[n].reshape(group * unit, keys_of),
                jnp.concatenate([values, ones], axis=1),
                preferred_element_type=F32,
            ).reshape(group, unit, 2 * HD)
        )
    pieces = [[] for _ in units]
    stats = [jnp.zeros((unit, STATS), F32) for _ in units]
    for n, (u, h) in enumerate(pairs):
        at = slice(u * unit, (u + 1) * unit)
        own_value = own[at, (h * 2 + 1) * HD : (h * 2 + 2) * HD]
        total = sums[n][:, :, HD:] + own_weights[n]
        result = (sums[n][:, :, :HD] + own_weights[n] * own_value[None]) / total
        lse = largest[n] + jnp.log2(total)
        for i in range(group):
            pieces[u].append(result[i])
            stats[u] = jnp.where(lane == h * group + i, lse[i], stats[u])
    out = jnp.concatenate([jnp.concatenate(x, axis=1) for x in pieces], axis=0).astype(BF16)
    out_ref[block, :] = out
    pick = pick_ref[...]
    here = iota((row_count, block_rows), 0) == iota((row_count, block_rows), 1) + first_row
    pick = jnp.dot(pick, here.astype(F32).astype(BF16), preferred_element_type=F32).astype(BF16)
    slot_out = jnp.dot(pick, out, preferred_element_type=F32)
    lse = jnp.concatenate(stats, axis=0)
    slot_lse = sum(
        jnp.dot(pick, part.astype(BF16), preferred_element_type=F32) for part in split_bf16(lse)
    )

    @pl.when(pl.program_id(0) == 0)
    def _():
        slot_out_ref[...] = slot_out
        slot_lse_ref[...] = slot_lse

    @pl.when(pl.program_id(0) > 0)
    def _():
        slot_out_ref[...] += slot_out
        slot_lse_ref[...] += slot_lse


def merge(pick_ref, cached_ref, slot_out_ref, slot_lse_ref, arrived_ref, out_ref):
    width = cached_ref.shape[1]
    pick = pick_ref[...]
    arrived = jnp.concatenate([arrived_ref[s].astype(F32) for s in range(arrived_ref.shape[0])], axis=0)
    arrived_lse = (
        arrived[:, width : width + STATS]
        + arrived[:, width + STATS : width + 2 * STATS]
        + arrived[:, width + 2 * STATS :]
    )
    cached_lse = slot_lse_ref[...]
    largest = jnp.maximum(cached_lse, arrived_lse)
    cached_weight = jnp.exp2(cached_lse - largest)
    arrived_weight = jnp.exp2(arrived_lse - largest)
    total = cached_weight + arrived_weight
    cached_weight = cached_weight / total
    arrived_weight = arrived_weight / total
    has = lax.dot_general(
        pick, jnp.ones((pick.shape[0], HD), BF16), TRANSPOSED, preferred_element_type=F32
    )
    for i in range(width // HD):
        at = slice(i * HD, (i + 1) * HD)
        merged = (
            slot_out_ref[:, at] * cached_weight[:, i : i + 1]
            + arrived[:, at] * arrived_weight[:, i : i + 1]
        )
        placed = lax.dot_general(
            pick, merged.astype(BF16), TRANSPOSED, preferred_element_type=F32
        )
        out_ref[:, at] = jnp.where(has > 0.5, placed, cached_ref[:, at].astype(F32)).astype(BF16)


def compiler_params(megabytes):
    return pltpu.CompilerParams(vmem_limit_bytes=megabytes * 1024 * 1024)


RESIDENT = pl.BlockSpec(memory_space=pltpu.VMEM)
REMAINS = pl.BlockSpec(memory_space=pl.ANY)


def in_vmem(x):
    return pltpu.with_memory_space_constraint(x, pltpu.VMEM)


def in_hbm(x):
    return pltpu.with_memory_space_constraint(x, pltpu.HBM)


def shards(
    prompts, decode_hidden, queries, kv_cache, cache_len, span_len, target_row, w_kv, kv_scale
):
    row_count = decode_hidden.shape[0]
    prompt_rows, features = prompts.shape
    sections = lax.axis_size("section")
    local_width = kv_cache.shape[2]
    query_width = queries.shape[1]
    slots = sections * CAP
    all_rows = prompt_rows + row_count
    scale = kv_scale.reshape(1, -1)
    lengths = cache_len.reshape(1, -1)

    pick, asked = pl.pallas_call(
        select_queries,
        in_specs=[RESIDENT, RESIDENT],
        out_specs=[RESIDENT] * 2,
        out_shape=[
            pltpu.VMEM((slots, row_count), BF16),
            pltpu.VMEM((sections, CAP, query_width), BF16),
        ],
        compiler_params=compiler_params(16),
        name="select_queries",
    )(in_hbm(target_row), in_hbm(queries))
    asked = lax.all_to_all(asked, "section", 0, 0)

    edges = (0, 256, 768, 1536, 2560, 4096, features)
    count = len(edges) - 1
    head = features // 3
    theirs, rows, w_head = pl.pallas_call(
        functools.partial(project_first, edges=edges),
        in_specs=[REMAINS] * 5,
        out_specs=[RESIDENT, RESIDENT, RESIDENT],
        scratch_shapes=[
            pltpu.VMEM((features, local_width), BF16),
            pltpu.VMEM((all_rows, local_width), F32),
            pltpu.VMEM((1, local_width), F32),
            pltpu.SemaphoreType.DMA((count,)),
            pltpu.SemaphoreType.DMA((count,)),
            pltpu.SemaphoreType.DMA((count,)),
            pltpu.SemaphoreType.DMA(()),
            pltpu.SemaphoreType.DMA(()),
        ],
        out_shape=[
            pltpu.VMEM((all_rows, local_width), BF16),
            pltpu.VMEM((all_rows, features), BF16),
            pltpu.VMEM((head, local_width), BF16),
        ],
        compiler_params=compiler_params(16),
        name="project_first",
    )(in_hbm(prompts), in_hbm(decode_hidden), in_hbm(w_kv), in_hbm(scale), in_vmem(asked))
    other = lax.ppermute(theirs, "tp", [(0, 1), (1, 0)])
    mine, cache_here, queries_here = pl.pallas_call(
        project_second,
        in_specs=[RESIDENT, RESIDENT] + [REMAINS] * 4,
        out_specs=[RESIDENT, RESIDENT, RESIDENT],
        scratch_shapes=[
            pltpu.VMEM((features - head, local_width), BF16),
            pltpu.VMEM((all_rows, local_width), F32),
            pltpu.VMEM((1, local_width), F32),
            pltpu.SemaphoreType.DMA(()),
            pltpu.SemaphoreType.DMA(()),
            pltpu.SemaphoreType.DMA(()),
            pltpu.SemaphoreType.DMA(()),
        ],
        out_shape=[
            pltpu.VMEM((all_rows, local_width), BF16),
            pltpu.VMEM(kv_cache.shape, BF16),
            pltpu.VMEM(queries.shape, BF16),
        ],
        compiler_params=compiler_params(16),
        name="project_second",
    )(
        in_vmem(rows),
        in_vmem(w_head),
        in_hbm(w_kv),
        in_hbm(scale),
        in_hbm(kv_cache),
        in_hbm(queries),
    )

    answer_width = query_width + 3 * STATS
    answers = pl.pallas_call(
        functools.partial(attend_arrived, row_count=row_count),
        in_specs=[RESIDENT] * 5,
        out_specs=RESIDENT,
        out_shape=pltpu.VMEM((sections, CAP, answer_width), BF16),
        compiler_params=compiler_params(24),
        name="attend_arrived",
    )(in_hbm(target_row), in_hbm(span_len), in_vmem(mine), in_vmem(other), in_vmem(asked))
    after = answers
    answers = lax.all_to_all(answers, "section", 0, 0)

    block = 32
    cached, slot_out, slot_lse = pl.pallas_call(
        functools.partial(attend_cache, block_rows=block),
        grid=(row_count // block,),
        in_specs=[RESIDENT] * 6 + [REMAINS],
        out_specs=[RESIDENT] * 3,
        out_shape=[
            pltpu.VMEM((row_count, query_width), BF16),
            pltpu.VMEM((slots, query_width), F32),
            pltpu.VMEM((slots, STATS), F32),
        ],
        compiler_params=compiler_params(24),
        name="attend_cache",
    )(
        in_vmem(queries_here),
        in_vmem(cache_here),
        in_hbm(lengths),
        in_vmem(mine),
        in_vmem(other),
        in_vmem(pick),
        in_vmem(after),
    )

    return pl.pallas_call(
        merge,
        in_specs=[RESIDENT] * 5,
        out_specs=RESIDENT,
        out_shape=jax.ShapeDtypeStruct((row_count, query_width), BF16),
        compiler_params=compiler_params(24),
        name="merge",
    )(*map(in_vmem, (pick, cached, slot_out, slot_lse, answers)))


def solution(mesh):
    in_specs = (
        P(("groups", "section"), "tp"),
        P(("groups", "section"), "tp"),
        P(("groups", "section"), "tp"),
        P(("groups", "section"), None, "tp"),
        P(("groups", "section")),
        P("groups", None),
        P("groups", None),
        P("tp", None),
        P(),
    )
    out_specs = P(("groups", "section"), "tp")
    return jax.shard_map(shards, mesh=mesh, in_specs=in_specs, out_specs=out_specs, check_vma=False)
```

```python
import functools
import math

import jax
import jax.numpy as jnp
from jax import lax
from jax.experimental import pallas as pl
from jax.experimental.pallas import tpu as pltpu
from jax.sharding import PartitionSpec as P

HD = 128
CAP = 2
STATS = 128
MASKED = -1e30
LOG2_SCALE = HD ** (-0.5) * math.log2(math.e)
F32 = jnp.float32
BF16 = jnp.bfloat16
TRANSPOSED = (((0,), (0,)), ((), ()))


def iota(shape, dim):
    return lax.broadcasted_iota(jnp.int32, shape, dim)


def one_hot(shape, dim, index):
    return (iota(shape, dim) == index).astype(F32).astype(BF16)


def select_queries(target_ref, queries_ref, pick_ref, asked_ref):
    sections, requests = target_ref.shape
    row_count = queries_ref.shape[0]
    slots = sections * CAP
    position = lax.axis_index("section")
    slot_id = iota((slots, requests), 0)
    table = jnp.zeros((slots, requests), jnp.int32)
    for k in range(sections):
        mine = (slot_id >= k * CAP) & (slot_id < (k + 1) * CAP)
        table = jnp.where(mine, target_ref[k : k + 1, :], table)
    local = table - position * row_count
    here = (local >= 0) & (local < row_count)
    square = (requests, requests)
    earlier = jnp.dot(
        here.astype(F32).astype(BF16),
        (iota(square, 0) < iota(square, 1)).astype(F32).astype(BF16),
        preferred_element_type=F32,
    )
    chosen = here & (earlier == lax.rem(slot_id, CAP).astype(F32))
    row = jnp.max(jnp.where(chosen, local.astype(F32), -1.0), axis=1, keepdims=True)
    pick = one_hot((slots, row_count), 1, row.astype(jnp.int32))
    pick_ref[...] = pick
    asked = jnp.dot(pick, queries_ref[...], preferred_element_type=F32).astype(BF16)
    for k in range(sections):
        asked_ref[k] = asked[k * CAP : (k + 1) * CAP]


def spans(edges):
    return [slice(a, b) for a, b in zip(edges[:-1], edges[1:])]


def accumulate(
    rows_ref, w_ref, total_ref, out_ref, scale_ref, chunks, block, waits, scale_copy
):
    for c, at in enumerate(chunks):
        for copy in waits[c]:
            copy.wait()
        if c == len(chunks) - 1:
            scale_copy.wait()
        for m in spans(range(0, rows_ref.shape[0] + 1, block)):
            part = jnp.dot(rows_ref[m, at], w_ref[at, :], preferred_element_type=F32)
            if c == 0:
                total_ref[m, :] = part
            elif c < len(chunks) - 1:
                total_ref[m, :] += part
            else:
                out_ref[m, :] = ((total_ref[m, :] + part) * scale_ref[...]).astype(BF16)


def project_first(
    prompts_ref,
    hidden_ref,
    w_ref,
    scale_ref,
    after_ref,
    out_ref,
    rows_ref,
    w_mine_ref,
    w_theirs_ref,
    total_ref,
    scale_here_ref,
    row_sems,
    hidden_sems,
    theirs_sems,
    mine_sem,
    scale_sem,
    *,
    edges,
    block,
):
    prompt_rows = prompts_ref.shape[0]
    width = out_ref.shape[1]
    tp = lax.axis_index("tp")
    theirs = pl.ds(pl.multiple_of((1 - tp) * width, width), width)
    half = w_mine_ref.shape[1]
    mine = pl.ds(pl.multiple_of(tp * width, half), half)
    chunks = spans(edges)
    waits = []
    for c, at in enumerate(chunks):
        copies = [
            pltpu.make_async_copy(
                w_ref.at[at, theirs], w_theirs_ref.at[at, :], theirs_sems.at[c]
            ),
            pltpu.make_async_copy(
                prompts_ref.at[:, at], rows_ref.at[:prompt_rows, at], row_sems.at[c]
            ),
            pltpu.make_async_copy(
                hidden_ref.at[:, at], rows_ref.at[prompt_rows:, at], hidden_sems.at[c]
            ),
        ]
        for copy in copies:
            copy.start()
        waits.append(copies)
    scale_copy = pltpu.make_async_copy(scale_ref.at[:, theirs], scale_here_ref, scale_sem)
    mine_copy = pltpu.make_async_copy(w_ref.at[:, mine], w_mine_ref, mine_sem)
    scale_copy.start()
    mine_copy.start()
    accumulate(
        rows_ref, w_theirs_ref, total_ref, out_ref, scale_here_ref, chunks, block, waits, scale_copy
    )
    mine_copy.wait()


def project_second(
    rows_ref,
    w_head_ref,
    w_ref,
    scale_ref,
    out_ref,
    w_tail_ref,
    scale_here_ref,
    tail_sem,
    scale_sem,
    *,
    block,
):
    width = out_ref.shape[1]
    half = w_head_ref.shape[1]
    tp = lax.axis_index("tp")
    mine = pl.ds(pl.multiple_of(tp * width, width), width)
    tail = pl.ds(pl.multiple_of(tp * width + half, half), half)
    tail_copy = pltpu.make_async_copy(w_ref.at[:, tail], w_tail_ref, tail_sem)
    scale_copy = pltpu.make_async_copy(scale_ref.at[:, mine], scale_here_ref, scale_sem)
    tail_copy.start()
    scale_copy.start()
    for part_ref, copy, first in ((w_head_ref, scale_copy, 0), (w_tail_ref, tail_copy, half)):
        at = slice(first, first + half)
        if copy is tail_copy:
            copy.wait()
        for m in spans(range(0, rows_ref.shape[0] + 1, block)):
            total = jnp.dot(rows_ref[m, :], part_ref[...], preferred_element_type=F32)
            if copy is scale_copy and m.start == 0:
                copy.wait()
            out_ref[m, at] = (total * scale_here_ref[:, at]).astype(BF16)


def split_bf16(x):
    high = x.astype(BF16).astype(F32)
    middle = (x - high).astype(BF16).astype(F32)
    return high, middle, (x - high - middle).astype(BF16).astype(F32)


def request_slots(target_ref, span_ref, row_count, padded):
    sections, requests = target_ref.shape
    position = lax.axis_index("section")
    target = target_ref[pl.ds(position, 1), :].astype(F32)
    span = span_ref[pl.ds(position, 1), :].astype(F32)
    diagonal = iota((padded, requests), 0) == iota((padded, requests), 1)
    target_col = jnp.sum(jnp.where(diagonal, target, 0.0), axis=1, keepdims=True)
    span_col = jnp.sum(jnp.where(diagonal, span, 0.0), axis=1, keepdims=True)
    section_row = jnp.zeros_like(target)
    section_col = jnp.zeros_like(target_col)
    for s in range(1, sections):
        section_row = section_row + (target >= s * row_count).astype(F32)
        section_col = section_col + (target_col >= s * row_count).astype(F32)
    before = (section_row == section_col) & (
        iota((padded, requests), 1) < iota((padded, requests), 0)
    )
    rank_col = jnp.sum(before.astype(F32), axis=1, keepdims=True).astype(jnp.int32)
    real = iota((padded, 1), 0) < requests
    slot_col = jnp.where(real, section_col.astype(jnp.int32) * CAP + rank_col, -1)
    return slot_col, span_col.astype(jnp.int32)


def attend_arrived(
    target_ref, span_ref, mine_ref, other_ref, asked_ref, out_ref, *, row_count
):
    sections, requests = target_ref.shape
    slots = sections * CAP
    padded = -(-requests // 16) * 16
    prompt_rows = mine_ref.shape[0] - row_count
    span_rows = prompt_rows // requests
    kv_heads = mine_ref.shape[1] // (2 * HD)
    group = asked_ref.shape[2] // (kv_heads * HD)
    slot_col, span_col = request_slots(target_ref, span_ref, row_count, padded)
    slot_of = one_hot((padded, slots), 1, slot_col)
    key = iota((padded, prompt_rows), 1) - iota((padded, prompt_rows), 0) * span_rows
    bias = jnp.where((key >= 0) & (key < span_col), 0.0, MASKED)
    asked = jnp.concatenate([asked_ref[s].astype(F32) for s in range(sections)], axis=0).astype(BF16)
    rows = jnp.dot(slot_of, asked, preferred_element_type=F32).astype(BF16)
    kv = (
        mine_ref[:prompt_rows, :].astype(F32) + other_ref[:prompt_rows, :].astype(F32)
    ).astype(BF16)
    scores = []
    for h in range(kv_heads):
        stacked = jnp.concatenate(
            [rows[:, (h * group + i) * HD : (h * group + i + 1) * HD] for i in range(group)],
            axis=0,
        )
        keys = kv[:, h * 2 * HD : (h * 2 + 1) * HD]
        scores.append(
            lax.dot_general(
                stacked, keys, (((1,), (1,)), ((), ())), preferred_element_type=F32
            )
        )
    scores = [
        x.reshape(group, padded, prompt_rows) * LOG2_SCALE + bias[None] for x in scores
    ]
    largest = [jnp.max(x, axis=2, keepdims=True) for x in scores]
    weights = [jnp.exp2(x - y) for x, y in zip(scores, largest)]
    totals = [jnp.sum(x, axis=2, keepdims=True) for x in weights]
    lane = iota((padded, STATS), 1)
    lse = jnp.zeros((padded, STATS), F32)
    pieces = []
    for h in range(kv_heads):
        values = jnp.dot(
            weights[h].reshape(group * padded, prompt_rows).astype(BF16),
            kv[:, (h * 2 + 1) * HD : (h * 2 + 2) * HD],
            preferred_element_type=F32,
        ).reshape(group, padded, HD)
        values = values / totals[h]
        head_lse = largest[h] + jnp.log2(totals[h])
        for i in range(group):
            pieces.append(values[i])
            lse = jnp.where(lane == h * group + i, head_lse[i], lse)
    result = jnp.concatenate(pieces + list(split_bf16(lse)), axis=1).astype(BF16)
    answers = lax.dot_general(slot_of, result, TRANSPOSED, preferred_element_type=F32).astype(BF16)
    for s in range(sections):
        out_ref[s] = answers[s * CAP : (s + 1) * CAP]


def attend_cache(
    queries_ref,
    cache_ref,
    len_ref,
    mine_ref,
    other_ref,
    pick_ref,
    after_ref,
    out_ref,
    slot_out_ref,
    slot_lse_ref,
    *,
    block_rows,
):
    cache_rows, width = cache_ref.shape[1:]
    row_count = len_ref.shape[1]
    kv_heads = width // (2 * HD)
    group = queries_ref.shape[1] // (kv_heads * HD)
    unit = 8
    keys_of = unit * cache_rows
    first_row = pl.multiple_of(pl.program_id(0) * block_rows, block_rows)
    block = pl.ds(first_row, block_rows)
    own_block = pl.ds(first_row + (mine_ref.shape[0] - row_count), block_rows)
    queries = queries_ref[...].astype(F32)
    own = mine_ref[own_block, :].astype(F32) + other_ref[own_block, :].astype(F32)
    own = own.astype(BF16).astype(F32)
    key = iota((unit, keys_of), 1) - iota((unit, keys_of), 0) * cache_rows
    lengths = len_ref[...].astype(F32)
    lane = iota((unit, STATS), 1)
    ones = jnp.ones((keys_of, HD), BF16)
    units = range(block_rows // unit)

    def rows_of(u):
        return slice(u * unit, (u + 1) * unit)

    pairs = [(u, h) for u in units for h in range(kv_heads)]
    bias = []
    for u in units:
        row = iota((unit, row_count), 0) + (first_row + u * unit)
        length = jnp.sum(
            jnp.where(iota((unit, row_count), 1) == row, lengths, 0.0), axis=1, keepdims=True
        ).astype(jnp.int32)
        bias.append(jnp.where((key >= 0) & (key < length), 0.0, MASKED))
    q, scores, own_scores = [], [], []
    for u, h in pairs:
        at = slice(u * unit, (u + 1) * unit)
        q.append(
            jnp.stack(
                [
                    queries[at, (h * group + i) * HD : (h * group + i + 1) * HD]
                    for i in range(group)
                ],
                axis=0,
            )
        )
        keys = cache_ref[rows_of(u), :, h * 2 * HD : (h * 2 + 1) * HD].reshape(keys_of, HD)
        scores.append(
            lax.dot_general(
                q[-1].reshape(group * unit, HD).astype(BF16),
                keys,
                (((1,), (1,)), ((), ())),
                preferred_element_type=F32,
            ).reshape(group, unit, keys_of)
        )
    for n, (u, h) in enumerate(pairs):
        at = slice(u * unit, (u + 1) * unit)
        own_key = own[at, h * 2 * HD : (h * 2 + 1) * HD]
        own_scores.append(jnp.sum(q[n] * own_key[None], axis=2, keepdims=True) * LOG2_SCALE)
    scores = [scores[n] * LOG2_SCALE + bias[u][None] for n, (u, h) in enumerate(pairs)]
    largest = [
        jnp.maximum(jnp.max(x, axis=2, keepdims=True), y) for x, y in zip(scores, own_scores)
    ]
    weights = [jnp.exp2(x - y).astype(BF16) for x, y in zip(scores, largest)]
    own_weights = [jnp.exp2(x - y) for x, y in zip(own_scores, largest)]
    sums = []
    for n, (u, h) in enumerate(pairs):
        at = slice(u * unit, (u + 1) * unit)
        values = cache_ref[rows_of(u), :, (h * 2 + 1) * HD : (h * 2 + 2) * HD].reshape(keys_of, HD)
        sums.append(
            jnp.dot(
                weights[n].reshape(group * unit, keys_of),
                jnp.concatenate([values, ones], axis=1),
                preferred_element_type=F32,
            ).reshape(group, unit, 2 * HD)
        )
    pieces = [[] for _ in units]
    stats = [jnp.zeros((unit, STATS), F32) for _ in units]
    for n, (u, h) in enumerate(pairs):
        at = slice(u * unit, (u + 1) * unit)
        own_value = own[at, (h * 2 + 1) * HD : (h * 2 + 2) * HD]
        total = sums[n][:, :, HD:] + own_weights[n]
        result = (sums[n][:, :, :HD] + own_weights[n] * own_value[None]) / total
        lse = largest[n] + jnp.log2(total)
        for i in range(group):
            pieces[u].append(result[i])
            stats[u] = jnp.where(lane == h * group + i, lse[i], stats[u])
    out = jnp.concatenate([jnp.concatenate(x, axis=1) for x in pieces], axis=0).astype(BF16)
    out_ref[block, :] = out
    pick = pick_ref[...]
    here = iota((row_count, block_rows), 0) == iota((row_count, block_rows), 1) + first_row
    pick = jnp.dot(pick, here.astype(F32).astype(BF16), preferred_element_type=F32).astype(BF16)
    slot_out = jnp.dot(pick, out, preferred_element_type=F32)
    lse = jnp.concatenate(stats, axis=0)
    slot_lse = sum(
        jnp.dot(pick, part.astype(BF16), preferred_element_type=F32) for part in split_bf16(lse)
    )

    @pl.when(pl.program_id(0) == 0)
    def _():
        slot_out_ref[...] = slot_out
        slot_lse_ref[...] = slot_lse

    @pl.when(pl.program_id(0) > 0)
    def _():
        slot_out_ref[...] += slot_out
        slot_lse_ref[...] += slot_lse


def merge(pick_ref, cached_ref, slot_out_ref, slot_lse_ref, arrived_ref, out_ref):
    width = cached_ref.shape[1]
    pick = pick_ref[...]
    arrived = jnp.concatenate([arrived_ref[s].astype(F32) for s in range(arrived_ref.shape[0])], axis=0)
    arrived_lse = (
        arrived[:, width : width + STATS]
        + arrived[:, width + STATS : width + 2 * STATS]
        + arrived[:, width + 2 * STATS :]
    )
    cached_lse = slot_lse_ref[...]
    largest = jnp.maximum(cached_lse, arrived_lse)
    cached_weight = jnp.exp2(cached_lse - largest)
    arrived_weight = jnp.exp2(arrived_lse - largest)
    total = cached_weight + arrived_weight
    cached_weight = cached_weight / total
    arrived_weight = arrived_weight / total
    has = lax.dot_general(
        pick, jnp.ones((pick.shape[0], HD), BF16), TRANSPOSED, preferred_element_type=F32
    )
    for i in range(width // HD):
        at = slice(i * HD, (i + 1) * HD)
        merged = (
            slot_out_ref[:, at] * cached_weight[:, i : i + 1]
            + arrived[:, at] * arrived_weight[:, i : i + 1]
        )
        placed = lax.dot_general(
            pick, merged.astype(BF16), TRANSPOSED, preferred_element_type=F32
        )
        out_ref[:, at] = jnp.where(has > 0.5, placed, cached_ref[:, at].astype(F32)).astype(BF16)


def compiler_params(megabytes):
    return pltpu.CompilerParams(vmem_limit_bytes=megabytes * 1024 * 1024)


RESIDENT = pl.BlockSpec(memory_space=pltpu.VMEM)
REMAINS = pl.BlockSpec(memory_space=pl.ANY)


def in_vmem(x):
    return pltpu.with_memory_space_constraint(x, pltpu.VMEM)


def in_hbm(x):
    return pltpu.with_memory_space_constraint(x, pltpu.HBM)


def shards(
    prompts, decode_hidden, queries, kv_cache, cache_len, span_len, target_row, w_kv, kv_scale
):
    row_count = decode_hidden.shape[0]
    prompt_rows, features = prompts.shape
    sections = lax.axis_size("section")
    local_width = kv_cache.shape[2]
    query_width = queries.shape[1]
    slots = sections * CAP
    all_rows = prompt_rows + row_count
    scale = kv_scale.reshape(1, -1)
    lengths = cache_len.reshape(1, -1)

    pick, asked = pl.pallas_call(
        select_queries,
        in_specs=[RESIDENT, RESIDENT],
        out_specs=[RESIDENT] * 2,
        out_shape=[
            pltpu.VMEM((slots, row_count), BF16),
            pltpu.VMEM((sections, CAP, query_width), BF16),
        ],
        compiler_params=compiler_params(16),
        name="select_queries",
    )(in_hbm(target_row), in_hbm(queries))
    asked = lax.all_to_all(asked, "section", 0, 0)

    edges = (0, 256, 768, 1536, 2560, 4096, features)
    count = len(edges) - 1
    half = local_width // 2
    block = all_rows // 2
    cost = pl.CostEstimate(
        flops=2 * all_rows * features * local_width,
        bytes_accessed=2 * features * (all_rows + local_width),
        transcendentals=0,
    )
    theirs, rows, w_head = pl.pallas_call(
        functools.partial(project_first, edges=edges, block=block),
        in_specs=[REMAINS] * 5,
        out_specs=[RESIDENT, RESIDENT, RESIDENT],
        scratch_shapes=[
            pltpu.VMEM((features, local_width), BF16),
            pltpu.VMEM((all_rows, local_width), F32),
            pltpu.VMEM((1, local_width), F32),
            pltpu.SemaphoreType.DMA((count,)),
            pltpu.SemaphoreType.DMA((count,)),
            pltpu.SemaphoreType.DMA((count,)),
            pltpu.SemaphoreType.DMA(()),
            pltpu.SemaphoreType.DMA(()),
        ],
        out_shape=[
            pltpu.VMEM((all_rows, local_width), BF16),
            pltpu.VMEM((all_rows, features), BF16),
            pltpu.VMEM((features, half), BF16),
        ],
        compiler_params=compiler_params(16),
        cost_estimate=cost,
        name="project_first",
    )(in_hbm(prompts), in_hbm(decode_hidden), in_hbm(w_kv), in_hbm(scale), in_vmem(pick))
    other = lax.ppermute(theirs, "tp", [(0, 1), (1, 0)])
    mine = pl.pallas_call(
        functools.partial(project_second, block=block),
        in_specs=[RESIDENT, RESIDENT, REMAINS, REMAINS],
        out_specs=RESIDENT,
        scratch_shapes=[
            pltpu.VMEM((features, local_width - half), BF16),
            pltpu.VMEM((1, local_width), F32),
            pltpu.SemaphoreType.DMA(()),
            pltpu.SemaphoreType.DMA(()),
        ],
        out_shape=pltpu.VMEM((all_rows, local_width), BF16),
        compiler_params=compiler_params(16),
        cost_estimate=cost,
        name="project_second",
    )(in_vmem(rows), in_vmem(w_head), in_hbm(w_kv), in_hbm(scale))

    answer_width = query_width + 3 * STATS
    answers = pl.pallas_call(
        functools.partial(attend_arrived, row_count=row_count),
        in_specs=[RESIDENT] * 5,
        out_specs=RESIDENT,
        out_shape=pltpu.VMEM((sections, CAP, answer_width), BF16),
        compiler_params=compiler_params(24),
        name="attend_arrived",
    )(in_hbm(target_row), in_hbm(span_len), in_vmem(mine), in_vmem(other), in_vmem(asked))
    after = answers
    answers = lax.all_to_all(answers, "section", 0, 0)

    block = 32
    cached, slot_out, slot_lse = pl.pallas_call(
        functools.partial(attend_cache, block_rows=block),
        grid=(row_count // block,),
        in_specs=[
            pl.BlockSpec((block, query_width), lambda b: (b, 0)),
            pl.BlockSpec((block, *kv_cache.shape[1:]), lambda b: (b, 0, 0)),
        ]
        + [RESIDENT] * 4
        + [REMAINS],
        out_specs=[RESIDENT] * 3,
        out_shape=[
            pltpu.VMEM((row_count, query_width), BF16),
            pltpu.VMEM((slots, query_width), F32),
            pltpu.VMEM((slots, STATS), F32),
        ],
        compiler_params=compiler_params(24),
        name="attend_cache",
    )(
        in_hbm(queries),
        in_hbm(kv_cache),
        in_hbm(lengths),
        in_vmem(mine),
        in_vmem(other),
        in_vmem(pick),
        in_vmem(after),
    )

    return pl.pallas_call(
        merge,
        in_specs=[RESIDENT] * 5,
        out_specs=RESIDENT,
        out_shape=jax.ShapeDtypeStruct((row_count, query_width), BF16),
        compiler_params=compiler_params(24),
        name="merge",
    )(*map(in_vmem, (pick, cached, slot_out, slot_lse, answers)))


def solution(mesh):
    in_specs = (
        P(("groups", "section"), "tp"),
        P(("groups", "section"), "tp"),
        P(("groups", "section"), "tp"),
        P(("groups", "section"), None, "tp"),
        P(("groups", "section")),
        P("groups", None),
        P("groups", None),
        P("tp", None),
        P(),
    )
    out_specs = P(("groups", "section"), "tp")
    return jax.shard_map(shards, mesh=mesh, in_specs=in_specs, out_specs=out_specs, check_vma=False)
```

```python
import functools
import math

import jax
import jax.numpy as jnp
from jax import lax
from jax.experimental import pallas as pl
from jax.experimental.pallas import tpu as pltpu
from jax.sharding import PartitionSpec as P

HD = 128
CAP = 2
STATS = 128
MASKED = -1e30
LOG2_SCALE = HD ** (-0.5) * math.log2(math.e)
F32 = jnp.float32
BF16 = jnp.bfloat16
TRANSPOSED = (((0,), (0,)), ((), ()))


def iota(shape, dim):
    return lax.broadcasted_iota(jnp.int32, shape, dim)


def one_hot(shape, dim, index):
    return (iota(shape, dim) == index).astype(F32).astype(BF16)


def select_queries(target_ref, queries_ref, pick_ref, asked_ref):
    sections, requests = target_ref.shape
    row_count = queries_ref.shape[0]
    slots = sections * CAP
    position = lax.axis_index("section")
    slot_id = iota((slots, requests), 0)
    table = jnp.zeros((slots, requests), jnp.int32)
    for k in range(sections):
        mine = (slot_id >= k * CAP) & (slot_id < (k + 1) * CAP)
        table = jnp.where(mine, target_ref[k : k + 1, :], table)
    local = table - position * row_count
    here = (local >= 0) & (local < row_count)
    square = (requests, requests)
    earlier = jnp.dot(
        here.astype(F32).astype(BF16),
        (iota(square, 0) < iota(square, 1)).astype(F32).astype(BF16),
        preferred_element_type=F32,
    )
    chosen = here & (earlier == lax.rem(slot_id, CAP).astype(F32))
    row = jnp.max(jnp.where(chosen, local.astype(F32), -1.0), axis=1, keepdims=True)
    pick = one_hot((slots, row_count), 1, row.astype(jnp.int32))
    pick_ref[...] = pick
    asked = jnp.dot(pick, queries_ref[...], preferred_element_type=F32).astype(BF16)
    for k in range(sections):
        asked_ref[k] = asked[k * CAP : (k + 1) * CAP]


def spans(edges):
    return [slice(a, b) for a, b in zip(edges[:-1], edges[1:])]


def project(
    prompts_ref,
    hidden_ref,
    w_ref,
    scale_ref,
    after_ref,
    mine_ref,
    theirs_ref,
    rows_ref,
    w_here_ref,
    total_ref,
    row_sems,
    hidden_sems,
    w_sems,
    *,
    edges,
    block,
):
    prompt_rows = prompts_ref.shape[0]
    width = mine_ref.shape[1]
    chunks = spans(edges)
    waits = []
    for c, at in enumerate(chunks):
        copies = [
            pltpu.make_async_copy(w_ref.at[at, :], w_here_ref.at[at, :], w_sems.at[c]),
            pltpu.make_async_copy(
                prompts_ref.at[:, at], rows_ref.at[:prompt_rows, at], row_sems.at[c]
            ),
            pltpu.make_async_copy(
                hidden_ref.at[:, at], rows_ref.at[prompt_rows:, at], hidden_sems.at[c]
            ),
        ]
        for copy in copies:
            copy.start()
        waits.append(copies)
    for c, at in enumerate(chunks[:-1]):
        for copy in waits[c]:
            copy.wait()
        for m in spans(range(0, rows_ref.shape[0] + 1, block)):
            part = jnp.dot(rows_ref[m, at], w_here_ref[at, :], preferred_element_type=F32)
            if c == 0:
                total_ref[m, :] = part
            else:
                total_ref[m, :] += part
    for copy in waits[-1]:
        copy.wait()
    first = lax.axis_index("tp") == 0
    for m in spans(range(0, rows_ref.shape[0] + 1, block)):
        part = jnp.dot(
            rows_ref[m, chunks[-1]], w_here_ref[chunks[-1], :], preferred_element_type=F32
        )
        term = ((total_ref[m, :] + part) * scale_ref[...]).astype(BF16)
        low, high = term[:, :width], term[:, width:]
        mine_ref[m, :] = jnp.where(first, low, high)
        theirs_ref[m, :] = jnp.where(first, high, low)


def split_bf16(x):
    high = x.astype(BF16).astype(F32)
    middle = (x - high).astype(BF16).astype(F32)
    return high, middle, (x - high - middle).astype(BF16).astype(F32)


def request_slots(target_ref, span_ref, row_count, padded):
    sections, requests = target_ref.shape
    position = lax.axis_index("section")
    target = target_ref[pl.ds(position, 1), :].astype(F32)
    span = span_ref[pl.ds(position, 1), :].astype(F32)
    diagonal = iota((padded, requests), 0) == iota((padded, requests), 1)
    target_col = jnp.sum(jnp.where(diagonal, target, 0.0), axis=1, keepdims=True)
    span_col = jnp.sum(jnp.where(diagonal, span, 0.0), axis=1, keepdims=True)
    section_row = jnp.zeros_like(target)
    section_col = jnp.zeros_like(target_col)
    for s in range(1, sections):
        section_row = section_row + (target >= s * row_count).astype(F32)
        section_col = section_col + (target_col >= s * row_count).astype(F32)
    before = (section_row == section_col) & (
        iota((padded, requests), 1) < iota((padded, requests), 0)
    )
    rank_col = jnp.sum(before.astype(F32), axis=1, keepdims=True).astype(jnp.int32)
    real = iota((padded, 1), 0) < requests
    slot_col = jnp.where(real, section_col.astype(jnp.int32) * CAP + rank_col, -1)
    return slot_col, span_col.astype(jnp.int32)


def attend_arrived(
    target_ref, span_ref, mine_ref, other_ref, asked_ref, after_ref, out_ref, *, row_count
):
    sections, requests = target_ref.shape
    slots = sections * CAP
    padded = -(-requests // 16) * 16
    prompt_rows = mine_ref.shape[0] - row_count
    span_rows = prompt_rows // requests
    kv_heads = mine_ref.shape[1] // (2 * HD)
    group = asked_ref.shape[2] // (kv_heads * HD)
    slot_col, span_col = request_slots(target_ref, span_ref, row_count, padded)
    slot_of = one_hot((padded, slots), 1, slot_col)
    key = iota((padded, prompt_rows), 1) - iota((padded, prompt_rows), 0) * span_rows
    bias = jnp.where((key >= 0) & (key < span_col), 0.0, MASKED)
    asked = jnp.concatenate([asked_ref[s].astype(F32) for s in range(sections)], axis=0).astype(BF16)
    rows = jnp.dot(slot_of, asked, preferred_element_type=F32).astype(BF16)
    kv = (
        mine_ref[:prompt_rows, :].astype(F32) + other_ref[:prompt_rows, :].astype(F32)
    ).astype(BF16)
    scores = []
    for h in range(kv_heads):
        stacked = jnp.concatenate(
            [rows[:, (h * group + i) * HD : (h * group + i + 1) * HD] for i in range(group)],
            axis=0,
        )
        keys = kv[:, h * 2 * HD : (h * 2 + 1) * HD]
        scores.append(
            lax.dot_general(
                stacked, keys, (((1,), (1,)), ((), ())), preferred_element_type=F32
            )
        )
    scores = [
        x.reshape(group, padded, prompt_rows) * LOG2_SCALE + bias[None] for x in scores
    ]
    largest = [jnp.max(x, axis=2, keepdims=True) for x in scores]
    weights = [jnp.exp2(x - y) for x, y in zip(scores, largest)]
    totals = [jnp.sum(x, axis=2, keepdims=True) for x in weights]
    lane = iota((padded, STATS), 1)
    lse = jnp.zeros((padded, STATS), F32)
    pieces = []
    for h in range(kv_heads):
        values = jnp.dot(
            weights[h].reshape(group * padded, prompt_rows).astype(BF16),
            kv[:, (h * 2 + 1) * HD : (h * 2 + 2) * HD],
            preferred_element_type=F32,
        ).reshape(group, padded, HD)
        values = values / totals[h]
        head_lse = largest[h] + jnp.log2(totals[h])
        for i in range(group):
            pieces.append(values[i])
            lse = jnp.where(lane == h * group + i, head_lse[i], lse)
    result = jnp.concatenate(pieces + list(split_bf16(lse)), axis=1).astype(BF16)
    answers = lax.dot_general(slot_of, result, TRANSPOSED, preferred_element_type=F32).astype(BF16)
    for s in range(sections):
        out_ref[s] = answers[s * CAP : (s + 1) * CAP]


def attend_cache(
    queries_ref,
    cache_ref,
    len_ref,
    mine_ref,
    other_ref,
    pick_ref,
    after_ref,
    out_ref,
    slot_out_ref,
    slot_lse_ref,
    *,
    block_rows,
    first_block,
):
    cache_rows, width = cache_ref.shape[1:]
    row_count = len_ref.shape[1]
    kv_heads = width // (2 * HD)
    group = queries_ref.shape[1] // (kv_heads * HD)
    unit = 8
    keys_of = unit * cache_rows
    step = pl.program_id(0)
    block = pl.ds(pl.multiple_of(step * block_rows, block_rows), block_rows)
    first_row = pl.multiple_of((step + first_block) * block_rows, block_rows)
    own_block = pl.ds(first_row + (mine_ref.shape[0] - row_count), block_rows)
    queries = queries_ref[...].astype(F32)
    own = mine_ref[own_block, :].astype(F32) + other_ref[own_block, :].astype(F32)
    own = own.astype(BF16).astype(F32)
    key = iota((unit, keys_of), 1) - iota((unit, keys_of), 0) * cache_rows
    lengths = len_ref[...].astype(F32)
    lane = iota((unit, STATS), 1)
    ones = jnp.ones((keys_of, HD), BF16)
    units = range(block_rows // unit)

    def rows_of(u):
        return slice(u * unit, (u + 1) * unit)

    pairs = [(u, h) for u in units for h in range(kv_heads)]
    bias = []
    for u in units:
        row = iota((unit, row_count), 0) + (first_row + u * unit)
        length = jnp.sum(
            jnp.where(iota((unit, row_count), 1) == row, lengths, 0.0), axis=1, keepdims=True
        ).astype(jnp.int32)
        bias.append(jnp.where((key >= 0) & (key < length), 0.0, MASKED))
    q, scores, own_scores = [], [], []
    for u, h in pairs:
        at = slice(u * unit, (u + 1) * unit)
        q.append(
            jnp.stack(
                [
                    queries[at, (h * group + i) * HD : (h * group + i + 1) * HD]
                    for i in range(group)
                ],
                axis=0,
            )
        )
        keys = cache_ref[rows_of(u), :, h * 2 * HD : (h * 2 + 1) * HD].reshape(keys_of, HD)
        scores.append(
            lax.dot_general(
                q[-1].reshape(group * unit, HD).astype(BF16),
                keys,
                (((1,), (1,)), ((), ())),
                preferred_element_type=F32,
            ).reshape(group, unit, keys_of)
        )
    for n, (u, h) in enumerate(pairs):
        at = slice(u * unit, (u + 1) * unit)
        own_key = own[at, h * 2 * HD : (h * 2 + 1) * HD]
        own_scores.append(jnp.sum(q[n] * own_key[None], axis=2, keepdims=True) * LOG2_SCALE)
    scores = [scores[n] * LOG2_SCALE + bias[u][None] for n, (u, h) in enumerate(pairs)]
    largest = [
        jnp.maximum(jnp.max(x, axis=2, keepdims=True), y) for x, y in zip(scores, own_scores)
    ]
    weights = [jnp.exp2(x - y).astype(BF16) for x, y in zip(scores, largest)]
    own_weights = [jnp.exp2(x - y) for x, y in zip(own_scores, largest)]
    sums = []
    for n, (u, h) in enumerate(pairs):
        at = slice(u * unit, (u + 1) * unit)
        values = cache_ref[rows_of(u), :, (h * 2 + 1) * HD : (h * 2 + 2) * HD].reshape(keys_of, HD)
        sums.append(
            jnp.dot(
                weights[n].reshape(group * unit, keys_of),
                jnp.concatenate([values, ones], axis=1),
                preferred_element_type=F32,
            ).reshape(group, unit, 2 * HD)
        )
    pieces = [[] for _ in units]
    stats = [jnp.zeros((unit, STATS), F32) for _ in units]
    for n, (u, h) in enumerate(pairs):
        at = slice(u * unit, (u + 1) * unit)
        own_value = own[at, (h * 2 + 1) * HD : (h * 2 + 2) * HD]
        total = sums[n][:, :, HD:] + own_weights[n]
        result = (sums[n][:, :, :HD] + own_weights[n] * own_value[None]) / total
        lse = largest[n] + jnp.log2(total)
        for i in range(group):
            pieces[u].append(result[i])
            stats[u] = jnp.where(lane == h * group + i, lse[i], stats[u])
    out = jnp.concatenate([jnp.concatenate(x, axis=1) for x in pieces], axis=0).astype(BF16)
    out_ref[block, :] = out
    pick = pick_ref[...]
    here = iota((row_count, block_rows), 0) == iota((row_count, block_rows), 1) + first_row
    pick = jnp.dot(pick, here.astype(F32).astype(BF16), preferred_element_type=F32).astype(BF16)
    slot_out = jnp.dot(pick, out, preferred_element_type=F32)
    lse = jnp.concatenate(stats, axis=0)
    slot_lse = sum(
        jnp.dot(pick, part.astype(BF16), preferred_element_type=F32) for part in split_bf16(lse)
    )

    @pl.when(step == 0)
    def _():
        slot_out_ref[...] = slot_out
        slot_lse_ref[...] = slot_lse

    @pl.when(step > 0)
    def _():
        slot_out_ref[...] += slot_out
        slot_lse_ref[...] += slot_lse


def merge(pick_ref, *refs):
    parts, arrived_ref, out_ref = refs[:-2], refs[-2], refs[-1]
    cached_refs, slot_out_refs, slot_lse_refs = parts[0::3], parts[1::3], parts[2::3]
    width = out_ref.shape[1]
    pick = pick_ref[...]
    arrived = jnp.concatenate(
        [arrived_ref[s].astype(F32) for s in range(arrived_ref.shape[0])], axis=0
    )
    arrived_lse = (
        arrived[:, width : width + STATS]
        + arrived[:, width + STATS : width + 2 * STATS]
        + arrived[:, width + 2 * STATS :]
    )
    cached_lse = sum(ref[...] for ref in slot_lse_refs)
    largest = jnp.maximum(cached_lse, arrived_lse)
    cached_weight = jnp.exp2(cached_lse - largest)
    arrived_weight = jnp.exp2(arrived_lse - largest)
    total = cached_weight + arrived_weight
    cached_weight = cached_weight / total
    arrived_weight = arrived_weight / total
    has = lax.dot_general(
        pick, jnp.ones((pick.shape[0], HD), BF16), TRANSPOSED, preferred_element_type=F32
    )
    for i in range(width // HD):
        at = slice(i * HD, (i + 1) * HD)
        merged = (
            sum(ref[:, at] for ref in slot_out_refs) * cached_weight[:, i : i + 1]
            + arrived[:, at] * arrived_weight[:, i : i + 1]
        )
        placed = lax.dot_general(
            pick, merged.astype(BF16), TRANSPOSED, preferred_element_type=F32
        )
        row = 0
        for ref in cached_refs:
            rows = slice(row, row + ref.shape[0])
            kept = ref[:, at].astype(F32)
            out_ref[rows, at] = jnp.where(has[rows] > 0.5, placed[rows], kept).astype(BF16)
            row += ref.shape[0]


def compiler_params(megabytes):
    return pltpu.CompilerParams(vmem_limit_bytes=megabytes * 1024 * 1024)


RESIDENT = pl.BlockSpec(memory_space=pltpu.VMEM)
REMAINS = pl.BlockSpec(memory_space=pl.ANY)


def in_vmem(x):
    return pltpu.with_memory_space_constraint(x, pltpu.VMEM)


def in_hbm(x):
    return pltpu.with_memory_space_constraint(x, pltpu.HBM)


def shards(
    prompts, decode_hidden, queries, kv_cache, cache_len, span_len, target_row, w_kv, kv_scale
):
    row_count = decode_hidden.shape[0]
    prompt_rows, features = prompts.shape
    sections = lax.axis_size("section")
    local_width = kv_cache.shape[2]
    query_width = queries.shape[1]
    slots = sections * CAP
    all_rows = prompt_rows + row_count
    scale = kv_scale.reshape(1, -1)
    lengths = cache_len.reshape(1, -1)

    pick, asked = pl.pallas_call(
        select_queries,
        in_specs=[RESIDENT, RESIDENT],
        out_specs=[RESIDENT] * 2,
        out_shape=[
            pltpu.VMEM((slots, row_count), BF16),
            pltpu.VMEM((sections, CAP, query_width), BF16),
        ],
        compiler_params=compiler_params(16),
        name="select_queries",
    )(in_hbm(target_row), in_hbm(queries))
    asked = lax.all_to_all(asked, "section", 0, 0)

    edges = (0, 512, 1152, 1920, 2944, 4224, features)
    count = len(edges) - 1
    mine, theirs = pl.pallas_call(
        functools.partial(project, edges=edges, block=all_rows // 2),
        in_specs=[REMAINS] * 3 + [RESIDENT, REMAINS],
        out_specs=[RESIDENT, RESIDENT],
        scratch_shapes=[
            pltpu.VMEM((all_rows, features), BF16),
            pltpu.VMEM(w_kv.shape, BF16),
            pltpu.VMEM((all_rows, w_kv.shape[1]), F32),
            pltpu.SemaphoreType.DMA((count,)),
            pltpu.SemaphoreType.DMA((count,)),
            pltpu.SemaphoreType.DMA((count,)),
        ],
        out_shape=[pltpu.VMEM((all_rows, local_width), BF16)] * 2,
        compiler_params=compiler_params(44),
        name="project",
    )(in_hbm(prompts), in_hbm(decode_hidden), in_hbm(w_kv), in_hbm(scale), in_vmem(pick))
    other = lax.ppermute(theirs, "tp", [(0, 1), (1, 0)])

    block = 32
    calls = 2
    call_rows = row_count // calls

    def cache_share(call, after):
        first_block = call * call_rows // block
        return pl.pallas_call(
            functools.partial(attend_cache, block_rows=block, first_block=first_block),
            grid=(call_rows // block,),
            in_specs=[
                pl.BlockSpec((block, query_width), lambda b: (first_block + b, 0)),
                pl.BlockSpec((block, *kv_cache.shape[1:]), lambda b: (first_block + b, 0, 0)),
            ]
            + [RESIDENT] * 4
            + [REMAINS],
            out_specs=[RESIDENT] * 3,
            out_shape=[
                pltpu.VMEM((call_rows, query_width), BF16),
                pltpu.VMEM((slots, query_width), F32),
                pltpu.VMEM((slots, STATS), F32),
            ],
            compiler_params=compiler_params(24),
            name="attend_cache",
        )(
            in_hbm(queries),
            in_hbm(kv_cache),
            in_hbm(lengths),
            in_vmem(mine),
            in_vmem(other),
            in_vmem(pick),
            in_vmem(after),
        )

    shares = cache_share(0, pick)

    answer_width = query_width + 3 * STATS
    answers = pl.pallas_call(
        functools.partial(attend_arrived, row_count=row_count),
        in_specs=[RESIDENT] * 5 + [REMAINS],
        out_specs=RESIDENT,
        out_shape=pltpu.VMEM((sections, CAP, answer_width), BF16),
        compiler_params=compiler_params(24),
        name="attend_arrived",
    )(
        in_hbm(target_row),
        in_hbm(span_len),
        in_vmem(mine),
        in_vmem(other),
        in_vmem(asked),
        in_vmem(shares[2]),
    )
    after = answers
    answers = lax.all_to_all(answers, "section", 0, 0)
    for call in range(1, calls):
        shares = [*shares, *cache_share(call, after)]

    return pl.pallas_call(
        merge,
        in_specs=[RESIDENT] * (2 + len(shares)),
        out_specs=RESIDENT,
        out_shape=jax.ShapeDtypeStruct((row_count, query_width), BF16),
        compiler_params=compiler_params(24),
        name="merge",
    )(*map(in_vmem, (pick, *shares, answers)))


def solution(mesh):
    in_specs = (
        P(("groups", "section"), "tp"),
        P(("groups", "section"), "tp"),
        P(("groups", "section"), "tp"),
        P(("groups", "section"), None, "tp"),
        P(("groups", "section")),
        P("groups", None),
        P("groups", None),
        P("tp", None),
        P(),
    )
    out_specs = P(("groups", "section"), "tp")
    return jax.shard_map(shards, mesh=mesh, in_specs=in_specs, out_specs=out_specs, check_vma=False)
```

```python
import functools
import math

import jax
import jax.numpy as jnp
from jax import lax
from jax.experimental import pallas as pl
from jax.experimental.pallas import tpu as pltpu
from jax.sharding import PartitionSpec as P

HD = 128
CAP = 2
STATS = 128
MASKED = -1e30
LOG2_SCALE = HD ** (-0.5) * math.log2(math.e)
F32 = jnp.float32
BF16 = jnp.bfloat16
TRANSPOSED = (((0,), (0,)), ((), ()))


def iota(shape, dim):
    return lax.broadcasted_iota(jnp.int32, shape, dim)


def one_hot(shape, dim, index):
    return (iota(shape, dim) == index).astype(F32).astype(BF16)


def select_queries(target_ref, queries_ref, pick_ref, asked_ref):
    sections, requests = target_ref.shape
    row_count = queries_ref.shape[0]
    slots = sections * CAP
    position = lax.axis_index("section")
    slot_id = iota((slots, requests), 0)
    table = jnp.zeros((slots, requests), jnp.int32)
    for k in range(sections):
        mine = (slot_id >= k * CAP) & (slot_id < (k + 1) * CAP)
        table = jnp.where(mine, target_ref[k : k + 1, :], table)
    local = table - position * row_count
    here = (local >= 0) & (local < row_count)
    square = (requests, requests)
    earlier = jnp.dot(
        here.astype(F32).astype(BF16),
        (iota(square, 0) < iota(square, 1)).astype(F32).astype(BF16),
        preferred_element_type=F32,
    )
    chosen = here & (earlier == lax.rem(slot_id, CAP).astype(F32))
    row = jnp.max(jnp.where(chosen, local.astype(F32), -1.0), axis=1, keepdims=True)
    pick = one_hot((slots, row_count), 1, row.astype(jnp.int32))
    pick_ref[...] = pick
    asked_ref[...] = jnp.dot(pick, queries_ref[...], preferred_element_type=F32).astype(BF16)


def spans(edges):
    return [slice(a, b) for a, b in zip(edges[:-1], edges[1:])]


def project(
    prompts_ref,
    hidden_ref,
    w_ref,
    scale_ref,
    after_ref,
    mine_ref,
    theirs_ref,
    rows_ref,
    w_here_ref,
    total_ref,
    row_sems,
    hidden_sems,
    w_sems,
    *,
    edges,
    block,
):
    prompt_rows = prompts_ref.shape[0]
    width = mine_ref.shape[1]
    chunks = spans(edges)
    waits = []
    for c, at in enumerate(chunks):
        copies = [
            pltpu.make_async_copy(w_ref.at[at, :], w_here_ref.at[at, :], w_sems.at[c]),
            pltpu.make_async_copy(
                prompts_ref.at[:, at], rows_ref.at[:prompt_rows, at], row_sems.at[c]
            ),
            pltpu.make_async_copy(
                hidden_ref.at[:, at], rows_ref.at[prompt_rows:, at], hidden_sems.at[c]
            ),
        ]
        for copy in copies:
            copy.start()
        waits.append(copies)
    for c, at in enumerate(chunks[:-1]):
        for copy in waits[c]:
            copy.wait()
        for m in spans(range(0, rows_ref.shape[0] + 1, block)):
            part = jnp.dot(rows_ref[m, at], w_here_ref[at, :], preferred_element_type=F32)
            if c == 0:
                total_ref[m, :] = part
            else:
                total_ref[m, :] += part
    for copy in waits[-1]:
        copy.wait()
    first = lax.axis_index("tp") == 0
    for m in spans(range(0, rows_ref.shape[0] + 1, block)):
        part = jnp.dot(
            rows_ref[m, chunks[-1]], w_here_ref[chunks[-1], :], preferred_element_type=F32
        )
        term = ((total_ref[m, :] + part) * scale_ref[...]).astype(BF16)
        low, high = term[:, :width], term[:, width:]
        mine_ref[m, :] = jnp.where(first, low, high)
        theirs_ref[m, :] = jnp.where(first, high, low)


def split_bf16(x):
    high = x.astype(BF16).astype(F32)
    middle = (x - high).astype(BF16).astype(F32)
    return high, middle, (x - high - middle).astype(BF16).astype(F32)


def request_slots(target_ref, span_ref, row_count, padded):
    sections, requests = target_ref.shape
    position = lax.axis_index("section")
    target = target_ref[pl.ds(position, 1), :].astype(F32)
    span = span_ref[pl.ds(position, 1), :].astype(F32)
    diagonal = iota((padded, requests), 0) == iota((padded, requests), 1)
    target_col = jnp.sum(jnp.where(diagonal, target, 0.0), axis=1, keepdims=True)
    span_col = jnp.sum(jnp.where(diagonal, span, 0.0), axis=1, keepdims=True)
    section_row = jnp.zeros_like(target)
    section_col = jnp.zeros_like(target_col)
    for s in range(1, sections):
        section_row = section_row + (target >= s * row_count).astype(F32)
        section_col = section_col + (target_col >= s * row_count).astype(F32)
    before = (section_row == section_col) & (
        iota((padded, requests), 1) < iota((padded, requests), 0)
    )
    rank_col = jnp.sum(before.astype(F32), axis=1, keepdims=True).astype(jnp.int32)
    real = iota((padded, 1), 0) < requests
    section_col = jnp.where(real, section_col.astype(jnp.int32), -1)
    return section_col, rank_col, span_col.astype(jnp.int32)


def attend_arrived(
    target_ref, span_ref, mine_ref, other_ref, asked_ref, after_ref, out_ref, *, row_count
):
    sections, requests = target_ref.shape
    slots = sections * CAP
    padded = -(-requests // 16) * 16
    prompt_rows = mine_ref.shape[0] - row_count
    span_rows = prompt_rows // requests
    kv_heads = mine_ref.shape[1] // (2 * HD)
    group = asked_ref.shape[1] // (kv_heads * HD)
    section_col, rank_col, span_col = request_slots(target_ref, span_ref, row_count, padded)
    slot = jnp.where(section_col >= 0, section_col * CAP + rank_col, -1)
    slot_of = one_hot((padded, slots), 1, slot)
    asked_slot = section_col * slots + lax.axis_index("section") * CAP + rank_col
    asked_slot = jnp.where(section_col >= 0, asked_slot, -1)
    asked_slot_of = one_hot((padded, sections * slots), 1, asked_slot)
    key = iota((padded, prompt_rows), 1) - iota((padded, prompt_rows), 0) * span_rows
    bias = jnp.where((key >= 0) & (key < span_col), 0.0, MASKED)
    rows = jnp.dot(asked_slot_of, asked_ref[...], preferred_element_type=F32).astype(BF16)
    kv = (
        mine_ref[:prompt_rows, :].astype(F32) + other_ref[:prompt_rows, :].astype(F32)
    ).astype(BF16)
    scores = []
    for h in range(kv_heads):
        stacked = jnp.concatenate(
            [rows[:, (h * group + i) * HD : (h * group + i + 1) * HD] for i in range(group)],
            axis=0,
        )
        keys = kv[:, h * 2 * HD : (h * 2 + 1) * HD]
        scores.append(
            lax.dot_general(
                stacked, keys, (((1,), (1,)), ((), ())), preferred_element_type=F32
            )
        )
    scores = [
        x.reshape(group, padded, prompt_rows) * LOG2_SCALE + bias[None] for x in scores
    ]
    largest = [jnp.max(x, axis=2, keepdims=True) for x in scores]
    weights = [jnp.exp2(x - y) for x, y in zip(scores, largest)]
    totals = [jnp.sum(x, axis=2, keepdims=True) for x in weights]
    lane = iota((padded, STATS), 1)
    lse = jnp.zeros((padded, STATS), F32)
    pieces = []
    for h in range(kv_heads):
        values = jnp.dot(
            weights[h].reshape(group * padded, prompt_rows).astype(BF16),
            kv[:, (h * 2 + 1) * HD : (h * 2 + 2) * HD],
            preferred_element_type=F32,
        ).reshape(group, padded, HD)
        values = values / totals[h]
        head_lse = largest[h] + jnp.log2(totals[h])
        for i in range(group):
            pieces.append(values[i])
            lse = jnp.where(lane == h * group + i, head_lse[i], lse)
    result = jnp.concatenate(pieces + list(split_bf16(lse)), axis=1).astype(BF16)
    answers = lax.dot_general(slot_of, result, TRANSPOSED, preferred_element_type=F32).astype(BF16)
    for s in range(sections):
        out_ref[s] = answers[s * CAP : (s + 1) * CAP]


def attend_cache(
    queries_ref,
    cache_ref,
    len_ref,
    mine_ref,
    other_ref,
    pick_ref,
    after_ref,
    out_ref,
    slot_out_ref,
    slot_lse_ref,
    *,
    block_rows,
    first_block,
):
    cache_rows, width = cache_ref.shape[1:]
    row_count = len_ref.shape[1]
    kv_heads = width // (2 * HD)
    group = queries_ref.shape[1] // (kv_heads * HD)
    unit = 8
    keys_of = unit * cache_rows
    step = pl.program_id(0)
    block = pl.ds(pl.multiple_of(step * block_rows, block_rows), block_rows)
    first_row = pl.multiple_of((step + first_block) * block_rows, block_rows)
    own_block = pl.ds(first_row + (mine_ref.shape[0] - row_count), block_rows)
    queries = queries_ref[...].astype(F32)
    own = mine_ref[own_block, :].astype(F32) + other_ref[own_block, :].astype(F32)
    own = own.astype(BF16).astype(F32)
    key = iota((unit, keys_of), 1) - iota((unit, keys_of), 0) * cache_rows
    lengths = len_ref[...].astype(F32)
    lane = iota((unit, STATS), 1)
    ones = jnp.ones((keys_of, HD), BF16)
    units = range(block_rows // unit)

    def rows_of(u):
        return slice(u * unit, (u + 1) * unit)

    pairs = [(u, h) for u in units for h in range(kv_heads)]
    bias = []
    for u in units:
        row = iota((unit, row_count), 0) + (first_row + u * unit)
        length = jnp.sum(
            jnp.where(iota((unit, row_count), 1) == row, lengths, 0.0), axis=1, keepdims=True
        ).astype(jnp.int32)
        bias.append(jnp.where((key >= 0) & (key < length), 0.0, MASKED))
    q, scores, own_scores = [], [], []
    for u, h in pairs:
        at = slice(u * unit, (u + 1) * unit)
        q.append(
            jnp.stack(
                [
                    queries[at, (h * group + i) * HD : (h * group + i + 1) * HD]
                    for i in range(group)
                ],
                axis=0,
            )
        )
        keys = cache_ref[rows_of(u), :, h * 2 * HD : (h * 2 + 1) * HD].reshape(keys_of, HD)
        scores.append(
            lax.dot_general(
                q[-1].reshape(group * unit, HD).astype(BF16),
                keys,
                (((1,), (1,)), ((), ())),
                preferred_element_type=F32,
            ).reshape(group, unit, keys_of)
        )
    for n, (u, h) in enumerate(pairs):
        at = slice(u * unit, (u + 1) * unit)
        own_key = own[at, h * 2 * HD : (h * 2 + 1) * HD]
        own_scores.append(jnp.sum(q[n] * own_key[None], axis=2, keepdims=True) * LOG2_SCALE)
    scores = [scores[n] * LOG2_SCALE + bias[u][None] for n, (u, h) in enumerate(pairs)]
    largest = [
        jnp.maximum(jnp.max(x, axis=2, keepdims=True), y) for x, y in zip(scores, own_scores)
    ]
    weights = [jnp.exp2(x - y).astype(BF16) for x, y in zip(scores, largest)]
    own_weights = [jnp.exp2(x - y) for x, y in zip(own_scores, largest)]
    sums = []
    for n, (u, h) in enumerate(pairs):
        at = slice(u * unit, (u + 1) * unit)
        values = cache_ref[rows_of(u), :, (h * 2 + 1) * HD : (h * 2 + 2) * HD].reshape(keys_of, HD)
        sums.append(
            jnp.dot(
                weights[n].reshape(group * unit, keys_of),
                jnp.concatenate([values, ones], axis=1),
                preferred_element_type=F32,
            ).reshape(group, unit, 2 * HD)
        )
    pieces = [[] for _ in units]
    stats = [jnp.zeros((unit, STATS), F32) for _ in units]
    for n, (u, h) in enumerate(pairs):
        at = slice(u * unit, (u + 1) * unit)
        own_value = own[at, (h * 2 + 1) * HD : (h * 2 + 2) * HD]
        total = sums[n][:, :, HD:] + own_weights[n]
        result = (sums[n][:, :, :HD] + own_weights[n] * own_value[None]) / total
        lse = largest[n] + jnp.log2(total)
        for i in range(group):
            pieces[u].append(result[i])
            stats[u] = jnp.where(lane == h * group + i, lse[i], stats[u])
    out = jnp.concatenate([jnp.concatenate(x, axis=1) for x in pieces], axis=0).astype(BF16)
    out_ref[block, :] = out
    pick = pick_ref[...]
    here = iota((row_count, block_rows), 0) == iota((row_count, block_rows), 1) + first_row
    pick = jnp.dot(pick, here.astype(F32).astype(BF16), preferred_element_type=F32).astype(BF16)
    slot_out = jnp.dot(pick, out, preferred_element_type=F32)
    lse = jnp.concatenate(stats, axis=0)
    slot_lse = sum(
        jnp.dot(pick, part.astype(BF16), preferred_element_type=F32) for part in split_bf16(lse)
    )

    @pl.when(step == 0)
    def _():
        slot_out_ref[...] = slot_out
        slot_lse_ref[...] = slot_lse

    @pl.when(step > 0)
    def _():
        slot_out_ref[...] += slot_out
        slot_lse_ref[...] += slot_lse


def merge(pick_ref, *refs):
    parts, arrived_ref, out_ref = refs[:-2], refs[-2], refs[-1]
    cached_refs, slot_out_refs, slot_lse_refs = parts[0::3], parts[1::3], parts[2::3]
    width = out_ref.shape[1]
    pick = pick_ref[...]
    arrived = jnp.concatenate(
        [arrived_ref[s].astype(F32) for s in range(arrived_ref.shape[0])], axis=0
    )
    arrived_lse = (
        arrived[:, width : width + STATS]
        + arrived[:, width + STATS : width + 2 * STATS]
        + arrived[:, width + 2 * STATS :]
    )
    cached_lse = sum(ref[...] for ref in slot_lse_refs)
    largest = jnp.maximum(cached_lse, arrived_lse)
    cached_weight = jnp.exp2(cached_lse - largest)
    arrived_weight = jnp.exp2(arrived_lse - largest)
    total = cached_weight + arrived_weight
    cached_weight = cached_weight / total
    arrived_weight = arrived_weight / total
    has = lax.dot_general(
        pick, jnp.ones((pick.shape[0], HD), BF16), TRANSPOSED, preferred_element_type=F32
    )
    for i in range(width // HD):
        at = slice(i * HD, (i + 1) * HD)
        merged = (
            sum(ref[:, at] for ref in slot_out_refs) * cached_weight[:, i : i + 1]
            + arrived[:, at] * arrived_weight[:, i : i + 1]
        )
        placed = lax.dot_general(
            pick, merged.astype(BF16), TRANSPOSED, preferred_element_type=F32
        )
        row = 0
        for ref in cached_refs:
            rows = slice(row, row + ref.shape[0])
            kept = ref[:, at].astype(F32)
            out_ref[rows, at] = jnp.where(has[rows] > 0.5, placed[rows], kept).astype(BF16)
            row += ref.shape[0]


def compiler_params(megabytes):
    return pltpu.CompilerParams(vmem_limit_bytes=megabytes * 1024 * 1024)


RESIDENT = pl.BlockSpec(memory_space=pltpu.VMEM)
REMAINS = pl.BlockSpec(memory_space=pl.ANY)


def in_vmem(x):
    return pltpu.with_memory_space_constraint(x, pltpu.VMEM)


def in_hbm(x):
    return pltpu.with_memory_space_constraint(x, pltpu.HBM)


def shards(
    prompts, decode_hidden, queries, kv_cache, cache_len, span_len, target_row, w_kv, kv_scale
):
    row_count = decode_hidden.shape[0]
    prompt_rows, features = prompts.shape
    sections = lax.axis_size("section")
    local_width = kv_cache.shape[2]
    query_width = queries.shape[1]
    slots = sections * CAP
    all_rows = prompt_rows + row_count
    scale = kv_scale.reshape(1, -1)
    lengths = cache_len.reshape(1, -1)

    pick, asked = pl.pallas_call(
        select_queries,
        in_specs=[RESIDENT, RESIDENT],
        out_specs=[RESIDENT] * 2,
        out_shape=[
            pltpu.VMEM((slots, row_count), BF16),
            jax.ShapeDtypeStruct((slots, query_width), BF16),
        ],
        compiler_params=compiler_params(16),
        name="select_queries",
    )(in_hbm(target_row), in_hbm(queries))
    asked = lax.all_gather(asked, "section", axis=0, tiled=True)

    edges = (0, 512, 1152, 1920, 2944, 4224, features)
    count = len(edges) - 1
    mine, theirs = pl.pallas_call(
        functools.partial(project, edges=edges, block=all_rows // 2),
        in_specs=[REMAINS] * 3 + [RESIDENT, REMAINS],
        out_specs=[RESIDENT, RESIDENT],
        scratch_shapes=[
            pltpu.VMEM((all_rows, features), BF16),
            pltpu.VMEM(w_kv.shape, BF16),
            pltpu.VMEM((all_rows, w_kv.shape[1]), F32),
            pltpu.SemaphoreType.DMA((count,)),
            pltpu.SemaphoreType.DMA((count,)),
            pltpu.SemaphoreType.DMA((count,)),
        ],
        out_shape=[pltpu.VMEM((all_rows, local_width), BF16)] * 2,
        compiler_params=compiler_params(44),
        name="project",
    )(in_hbm(prompts), in_hbm(decode_hidden), in_hbm(w_kv), in_hbm(scale), in_vmem(pick))
    theirs, asked = lax.optimization_barrier((theirs, asked))
    other = lax.ppermute(theirs, "tp", [(0, 1), (1, 0)])

    block = 32
    calls = 2
    call_rows = row_count // calls

    def cache_share(call, after):
        first_block = call * call_rows // block
        return pl.pallas_call(
            functools.partial(attend_cache, block_rows=block, first_block=first_block),
            grid=(call_rows // block,),
            in_specs=[
                pl.BlockSpec((block, query_width), lambda b: (first_block + b, 0)),
                pl.BlockSpec((block, *kv_cache.shape[1:]), lambda b: (first_block + b, 0, 0)),
            ]
            + [RESIDENT] * 4
            + [REMAINS],
            out_specs=[RESIDENT] * 3,
            out_shape=[
                pltpu.VMEM((call_rows, query_width), BF16),
                pltpu.VMEM((slots, query_width), F32),
                pltpu.VMEM((slots, STATS), F32),
            ],
            compiler_params=compiler_params(24),
            name="attend_cache",
        )(
            in_hbm(queries),
            in_hbm(kv_cache),
            in_hbm(lengths),
            in_vmem(mine),
            in_vmem(other),
            in_vmem(pick),
            after,
        )

    shares = cache_share(0, in_hbm(asked))

    answer_width = query_width + 3 * STATS
    answers = pl.pallas_call(
        functools.partial(attend_arrived, row_count=row_count),
        in_specs=[RESIDENT] * 5 + [REMAINS],
        out_specs=RESIDENT,
        out_shape=pltpu.VMEM((sections, CAP, answer_width), BF16),
        compiler_params=compiler_params(24),
        name="attend_arrived",
    )(
        in_hbm(target_row),
        in_hbm(span_len),
        in_vmem(mine),
        in_vmem(other),
        in_hbm(asked),
        in_vmem(shares[2]),
    )
    after = answers
    answers = lax.all_to_all(answers, "section", 0, 0)
    for call in range(1, calls):
        shares = [*shares, *cache_share(call, after)]

    return pl.pallas_call(
        merge,
        in_specs=[RESIDENT] * (2 + len(shares)),
        out_specs=RESIDENT,
        out_shape=jax.ShapeDtypeStruct((row_count, query_width), BF16),
        compiler_params=compiler_params(24),
        name="merge",
    )(*map(in_vmem, (pick, *shares, answers)))


def solution(mesh):
    in_specs = (
        P(("groups", "section"), "tp"),
        P(("groups", "section"), "tp"),
        P(("groups", "section"), "tp"),
        P(("groups", "section"), None, "tp"),
        P(("groups", "section")),
        P("groups", None),
        P("groups", None),
        P("tp", None),
        P(),
    )
    out_specs = P(("groups", "section"), "tp")
    return jax.shard_map(shards, mesh=mesh, in_specs=in_specs, out_specs=out_specs, check_vma=False)
```

```python
import functools
import math

import jax
import jax.numpy as jnp
from jax import lax
from jax.experimental import pallas as pl
from jax.experimental.pallas import tpu as pltpu
from jax.sharding import PartitionSpec as P

HD = 128
CAP = 2
STATS = 128
MASKED = -1e30
LOG2_SCALE = HD ** (-0.5) * math.log2(math.e)
F32 = jnp.float32
BF16 = jnp.bfloat16
TRANSPOSED = (((0,), (0,)), ((), ()))


def iota(shape, dim):
    return lax.broadcasted_iota(jnp.int32, shape, dim)


def one_hot(shape, dim, index):
    return (iota(shape, dim) == index).astype(F32).astype(BF16)


def select_queries(target_ref, queries_ref, pick_ref, asked_ref):
    sections, requests = target_ref.shape
    row_count = queries_ref.shape[0]
    slots = sections * CAP
    position = lax.axis_index("section")
    slot_id = iota((slots, requests), 0)
    table = jnp.zeros((slots, requests), jnp.int32)
    for k in range(sections):
        mine = (slot_id >= k * CAP) & (slot_id < (k + 1) * CAP)
        table = jnp.where(mine, target_ref[k : k + 1, :], table)
    local = table - position * row_count
    here = (local >= 0) & (local < row_count)
    square = (requests, requests)
    earlier = jnp.dot(
        here.astype(F32).astype(BF16),
        (iota(square, 0) < iota(square, 1)).astype(F32).astype(BF16),
        preferred_element_type=F32,
    )
    chosen = here & (earlier == lax.rem(slot_id, CAP).astype(F32))
    row = jnp.max(jnp.where(chosen, local.astype(F32), -1.0), axis=1, keepdims=True)
    pick = one_hot((slots, row_count), 1, row.astype(jnp.int32))
    pick_ref[...] = pick
    asked = jnp.dot(pick, queries_ref[...], preferred_element_type=F32).astype(BF16)
    for k in range(sections):
        asked_ref[k] = asked[k * CAP : (k + 1) * CAP]


def spans(edges):
    return [slice(a, b) for a, b in zip(edges[:-1], edges[1:])]


def project(
    prompts_ref,
    hidden_ref,
    w_ref,
    scale_ref,
    after_ref,
    mine_ref,
    theirs_ref,
    rows_ref,
    w_here_ref,
    total_ref,
    row_sems,
    hidden_sems,
    w_sems,
    *,
    edges,
    block,
):
    prompt_rows = prompts_ref.shape[0]
    width = mine_ref.shape[1]
    chunks = spans(edges)
    waits = []
    for c, at in enumerate(chunks):
        copies = [
            pltpu.make_async_copy(w_ref.at[at, :], w_here_ref.at[at, :], w_sems.at[c]),
            pltpu.make_async_copy(
                prompts_ref.at[:, at], rows_ref.at[:prompt_rows, at], row_sems.at[c]
            ),
            pltpu.make_async_copy(
                hidden_ref.at[:, at], rows_ref.at[prompt_rows:, at], hidden_sems.at[c]
            ),
        ]
        for copy in copies:
            copy.start()
        waits.append(copies)
    for c, at in enumerate(chunks[:-1]):
        for copy in waits[c]:
            copy.wait()
        for m in spans(range(0, rows_ref.shape[0] + 1, block)):
            part = jnp.dot(rows_ref[m, at], w_here_ref[at, :], preferred_element_type=F32)
            if c == 0:
                total_ref[m, :] = part
            else:
                total_ref[m, :] += part
    for copy in waits[-1]:
        copy.wait()
    first = lax.axis_index("tp") == 0
    for m in spans(range(0, rows_ref.shape[0] + 1, block)):
        part = jnp.dot(
            rows_ref[m, chunks[-1]], w_here_ref[chunks[-1], :], preferred_element_type=F32
        )
        term = ((total_ref[m, :] + part) * scale_ref[...]).astype(BF16)
        low, high = term[:, :width], term[:, width:]
        mine_ref[m, :] = jnp.where(first, low, high)
        theirs_ref[m, :] = jnp.where(first, high, low)


def split_bf16(x):
    high = x.astype(BF16).astype(F32)
    middle = (x - high).astype(BF16).astype(F32)
    return high, middle, (x - high - middle).astype(BF16).astype(F32)


def request_slots(target_ref, span_ref, row_count, padded):
    sections, requests = target_ref.shape
    position = lax.axis_index("section")
    target = target_ref[pl.ds(position, 1), :].astype(F32)
    span = span_ref[pl.ds(position, 1), :].astype(F32)
    diagonal = iota((padded, requests), 0) == iota((padded, requests), 1)
    target_col = jnp.sum(jnp.where(diagonal, target, 0.0), axis=1, keepdims=True)
    span_col = jnp.sum(jnp.where(diagonal, span, 0.0), axis=1, keepdims=True)
    section_row = jnp.zeros_like(target)
    section_col = jnp.zeros_like(target_col)
    for s in range(1, sections):
        section_row = section_row + (target >= s * row_count).astype(F32)
        section_col = section_col + (target_col >= s * row_count).astype(F32)
    before = (section_row == section_col) & (
        iota((padded, requests), 1) < iota((padded, requests), 0)
    )
    rank_col = jnp.sum(before.astype(F32), axis=1, keepdims=True).astype(jnp.int32)
    real = iota((padded, 1), 0) < requests
    slot_col = jnp.where(real, section_col.astype(jnp.int32) * CAP + rank_col, -1)
    return slot_col, span_col.astype(jnp.int32)


def attend_arrived(
    target_ref, span_ref, mine_ref, other_ref, asked_ref, out_ref, *, row_count
):
    sections, requests = target_ref.shape
    slots = sections * CAP
    padded = -(-requests // 16) * 16
    prompt_rows = mine_ref.shape[0] - row_count
    span_rows = prompt_rows // requests
    kv_heads = mine_ref.shape[1] // (2 * HD)
    group = asked_ref.shape[2] // (kv_heads * HD)
    slot_col, span_col = request_slots(target_ref, span_ref, row_count, padded)
    slot_of = one_hot((padded, slots), 1, slot_col)
    key = iota((padded, prompt_rows), 1) - iota((padded, prompt_rows), 0) * span_rows
    bias = jnp.where((key >= 0) & (key < span_col), 0.0, MASKED)
    asked = jnp.concatenate([asked_ref[s].astype(F32) for s in range(sections)], axis=0).astype(BF16)
    rows = jnp.dot(slot_of, asked, preferred_element_type=F32).astype(BF16)
    kv = (
        mine_ref[:prompt_rows, :].astype(F32) + other_ref[:prompt_rows, :].astype(F32)
    ).astype(BF16)
    scores = []
    for h in range(kv_heads):
        stacked = jnp.concatenate(
            [rows[:, (h * group + i) * HD : (h * group + i + 1) * HD] for i in range(group)],
            axis=0,
        )
        keys = kv[:, h * 2 * HD : (h * 2 + 1) * HD]
        scores.append(
            lax.dot_general(
                stacked, keys, (((1,), (1,)), ((), ())), preferred_element_type=F32
            )
        )
    scores = [
        x.reshape(group, padded, prompt_rows) * LOG2_SCALE + bias[None] for x in scores
    ]
    largest = [jnp.max(x, axis=2, keepdims=True) for x in scores]
    weights = [jnp.exp2(x - y) for x, y in zip(scores, largest)]
    totals = [jnp.sum(x, axis=2, keepdims=True) for x in weights]
    lane = iota((padded, STATS), 1)
    lse = jnp.zeros((padded, STATS), F32)
    pieces = []
    for h in range(kv_heads):
        values = jnp.dot(
            weights[h].reshape(group * padded, prompt_rows).astype(BF16),
            kv[:, (h * 2 + 1) * HD : (h * 2 + 2) * HD],
            preferred_element_type=F32,
        ).reshape(group, padded, HD)
        values = values / totals[h]
        head_lse = largest[h] + jnp.log2(totals[h])
        for i in range(group):
            pieces.append(values[i])
            lse = jnp.where(lane == h * group + i, head_lse[i], lse)
    result = jnp.concatenate(pieces + list(split_bf16(lse)), axis=1).astype(BF16)
    answers = lax.dot_general(slot_of, result, TRANSPOSED, preferred_element_type=F32).astype(BF16)
    for s in range(sections):
        out_ref[s] = answers[s * CAP : (s + 1) * CAP]


def attend_cache(
    queries_ref,
    cache_ref,
    len_ref,
    mine_ref,
    other_ref,
    pick_ref,
    after_ref,
    out_ref,
    slot_out_ref,
    slot_lse_ref,
    *,
    block_rows,
    first_block,
):
    cache_rows, width = cache_ref.shape[1:]
    row_count = len_ref.shape[1]
    kv_heads = width // (2 * HD)
    group = queries_ref.shape[1] // (kv_heads * HD)
    unit = 8
    keys_of = unit * cache_rows
    step = pl.program_id(0)
    block = pl.ds(pl.multiple_of(step * block_rows, block_rows), block_rows)
    first_row = pl.multiple_of((step + first_block) * block_rows, block_rows)
    own_block = pl.ds(first_row + (mine_ref.shape[0] - row_count), block_rows)
    queries = queries_ref[...].astype(F32)
    own = mine_ref[own_block, :].astype(F32) + other_ref[own_block, :].astype(F32)
    own = own.astype(BF16).astype(F32)
    key = iota((unit, keys_of), 1) - iota((unit, keys_of), 0) * cache_rows
    lengths = len_ref[...].astype(F32)
    lane = iota((unit, STATS), 1)
    ones = jnp.ones((keys_of, HD), BF16)
    units = range(block_rows // unit)

    def rows_of(u):
        return slice(u * unit, (u + 1) * unit)

    pairs = [(u, h) for u in units for h in range(kv_heads)]
    bias = []
    for u in units:
        row = iota((unit, row_count), 0) + (first_row + u * unit)
        length = jnp.sum(
            jnp.where(iota((unit, row_count), 1) == row, lengths, 0.0), axis=1, keepdims=True
        ).astype(jnp.int32)
        bias.append(jnp.where((key >= 0) & (key < length), 0.0, MASKED))
    q, scores, own_scores = [], [], []
    for u, h in pairs:
        at = slice(u * unit, (u + 1) * unit)
        q.append(
            jnp.stack(
                [
                    queries[at, (h * group + i) * HD : (h * group + i + 1) * HD]
                    for i in range(group)
                ],
                axis=0,
            )
        )
        keys = cache_ref[rows_of(u), :, h * 2 * HD : (h * 2 + 1) * HD].reshape(keys_of, HD)
        scores.append(
            lax.dot_general(
                q[-1].reshape(group * unit, HD).astype(BF16),
                keys,
                (((1,), (1,)), ((), ())),
                preferred_element_type=F32,
            ).reshape(group, unit, keys_of)
        )
    for n, (u, h) in enumerate(pairs):
        at = slice(u * unit, (u + 1) * unit)
        own_key = own[at, h * 2 * HD : (h * 2 + 1) * HD]
        own_scores.append(jnp.sum(q[n] * own_key[None], axis=2, keepdims=True) * LOG2_SCALE)
    scores = [scores[n] * LOG2_SCALE + bias[u][None] for n, (u, h) in enumerate(pairs)]
    largest = [
        jnp.maximum(jnp.max(x, axis=2, keepdims=True), y) for x, y in zip(scores, own_scores)
    ]
    weights = [jnp.exp2(x - y).astype(BF16) for x, y in zip(scores, largest)]
    own_weights = [jnp.exp2(x - y) for x, y in zip(own_scores, largest)]
    sums = []
    for n, (u, h) in enumerate(pairs):
        at = slice(u * unit, (u + 1) * unit)
        values = cache_ref[rows_of(u), :, (h * 2 + 1) * HD : (h * 2 + 2) * HD].reshape(keys_of, HD)
        sums.append(
            jnp.dot(
                weights[n].reshape(group * unit, keys_of),
                jnp.concatenate([values, ones], axis=1),
                preferred_element_type=F32,
            ).reshape(group, unit, 2 * HD)
        )
    pieces = [[] for _ in units]
    stats = [jnp.zeros((unit, STATS), F32) for _ in units]
    for n, (u, h) in enumerate(pairs):
        at = slice(u * unit, (u + 1) * unit)
        own_value = own[at, (h * 2 + 1) * HD : (h * 2 + 2) * HD]
        total = sums[n][:, :, HD:] + own_weights[n]
        result = (sums[n][:, :, :HD] + own_weights[n] * own_value[None]) / total
        lse = largest[n] + jnp.log2(total)
        for i in range(group):
            pieces[u].append(result[i])
            stats[u] = jnp.where(lane == h * group + i, lse[i], stats[u])
    out = jnp.concatenate([jnp.concatenate(x, axis=1) for x in pieces], axis=0).astype(BF16)
    out_ref[block, :] = out
    pick = pick_ref[...]
    here = iota((row_count, block_rows), 0) == iota((row_count, block_rows), 1) + first_row
    pick = jnp.dot(pick, here.astype(F32).astype(BF16), preferred_element_type=F32).astype(BF16)
    slot_out = jnp.dot(pick, out, preferred_element_type=F32)
    lse = jnp.concatenate(stats, axis=0)
    slot_lse = sum(
        jnp.dot(pick, part.astype(BF16), preferred_element_type=F32) for part in split_bf16(lse)
    )

    @pl.when(step == 0)
    def _():
        slot_out_ref[...] = slot_out
        slot_lse_ref[...] = slot_lse

    @pl.when(step > 0)
    def _():
        slot_out_ref[...] += slot_out
        slot_lse_ref[...] += slot_lse


def merge(pick_ref, *refs):
    parts, arrived_ref, out_ref = refs[:-2], refs[-2], refs[-1]
    cached_refs, slot_out_refs, slot_lse_refs = parts[0::3], parts[1::3], parts[2::3]
    width = out_ref.shape[1]
    pick = pick_ref[...]
    arrived = jnp.concatenate(
        [arrived_ref[s].astype(F32) for s in range(arrived_ref.shape[0])], axis=0
    )
    arrived_lse = (
        arrived[:, width : width + STATS]
        + arrived[:, width + STATS : width + 2 * STATS]
        + arrived[:, width + 2 * STATS :]
    )
    cached_lse = sum(ref[...] for ref in slot_lse_refs)
    largest = jnp.maximum(cached_lse, arrived_lse)
    cached_weight = jnp.exp2(cached_lse - largest)
    arrived_weight = jnp.exp2(arrived_lse - largest)
    total = cached_weight + arrived_weight
    cached_weight = cached_weight / total
    arrived_weight = arrived_weight / total
    has = lax.dot_general(
        pick, jnp.ones((pick.shape[0], HD), BF16), TRANSPOSED, preferred_element_type=F32
    )
    for i in range(width // HD):
        at = slice(i * HD, (i + 1) * HD)
        merged = (
            sum(ref[:, at] for ref in slot_out_refs) * cached_weight[:, i : i + 1]
            + arrived[:, at] * arrived_weight[:, i : i + 1]
        )
        placed = lax.dot_general(
            pick, merged.astype(BF16), TRANSPOSED, preferred_element_type=F32
        )
        row = 0
        for ref in cached_refs:
            rows = slice(row, row + ref.shape[0])
            kept = ref[:, at].astype(F32)
            out_ref[rows, at] = jnp.where(has[rows] > 0.5, placed[rows], kept).astype(BF16)
            row += ref.shape[0]


def compiler_params(megabytes):
    return pltpu.CompilerParams(vmem_limit_bytes=megabytes * 1024 * 1024)


RESIDENT = pl.BlockSpec(memory_space=pltpu.VMEM)
REMAINS = pl.BlockSpec(memory_space=pl.ANY)


def in_vmem(x):
    return pltpu.with_memory_space_constraint(x, pltpu.VMEM)


def in_hbm(x):
    return pltpu.with_memory_space_constraint(x, pltpu.HBM)


def shards(
    prompts, decode_hidden, queries, kv_cache, cache_len, span_len, target_row, w_kv, kv_scale
):
    row_count = decode_hidden.shape[0]
    prompt_rows, features = prompts.shape
    sections = lax.axis_size("section")
    local_width = kv_cache.shape[2]
    query_width = queries.shape[1]
    slots = sections * CAP
    all_rows = prompt_rows + row_count
    scale = kv_scale.reshape(1, -1)
    lengths = cache_len.reshape(1, -1)

    pick, asked = pl.pallas_call(
        select_queries,
        in_specs=[RESIDENT, RESIDENT],
        out_specs=[RESIDENT] * 2,
        out_shape=[
            pltpu.VMEM((slots, row_count), BF16),
            pltpu.VMEM((sections, CAP, query_width), BF16),
        ],
        compiler_params=compiler_params(16),
        name="select_queries",
    )(in_hbm(target_row), in_hbm(queries))
    asked = lax.all_to_all(asked, "section", 0, 0)

    edges = (0, 512, 1152, 1920, 2944, 4224, features)
    count = len(edges) - 1
    mine, theirs = pl.pallas_call(
        functools.partial(project, edges=edges, block=all_rows // 2),
        in_specs=[REMAINS] * 3 + [RESIDENT, REMAINS],
        out_specs=[RESIDENT, RESIDENT],
        scratch_shapes=[
            pltpu.VMEM((all_rows, features), BF16),
            pltpu.VMEM(w_kv.shape, BF16),
            pltpu.VMEM((all_rows, w_kv.shape[1]), F32),
            pltpu.SemaphoreType.DMA((count,)),
            pltpu.SemaphoreType.DMA((count,)),
            pltpu.SemaphoreType.DMA((count,)),
        ],
        out_shape=[pltpu.VMEM((all_rows, local_width), BF16)] * 2,
        compiler_params=compiler_params(44),
        name="project",
    )(in_hbm(prompts), in_hbm(decode_hidden), in_hbm(w_kv), in_hbm(scale), in_vmem(pick))
    theirs, asked = lax.optimization_barrier((theirs, asked))
    other = lax.ppermute(theirs, "tp", [(0, 1), (1, 0)])

    block = 32
    calls = 1
    call_rows = row_count // calls

    def cache_share(call, after):
        first_block = call * call_rows // block
        return pl.pallas_call(
            functools.partial(attend_cache, block_rows=block, first_block=first_block),
            grid=(call_rows // block,),
            in_specs=[
                pl.BlockSpec((block, query_width), lambda b: (first_block + b, 0)),
                pl.BlockSpec((block, *kv_cache.shape[1:]), lambda b: (first_block + b, 0, 0)),
            ]
            + [RESIDENT] * 4
            + [REMAINS],
            out_specs=[RESIDENT] * 3,
            out_shape=[
                pltpu.VMEM((call_rows, query_width), BF16),
                pltpu.VMEM((slots, query_width), F32),
                pltpu.VMEM((slots, STATS), F32),
            ],
            compiler_params=compiler_params(24),
            name="attend_cache",
        )(
            in_hbm(queries),
            in_hbm(kv_cache),
            in_hbm(lengths),
            in_vmem(mine),
            in_vmem(other),
            in_vmem(pick),
            in_vmem(after),
        )

    answer_width = query_width + 3 * STATS
    answers = pl.pallas_call(
        functools.partial(attend_arrived, row_count=row_count),
        in_specs=[RESIDENT] * 5,
        out_specs=RESIDENT,
        out_shape=pltpu.VMEM((sections, CAP, answer_width), BF16),
        compiler_params=compiler_params(24),
        name="attend_arrived",
    )(
        in_hbm(target_row),
        in_hbm(span_len),
        in_vmem(mine),
        in_vmem(other),
        in_vmem(asked),
    )
    after = answers
    answers = lax.all_to_all(answers, "section", 0, 0)
    shares = []
    for call in range(calls):
        shares += cache_share(call, after)

    return pl.pallas_call(
        merge,
        in_specs=[RESIDENT] * (2 + len(shares)),
        out_specs=RESIDENT,
        out_shape=jax.ShapeDtypeStruct((row_count, query_width), BF16),
        compiler_params=compiler_params(24),
        name="merge",
    )(*map(in_vmem, (pick, *shares, answers)))


def solution(mesh):
    in_specs = (
        P(("groups", "section"), "tp"),
        P(("groups", "section"), "tp"),
        P(("groups", "section"), "tp"),
        P(("groups", "section"), None, "tp"),
        P(("groups", "section")),
        P("groups", None),
        P("groups", None),
        P("tp", None),
        P(),
    )
    out_specs = P(("groups", "section"), "tp")
    return jax.shard_map(shards, mesh=mesh, in_specs=in_specs, out_specs=out_specs, check_vma=False)
```

```python
import functools
import math

import jax
import jax.numpy as jnp
from jax import lax
from jax.experimental import pallas as pl
from jax.experimental.pallas import tpu as pltpu
from jax.sharding import PartitionSpec as P

HD = 128
CAP = 2
STATS = 128
MASKED = -1e30
PITCH = 8
LOG2_SCALE = HD ** (-0.5) * math.log2(math.e)
F32 = jnp.float32
BF16 = jnp.bfloat16
TRANSPOSED = (((0,), (0,)), ((), ()))


def iota(shape, dim):
    return lax.broadcasted_iota(jnp.int32, shape, dim)


def one_hot(shape, dim, index):
    return (iota(shape, dim) == index).astype(F32).astype(BF16)


def pick_rows(target_ref, row_count, pitch):
    sections, requests = target_ref.shape
    shape = (sections * pitch, requests)
    position = lax.axis_index("section")
    slot_id = iota(shape, 0)
    table = jnp.zeros(shape, jnp.int32)
    for s in range(sections):
        mine = (slot_id >= s * pitch) & (slot_id < (s + 1) * pitch)
        table = jnp.where(mine, target_ref[s : s + 1, :], table)
    local = table - position * row_count
    here = (local >= 0) & (local < row_count)
    square = (requests, requests)
    earlier = jnp.dot(
        here.astype(F32).astype(BF16),
        (iota(square, 0) < iota(square, 1)).astype(F32).astype(BF16),
        preferred_element_type=F32,
    )
    chosen = here & (earlier == lax.rem(slot_id, pitch).astype(F32))
    row = jnp.max(jnp.where(chosen, local.astype(F32), -1.0), axis=1, keepdims=True)
    return one_hot((shape[0], row_count), 1, row.astype(jnp.int32))


def select_queries(
    target_ref,
    queries_ref,
    prompts_ref,
    hidden_ref,
    w_ref,
    pick_ref,
    asked_ref,
    rows_ref,
    w_head_ref,
    queries_here_ref,
    sems,
):
    sections = target_ref.shape[0]
    row_count = queries_ref.shape[0]
    prompt_rows = prompts_ref.shape[0]
    depth = w_head_ref.shape[0]
    copies = [
        pltpu.make_async_copy(queries_ref, queries_here_ref, sems.at[0]),
        pltpu.make_async_copy(w_ref.at[:depth, :], w_head_ref, sems.at[1]),
        pltpu.make_async_copy(prompts_ref.at[:, :depth], rows_ref.at[:prompt_rows, :], sems.at[2]),
        pltpu.make_async_copy(hidden_ref.at[:, :depth], rows_ref.at[prompt_rows:, :], sems.at[3]),
    ]
    for copy in copies:
        copy.start()
    pick = pick_rows(target_ref, row_count, PITCH)
    pick_ref[...] = pick_rows(target_ref, row_count, CAP)
    copies[0].wait()
    asked = jnp.dot(pick, queries_here_ref[...], preferred_element_type=F32)
    for s in range(sections):
        asked_ref[s] = asked[s * PITCH : s * PITCH + CAP].astype(BF16)
    for copy in copies[1:]:
        copy.wait()


def spans(edges):
    return [slice(a, b) for a, b in zip(edges[:-1], edges[1:])]


def project(
    rows_head_ref,
    w_head_ref,
    prompts_ref,
    hidden_ref,
    w_ref,
    scale_ref,
    mine_ref,
    theirs_ref,
    rows_ref,
    w_here_ref,
    total_ref,
    row_sems,
    hidden_sems,
    w_sems,
    *,
    edges,
    block,
):
    prompt_rows = prompts_ref.shape[0]
    width = mine_ref.shape[1]
    head = w_head_ref.shape[0]
    chunks = spans(edges)
    waits = []
    for c, at in enumerate(chunks):
        there = slice(head + at.start, head + at.stop)
        copies = [
            pltpu.make_async_copy(w_ref.at[there, :], w_here_ref.at[at, :], w_sems.at[c]),
            pltpu.make_async_copy(
                prompts_ref.at[:, there], rows_ref.at[:prompt_rows, at], row_sems.at[c]
            ),
            pltpu.make_async_copy(
                hidden_ref.at[:, there], rows_ref.at[prompt_rows:, at], hidden_sems.at[c]
            ),
        ]
        for copy in copies:
            copy.start()
        waits.append(copies)
    first = lax.axis_index("tp") == 0
    blocks = spans(range(0, total_ref.shape[0] + 1, block))
    halves = (slice(0, width), slice(width, 2 * width))
    for m in blocks:
        for n in halves:
            total_ref[m, n] = jnp.dot(
                rows_head_ref[m, :], w_head_ref[:, n], preferred_element_type=F32
            )
    for c, at in enumerate(chunks):
        for copy in waits[c]:
            copy.wait()
        for m in blocks:
            for n in halves:
                total_ref[m, n] += jnp.dot(
                    rows_ref[m, at], w_here_ref[at, n], preferred_element_type=F32
                )
    for m in blocks:
        low, high = ((total_ref[m, n] * scale_ref[:, n]).astype(BF16) for n in halves)
        mine_ref[m, :] = jnp.where(first, low, high)
        theirs_ref[m, :] = jnp.where(first, high, low)


def split_bf16(x):
    high = x.astype(BF16).astype(F32)
    middle = (x - high).astype(BF16).astype(F32)
    return high, middle, (x - high - middle).astype(BF16).astype(F32)


def request_slots(target_ref, span_ref, row_count, padded):
    sections, requests = target_ref.shape
    position = lax.axis_index("section")
    target = target_ref[pl.ds(position, 1), :].astype(F32)
    span = span_ref[pl.ds(position, 1), :].astype(F32)
    diagonal = iota((padded, requests), 0) == iota((padded, requests), 1)
    target_col = jnp.sum(jnp.where(diagonal, target, 0.0), axis=1, keepdims=True)
    span_col = jnp.sum(jnp.where(diagonal, span, 0.0), axis=1, keepdims=True)
    section_row = jnp.zeros_like(target)
    section_col = jnp.zeros_like(target_col)
    for s in range(1, sections):
        section_row = section_row + (target >= s * row_count).astype(F32)
        section_col = section_col + (target_col >= s * row_count).astype(F32)
    before = (section_row == section_col) & (
        iota((padded, requests), 1) < iota((padded, requests), 0)
    )
    rank_col = jnp.sum(before.astype(F32), axis=1, keepdims=True).astype(jnp.int32)
    real = iota((padded, 1), 0) < requests
    section_col = jnp.where(real, section_col.astype(jnp.int32), -1)
    return section_col, rank_col, span_col.astype(jnp.int32)


def prepare_arrived(
    target_ref, span_ref, asked_ref, rows_ref, slot_of_ref, bias_ref, *, row_count
):
    sections, requests = target_ref.shape
    padded, prompt_rows = bias_ref.shape
    span_rows = prompt_rows // requests
    section_col, rank_col, span_col = request_slots(target_ref, span_ref, row_count, padded)
    slot = jnp.where(section_col >= 0, section_col * PITCH + rank_col, -1)
    slot_of_ref[...] = one_hot((padded, sections * PITCH), 1, slot)
    slot = jnp.where(section_col >= 0, section_col * CAP + rank_col, -1)
    asked = jnp.concatenate([asked_ref[s].astype(F32) for s in range(sections)], axis=0)
    rows_ref[...] = jnp.dot(
        one_hot((padded, sections * CAP), 1, slot),
        asked.astype(BF16),
        preferred_element_type=F32,
    ).astype(BF16)
    key = iota((padded, prompt_rows), 1) - iota((padded, prompt_rows), 0) * span_rows
    bias_ref[...] = jnp.where((key >= 0) & (key < span_col), 0.0, MASKED)


def attend_arrived(rows_ref, slot_of_ref, bias_ref, mine_ref, other_ref, out_ref):
    padded, prompt_rows = bias_ref.shape
    kv_heads = mine_ref.shape[1] // (2 * HD)
    group = rows_ref.shape[1] // (kv_heads * HD)
    rows = rows_ref[...]
    slot_of = slot_of_ref[...]
    bias = bias_ref[...]
    kv = (
        mine_ref[:prompt_rows, :].astype(F32) + other_ref[:prompt_rows, :].astype(F32)
    ).astype(BF16)
    scores = []
    for h in range(kv_heads):
        stacked = jnp.concatenate(
            [rows[:, (h * group + i) * HD : (h * group + i + 1) * HD] for i in range(group)],
            axis=0,
        )
        keys = kv[:, h * 2 * HD : (h * 2 + 1) * HD]
        scores.append(
            lax.dot_general(
                stacked, keys, (((1,), (1,)), ((), ())), preferred_element_type=F32
            )
        )
    scores = [
        x.reshape(group, padded, prompt_rows) * LOG2_SCALE + bias[None] for x in scores
    ]
    largest = [jnp.max(x, axis=2, keepdims=True) for x in scores]
    weights = [jnp.exp2(x - y) for x, y in zip(scores, largest)]
    totals = [jnp.sum(x, axis=2, keepdims=True) for x in weights]
    lane = iota((padded, STATS), 1)
    lse = jnp.zeros((padded, STATS), F32)
    pieces = []
    for h in range(kv_heads):
        values = jnp.dot(
            weights[h].reshape(group * padded, prompt_rows).astype(BF16),
            kv[:, (h * 2 + 1) * HD : (h * 2 + 2) * HD],
            preferred_element_type=F32,
        ).reshape(group, padded, HD)
        values = values / totals[h]
        head_lse = largest[h] + jnp.log2(totals[h])
        for i in range(group):
            pieces.append(values[i])
            lse = jnp.where(lane == h * group + i, head_lse[i], lse)
    result = jnp.concatenate(pieces + list(split_bf16(lse)), axis=1).astype(BF16)
    answers = lax.dot_general(slot_of, result, TRANSPOSED, preferred_element_type=F32)
    for s in range(out_ref.shape[0]):
        out_ref[s] = answers[s * PITCH : s * PITCH + CAP].astype(BF16)


def attend_cache(
    queries_ref,
    cache_ref,
    len_ref,
    mine_ref,
    other_ref,
    pick_ref,
    after_ref,
    out_ref,
    slot_out_ref,
    slot_lse_ref,
    *,
    block_rows,
    first_block,
):
    cache_rows, width = cache_ref.shape[1:]
    row_count = len_ref.shape[1]
    kv_heads = width // (2 * HD)
    group = queries_ref.shape[1] // (kv_heads * HD)
    unit = 8
    keys_of = unit * cache_rows
    step = pl.program_id(0)
    block = pl.ds(pl.multiple_of(step * block_rows, block_rows), block_rows)
    first_row = pl.multiple_of((step + first_block) * block_rows, block_rows)
    own_block = pl.ds(first_row + (mine_ref.shape[0] - row_count), block_rows)
    queries = queries_ref[...].astype(F32)
    own = mine_ref[own_block, :].astype(F32) + other_ref[own_block, :].astype(F32)
    own = own.astype(BF16).astype(F32)
    key = iota((unit, keys_of), 1) - iota((unit, keys_of), 0) * cache_rows
    lengths = len_ref[...].astype(F32)
    lane = iota((unit, STATS), 1)
    ones = jnp.ones((keys_of, HD), BF16)
    units = range(block_rows // unit)

    def rows_of(u):
        return slice(u * unit, (u + 1) * unit)

    pairs = [(u, h) for u in units for h in range(kv_heads)]
    bias = []
    for u in units:
        row = iota((unit, row_count), 0) + (first_row + u * unit)
        length = jnp.sum(
            jnp.where(iota((unit, row_count), 1) == row, lengths, 0.0), axis=1, keepdims=True
        ).astype(jnp.int32)
        bias.append(jnp.where((key >= 0) & (key < length), 0.0, MASKED))
    q, scores, own_scores = [], [], []
    for u, h in pairs:
        at = slice(u * unit, (u + 1) * unit)
        q.append(
            jnp.stack(
                [
                    queries[at, (h * group + i) * HD : (h * group + i + 1) * HD]
                    for i in range(group)
                ],
                axis=0,
            )
        )
        keys = cache_ref[rows_of(u), :, h * 2 * HD : (h * 2 + 1) * HD].reshape(keys_of, HD)
        scores.append(
            lax.dot_general(
                q[-1].reshape(group * unit, HD).astype(BF16),
                keys,
                (((1,), (1,)), ((), ())),
                preferred_element_type=F32,
            ).reshape(group, unit, keys_of)
        )
    for n, (u, h) in enumerate(pairs):
        at = slice(u * unit, (u + 1) * unit)
        own_key = own[at, h * 2 * HD : (h * 2 + 1) * HD]
        own_scores.append(jnp.sum(q[n] * own_key[None], axis=2, keepdims=True) * LOG2_SCALE)
    scores = [scores[n] * LOG2_SCALE + bias[u][None] for n, (u, h) in enumerate(pairs)]
    largest = [
        jnp.maximum(jnp.max(x, axis=2, keepdims=True), y) for x, y in zip(scores, own_scores)
    ]
    weights = [jnp.exp2(x - y).astype(BF16) for x, y in zip(scores, largest)]
    own_weights = [jnp.exp2(x - y) for x, y in zip(own_scores, largest)]
    sums = []
    for n, (u, h) in enumerate(pairs):
        at = slice(u * unit, (u + 1) * unit)
        values = cache_ref[rows_of(u), :, (h * 2 + 1) * HD : (h * 2 + 2) * HD].reshape(keys_of, HD)
        sums.append(
            jnp.dot(
                weights[n].reshape(group * unit, keys_of),
                jnp.concatenate([values, ones], axis=1),
                preferred_element_type=F32,
            ).reshape(group, unit, 2 * HD)
        )
    pieces = [[] for _ in units]
    stats = [jnp.zeros((unit, STATS), F32) for _ in units]
    for n, (u, h) in enumerate(pairs):
        at = slice(u * unit, (u + 1) * unit)
        own_value = own[at, (h * 2 + 1) * HD : (h * 2 + 2) * HD]
        total = sums[n][:, :, HD:] + own_weights[n]
        result = (sums[n][:, :, :HD] + own_weights[n] * own_value[None]) / total
        lse = largest[n] + jnp.log2(total)
        for i in range(group):
            pieces[u].append(result[i])
            stats[u] = jnp.where(lane == h * group + i, lse[i], stats[u])
    out = jnp.concatenate([jnp.concatenate(x, axis=1) for x in pieces], axis=0).astype(BF16)
    out_ref[block, :] = out
    pick = pick_ref[...]
    here = iota((row_count, block_rows), 0) == iota((row_count, block_rows), 1) + first_row
    pick = jnp.dot(pick, here.astype(F32).astype(BF16), preferred_element_type=F32).astype(BF16)
    slot_out = jnp.dot(pick, out, preferred_element_type=F32)
    lse = jnp.concatenate(stats, axis=0)
    slot_lse = sum(
        jnp.dot(pick, part.astype(BF16), preferred_element_type=F32) for part in split_bf16(lse)
    )

    @pl.when(step == 0)
    def _():
        slot_out_ref[...] = slot_out
        slot_lse_ref[...] = slot_lse

    @pl.when(step > 0)
    def _():
        slot_out_ref[...] += slot_out
        slot_lse_ref[...] += slot_lse


def merge(pick_ref, *refs):
    parts, arrived_ref, out_ref = refs[:-2], refs[-2], refs[-1]
    cached_refs, slot_out_refs, slot_lse_refs = parts[0::3], parts[1::3], parts[2::3]
    width = out_ref.shape[1]
    pick = pick_ref[...]
    arrived = jnp.concatenate(
        [arrived_ref[s].astype(F32) for s in range(arrived_ref.shape[0])], axis=0
    )
    arrived_lse = (
        arrived[:, width : width + STATS]
        + arrived[:, width + STATS : width + 2 * STATS]
        + arrived[:, width + 2 * STATS :]
    )
    cached_lse = sum(ref[...] for ref in slot_lse_refs)
    largest = jnp.maximum(cached_lse, arrived_lse)
    cached_weight = jnp.exp2(cached_lse - largest)
    arrived_weight = jnp.exp2(arrived_lse - largest)
    total = cached_weight + arrived_weight
    cached_weight = cached_weight / total
    arrived_weight = arrived_weight / total
    has = lax.dot_general(
        pick, jnp.ones((pick.shape[0], HD), BF16), TRANSPOSED, preferred_element_type=F32
    )
    for i in range(width // HD):
        at = slice(i * HD, (i + 1) * HD)
        merged = (
            sum(ref[:, at] for ref in slot_out_refs) * cached_weight[:, i : i + 1]
            + arrived[:, at] * arrived_weight[:, i : i + 1]
        )
        placed = lax.dot_general(
            pick, merged.astype(BF16), TRANSPOSED, preferred_element_type=F32
        )
        row = 0
        for ref in cached_refs:
            rows = slice(row, row + ref.shape[0])
            kept = ref[:, at].astype(F32)
            out_ref[rows, at] = jnp.where(has[rows] > 0.5, placed[rows], kept).astype(BF16)
            row += ref.shape[0]


def compiler_params(megabytes):
    return pltpu.CompilerParams(vmem_limit_bytes=megabytes * 1024 * 1024)


RESIDENT = pl.BlockSpec(memory_space=pltpu.VMEM)
REMAINS = pl.BlockSpec(memory_space=pl.ANY)


def in_vmem(x):
    return pltpu.with_memory_space_constraint(x, pltpu.VMEM)


def in_hbm(x):
    return pltpu.with_memory_space_constraint(x, pltpu.HBM)


def shards(
    prompts, decode_hidden, queries, kv_cache, cache_len, span_len, target_row, w_kv, kv_scale
):
    row_count = decode_hidden.shape[0]
    prompt_rows, features = prompts.shape
    sections = lax.axis_size("section")
    local_width = kv_cache.shape[2]
    query_width = queries.shape[1]
    slots = sections * CAP
    all_rows = prompt_rows + row_count
    scale = kv_scale.reshape(1, -1)
    lengths = cache_len.reshape(1, -1)

    depth = 512
    pick, asked, rows_head, w_head = pl.pallas_call(
        select_queries,
        in_specs=[RESIDENT] + [REMAINS] * 4,
        out_specs=[RESIDENT] * 4,
        out_shape=[
            pltpu.VMEM((slots, row_count), BF16),
            jax.ShapeDtypeStruct((sections, CAP, query_width), BF16),
            pltpu.VMEM((all_rows, depth), BF16),
            pltpu.VMEM((depth, w_kv.shape[1]), BF16),
        ],
        scratch_shapes=[pltpu.VMEM(queries.shape, BF16), pltpu.SemaphoreType.DMA((4,))],
        compiler_params=compiler_params(16),
        name="select_queries",
    )(in_hbm(target_row), in_hbm(queries), in_hbm(prompts), in_hbm(decode_hidden), in_hbm(w_kv))
    asked = lax.all_to_all(asked, "section", 0, 0)

    rest = features - depth
    edges = (0, 512, 1408, 2816, 4096, rest)
    count = len(edges) - 1
    mine, theirs = pl.pallas_call(
        functools.partial(project, edges=edges, block=all_rows // 2),
        in_specs=[RESIDENT] * 2 + [REMAINS] * 3 + [RESIDENT],
        out_specs=[RESIDENT, RESIDENT],
        scratch_shapes=[
            pltpu.VMEM((all_rows, rest), BF16),
            pltpu.VMEM((rest, w_kv.shape[1]), BF16),
            pltpu.VMEM((all_rows, w_kv.shape[1]), F32),
            pltpu.SemaphoreType.DMA((count,)),
            pltpu.SemaphoreType.DMA((count,)),
            pltpu.SemaphoreType.DMA((count,)),
        ],
        out_shape=[pltpu.VMEM((all_rows, local_width), BF16)] * 2,
        compiler_params=compiler_params(44),
        name="project",
    )(
        in_vmem(rows_head),
        in_vmem(w_head),
        in_hbm(prompts),
        in_hbm(decode_hidden),
        in_hbm(w_kv),
        in_hbm(scale),
    )
    theirs, asked = lax.optimization_barrier((theirs, asked))
    other = lax.ppermute(theirs, "tp", [(0, 1), (1, 0)])

    block = 32
    calls = 1
    call_rows = row_count // calls

    def cache_share(call, after):
        first_block = call * call_rows // block
        return pl.pallas_call(
            functools.partial(attend_cache, block_rows=block, first_block=first_block),
            grid=(call_rows // block,),
            in_specs=[
                pl.BlockSpec((block, query_width), lambda b: (first_block + b, 0)),
                pl.BlockSpec((block, *kv_cache.shape[1:]), lambda b: (first_block + b, 0, 0)),
            ]
            + [RESIDENT] * 4
            + [REMAINS],
            out_specs=[RESIDENT] * 3,
            out_shape=[
                pltpu.VMEM((call_rows, query_width), BF16),
                pltpu.VMEM((slots, query_width), F32),
                pltpu.VMEM((slots, STATS), F32),
            ],
            compiler_params=compiler_params(24),
            name="attend_cache",
        )(
            in_hbm(queries),
            in_hbm(kv_cache),
            in_hbm(lengths),
            in_vmem(mine),
            in_vmem(other),
            in_vmem(pick),
            after,
        )

    padded = -(-span_len.shape[1] // 16) * 16
    prepared = pl.pallas_call(
        functools.partial(prepare_arrived, row_count=row_count),
        in_specs=[RESIDENT] * 3,
        out_specs=[RESIDENT] * 3,
        out_shape=[
            pltpu.VMEM((padded, query_width), BF16),
            pltpu.VMEM((padded, sections * PITCH), BF16),
            pltpu.VMEM((padded, prompt_rows), F32),
        ],
        compiler_params=compiler_params(16),
        name="prepare_arrived",
    )(in_hbm(target_row), in_hbm(span_len), in_vmem(asked))
    answer_width = query_width + 3 * STATS
    answers = pl.pallas_call(
        attend_arrived,
        in_specs=[RESIDENT] * 5,
        out_specs=RESIDENT,
        out_shape=jax.ShapeDtypeStruct((sections, CAP, answer_width), BF16),
        compiler_params=compiler_params(24),
        name="attend_arrived",
    )(*map(in_vmem, (*prepared, mine, other)))
    after = answers
    answers = lax.all_to_all(answers, "section", 0, 0)
    shares = []
    for call in range(calls):
        shares += cache_share(call, after)

    return pl.pallas_call(
        merge,
        in_specs=[RESIDENT] * (2 + len(shares)),
        out_specs=RESIDENT,
        out_shape=jax.ShapeDtypeStruct((row_count, query_width), BF16),
        compiler_params=compiler_params(24),
        name="merge",
    )(*map(in_vmem, (pick, *shares, answers)))


def solution(mesh):
    in_specs = (
        P(("groups", "section"), "tp"),
        P(("groups", "section"), "tp"),
        P(("groups", "section"), "tp"),
        P(("groups", "section"), None, "tp"),
        P(("groups", "section")),
        P("groups", None),
        P("groups", None),
        P("tp", None),
        P(),
    )
    out_specs = P(("groups", "section"), "tp")
    return jax.shard_map(shards, mesh=mesh, in_specs=in_specs, out_specs=out_specs, check_vma=False)
```

```python
import functools
import math

import jax
import jax.numpy as jnp
from jax import lax
from jax.experimental import pallas as pl
from jax.experimental.pallas import tpu as pltpu
from jax.sharding import PartitionSpec as P

HD = 128
CAP = 2
STATS = 128
MASKED = -1e30
PITCH = 8
LOG2_SCALE = HD ** (-0.5) * math.log2(math.e)
F32 = jnp.float32
BF16 = jnp.bfloat16
TRANSPOSED = (((0,), (0,)), ((), ()))


def iota(shape, dim):
    return lax.broadcasted_iota(jnp.int32, shape, dim)


def one_hot(shape, dim, index):
    return (iota(shape, dim) == index).astype(F32).astype(BF16)


def pick_rows(target_ref, row_count, pitch):
    sections, requests = target_ref.shape
    shape = (sections * pitch, requests)
    position = lax.axis_index("section")
    slot_id = iota(shape, 0)
    table = jnp.zeros(shape, jnp.int32)
    for s in range(sections):
        mine = (slot_id >= s * pitch) & (slot_id < (s + 1) * pitch)
        table = jnp.where(mine, target_ref[s : s + 1, :], table)
    local = table - position * row_count
    here = (local >= 0) & (local < row_count)
    square = (requests, requests)
    earlier = jnp.dot(
        here.astype(F32).astype(BF16),
        (iota(square, 0) < iota(square, 1)).astype(F32).astype(BF16),
        preferred_element_type=F32,
    )
    chosen = here & (earlier == lax.rem(slot_id, pitch).astype(F32))
    row = jnp.max(jnp.where(chosen, local.astype(F32), -1.0), axis=1, keepdims=True)
    return one_hot((shape[0], row_count), 1, row.astype(jnp.int32))


def select_queries(target_ref, queries_ref, pick_ref, asked_ref, queries_here_ref, sem):
    row_count = queries_ref.shape[0]
    copy = pltpu.make_async_copy(queries_ref, queries_here_ref, sem)
    copy.start()
    pick = pick_rows(target_ref, row_count, PITCH)
    pick_ref[...] = pick_rows(target_ref, row_count, CAP)
    copy.wait()
    asked = jnp.dot(pick, queries_here_ref[...], preferred_element_type=F32)
    for s in range(asked_ref.shape[0]):
        asked_ref[s] = asked[s * PITCH : s * PITCH + CAP].astype(BF16)


def spans(edges):
    return [slice(a, b) for a, b in zip(edges[:-1], edges[1:])]


def project_first(
    prompts_ref,
    hidden_ref,
    w_ref,
    scale_ref,
    theirs_ref,
    total_mine_ref,
    rows_ref,
    w_mine_ref,
    w_theirs_ref,
    total_ref,
    scale_here_ref,
    row_sems,
    hidden_sems,
    theirs_sems,
    mine_sems,
    scale_sem,
    *,
    edges,
    head,
):
    prompt_rows = prompts_ref.shape[0]
    features, width = w_mine_ref.shape
    tp = lax.axis_index("tp")
    theirs = pl.ds(pl.multiple_of((1 - tp) * width, width), width)
    mine = pl.ds(pl.multiple_of(tp * width, width), width)
    chunks = spans(edges)
    waits = []
    for c, at in enumerate(chunks):
        copies = [
            pltpu.make_async_copy(
                w_ref.at[at, theirs], w_theirs_ref.at[at, :], theirs_sems.at[c]
            ),
            pltpu.make_async_copy(
                prompts_ref.at[:, at], rows_ref.at[:prompt_rows, at], row_sems.at[c]
            ),
            pltpu.make_async_copy(
                hidden_ref.at[:, at], rows_ref.at[prompt_rows:, at], hidden_sems.at[c]
            ),
        ]
        for copy in copies:
            copy.start()
        waits.append(copies)
    later = [
        pltpu.make_async_copy(scale_ref.at[:, theirs], scale_here_ref, scale_sem),
        pltpu.make_async_copy(
            w_ref.at[:head, mine], w_mine_ref.at[:head, :], mine_sems.at[0]
        ),
        pltpu.make_async_copy(
            w_ref.at[head:, mine], w_mine_ref.at[head:, :], mine_sems.at[1]
        ),
    ]
    for copy in later:
        copy.start()
    for c, at in enumerate(chunks):
        for copy in waits[c]:
            copy.wait()
        part = jnp.dot(rows_ref[:, at], w_theirs_ref[at, :], preferred_element_type=F32)
        if c == 0:
            total_ref[...] = part
        elif c < len(chunks) - 1:
            total_ref[...] += part
        else:
            later[0].wait()
            theirs_ref[...] = ((total_ref[...] + part) * scale_here_ref[...]).astype(BF16)
    later[1].wait()
    total_mine_ref[...] = jnp.dot(
        rows_ref[:, :head], w_mine_ref[:head, :], preferred_element_type=F32
    )
    later[2].wait()


def project_second(
    rows_ref, w_mine_ref, total_ref, scale_ref, out_ref, scale_here_ref, scale_sem, *, head, block
):
    width = out_ref.shape[1]
    mine = pl.ds(pl.multiple_of(lax.axis_index("tp") * width, width), width)
    copy = pltpu.make_async_copy(scale_ref.at[:, mine], scale_here_ref, scale_sem)
    copy.start()
    for m in spans(range(0, out_ref.shape[0] + 1, block)):
        part = jnp.dot(rows_ref[m, head:], w_mine_ref[head:, :], preferred_element_type=F32)
        if m.start == 0:
            copy.wait()
        out_ref[m, :] = ((total_ref[m, :] + part) * scale_here_ref[...]).astype(BF16)


def split_bf16(x):
    high = x.astype(BF16).astype(F32)
    middle = (x - high).astype(BF16).astype(F32)
    return high, middle, (x - high - middle).astype(BF16).astype(F32)


def request_slots(target_ref, span_ref, row_count, padded):
    sections, requests = target_ref.shape
    position = lax.axis_index("section")
    target = target_ref[pl.ds(position, 1), :].astype(F32)
    span = span_ref[pl.ds(position, 1), :].astype(F32)
    diagonal = iota((padded, requests), 0) == iota((padded, requests), 1)
    target_col = jnp.sum(jnp.where(diagonal, target, 0.0), axis=1, keepdims=True)
    span_col = jnp.sum(jnp.where(diagonal, span, 0.0), axis=1, keepdims=True)
    section_row = jnp.zeros_like(target)
    section_col = jnp.zeros_like(target_col)
    for s in range(1, sections):
        section_row = section_row + (target >= s * row_count).astype(F32)
        section_col = section_col + (target_col >= s * row_count).astype(F32)
    before = (section_row == section_col) & (
        iota((padded, requests), 1) < iota((padded, requests), 0)
    )
    rank_col = jnp.sum(before.astype(F32), axis=1, keepdims=True).astype(jnp.int32)
    real = iota((padded, 1), 0) < requests
    section_col = jnp.where(real, section_col.astype(jnp.int32), -1)
    return section_col, rank_col, span_col.astype(jnp.int32)


def prepare_arrived(
    target_ref, span_ref, asked_ref, rows_ref, slot_of_ref, bias_ref, *, row_count
):
    sections, requests = target_ref.shape
    padded, prompt_rows = bias_ref.shape
    span_rows = prompt_rows // requests
    section_col, rank_col, span_col = request_slots(target_ref, span_ref, row_count, padded)
    slot = jnp.where(section_col >= 0, section_col * PITCH + rank_col, -1)
    slot_of_ref[...] = one_hot((padded, sections * PITCH), 1, slot)
    slot = jnp.where(section_col >= 0, section_col * CAP + rank_col, -1)
    asked = jnp.concatenate([asked_ref[s].astype(F32) for s in range(sections)], axis=0)
    rows_ref[...] = jnp.dot(
        one_hot((padded, sections * CAP), 1, slot),
        asked.astype(BF16),
        preferred_element_type=F32,
    ).astype(BF16)
    key = iota((padded, prompt_rows), 1) - iota((padded, prompt_rows), 0) * span_rows
    bias_ref[...] = jnp.where((key >= 0) & (key < span_col), 0.0, MASKED)


def attend_arrived(rows_ref, slot_of_ref, bias_ref, mine_ref, other_ref, out_ref):
    padded, prompt_rows = bias_ref.shape
    kv_heads = mine_ref.shape[1] // (2 * HD)
    group = rows_ref.shape[1] // (kv_heads * HD)
    rows = rows_ref[...]
    slot_of = slot_of_ref[...]
    bias = bias_ref[...]
    kv = (
        mine_ref[:prompt_rows, :].astype(F32) + other_ref[:prompt_rows, :].astype(F32)
    ).astype(BF16)
    scores = []
    for h in range(kv_heads):
        stacked = jnp.concatenate(
            [rows[:, (h * group + i) * HD : (h * group + i + 1) * HD] for i in range(group)],
            axis=0,
        )
        keys = kv[:, h * 2 * HD : (h * 2 + 1) * HD]
        scores.append(
            lax.dot_general(
                stacked, keys, (((1,), (1,)), ((), ())), preferred_element_type=F32
            )
        )
    scores = [
        x.reshape(group, padded, prompt_rows) * LOG2_SCALE + bias[None] for x in scores
    ]
    largest = [jnp.max(x, axis=2, keepdims=True) for x in scores]
    weights = [jnp.exp2(x - y) for x, y in zip(scores, largest)]
    totals = [jnp.sum(x, axis=2, keepdims=True) for x in weights]
    lane = iota((padded, STATS), 1)
    lse = jnp.zeros((padded, STATS), F32)
    pieces = []
    for h in range(kv_heads):
        values = jnp.dot(
            weights[h].reshape(group * padded, prompt_rows).astype(BF16),
            kv[:, (h * 2 + 1) * HD : (h * 2 + 2) * HD],
            preferred_element_type=F32,
        ).reshape(group, padded, HD)
        values = values / totals[h]
        head_lse = largest[h] + jnp.log2(totals[h])
        for i in range(group):
            pieces.append(values[i])
            lse = jnp.where(lane == h * group + i, head_lse[i], lse)
    result = jnp.concatenate(pieces + list(split_bf16(lse)), axis=1).astype(BF16)
    answers = lax.dot_general(slot_of, result, TRANSPOSED, preferred_element_type=F32)
    for s in range(out_ref.shape[0]):
        out_ref[s] = answers[s * PITCH : s * PITCH + CAP].astype(BF16)


def attend_cache(
    queries_ref,
    cache_ref,
    len_ref,
    mine_ref,
    other_ref,
    pick_ref,
    after_ref,
    out_ref,
    slot_out_ref,
    slot_lse_ref,
    *,
    block_rows,
    first_block,
):
    cache_rows, width = cache_ref.shape[1:]
    row_count = len_ref.shape[1]
    kv_heads = width // (2 * HD)
    group = queries_ref.shape[1] // (kv_heads * HD)
    unit = 8
    keys_of = unit * cache_rows
    step = pl.program_id(0)
    block = pl.ds(pl.multiple_of(step * block_rows, block_rows), block_rows)
    first_row = pl.multiple_of((step + first_block) * block_rows, block_rows)
    own_block = pl.ds(first_row + (mine_ref.shape[0] - row_count), block_rows)
    queries = queries_ref[...].astype(F32)
    own = mine_ref[own_block, :].astype(F32) + other_ref[own_block, :].astype(F32)
    own = own.astype(BF16).astype(F32)
    key = iota((unit, keys_of), 1) - iota((unit, keys_of), 0) * cache_rows
    lengths = len_ref[...].astype(F32)
    lane = iota((unit, STATS), 1)
    ones = jnp.ones((keys_of, HD), BF16)
    units = range(block_rows // unit)

    def rows_of(u):
        return slice(u * unit, (u + 1) * unit)

    pairs = [(u, h) for u in units for h in range(kv_heads)]
    bias = []
    for u in units:
        row = iota((unit, row_count), 0) + (first_row + u * unit)
        length = jnp.sum(
            jnp.where(iota((unit, row_count), 1) == row, lengths, 0.0), axis=1, keepdims=True
        ).astype(jnp.int32)
        bias.append(jnp.where((key >= 0) & (key < length), 0.0, MASKED))
    q, scores, own_scores = [], [], []
    for u, h in pairs:
        at = slice(u * unit, (u + 1) * unit)
        q.append(
            jnp.stack(
                [
                    queries[at, (h * group + i) * HD : (h * group + i + 1) * HD]
                    for i in range(group)
                ],
                axis=0,
            )
        )
        keys = cache_ref[rows_of(u), :, h * 2 * HD : (h * 2 + 1) * HD].reshape(keys_of, HD)
        scores.append(
            lax.dot_general(
                q[-1].reshape(group * unit, HD).astype(BF16),
                keys,
                (((1,), (1,)), ((), ())),
                preferred_element_type=F32,
            ).reshape(group, unit, keys_of)
        )
    for n, (u, h) in enumerate(pairs):
        at = slice(u * unit, (u + 1) * unit)
        own_key = own[at, h * 2 * HD : (h * 2 + 1) * HD]
        own_scores.append(jnp.sum(q[n] * own_key[None], axis=2, keepdims=True) * LOG2_SCALE)
    scores = [scores[n] * LOG2_SCALE + bias[u][None] for n, (u, h) in enumerate(pairs)]
    largest = [
        jnp.maximum(jnp.max(x, axis=2, keepdims=True), y) for x, y in zip(scores, own_scores)
    ]
    weights = [jnp.exp2(x - y).astype(BF16) for x, y in zip(scores, largest)]
    own_weights = [jnp.exp2(x - y) for x, y in zip(own_scores, largest)]
    sums = []
    for n, (u, h) in enumerate(pairs):
        at = slice(u * unit, (u + 1) * unit)
        values = cache_ref[rows_of(u), :, (h * 2 + 1) * HD : (h * 2 + 2) * HD].reshape(keys_of, HD)
        sums.append(
            jnp.dot(
                weights[n].reshape(group * unit, keys_of),
                jnp.concatenate([values, ones], axis=1),
                preferred_element_type=F32,
            ).reshape(group, unit, 2 * HD)
        )
    pieces = [[] for _ in units]
    stats = [jnp.zeros((unit, STATS), F32) for _ in units]
    for n, (u, h) in enumerate(pairs):
        at = slice(u * unit, (u + 1) * unit)
        own_value = own[at, (h * 2 + 1) * HD : (h * 2 + 2) * HD]
        total = sums[n][:, :, HD:] + own_weights[n]
        result = (sums[n][:, :, :HD] + own_weights[n] * own_value[None]) / total
        lse = largest[n] + jnp.log2(total)
        for i in range(group):
            pieces[u].append(result[i])
            stats[u] = jnp.where(lane == h * group + i, lse[i], stats[u])
    out = jnp.concatenate([jnp.concatenate(x, axis=1) for x in pieces], axis=0).astype(BF16)
    out_ref[block, :] = out
    pick = pick_ref[...]
    here = iota((row_count, block_rows), 0) == iota((row_count, block_rows), 1) + first_row
    pick = jnp.dot(pick, here.astype(F32).astype(BF16), preferred_element_type=F32).astype(BF16)
    slot_out = jnp.dot(pick, out, preferred_element_type=F32)
    lse = jnp.concatenate(stats, axis=0)
    slot_lse = sum(
        jnp.dot(pick, part.astype(BF16), preferred_element_type=F32) for part in split_bf16(lse)
    )

    @pl.when(step == 0)
    def _():
        slot_out_ref[...] = slot_out
        slot_lse_ref[...] = slot_lse

    @pl.when(step > 0)
    def _():
        slot_out_ref[...] += slot_out
        slot_lse_ref[...] += slot_lse


def merge(pick_ref, *refs):
    parts, arrived_ref, out_ref = refs[:-2], refs[-2], refs[-1]
    cached_refs, slot_out_refs, slot_lse_refs = parts[0::3], parts[1::3], parts[2::3]
    width = out_ref.shape[1]
    pick = pick_ref[...]
    arrived = jnp.concatenate(
        [arrived_ref[s].astype(F32) for s in range(arrived_ref.shape[0])], axis=0
    )
    arrived_lse = (
        arrived[:, width : width + STATS]
        + arrived[:, width + STATS : width + 2 * STATS]
        + arrived[:, width + 2 * STATS :]
    )
    cached_lse = sum(ref[...] for ref in slot_lse_refs)
    largest = jnp.maximum(cached_lse, arrived_lse)
    cached_weight = jnp.exp2(cached_lse - largest)
    arrived_weight = jnp.exp2(arrived_lse - largest)
    total = cached_weight + arrived_weight
    cached_weight = cached_weight / total
    arrived_weight = arrived_weight / total
    has = lax.dot_general(
        pick, jnp.ones((pick.shape[0], HD), BF16), TRANSPOSED, preferred_element_type=F32
    )
    for i in range(width // HD):
        at = slice(i * HD, (i + 1) * HD)
        merged = (
            sum(ref[:, at] for ref in slot_out_refs) * cached_weight[:, i : i + 1]
            + arrived[:, at] * arrived_weight[:, i : i + 1]
        )
        placed = lax.dot_general(
            pick, merged.astype(BF16), TRANSPOSED, preferred_element_type=F32
        )
        row = 0
        for ref in cached_refs:
            rows = slice(row, row + ref.shape[0])
            kept = ref[:, at].astype(F32)
            out_ref[rows, at] = jnp.where(has[rows] > 0.5, placed[rows], kept).astype(BF16)
            row += ref.shape[0]


def compiler_params(megabytes):
    return pltpu.CompilerParams(vmem_limit_bytes=megabytes * 1024 * 1024)


RESIDENT = pl.BlockSpec(memory_space=pltpu.VMEM)
REMAINS = pl.BlockSpec(memory_space=pl.ANY)


def in_vmem(x):
    return pltpu.with_memory_space_constraint(x, pltpu.VMEM)


def in_hbm(x):
    return pltpu.with_memory_space_constraint(x, pltpu.HBM)


def shards(
    prompts, decode_hidden, queries, kv_cache, cache_len, span_len, target_row, w_kv, kv_scale
):
    row_count = decode_hidden.shape[0]
    prompt_rows, features = prompts.shape
    sections = lax.axis_size("section")
    local_width = kv_cache.shape[2]
    query_width = queries.shape[1]
    slots = sections * CAP
    all_rows = prompt_rows + row_count
    scale = kv_scale.reshape(1, -1)
    lengths = cache_len.reshape(1, -1)

    pick, asked = pl.pallas_call(
        select_queries,
        in_specs=[RESIDENT, REMAINS],
        out_specs=[RESIDENT] * 2,
        out_shape=[
            pltpu.VMEM((slots, row_count), BF16),
            jax.ShapeDtypeStruct((sections, CAP, query_width), BF16),
        ],
        scratch_shapes=[pltpu.VMEM(queries.shape, BF16), pltpu.SemaphoreType.DMA(())],
        compiler_params=compiler_params(16),
        name="select_queries",
    )(in_hbm(target_row), in_hbm(queries))
    asked = lax.all_to_all(asked, "section", 0, 0)

    edges = (0, 256, 768, 1536, 2560, 4096, features)
    count = len(edges) - 1
    head = features // 3
    theirs, total_mine, rows, w_mine = pl.pallas_call(
        functools.partial(project_first, edges=edges, head=head),
        in_specs=[REMAINS] * 4,
        out_specs=[RESIDENT] * 4,
        scratch_shapes=[
            pltpu.VMEM((features, local_width), BF16),
            pltpu.VMEM((all_rows, local_width), F32),
            pltpu.VMEM((1, local_width), F32),
            pltpu.SemaphoreType.DMA((count,)),
            pltpu.SemaphoreType.DMA((count,)),
            pltpu.SemaphoreType.DMA((count,)),
            pltpu.SemaphoreType.DMA((2,)),
            pltpu.SemaphoreType.DMA(()),
        ],
        out_shape=[
            pltpu.VMEM((all_rows, local_width), BF16),
            pltpu.VMEM((all_rows, local_width), F32),
            pltpu.VMEM((all_rows, features), BF16),
            pltpu.VMEM((features, local_width), BF16),
        ],
        compiler_params=compiler_params(16),
        name="project_first",
    )(in_hbm(prompts), in_hbm(decode_hidden), in_hbm(w_kv), in_hbm(scale))
    theirs, asked = lax.optimization_barrier((theirs, asked))
    other = lax.ppermute(theirs, "tp", [(0, 1), (1, 0)])
    mine = pl.pallas_call(
        functools.partial(project_second, head=head, block=all_rows // 2),
        in_specs=[RESIDENT] * 3 + [REMAINS],
        out_specs=RESIDENT,
        scratch_shapes=[pltpu.VMEM((1, local_width), F32), pltpu.SemaphoreType.DMA(())],
        out_shape=pltpu.VMEM((all_rows, local_width), BF16),
        compiler_params=compiler_params(16),
        name="project_second",
    )(*map(in_vmem, (rows, w_mine, total_mine)), in_hbm(scale))

    block = 32
    calls = 1
    call_rows = row_count // calls

    def cache_share(call, after):
        first_block = call * call_rows // block
        return pl.pallas_call(
            functools.partial(attend_cache, block_rows=block, first_block=first_block),
            grid=(call_rows // block,),
            in_specs=[
                pl.BlockSpec((block, query_width), lambda b: (first_block + b, 0)),
                pl.BlockSpec((block, *kv_cache.shape[1:]), lambda b: (first_block + b, 0, 0)),
            ]
            + [RESIDENT] * 4
            + [REMAINS],
            out_specs=[RESIDENT] * 3,
            out_shape=[
                pltpu.VMEM((call_rows, query_width), BF16),
                pltpu.VMEM((slots, query_width), F32),
                pltpu.VMEM((slots, STATS), F32),
            ],
            compiler_params=compiler_params(24),
            name="attend_cache",
        )(
            in_hbm(queries),
            in_hbm(kv_cache),
            in_hbm(lengths),
            in_vmem(mine),
            in_vmem(other),
            in_vmem(pick),
            after,
        )

    padded = -(-span_len.shape[1] // 16) * 16
    prepared = pl.pallas_call(
        functools.partial(prepare_arrived, row_count=row_count),
        in_specs=[RESIDENT] * 3,
        out_specs=[RESIDENT] * 3,
        out_shape=[
            pltpu.VMEM((padded, query_width), BF16),
            pltpu.VMEM((padded, sections * PITCH), BF16),
            pltpu.VMEM((padded, prompt_rows), F32),
        ],
        compiler_params=compiler_params(16),
        name="prepare_arrived",
    )(in_hbm(target_row), in_hbm(span_len), in_vmem(asked))
    answer_width = query_width + 3 * STATS
    answers = pl.pallas_call(
        attend_arrived,
        in_specs=[RESIDENT] * 5,
        out_specs=RESIDENT,
        out_shape=jax.ShapeDtypeStruct((sections, CAP, answer_width), BF16),
        compiler_params=compiler_params(24),
        name="attend_arrived",
    )(*map(in_vmem, (*prepared, mine, other)))
    after = answers
    answers = lax.all_to_all(answers, "section", 0, 0)
    shares = []
    for call in range(calls):
        shares += cache_share(call, after)

    return pl.pallas_call(
        merge,
        in_specs=[RESIDENT] * (2 + len(shares)),
        out_specs=RESIDENT,
        out_shape=jax.ShapeDtypeStruct((row_count, query_width), BF16),
        compiler_params=compiler_params(24),
        name="merge",
    )(*map(in_vmem, (pick, *shares, answers)))


def solution(mesh):
    in_specs = (
        P(("groups", "section"), "tp"),
        P(("groups", "section"), "tp"),
        P(("groups", "section"), "tp"),
        P(("groups", "section"), None, "tp"),
        P(("groups", "section")),
        P("groups", None),
        P("groups", None),
        P("tp", None),
        P(),
    )
    out_specs = P(("groups", "section"), "tp")
    return jax.shard_map(shards, mesh=mesh, in_specs=in_specs, out_specs=out_specs, check_vma=False)
```

```python
import functools
import math

import jax
import jax.numpy as jnp
from jax import lax
from jax.experimental import pallas as pl
from jax.experimental.pallas import tpu as pltpu
from jax.sharding import PartitionSpec as P

HD = 128
CAP = 2
STATS = 128
MASKED = -1e30
LSE_PITCH = 40
PITCH = 8
LOG2_SCALE = HD ** (-0.5) * math.log2(math.e)
F32 = jnp.float32
BF16 = jnp.bfloat16
TRANSPOSED = (((0,), (0,)), ((), ()))


def iota(shape, dim):
    return lax.broadcasted_iota(jnp.int32, shape, dim)


def one_hot(shape, dim, index):
    return (iota(shape, dim) == index).astype(F32).astype(BF16)


def pick_rows(target_ref, row_count, pitch):
    sections, requests = target_ref.shape
    shape = (sections * pitch, requests)
    position = lax.axis_index("section")
    slot_id = iota(shape, 0)
    table = jnp.zeros(shape, jnp.int32)
    for s in range(sections):
        mine = (slot_id >= s * pitch) & (slot_id < (s + 1) * pitch)
        table = jnp.where(mine, target_ref[s : s + 1, :], table)
    local = table - position * row_count
    here = (local >= 0) & (local < row_count)
    square = (requests, requests)
    earlier = jnp.dot(
        here.astype(F32).astype(BF16),
        (iota(square, 0) < iota(square, 1)).astype(F32).astype(BF16),
        preferred_element_type=F32,
    )
    chosen = here & (earlier == lax.rem(slot_id, pitch).astype(F32))
    row = jnp.max(jnp.where(chosen, local.astype(F32), -1.0), axis=1, keepdims=True)
    return one_hot((shape[0], row_count), 1, row.astype(jnp.int32))


def select_queries(target_ref, queries_ref, pick_ref, asked_ref):
    pick = pick_rows(target_ref, queries_ref.shape[0], CAP)
    pick_ref[...] = pick
    asked = jnp.dot(pick, queries_ref[...], preferred_element_type=F32).astype(BF16)
    for s in range(asked_ref.shape[0]):
        asked_ref[s] = asked[s * CAP : (s + 1) * CAP]


def spans(edges):
    return [slice(a, b) for a, b in zip(edges[:-1], edges[1:])]


def project(
    prompts_ref,
    hidden_ref,
    w_ref,
    scale_ref,
    mine_ref,
    theirs_ref,
    rows_ref,
    w_mine_ref,
    w_theirs_ref,
    total_ref,
    scale_here_ref,
    row_sems,
    hidden_sems,
    theirs_sems,
    mine_sem,
    scale_sems,
    *,
    edges,
    block,
):
    prompt_rows = prompts_ref.shape[0]
    width = mine_ref.shape[1]
    tp = lax.axis_index("tp")
    theirs = pl.ds(pl.multiple_of((1 - tp) * width, width), width)
    mine = pl.ds(pl.multiple_of(tp * width, width), width)
    chunks = spans(edges)
    waits = []
    for c, at in enumerate(chunks):
        copies = [
            pltpu.make_async_copy(
                w_ref.at[at, theirs], w_theirs_ref.at[at, :], theirs_sems.at[c]
            ),
            pltpu.make_async_copy(
                prompts_ref.at[:, at], rows_ref.at[:prompt_rows, at], row_sems.at[c]
            ),
            pltpu.make_async_copy(
                hidden_ref.at[:, at], rows_ref.at[prompt_rows:, at], hidden_sems.at[c]
            ),
        ]
        for copy in copies:
            copy.start()
        waits.append(copies)
    later = [
        pltpu.make_async_copy(
            scale_ref.at[:, theirs], scale_here_ref.at[0], scale_sems.at[0]
        ),
        pltpu.make_async_copy(scale_ref.at[:, mine], scale_here_ref.at[1], scale_sems.at[1]),
        pltpu.make_async_copy(w_ref.at[:, mine], w_mine_ref, mine_sem),
    ]
    for copy in later:
        copy.start()
    for c, at in enumerate(chunks):
        for copy in waits[c]:
            copy.wait()
        part = jnp.dot(rows_ref[:, at], w_theirs_ref[at, :], preferred_element_type=F32)
        if c == 0:
            total_ref[...] = part
        elif c < len(chunks) - 1:
            total_ref[...] += part
        else:
            later[0].wait()
            theirs_ref[...] = ((total_ref[...] + part) * scale_here_ref[0]).astype(BF16)
    for copy in later[1:]:
        copy.wait()
    for m in spans(range(0, rows_ref.shape[0] + 1, block)):
        total = jnp.dot(rows_ref[m, :], w_mine_ref[...], preferred_element_type=F32)
        mine_ref[m, :] = (total * scale_here_ref[1]).astype(BF16)


def split_bf16(x):
    high = x.astype(BF16).astype(F32)
    middle = (x - high).astype(BF16).astype(F32)
    return high, middle, (x - high - middle).astype(BF16).astype(F32)


def request_slots(target_ref, span_ref, row_count, padded):
    sections, requests = target_ref.shape
    position = lax.axis_index("section")
    target = target_ref[pl.ds(position, 1), :].astype(F32)
    span = span_ref[pl.ds(position, 1), :].astype(F32)
    diagonal = iota((padded, requests), 0) == iota((padded, requests), 1)
    target_col = jnp.sum(jnp.where(diagonal, target, 0.0), axis=1, keepdims=True)
    span_col = jnp.sum(jnp.where(diagonal, span, 0.0), axis=1, keepdims=True)
    section_row = jnp.zeros_like(target)
    section_col = jnp.zeros_like(target_col)
    for s in range(1, sections):
        section_row = section_row + (target >= s * row_count).astype(F32)
        section_col = section_col + (target_col >= s * row_count).astype(F32)
    before = (section_row == section_col) & (
        iota((padded, requests), 1) < iota((padded, requests), 0)
    )
    rank_col = jnp.sum(before.astype(F32), axis=1, keepdims=True).astype(jnp.int32)
    real = iota((padded, 1), 0) < requests
    section_col = jnp.where(real, section_col.astype(jnp.int32), -1)
    return section_col, rank_col, span_col.astype(jnp.int32)


def prepare_arrived(
    target_ref, span_ref, asked_ref, rows_ref, slot_of_ref, bias_ref, *, row_count
):
    sections, requests = target_ref.shape
    padded, prompt_rows = bias_ref.shape
    span_rows = prompt_rows // requests
    section_col, rank_col, span_col = request_slots(target_ref, span_ref, row_count, padded)
    slot = jnp.where(section_col >= 0, section_col * PITCH + rank_col, -1)
    slot_of_ref[...] = one_hot((padded, sections * PITCH), 1, slot)
    slot = jnp.where(section_col >= 0, section_col * CAP + rank_col, -1)
    asked = jnp.concatenate([asked_ref[s].astype(F32) for s in range(sections)], axis=0)
    rows_ref[...] = jnp.dot(
        one_hot((padded, sections * CAP), 1, slot),
        asked.astype(BF16),
        preferred_element_type=F32,
    ).astype(BF16)
    key = iota((padded, prompt_rows), 1) - iota((padded, prompt_rows), 0) * span_rows
    bias_ref[...] = jnp.where((key >= 0) & (key < span_col), 0.0, MASKED)


def attend_arrived(rows_ref, slot_of_ref, bias_ref, mine_ref, other_ref, out_ref):
    padded, prompt_rows = bias_ref.shape
    kv_heads = mine_ref.shape[1] // (2 * HD)
    group = rows_ref.shape[1] // (kv_heads * HD)
    rows = rows_ref[...]
    slot_of = slot_of_ref[...]
    bias = bias_ref[...]
    kv = (
        mine_ref[:prompt_rows, :].astype(F32) + other_ref[:prompt_rows, :].astype(F32)
    ).astype(BF16)
    scores = []
    for h in range(kv_heads):
        stacked = jnp.concatenate(
            [rows[:, (h * group + i) * HD : (h * group + i + 1) * HD] for i in range(group)],
            axis=0,
        )
        keys = kv[:, h * 2 * HD : (h * 2 + 1) * HD]
        scores.append(
            lax.dot_general(
                stacked, keys, (((1,), (1,)), ((), ())), preferred_element_type=F32
            )
        )
    scores = [
        x.reshape(group, padded, prompt_rows) * LOG2_SCALE + bias[None] for x in scores
    ]
    largest = [jnp.max(x, axis=2, keepdims=True) for x in scores]
    weights = [jnp.exp2(x - y) for x, y in zip(scores, largest)]
    totals = [jnp.sum(x, axis=2, keepdims=True) for x in weights]
    lane = iota((padded, STATS), 1)
    lse = jnp.zeros((padded, STATS), F32)
    pieces = []
    for h in range(kv_heads):
        values = jnp.dot(
            weights[h].reshape(group * padded, prompt_rows).astype(BF16),
            kv[:, (h * 2 + 1) * HD : (h * 2 + 2) * HD],
            preferred_element_type=F32,
        ).reshape(group, padded, HD)
        values = values / totals[h]
        head_lse = largest[h] + jnp.log2(totals[h])
        for i in range(group):
            pieces.append(values[i])
            lse = jnp.where(lane == h * group + i, head_lse[i], lse)
    high, middle, low = split_bf16(lse)
    stats = high + pltpu.roll(middle, LSE_PITCH, 1) + pltpu.roll(low, 2 * LSE_PITCH, 1)
    result = jnp.concatenate(pieces + [stats], axis=1).astype(BF16)
    answers = lax.dot_general(slot_of, result, TRANSPOSED, preferred_element_type=F32)
    for s in range(out_ref.shape[0]):
        out_ref[s] = answers[s * PITCH : s * PITCH + CAP].astype(BF16)


def attend_cache(
    queries_ref,
    cache_ref,
    len_ref,
    mine_ref,
    other_ref,
    pick_ref,
    after_ref,
    out_ref,
    slot_out_ref,
    slot_lse_ref,
    *,
    block_rows,
    first_block,
):
    cache_rows, width = cache_ref.shape[1:]
    row_count = len_ref.shape[1]
    kv_heads = width // (2 * HD)
    group = queries_ref.shape[1] // (kv_heads * HD)
    unit = 8
    keys_of = unit * cache_rows
    step = pl.program_id(0)
    block = pl.ds(pl.multiple_of(step * block_rows, block_rows), block_rows)
    first_row = pl.multiple_of((step + first_block) * block_rows, block_rows)
    own_block = pl.ds(first_row + (mine_ref.shape[0] - row_count), block_rows)
    queries = queries_ref[...].astype(F32)
    own = mine_ref[own_block, :].astype(F32) + other_ref[own_block, :].astype(F32)
    own = own.astype(BF16).astype(F32)
    key = iota((unit, keys_of), 1) - iota((unit, keys_of), 0) * cache_rows
    lengths = len_ref[...].astype(F32)
    lane = iota((unit, STATS), 1)
    ones = jnp.ones((keys_of, HD), BF16)
    units = range(block_rows // unit)

    def rows_of(u):
        return slice(u * unit, (u + 1) * unit)

    pairs = [(u, h) for u in units for h in range(kv_heads)]
    bias = []
    for u in units:
        row = iota((unit, row_count), 0) + (first_row + u * unit)
        length = jnp.sum(
            jnp.where(iota((unit, row_count), 1) == row, lengths, 0.0), axis=1, keepdims=True
        ).astype(jnp.int32)
        bias.append(jnp.where((key >= 0) & (key < length), 0.0, MASKED))
    q, scores, own_scores = [], [], []
    for u, h in pairs:
        at = slice(u * unit, (u + 1) * unit)
        q.append(
            jnp.stack(
                [
                    queries[at, (h * group + i) * HD : (h * group + i + 1) * HD]
                    for i in range(group)
                ],
                axis=0,
            )
        )
        keys = cache_ref[rows_of(u), :, h * 2 * HD : (h * 2 + 1) * HD].reshape(keys_of, HD)
        scores.append(
            lax.dot_general(
                q[-1].reshape(group * unit, HD).astype(BF16),
                keys,
                (((1,), (1,)), ((), ())),
                preferred_element_type=F32,
            ).reshape(group, unit, keys_of)
        )
    for n, (u, h) in enumerate(pairs):
        at = slice(u * unit, (u + 1) * unit)
        own_key = own[at, h * 2 * HD : (h * 2 + 1) * HD]
        own_scores.append(jnp.sum(q[n] * own_key[None], axis=2, keepdims=True) * LOG2_SCALE)
    scores = [scores[n] * LOG2_SCALE + bias[u][None] for n, (u, h) in enumerate(pairs)]
    largest = [
        jnp.maximum(jnp.max(x, axis=2, keepdims=True), y) for x, y in zip(scores, own_scores)
    ]
    weights = [jnp.exp2(x - y).astype(BF16) for x, y in zip(scores, largest)]
    own_weights = [jnp.exp2(x - y) for x, y in zip(own_scores, largest)]
    sums = []
    for n, (u, h) in enumerate(pairs):
        at = slice(u * unit, (u + 1) * unit)
        values = cache_ref[rows_of(u), :, (h * 2 + 1) * HD : (h * 2 + 2) * HD].reshape(keys_of, HD)
        sums.append(
            jnp.dot(
                weights[n].reshape(group * unit, keys_of),
                jnp.concatenate([values, ones], axis=1),
                preferred_element_type=F32,
            ).reshape(group, unit, 2 * HD)
        )
    pieces = [[] for _ in units]
    stats = [jnp.zeros((unit, STATS), F32) for _ in units]
    for n, (u, h) in enumerate(pairs):
        at = slice(u * unit, (u + 1) * unit)
        own_value = own[at, (h * 2 + 1) * HD : (h * 2 + 2) * HD]
        total = sums[n][:, :, HD:] + own_weights[n]
        result = (sums[n][:, :, :HD] + own_weights[n] * own_value[None]) / total
        lse = largest[n] + jnp.log2(total)
        for i in range(group):
            pieces[u].append(result[i])
            stats[u] = jnp.where(lane == h * group + i, lse[i], stats[u])
    out = jnp.concatenate([jnp.concatenate(x, axis=1) for x in pieces], axis=0).astype(BF16)
    out_ref[block, :] = out
    pick = pick_ref[...]
    here = iota((row_count, block_rows), 0) == iota((row_count, block_rows), 1) + first_row
    pick = jnp.dot(pick, here.astype(F32).astype(BF16), preferred_element_type=F32).astype(BF16)
    slot_out = jnp.dot(pick, out, preferred_element_type=F32)
    lse = jnp.concatenate(stats, axis=0)
    slot_lse = sum(
        jnp.dot(pick, part.astype(BF16), preferred_element_type=F32) for part in split_bf16(lse)
    )

    @pl.when(step == 0)
    def _():
        slot_out_ref[...] = slot_out
        slot_lse_ref[...] = slot_lse

    @pl.when(step > 0)
    def _():
        slot_out_ref[...] += slot_out
        slot_lse_ref[...] += slot_lse


def merge(pick_ref, *refs):
    parts, arrived_ref, out_ref = refs[:-2], refs[-2], refs[-1]
    cached_refs, slot_out_refs, slot_lse_refs = parts[0::3], parts[1::3], parts[2::3]
    width = out_ref.shape[1]
    pick = pick_ref[...]
    arrived = jnp.concatenate(
        [arrived_ref[s].astype(F32) for s in range(arrived_ref.shape[0])], axis=0
    )
    stats = arrived[:, width:]
    arrived_lse = (
        stats
        + pltpu.roll(stats, STATS - LSE_PITCH, 1)
        + pltpu.roll(stats, STATS - 2 * LSE_PITCH, 1)
    )
    cached_lse = sum(ref[...] for ref in slot_lse_refs)
    largest = jnp.maximum(cached_lse, arrived_lse)
    cached_weight = jnp.exp2(cached_lse - largest)
    arrived_weight = jnp.exp2(arrived_lse - largest)
    total = cached_weight + arrived_weight
    cached_weight = cached_weight / total
    arrived_weight = arrived_weight / total
    has = lax.dot_general(
        pick, jnp.ones((pick.shape[0], HD), BF16), TRANSPOSED, preferred_element_type=F32
    )
    for i in range(width // HD):
        at = slice(i * HD, (i + 1) * HD)
        merged = (
            sum(ref[:, at] for ref in slot_out_refs) * cached_weight[:, i : i + 1]
            + arrived[:, at] * arrived_weight[:, i : i + 1]
        )
        placed = lax.dot_general(
            pick, merged.astype(BF16), TRANSPOSED, preferred_element_type=F32
        )
        row = 0
        for ref in cached_refs:
            rows = slice(row, row + ref.shape[0])
            kept = ref[:, at].astype(F32)
            out_ref[rows, at] = jnp.where(has[rows] > 0.5, placed[rows], kept).astype(BF16)
            row += ref.shape[0]


def compiler_params(megabytes):
    return pltpu.CompilerParams(vmem_limit_bytes=megabytes * 1024 * 1024)


RESIDENT = pl.BlockSpec(memory_space=pltpu.VMEM)
REMAINS = pl.BlockSpec(memory_space=pl.ANY)


def in_vmem(x):
    return pltpu.with_memory_space_constraint(x, pltpu.VMEM)


def in_hbm(x):
    return pltpu.with_memory_space_constraint(x, pltpu.HBM)


def shards(
    prompts, decode_hidden, queries, kv_cache, cache_len, span_len, target_row, w_kv, kv_scale
):
    row_count = decode_hidden.shape[0]
    prompt_rows, features = prompts.shape
    sections = lax.axis_size("section")
    local_width = kv_cache.shape[2]
    query_width = queries.shape[1]
    slots = sections * CAP
    all_rows = prompt_rows + row_count
    scale = kv_scale.reshape(1, -1)
    lengths = cache_len.reshape(1, -1)

    pick, asked = pl.pallas_call(
        select_queries,
        in_specs=[RESIDENT, RESIDENT],
        out_specs=[RESIDENT] * 2,
        out_shape=[
            pltpu.VMEM((slots, row_count), BF16),
            jax.ShapeDtypeStruct((sections, CAP, query_width), BF16),
        ],
        compiler_params=compiler_params(16),
        name="select_queries",
    )(in_hbm(target_row), in_hbm(queries))
    asked = lax.all_to_all(asked, "section", 0, 0)

    edges = (0, 256, 768, 1536, 2560, 4096, features)
    count = len(edges) - 1
    mine, theirs = pl.pallas_call(
        functools.partial(project, edges=edges, block=all_rows // 2),
        in_specs=[REMAINS] * 4,
        out_specs=[RESIDENT] * 2,
        scratch_shapes=[
            pltpu.VMEM((all_rows, features), BF16),
            pltpu.VMEM((features, local_width), BF16),
            pltpu.VMEM((features, local_width), BF16),
            pltpu.VMEM((all_rows, local_width), F32),
            pltpu.VMEM((2, 1, local_width), F32),
            pltpu.SemaphoreType.DMA((count,)),
            pltpu.SemaphoreType.DMA((count,)),
            pltpu.SemaphoreType.DMA((count,)),
            pltpu.SemaphoreType.DMA(()),
            pltpu.SemaphoreType.DMA((2,)),
        ],
        out_shape=[pltpu.VMEM((all_rows, local_width), BF16)] * 2,
        compiler_params=compiler_params(44),
        name="project",
    )(in_hbm(prompts), in_hbm(decode_hidden), in_hbm(w_kv), in_hbm(scale))
    theirs, asked = lax.optimization_barrier((theirs, asked))
    other = lax.ppermute(theirs, "tp", [(0, 1), (1, 0)])
    block = 32
    calls = 1
    call_rows = row_count // calls

    def cache_share(call, after):
        first_block = call * call_rows // block
        return pl.pallas_call(
            functools.partial(attend_cache, block_rows=block, first_block=first_block),
            grid=(call_rows // block,),
            in_specs=[
                pl.BlockSpec((block, query_width), lambda b: (first_block + b, 0)),
                pl.BlockSpec((block, *kv_cache.shape[1:]), lambda b: (first_block + b, 0, 0)),
            ]
            + [RESIDENT] * 4
            + [REMAINS],
            out_specs=[RESIDENT] * 3,
            out_shape=[
                pltpu.VMEM((call_rows, query_width), BF16),
                pltpu.VMEM((slots, query_width), F32),
                pltpu.VMEM((slots, STATS), F32),
            ],
            compiler_params=compiler_params(24),
            name="attend_cache",
        )(
            in_hbm(queries),
            in_hbm(kv_cache),
            in_hbm(lengths),
            in_vmem(mine),
            in_vmem(other),
            in_vmem(pick),
            after,
        )

    padded = -(-span_len.shape[1] // 16) * 16
    prepared = pl.pallas_call(
        functools.partial(prepare_arrived, row_count=row_count),
        in_specs=[RESIDENT] * 3,
        out_specs=[RESIDENT] * 3,
        out_shape=[
            pltpu.VMEM((padded, query_width), BF16),
            pltpu.VMEM((padded, sections * PITCH), BF16),
            pltpu.VMEM((padded, prompt_rows), F32),
        ],
        compiler_params=compiler_params(16),
        name="prepare_arrived",
    )(in_hbm(target_row), in_hbm(span_len), in_vmem(asked))
    answer_width = query_width + STATS
    answers = pl.pallas_call(
        attend_arrived,
        in_specs=[RESIDENT] * 5,
        out_specs=RESIDENT,
        out_shape=jax.ShapeDtypeStruct((sections, CAP, answer_width), BF16),
        compiler_params=compiler_params(24),
        name="attend_arrived",
    )(*map(in_vmem, (*prepared, mine, other)))
    after = answers
    answers = lax.all_to_all(answers, "section", 0, 0)
    shares = []
    for call in range(calls):
        shares += cache_share(call, after)

    return pl.pallas_call(
        merge,
        in_specs=[RESIDENT] * (2 + len(shares)),
        out_specs=RESIDENT,
        out_shape=jax.ShapeDtypeStruct((row_count, query_width), BF16),
        compiler_params=compiler_params(24),
        name="merge",
    )(*map(in_vmem, (pick, *shares, answers)))


def solution(mesh):
    in_specs = (
        P(("groups", "section"), "tp"),
        P(("groups", "section"), "tp"),
        P(("groups", "section"), "tp"),
        P(("groups", "section"), None, "tp"),
        P(("groups", "section")),
        P("groups", None),
        P("groups", None),
        P("tp", None),
        P(),
    )
    out_specs = P(("groups", "section"), "tp")
    return jax.shard_map(shards, mesh=mesh, in_specs=in_specs, out_specs=out_specs, check_vma=False)
```

```python
import functools
import math

import jax
import jax.numpy as jnp
from jax import lax
from jax.experimental import pallas as pl
from jax.experimental.pallas import tpu as pltpu
from jax.sharding import PartitionSpec as P

HD = 128
CAP = 2
STATS = 128
MASKED = -1e30
LSE_PITCH = 40
PITCH = 8
LOG2_SCALE = HD ** (-0.5) * math.log2(math.e)
F32 = jnp.float32
BF16 = jnp.bfloat16
TRANSPOSED = (((0,), (0,)), ((), ()))


def iota(shape, dim):
    return lax.broadcasted_iota(jnp.int32, shape, dim)


def one_hot(shape, dim, index):
    return (iota(shape, dim) == index).astype(F32).astype(BF16)


def pick_rows(target_ref, row_count, pitch):
    sections, requests = target_ref.shape
    shape = (sections * pitch, requests)
    position = lax.axis_index("section")
    slot_id = iota(shape, 0)
    table = jnp.zeros(shape, jnp.int32)
    for s in range(sections):
        mine = (slot_id >= s * pitch) & (slot_id < (s + 1) * pitch)
        table = jnp.where(mine, target_ref[s : s + 1, :], table)
    local = table - position * row_count
    here = (local >= 0) & (local < row_count)
    square = (requests, requests)
    earlier = jnp.dot(
        here.astype(F32).astype(BF16),
        (iota(square, 0) < iota(square, 1)).astype(F32).astype(BF16),
        preferred_element_type=F32,
    )
    chosen = here & (earlier == lax.rem(slot_id, pitch).astype(F32))
    row = jnp.max(jnp.where(chosen, local.astype(F32), -1.0), axis=1, keepdims=True)
    return one_hot((shape[0], row_count), 1, row.astype(jnp.int32))


def select_queries(target_ref, queries_ref, pick_ref, *refs):
    asked_refs, asked_ref = refs[:-1], refs[-1]
    sections = target_ref.shape[0]
    position = lax.axis_index("section")
    pick = pick_rows(target_ref, queries_ref.shape[0], CAP)
    pick_ref[...] = pick
    asked = jnp.dot(pick, queries_ref[...], preferred_element_type=F32)
    for s in range(sections):
        asked_ref[s] = asked[s * CAP : (s + 1) * CAP]
    for k in range(sections):
        asked_refs[k][...] = asked_ref[position ^ k].astype(BF16)


def spans(edges):
    return [slice(a, b) for a, b in zip(edges[:-1], edges[1:])]


def project(
    prompts_ref,
    hidden_ref,
    w_ref,
    scale_ref,
    mine_ref,
    theirs_ref,
    rows_ref,
    w_mine_ref,
    w_theirs_ref,
    total_ref,
    scale_here_ref,
    row_sems,
    hidden_sems,
    theirs_sems,
    mine_sem,
    scale_sems,
    *,
    edges,
    block,
):
    prompt_rows = prompts_ref.shape[0]
    width = mine_ref.shape[1]
    tp = lax.axis_index("tp")
    theirs = pl.ds(pl.multiple_of((1 - tp) * width, width), width)
    mine = pl.ds(pl.multiple_of(tp * width, width), width)
    chunks = spans(edges)
    waits = []
    for c, at in enumerate(chunks):
        copies = [
            pltpu.make_async_copy(
                w_ref.at[at, theirs], w_theirs_ref.at[at, :], theirs_sems.at[c]
            ),
            pltpu.make_async_copy(
                prompts_ref.at[:, at], rows_ref.at[:prompt_rows, at], row_sems.at[c]
            ),
            pltpu.make_async_copy(
                hidden_ref.at[:, at], rows_ref.at[prompt_rows:, at], hidden_sems.at[c]
            ),
        ]
        for copy in copies:
            copy.start()
        waits.append(copies)
    later = [
        pltpu.make_async_copy(
            scale_ref.at[:, theirs], scale_here_ref.at[0], scale_sems.at[0]
        ),
        pltpu.make_async_copy(scale_ref.at[:, mine], scale_here_ref.at[1], scale_sems.at[1]),
        pltpu.make_async_copy(w_ref.at[:, mine], w_mine_ref, mine_sem),
    ]
    for copy in later:
        copy.start()
    for c, at in enumerate(chunks):
        for copy in waits[c]:
            copy.wait()
        part = jnp.dot(rows_ref[:, at], w_theirs_ref[at, :], preferred_element_type=F32)
        if c == 0:
            total_ref[...] = part
        elif c < len(chunks) - 1:
            total_ref[...] += part
        else:
            later[0].wait()
            theirs_ref[...] = ((total_ref[...] + part) * scale_here_ref[0]).astype(BF16)
    for copy in later[1:]:
        copy.wait()
    for m in spans(range(0, rows_ref.shape[0] + 1, block)):
        total = jnp.dot(rows_ref[m, :], w_mine_ref[...], preferred_element_type=F32)
        mine_ref[m, :] = (total * scale_here_ref[1]).astype(BF16)


def split_bf16(x):
    high = x.astype(BF16).astype(F32)
    middle = (x - high).astype(BF16).astype(F32)
    return high, middle, (x - high - middle).astype(BF16).astype(F32)


def request_slots(target_ref, span_ref, row_count, padded):
    sections, requests = target_ref.shape
    position = lax.axis_index("section")
    target = target_ref[pl.ds(position, 1), :].astype(F32)
    span = span_ref[pl.ds(position, 1), :].astype(F32)
    diagonal = iota((padded, requests), 0) == iota((padded, requests), 1)
    target_col = jnp.sum(jnp.where(diagonal, target, 0.0), axis=1, keepdims=True)
    span_col = jnp.sum(jnp.where(diagonal, span, 0.0), axis=1, keepdims=True)
    section_row = jnp.zeros_like(target)
    section_col = jnp.zeros_like(target_col)
    for s in range(1, sections):
        section_row = section_row + (target >= s * row_count).astype(F32)
        section_col = section_col + (target_col >= s * row_count).astype(F32)
    before = (section_row == section_col) & (
        iota((padded, requests), 1) < iota((padded, requests), 0)
    )
    rank_col = jnp.sum(before.astype(F32), axis=1, keepdims=True).astype(jnp.int32)
    real = iota((padded, 1), 0) < requests
    section_col = jnp.where(real, section_col.astype(jnp.int32), -1)
    return section_col, rank_col, span_col.astype(jnp.int32)


def prepare_arrived(
    target_ref, span_ref, *refs, row_count
):
    sections, requests = target_ref.shape
    asked_refs, (rows_ref, slot_of_ref, bias_ref) = refs[:sections], refs[sections:]
    padded, prompt_rows = bias_ref.shape
    span_rows = prompt_rows // requests
    section_col, rank_col, span_col = request_slots(target_ref, span_ref, row_count, padded)
    slot = jnp.where(section_col >= 0, section_col * PITCH + rank_col, -1)
    slot_of_ref[...] = one_hot((padded, sections * PITCH), 1, slot)
    step = section_col ^ lax.axis_index("section")
    slot = jnp.where(section_col >= 0, step * CAP + rank_col, -1)
    asked = jnp.concatenate([ref[...].astype(F32) for ref in asked_refs], axis=0)
    rows_ref[...] = jnp.dot(
        one_hot((padded, sections * CAP), 1, slot),
        asked.astype(BF16),
        preferred_element_type=F32,
    ).astype(BF16)
    key = iota((padded, prompt_rows), 1) - iota((padded, prompt_rows), 0) * span_rows
    bias_ref[...] = jnp.where((key >= 0) & (key < span_col), 0.0, MASKED)


def attend_arrived(rows_ref, slot_of_ref, bias_ref, mine_ref, other_ref, out_ref):
    padded, prompt_rows = bias_ref.shape
    kv_heads = mine_ref.shape[1] // (2 * HD)
    group = rows_ref.shape[1] // (kv_heads * HD)
    rows = rows_ref[...]
    slot_of = slot_of_ref[...]
    bias = bias_ref[...]
    kv = (
        mine_ref[:prompt_rows, :].astype(F32) + other_ref[:prompt_rows, :].astype(F32)
    ).astype(BF16)
    scores = []
    for h in range(kv_heads):
        stacked = jnp.concatenate(
            [rows[:, (h * group + i) * HD : (h * group + i + 1) * HD] for i in range(group)],
            axis=0,
        )
        keys = kv[:, h * 2 * HD : (h * 2 + 1) * HD]
        scores.append(
            lax.dot_general(
                stacked, keys, (((1,), (1,)), ((), ())), preferred_element_type=F32
            )
        )
    scores = [
        x.reshape(group, padded, prompt_rows) * LOG2_SCALE + bias[None] for x in scores
    ]
    largest = [jnp.max(x, axis=2, keepdims=True) for x in scores]
    weights = [jnp.exp2(x - y) for x, y in zip(scores, largest)]
    totals = [jnp.sum(x, axis=2, keepdims=True) for x in weights]
    lane = iota((padded, STATS), 1)
    lse = jnp.zeros((padded, STATS), F32)
    pieces = []
    for h in range(kv_heads):
        values = jnp.dot(
            weights[h].reshape(group * padded, prompt_rows).astype(BF16),
            kv[:, (h * 2 + 1) * HD : (h * 2 + 2) * HD],
            preferred_element_type=F32,
        ).reshape(group, padded, HD)
        values = values / totals[h]
        head_lse = largest[h] + jnp.log2(totals[h])
        for i in range(group):
            pieces.append(values[i])
            lse = jnp.where(lane == h * group + i, head_lse[i], lse)
    high, middle, low = split_bf16(lse)
    stats = high + pltpu.roll(middle, LSE_PITCH, 1) + pltpu.roll(low, 2 * LSE_PITCH, 1)
    result = jnp.concatenate(pieces + [stats], axis=1).astype(BF16)
    answers = lax.dot_general(slot_of, result, TRANSPOSED, preferred_element_type=F32)
    for s in range(out_ref.shape[0]):
        out_ref[s] = answers[s * PITCH : s * PITCH + CAP].astype(BF16)


def attend_cache(
    queries_ref,
    cache_ref,
    len_ref,
    mine_ref,
    other_ref,
    pick_ref,
    after_ref,
    out_ref,
    slot_out_ref,
    slot_lse_ref,
    *,
    block_rows,
    first_block,
):
    cache_rows, width = cache_ref.shape[1:]
    row_count = len_ref.shape[1]
    kv_heads = width // (2 * HD)
    group = queries_ref.shape[1] // (kv_heads * HD)
    unit = 8
    keys_of = unit * cache_rows
    step = pl.program_id(0)
    block = pl.ds(pl.multiple_of(step * block_rows, block_rows), block_rows)
    first_row = pl.multiple_of((step + first_block) * block_rows, block_rows)
    own_block = pl.ds(first_row + (mine_ref.shape[0] - row_count), block_rows)
    queries = queries_ref[...].astype(F32)
    own = mine_ref[own_block, :].astype(F32) + other_ref[own_block, :].astype(F32)
    own = own.astype(BF16).astype(F32)
    key = iota((unit, keys_of), 1) - iota((unit, keys_of), 0) * cache_rows
    lengths = len_ref[...].astype(F32)
    lane = iota((unit, STATS), 1)
    ones = jnp.ones((keys_of, HD), BF16)
    units = range(block_rows // unit)

    def rows_of(u):
        return slice(u * unit, (u + 1) * unit)

    pairs = [(u, h) for u in units for h in range(kv_heads)]
    bias = []
    for u in units:
        row = iota((unit, row_count), 0) + (first_row + u * unit)
        length = jnp.sum(
            jnp.where(iota((unit, row_count), 1) == row, lengths, 0.0), axis=1, keepdims=True
        ).astype(jnp.int32)
        bias.append(jnp.where((key >= 0) & (key < length), 0.0, MASKED))
    q, scores, own_scores = [], [], []
    for u, h in pairs:
        at = slice(u * unit, (u + 1) * unit)
        q.append(
            jnp.stack(
                [
                    queries[at, (h * group + i) * HD : (h * group + i + 1) * HD]
                    for i in range(group)
                ],
                axis=0,
            )
        )
        keys = cache_ref[rows_of(u), :, h * 2 * HD : (h * 2 + 1) * HD].reshape(keys_of, HD)
        scores.append(
            lax.dot_general(
                q[-1].reshape(group * unit, HD).astype(BF16),
                keys,
                (((1,), (1,)), ((), ())),
                preferred_element_type=F32,
            ).reshape(group, unit, keys_of)
        )
    for n, (u, h) in enumerate(pairs):
        at = slice(u * unit, (u + 1) * unit)
        own_key = own[at, h * 2 * HD : (h * 2 + 1) * HD]
        own_scores.append(jnp.sum(q[n] * own_key[None], axis=2, keepdims=True) * LOG2_SCALE)
    scores = [scores[n] * LOG2_SCALE + bias[u][None] for n, (u, h) in enumerate(pairs)]
    largest = [
        jnp.maximum(jnp.max(x, axis=2, keepdims=True), y) for x, y in zip(scores, own_scores)
    ]
    weights = [jnp.exp2(x - y).astype(BF16) for x, y in zip(scores, largest)]
    own_weights = [jnp.exp2(x - y) for x, y in zip(own_scores, largest)]
    sums = []
    for n, (u, h) in enumerate(pairs):
        at = slice(u * unit, (u + 1) * unit)
        values = cache_ref[rows_of(u), :, (h * 2 + 1) * HD : (h * 2 + 2) * HD].reshape(keys_of, HD)
        sums.append(
            jnp.dot(
                weights[n].reshape(group * unit, keys_of),
                jnp.concatenate([values, ones], axis=1),
                preferred_element_type=F32,
            ).reshape(group, unit, 2 * HD)
        )
    pieces = [[] for _ in units]
    stats = [jnp.zeros((unit, STATS), F32) for _ in units]
    for n, (u, h) in enumerate(pairs):
        at = slice(u * unit, (u + 1) * unit)
        own_value = own[at, (h * 2 + 1) * HD : (h * 2 + 2) * HD]
        total = sums[n][:, :, HD:] + own_weights[n]
        result = (sums[n][:, :, :HD] + own_weights[n] * own_value[None]) / total
        lse = largest[n] + jnp.log2(total)
        for i in range(group):
            pieces[u].append(result[i])
            stats[u] = jnp.where(lane == h * group + i, lse[i], stats[u])
    out = jnp.concatenate([jnp.concatenate(x, axis=1) for x in pieces], axis=0).astype(BF16)
    out_ref[block, :] = out
    pick = pick_ref[...]
    here = iota((row_count, block_rows), 0) == iota((row_count, block_rows), 1) + first_row
    pick = jnp.dot(pick, here.astype(F32).astype(BF16), preferred_element_type=F32).astype(BF16)
    slot_out = jnp.dot(pick, out, preferred_element_type=F32)
    lse = jnp.concatenate(stats, axis=0)
    slot_lse = sum(
        jnp.dot(pick, part.astype(BF16), preferred_element_type=F32) for part in split_bf16(lse)
    )

    @pl.when(step == 0)
    def _():
        slot_out_ref[...] = slot_out
        slot_lse_ref[...] = slot_lse

    @pl.when(step > 0)
    def _():
        slot_out_ref[...] += slot_out
        slot_lse_ref[...] += slot_lse


def merge(pick_ref, *refs):
    parts, arrived_ref, out_ref = refs[:-2], refs[-2], refs[-1]
    cached_refs, slot_out_refs, slot_lse_refs = parts[0::3], parts[1::3], parts[2::3]
    width = out_ref.shape[1]
    pick = pick_ref[...]
    arrived = jnp.concatenate(
        [arrived_ref[s].astype(F32) for s in range(arrived_ref.shape[0])], axis=0
    )
    stats = arrived[:, width:]
    arrived_lse = (
        stats
        + pltpu.roll(stats, STATS - LSE_PITCH, 1)
        + pltpu.roll(stats, STATS - 2 * LSE_PITCH, 1)
    )
    cached_lse = sum(ref[...] for ref in slot_lse_refs)
    largest = jnp.maximum(cached_lse, arrived_lse)
    cached_weight = jnp.exp2(cached_lse - largest)
    arrived_weight = jnp.exp2(arrived_lse - largest)
    total = cached_weight + arrived_weight
    cached_weight = cached_weight / total
    arrived_weight = arrived_weight / total
    has = lax.dot_general(
        pick, jnp.ones((pick.shape[0], HD), BF16), TRANSPOSED, preferred_element_type=F32
    )
    for i in range(width // HD):
        at = slice(i * HD, (i + 1) * HD)
        merged = (
            sum(ref[:, at] for ref in slot_out_refs) * cached_weight[:, i : i + 1]
            + arrived[:, at] * arrived_weight[:, i : i + 1]
        )
        placed = lax.dot_general(
            pick, merged.astype(BF16), TRANSPOSED, preferred_element_type=F32
        )
        row = 0
        for ref in cached_refs:
            rows = slice(row, row + ref.shape[0])
            kept = ref[:, at].astype(F32)
            out_ref[rows, at] = jnp.where(has[rows] > 0.5, placed[rows], kept).astype(BF16)
            row += ref.shape[0]


def compiler_params(megabytes):
    return pltpu.CompilerParams(vmem_limit_bytes=megabytes * 1024 * 1024)


RESIDENT = pl.BlockSpec(memory_space=pltpu.VMEM)
REMAINS = pl.BlockSpec(memory_space=pl.ANY)


def in_vmem(x):
    return pltpu.with_memory_space_constraint(x, pltpu.VMEM)


def in_hbm(x):
    return pltpu.with_memory_space_constraint(x, pltpu.HBM)


def shards(
    prompts, decode_hidden, queries, kv_cache, cache_len, span_len, target_row, w_kv, kv_scale
):
    row_count = decode_hidden.shape[0]
    prompt_rows, features = prompts.shape
    sections = lax.axis_size("section")
    local_width = kv_cache.shape[2]
    query_width = queries.shape[1]
    slots = sections * CAP
    all_rows = prompt_rows + row_count
    scale = kv_scale.reshape(1, -1)
    lengths = cache_len.reshape(1, -1)

    pick, *asked = pl.pallas_call(
        select_queries,
        in_specs=[RESIDENT, RESIDENT],
        out_specs=[RESIDENT] * (1 + sections),
        out_shape=[pltpu.VMEM((slots, row_count), BF16)]
        + [pltpu.VMEM((CAP, query_width), BF16)] * sections,
        scratch_shapes=[pltpu.VMEM((sections, CAP, query_width), F32)],
        compiler_params=compiler_params(16),
        name="select_queries",
    )(in_hbm(target_row), in_hbm(queries))
    for k in range(1, sections):
        pairs = [(s, k ^ s) for s in range(sections)]
        asked[k] = lax.ppermute(asked[k], "section", pairs)

    edges = (0, 256, 768, 1536, 2560, 4096, features)
    count = len(edges) - 1
    mine, theirs = pl.pallas_call(
        functools.partial(project, edges=edges, block=all_rows // 4),
        in_specs=[REMAINS] * 4,
        out_specs=[RESIDENT] * 2,
        scratch_shapes=[
            pltpu.VMEM((all_rows, features), BF16),
            pltpu.VMEM((features, local_width), BF16),
            pltpu.VMEM((features, local_width), BF16),
            pltpu.VMEM((all_rows, local_width), F32),
            pltpu.VMEM((2, 1, local_width), F32),
            pltpu.SemaphoreType.DMA((count,)),
            pltpu.SemaphoreType.DMA((count,)),
            pltpu.SemaphoreType.DMA((count,)),
            pltpu.SemaphoreType.DMA(()),
            pltpu.SemaphoreType.DMA((2,)),
        ],
        out_shape=[pltpu.VMEM((all_rows, local_width), BF16)] * 2,
        compiler_params=compiler_params(44),
        name="project",
    )(in_hbm(prompts), in_hbm(decode_hidden), in_hbm(w_kv), in_hbm(scale))
    theirs, *asked = lax.optimization_barrier((theirs, *asked))
    other = lax.ppermute(theirs, "tp", [(0, 1), (1, 0)])
    block = 32
    calls = 1
    call_rows = row_count // calls

    def cache_share(call, after):
        first_block = call * call_rows // block
        return pl.pallas_call(
            functools.partial(attend_cache, block_rows=block, first_block=first_block),
            grid=(call_rows // block,),
            in_specs=[
                pl.BlockSpec((block, query_width), lambda b: (first_block + b, 0)),
                pl.BlockSpec((block, *kv_cache.shape[1:]), lambda b: (first_block + b, 0, 0)),
            ]
            + [RESIDENT] * 4
            + [REMAINS],
            out_specs=[RESIDENT] * 3,
            out_shape=[
                pltpu.VMEM((call_rows, query_width), BF16),
                pltpu.VMEM((slots, query_width), F32),
                pltpu.VMEM((slots, STATS), F32),
            ],
            compiler_params=compiler_params(24),
            name="attend_cache",
        )(
            in_hbm(queries),
            in_hbm(kv_cache),
            in_hbm(lengths),
            in_vmem(mine),
            in_vmem(other),
            in_vmem(pick),
            after,
        )

    padded = -(-span_len.shape[1] // 16) * 16
    prepared = pl.pallas_call(
        functools.partial(prepare_arrived, row_count=row_count),
        in_specs=[RESIDENT] * (2 + sections),
        out_specs=[RESIDENT] * 3,
        out_shape=[
            pltpu.VMEM((padded, query_width), BF16),
            pltpu.VMEM((padded, sections * PITCH), BF16),
            pltpu.VMEM((padded, prompt_rows), F32),
        ],
        compiler_params=compiler_params(16),
        name="prepare_arrived",
    )(in_hbm(target_row), in_hbm(span_len), *map(in_vmem, asked))
    answer_width = query_width + STATS
    answers = pl.pallas_call(
        attend_arrived,
        in_specs=[RESIDENT] * 5,
        out_specs=RESIDENT,
        out_shape=jax.ShapeDtypeStruct((sections, CAP, answer_width), BF16),
        compiler_params=compiler_params(24),
        name="attend_arrived",
    )(*map(in_vmem, (*prepared, mine, other)))
    after = answers
    answers = lax.all_to_all(answers, "section", 0, 0)
    shares = []
    for call in range(calls):
        shares += cache_share(call, after)

    return pl.pallas_call(
        merge,
        in_specs=[RESIDENT] * (2 + len(shares)),
        out_specs=RESIDENT,
        out_shape=jax.ShapeDtypeStruct((row_count, query_width), BF16),
        compiler_params=compiler_params(24),
        name="merge",
    )(*map(in_vmem, (pick, *shares, answers)))


def solution(mesh):
    in_specs = (
        P(("groups", "section"), "tp"),
        P(("groups", "section"), "tp"),
        P(("groups", "section"), "tp"),
        P(("groups", "section"), None, "tp"),
        P(("groups", "section")),
        P("groups", None),
        P("groups", None),
        P("tp", None),
        P(),
    )
    out_specs = P(("groups", "section"), "tp")
    return jax.shard_map(shards, mesh=mesh, in_specs=in_specs, out_specs=out_specs, check_vma=False)
```

```python
import functools
import math

import jax
import jax.numpy as jnp
from jax import lax
from jax.experimental import pallas as pl
from jax.experimental.pallas import tpu as pltpu
from jax.sharding import PartitionSpec as P

HD = 128
CAP = 2
STATS = 128
MASKED = -1e30
LSE_PITCH = 40
PITCH = 8
LOG2_SCALE = HD ** (-0.5) * math.log2(math.e)
F32 = jnp.float32
BF16 = jnp.bfloat16
TRANSPOSED = (((0,), (0,)), ((), ()))


def iota(shape, dim):
    return lax.broadcasted_iota(jnp.int32, shape, dim)


def one_hot(shape, dim, index):
    return (iota(shape, dim) == index).astype(F32).astype(BF16)


def pick_rows(target_ref, row_count):
    sections, requests = target_ref.shape
    shape = (sections * CAP, requests)
    position = lax.axis_index("section")
    slot_id = iota(shape, 0)
    table = jnp.zeros(shape, jnp.int32)
    for k in range(sections):
        mine = (slot_id >= k * CAP) & (slot_id < (k + 1) * CAP)
        table = jnp.where(mine, target_ref[pl.ds(position ^ k, 1), :], table)
    local = table - position * row_count
    here = (local >= 0) & (local < row_count)
    square = (requests, requests)
    earlier = jnp.dot(
        here.astype(F32).astype(BF16),
        (iota(square, 0) < iota(square, 1)).astype(F32).astype(BF16),
        preferred_element_type=F32,
    )
    chosen = here & (earlier == lax.rem(slot_id, CAP).astype(F32))
    row = jnp.max(jnp.where(chosen, local.astype(F32), -1.0), axis=1, keepdims=True)
    return one_hot((shape[0], row_count), 1, row.astype(jnp.int32))


def steps_of(sections):
    steps = []
    bit = sections // 2
    while bit:
        sent = [k for k in range(sections) if k & bit]
        steps.append((bit, sent, [k for k in range(sections) if not k & bit]))
        bit //= 2
    return steps


def regroup(kept_ref, got_ref, after_ref, keep_ref, send_ref, *, steps, done):
    where = {k: (got_ref, i) for i, k in enumerate(steps[done - 1][1])}
    where |= {k: (kept_ref, i) for i, k in enumerate(steps[done - 1][2])}
    for out_ref, blocks in ((send_ref, steps[done][1]), (keep_ref, steps[done][2])):
        for i, k in enumerate(blocks):
            ref, at = where[k]
            out_ref[i] = ref[at]


def all_blocks(steps, kept_ref, got_ref):
    where = {k: got_ref[i] for i, k in enumerate(steps[-1][1])}
    where |= {k: kept_ref[i] for i, k in enumerate(steps[-1][2])}
    return jnp.concatenate([where[k].astype(F32) for k in range(len(where))], axis=0)


def select_queries(target_ref, queries_ref, pick_ref, keep_ref, send_ref):
    _, sent, kept = steps_of(target_ref.shape[0])[0]
    pick = pick_rows(target_ref, queries_ref.shape[0])
    pick_ref[...] = pick
    asked = jnp.dot(pick, queries_ref[...], preferred_element_type=F32)
    for ref, blocks in ((send_ref, sent), (keep_ref, kept)):
        for i, k in enumerate(blocks):
            ref[i] = asked[k * CAP : (k + 1) * CAP].astype(BF16)


def spans(edges):
    return [slice(a, b) for a, b in zip(edges[:-1], edges[1:])]


def load_rows(prompts_ref, hidden_ref, there, rows_ref, here, sems):
    prompt_rows = prompts_ref.shape[0]
    return [
        pltpu.make_async_copy(
            prompts_ref.at[:, there], rows_ref.at[:prompt_rows, here], sems.at[0]
        ),
        pltpu.make_async_copy(
            hidden_ref.at[:, there], rows_ref.at[prompt_rows:, here], sems.at[1]
        ),
    ]


def channels(offset, width):
    tp = lax.axis_index("tp")
    return pl.ds(pl.multiple_of(((tp + offset) & 1) * width, width), width)


def project_first(
    prompts_ref, hidden_ref, w_ref, rows_ref, w_tail_ref, total_ref, w_head_ref, sems, *, edges
):
    theirs = channels(1, total_ref.shape[1])
    chunks = spans(edges)
    head = edges[-2]
    waits = []
    for c, at in enumerate(chunks):
        here = at if at.stop <= head else slice(0, at.stop - head)
        w_here_ref = w_head_ref if at.stop <= head else w_tail_ref
        copies = load_rows(prompts_ref, hidden_ref, at, rows_ref, at, sems.at[c])
        copies.append(
            pltpu.make_async_copy(w_ref.at[at, theirs], w_here_ref.at[here, :], sems.at[c, 2])
        )
        for copy in copies:
            copy.start()
        waits.append(copies)
    for c, at in enumerate(chunks):
        for copy in waits[c]:
            copy.wait()
        if at.stop <= head:
            part = jnp.dot(rows_ref[:, at], w_head_ref[at, :], preferred_element_type=F32)
            if c == 0:
                total_ref[...] = part
            else:
                total_ref[...] += part


def project_rest(
    prompts_ref,
    hidden_ref,
    w_ref,
    scale_ref,
    rows_ref,
    w_tail_ref,
    total_ref,
    after_ref,
    theirs_ref,
    rows_rest_ref,
    w_mine_ref,
    w_rest_ref,
    scale_here_ref,
    sems,
):
    width = theirs_ref.shape[1]
    theirs, mine = channels(1, width), channels(0, width)
    depth = rows_ref.shape[1]
    head = depth - w_tail_ref.shape[0]
    rest = slice(depth, depth + rows_rest_ref.shape[1])
    copies = load_rows(prompts_ref, hidden_ref, rest, rows_rest_ref, slice(None), sems)
    copies += [
        pltpu.make_async_copy(w_ref.at[rest, theirs], w_rest_ref, sems.at[2]),
        pltpu.make_async_copy(scale_ref.at[:, theirs], scale_here_ref, sems.at[3]),
        pltpu.make_async_copy(w_ref.at[:, mine], w_mine_ref, sems.at[4]),
    ]
    for copy in copies:
        copy.start()
    total = total_ref[...] + jnp.dot(
        rows_ref[:, head:], w_tail_ref[...], preferred_element_type=F32
    )
    for copy in copies[:-1]:
        copy.wait()
    total += jnp.dot(rows_rest_ref[...], w_rest_ref[...], preferred_element_type=F32)
    theirs_ref[...] = (total * scale_here_ref[...]).astype(BF16)
    copies[-1].wait()


def project_mine(rows_ref, rows_rest_ref, w_mine_ref, scale_ref, after_ref, *refs, at, last):
    refs, (scale_here_ref, sems) = refs[:-2], refs[-2:]
    if last:
        cache_ref, queries_ref, out_ref, cache_here_ref, queries_here_ref = refs
    else:
        (out_ref,) = refs
    mine = channels(0, out_ref.shape[1])
    copies = [pltpu.make_async_copy(scale_ref.at[:, mine], scale_here_ref, sems.at[0])]
    if last:
        copies.append(pltpu.make_async_copy(queries_ref, queries_here_ref, sems.at[1]))
        copies.append(pltpu.make_async_copy(cache_ref, cache_here_ref, sems.at[2]))
    for copy in copies:
        copy.start()
    depth = rows_ref.shape[1]
    count = at.stop - at.start
    block = count // 2 if count % 32 == 0 else count
    for m in spans(range(0, count + 1, block)):
        there = slice(at.start + m.start, at.start + m.stop)
        total = jnp.dot(rows_ref[there, :], w_mine_ref[:depth, :], preferred_element_type=F32)
        total += jnp.dot(
            rows_rest_ref[there, :], w_mine_ref[depth:, :], preferred_element_type=F32
        )
        if m.start == 0:
            copies[0].wait()
        out_ref[m, :] = (total * scale_here_ref[...]).astype(BF16)
    for copy in copies[1:]:
        copy.wait()


def split_bf16(x):
    high = x.astype(BF16).astype(F32)
    middle = (x - high).astype(BF16).astype(F32)
    return high, middle, (x - high - middle).astype(BF16).astype(F32)


def request_slots(target_ref, span_ref, row_count, padded):
    sections, requests = target_ref.shape
    position = lax.axis_index("section")
    target = target_ref[pl.ds(position, 1), :].astype(F32)
    span = span_ref[pl.ds(position, 1), :].astype(F32)
    diagonal = iota((padded, requests), 0) == iota((padded, requests), 1)
    target_col = jnp.sum(jnp.where(diagonal, target, 0.0), axis=1, keepdims=True)
    span_col = jnp.sum(jnp.where(diagonal, span, 0.0), axis=1, keepdims=True)
    section_row = jnp.zeros_like(target)
    section_col = jnp.zeros_like(target_col)
    for s in range(1, sections):
        section_row = section_row + (target >= s * row_count).astype(F32)
        section_col = section_col + (target_col >= s * row_count).astype(F32)
    before = (section_row == section_col) & (
        iota((padded, requests), 1) < iota((padded, requests), 0)
    )
    rank_col = jnp.sum(before.astype(F32), axis=1, keepdims=True).astype(jnp.int32)
    real = iota((padded, 1), 0) < requests
    section_col = jnp.where(real, section_col.astype(jnp.int32), -1)
    return section_col, rank_col, span_col.astype(jnp.int32)


def prepare_arrived(
    target_ref, span_ref, kept_ref, got_ref, rows_ref, slot_of_ref, bias_ref, *, row_count
):
    sections, requests = target_ref.shape
    padded, prompt_rows = bias_ref.shape
    span_rows = prompt_rows // requests
    section_col, rank_col, span_col = request_slots(target_ref, span_ref, row_count, padded)
    block = section_col ^ lax.axis_index("section")
    slot = jnp.where(section_col >= 0, block * PITCH + rank_col, -1)
    slot_of_ref[...] = one_hot((padded, sections * PITCH), 1, slot)
    slot = jnp.where(section_col >= 0, block * CAP + rank_col, -1)
    rows_ref[...] = jnp.dot(
        one_hot((padded, sections * CAP), 1, slot),
        all_blocks(steps_of(sections), kept_ref, got_ref).astype(BF16),
        preferred_element_type=F32,
    ).astype(BF16)
    key = iota((padded, prompt_rows), 1) - iota((padded, prompt_rows), 0) * span_rows
    bias_ref[...] = jnp.where((key >= 0) & (key < span_col), 0.0, MASKED)


def attend_arrived(rows_ref, slot_of_ref, bias_ref, other_ref, *refs):
    mine_refs, (keep_ref, send_ref) = refs[:-2], refs[-2:]
    padded, prompt_rows = bias_ref.shape
    kv_heads = other_ref.shape[1] // (2 * HD)
    group = rows_ref.shape[1] // (kv_heads * HD)
    rows = rows_ref[...]
    slot_of = slot_of_ref[...]
    bias = bias_ref[...]
    mine = jnp.concatenate([ref[...] for ref in mine_refs], axis=0)
    kv = (mine[:prompt_rows].astype(F32) + other_ref[:prompt_rows, :].astype(F32)).astype(BF16)
    scores = []
    for h in range(kv_heads):
        stacked = jnp.concatenate(
            [rows[:, (h * group + i) * HD : (h * group + i + 1) * HD] for i in range(group)],
            axis=0,
        )
        keys = kv[:, h * 2 * HD : (h * 2 + 1) * HD]
        scores.append(
            lax.dot_general(
                stacked, keys, (((1,), (1,)), ((), ())), preferred_element_type=F32
            )
        )
    scores = [
        x.reshape(group, padded, prompt_rows) * LOG2_SCALE + bias[None] for x in scores
    ]
    largest = [jnp.max(x, axis=2, keepdims=True) for x in scores]
    weights = [jnp.exp2(x - y) for x, y in zip(scores, largest)]
    totals = [jnp.sum(x, axis=2, keepdims=True) for x in weights]
    lane = iota((padded, STATS), 1)
    lse = jnp.zeros((padded, STATS), F32)
    pieces = []
    for h in range(kv_heads):
        values = jnp.dot(
            weights[h].reshape(group * padded, prompt_rows).astype(BF16),
            kv[:, (h * 2 + 1) * HD : (h * 2 + 2) * HD],
            preferred_element_type=F32,
        ).reshape(group, padded, HD)
        values = values / totals[h]
        head_lse = largest[h] + jnp.log2(totals[h])
        for i in range(group):
            pieces.append(values[i])
            lse = jnp.where(lane == h * group + i, head_lse[i], lse)
    high, middle, low = split_bf16(lse)
    stats = high + pltpu.roll(middle, LSE_PITCH, 1) + pltpu.roll(low, 2 * LSE_PITCH, 1)
    result = jnp.concatenate(pieces + [stats], axis=1).astype(BF16)
    answers = lax.dot_general(slot_of, result, TRANSPOSED, preferred_element_type=F32)
    _, sent, kept = steps_of(2 * keep_ref.shape[0])[0]
    for ref, blocks in ((send_ref, sent), (keep_ref, kept)):
        for i, k in enumerate(blocks):
            ref[i] = answers[k * PITCH : k * PITCH + CAP].astype(BF16)


def attend_cache(
    queries_ref,
    cache_ref,
    len_ref,
    mine_ref,
    other_ref,
    pick_ref,
    after_ref,
    out_ref,
    slot_out_ref,
    slot_lse_ref,
    *,
    rows_at,
):
    row_count, cache_rows, width = cache_ref.shape
    first_row, block_rows = rows_at.start, rows_at.stop - rows_at.start
    kv_heads = width // (2 * HD)
    group = queries_ref.shape[1] // (kv_heads * HD)
    unit = 8
    keys_of = unit * cache_rows
    queries = queries_ref[rows_at, :].astype(F32)
    own = sum(
        ref[pl.ds(ref.shape[0] - row_count + first_row, block_rows), :].astype(F32)
        for ref in (mine_ref, other_ref)
    )
    own = own.astype(BF16).astype(F32)
    key = iota((unit, keys_of), 1) - iota((unit, keys_of), 0) * cache_rows
    lengths = len_ref[...].astype(F32)
    lane = iota((unit, STATS), 1)
    ones = jnp.ones((keys_of, HD), BF16)
    units = range(block_rows // unit)

    def rows_of(u):
        return slice(first_row + u * unit, first_row + (u + 1) * unit)

    pairs = [(u, h) for u in units for h in range(kv_heads)]
    bias = []
    for u in units:
        row = iota((unit, row_count), 0) + (first_row + u * unit)
        length = jnp.sum(
            jnp.where(iota((unit, row_count), 1) == row, lengths, 0.0), axis=1, keepdims=True
        ).astype(jnp.int32)
        bias.append(jnp.where((key >= 0) & (key < length), 0.0, MASKED))
    q, scores, own_scores = [], [], []
    for u, h in pairs:
        at = slice(u * unit, (u + 1) * unit)
        q.append(
            jnp.stack(
                [
                    queries[at, (h * group + i) * HD : (h * group + i + 1) * HD]
                    for i in range(group)
                ],
                axis=0,
            )
        )
        keys = cache_ref[rows_of(u), :, h * 2 * HD : (h * 2 + 1) * HD].reshape(keys_of, HD)
        scores.append(
            lax.dot_general(
                q[-1].reshape(group * unit, HD).astype(BF16),
                keys,
                (((1,), (1,)), ((), ())),
                preferred_element_type=F32,
            ).reshape(group, unit, keys_of)
        )
    for n, (u, h) in enumerate(pairs):
        at = slice(u * unit, (u + 1) * unit)
        own_key = own[at, h * 2 * HD : (h * 2 + 1) * HD]
        own_scores.append(jnp.sum(q[n] * own_key[None], axis=2, keepdims=True) * LOG2_SCALE)
    scores = [scores[n] * LOG2_SCALE + bias[u][None] for n, (u, h) in enumerate(pairs)]
    largest = [
        jnp.maximum(jnp.max(x, axis=2, keepdims=True), y) for x, y in zip(scores, own_scores)
    ]
    weights = [jnp.exp2(x - y).astype(BF16) for x, y in zip(scores, largest)]
    own_weights = [jnp.exp2(x - y) for x, y in zip(own_scores, largest)]
    sums = []
    for n, (u, h) in enumerate(pairs):
        at = slice(u * unit, (u + 1) * unit)
        values = cache_ref[rows_of(u), :, (h * 2 + 1) * HD : (h * 2 + 2) * HD].reshape(keys_of, HD)
        sums.append(
            jnp.dot(
                weights[n].reshape(group * unit, keys_of),
                jnp.concatenate([values, ones], axis=1),
                preferred_element_type=F32,
            ).reshape(group, unit, 2 * HD)
        )
    pieces = [[] for _ in units]
    stats = [jnp.zeros((unit, STATS), F32) for _ in units]
    for n, (u, h) in enumerate(pairs):
        at = slice(u * unit, (u + 1) * unit)
        own_value = own[at, (h * 2 + 1) * HD : (h * 2 + 2) * HD]
        total = sums[n][:, :, HD:] + own_weights[n]
        result = (sums[n][:, :, :HD] + own_weights[n] * own_value[None]) / total
        lse = largest[n] + jnp.log2(total)
        for i in range(group):
            pieces[u].append(result[i])
            stats[u] = jnp.where(lane == h * group + i, lse[i], stats[u])
    out = jnp.concatenate([jnp.concatenate(x, axis=1) for x in pieces], axis=0).astype(BF16)
    out_ref[...] = out
    here = iota((row_count, block_rows), 0) == iota((row_count, block_rows), 1) + first_row
    pick = jnp.dot(
        pick_ref[...], here.astype(F32).astype(BF16), preferred_element_type=F32
    ).astype(BF16)
    slot_out_ref[...] = jnp.dot(pick, out, preferred_element_type=F32)
    lse = jnp.concatenate(stats, axis=0)
    slot_lse_ref[...] = sum(
        jnp.dot(pick, part.astype(BF16), preferred_element_type=F32) for part in split_bf16(lse)
    )


def merge(pick_ref, *refs):
    parts, (kept_ref, got_ref, out_ref) = refs[:-3], refs[-3:]
    cached_refs, slot_out_refs, slot_lse_refs = parts[0::3], parts[1::3], parts[2::3]
    width = out_ref.shape[1]
    pick = pick_ref[...]
    arrived = all_blocks(steps_of(2 * kept_ref.shape[0]), kept_ref, got_ref)
    stats = arrived[:, width:]
    arrived_lse = (
        stats
        + pltpu.roll(stats, STATS - LSE_PITCH, 1)
        + pltpu.roll(stats, STATS - 2 * LSE_PITCH, 1)
    )
    cached_lse = sum(ref[...] for ref in slot_lse_refs)
    largest = jnp.maximum(cached_lse, arrived_lse)
    cached_weight = jnp.exp2(cached_lse - largest)
    arrived_weight = jnp.exp2(arrived_lse - largest)
    total = cached_weight + arrived_weight
    cached_weight = cached_weight / total
    arrived_weight = arrived_weight / total
    has = lax.dot_general(
        pick, jnp.ones((pick.shape[0], HD), BF16), TRANSPOSED, preferred_element_type=F32
    )
    for i in range(width // HD):
        at = slice(i * HD, (i + 1) * HD)
        merged = (
            sum(ref[:, at] for ref in slot_out_refs) * cached_weight[:, i : i + 1]
            + arrived[:, at] * arrived_weight[:, i : i + 1]
        )
        placed = lax.dot_general(
            pick, merged.astype(BF16), TRANSPOSED, preferred_element_type=F32
        )
        row = 0
        for ref in cached_refs:
            rows = slice(row, row + ref.shape[0])
            kept = ref[:, at].astype(F32)
            out_ref[rows, at] = jnp.where(has[rows] > 0.5, placed[rows], kept).astype(BF16)
            row += ref.shape[0]


def compiler_params(megabytes):
    return pltpu.CompilerParams(vmem_limit_bytes=megabytes * 1024 * 1024)


RESIDENT = pl.BlockSpec(memory_space=pltpu.VMEM)
REMAINS = pl.BlockSpec(memory_space=pl.ANY)


def in_vmem(x):
    return pltpu.with_memory_space_constraint(x, pltpu.VMEM)


def in_hbm(x):
    return pltpu.with_memory_space_constraint(x, pltpu.HBM)


def shards(
    prompts, decode_hidden, queries, kv_cache, cache_len, span_len, target_row, w_kv, kv_scale
):
    row_count = decode_hidden.shape[0]
    prompt_rows, features = prompts.shape
    sections = lax.axis_size("section")
    local_width = kv_cache.shape[2]
    query_width = queries.shape[1]
    slots = sections * CAP
    all_rows = prompt_rows + row_count
    scale = kv_scale.reshape(1, -1)
    lengths = cache_len.reshape(1, -1)

    steps = steps_of(sections)
    half = sections // 2
    prompts, decode_hidden, w_kv, scale = map(in_hbm, (prompts, decode_hidden, w_kv, scale))
    target_row, span_len, queries = map(in_hbm, (target_row, span_len, queries))
    kv_cache, lengths = map(in_hbm, (kv_cache, lengths))

    def block_pair(width):
        return [pltpu.VMEM((half, CAP, width), BF16)] * 2

    def swapped(blocks, done):
        pairs = [(i, i ^ steps[done][0]) for i in range(sections)]
        return in_vmem(lax.ppermute(blocks, "section", pairs))

    pick, keep, send = pl.pallas_call(
        select_queries,
        in_specs=[RESIDENT, RESIDENT],
        out_specs=[RESIDENT] * 3,
        out_shape=[pltpu.VMEM((slots, row_count), BF16)] + block_pair(query_width),
        compiler_params=compiler_params(16),
        name="select_queries",
    )(target_row, queries)
    got = swapped(send, 0)

    def regrouped(blocks, got, done, after):
        return pl.pallas_call(
            functools.partial(regroup, steps=steps, done=done),
            in_specs=[RESIDENT] * 2 + [REMAINS],
            out_specs=[RESIDENT] * 2,
            out_shape=block_pair(blocks.shape[2]),
            compiler_params=compiler_params(16),
            name="regroup",
        )(in_vmem(blocks), got, in_vmem(after))

    edges = (0, 256, 768, 1536, 2560, 4096)
    depth, head = edges[-1], edges[-2]
    rows, w_tail, total = pl.pallas_call(
        functools.partial(project_first, edges=edges),
        in_specs=[REMAINS] * 3,
        out_specs=[RESIDENT] * 3,
        out_shape=[
            pltpu.VMEM((all_rows, depth), BF16),
            pltpu.VMEM((depth - head, local_width), BF16),
            pltpu.VMEM((all_rows, local_width), F32),
        ],
        scratch_shapes=[
            pltpu.VMEM((head, local_width), BF16),
            pltpu.SemaphoreType.DMA((len(edges) - 1, 3)),
        ],
        compiler_params=compiler_params(12),
        name="project_first",
    )(prompts, decode_hidden, w_kv)
    keep, send = regrouped(keep, got, 1, total)
    got = swapped(send, 1)
    theirs, rows_rest, w_mine = pl.pallas_call(
        project_rest,
        in_specs=[REMAINS] * 4 + [RESIDENT] * 3 + [REMAINS],
        out_specs=[RESIDENT] * 3,
        out_shape=[
            pltpu.VMEM((all_rows, local_width), BF16),
            pltpu.VMEM((all_rows, features - depth), BF16),
            pltpu.VMEM((features, local_width), BF16),
        ],
        scratch_shapes=[
            pltpu.VMEM((features - depth, local_width), BF16),
            pltpu.VMEM((1, local_width), F32),
            pltpu.SemaphoreType.DMA((5,)),
        ],
        compiler_params=compiler_params(16),
        name="project_rest",
    )(prompts, decode_hidden, w_kv, scale, *map(in_vmem, (rows, w_tail, total, keep)))
    theirs, got = lax.optimization_barrier((theirs, got))
    got = in_vmem(got)
    other = in_vmem(lax.ppermute(theirs, "tp", [(0, 1), (1, 0)]))

    mine = []
    pieces = max(len(steps) - 2, 1)
    bounds = [all_rows * i // (16 * pieces) * 16 for i in range(pieces)] + [all_rows]
    after = theirs
    for piece, at in enumerate(spans(bounds)):
        if piece + 2 < len(steps):
            keep, send = regrouped(keep, got, piece + 2, after)
            got = swapped(send, piece + 2)
        last = piece == pieces - 1
        extra = [kv_cache, queries] if last else []
        part, *here = pl.pallas_call(
            functools.partial(project_mine, at=at, last=last),
            in_specs=[RESIDENT] * 3 + [REMAINS] * (2 + len(extra)),
            out_specs=[RESIDENT] * (1 + len(extra)),
            out_shape=[pltpu.VMEM((at.stop - at.start, local_width), BF16)]
            + [pltpu.VMEM(x.shape, BF16) for x in extra],
            scratch_shapes=[pltpu.VMEM((1, local_width), F32), pltpu.SemaphoreType.DMA((3,))],
            compiler_params=compiler_params(16),
            name="project_mine",
        )(*map(in_vmem, (rows, rows_rest, w_mine)), scale, in_vmem(keep), *extra)
        after = part
        mine.append(in_vmem(part))
    kv_here, queries_here = map(in_vmem, here)

    padded = -(-span_len.shape[1] // 16) * 16
    prepared = pl.pallas_call(
        functools.partial(prepare_arrived, row_count=row_count),
        in_specs=[RESIDENT] * 4,
        out_specs=[RESIDENT] * 3,
        out_shape=[
            pltpu.VMEM((padded, query_width), BF16),
            pltpu.VMEM((padded, sections * PITCH), BF16),
            pltpu.VMEM((padded, prompt_rows), F32),
        ],
        compiler_params=compiler_params(16),
        name="prepare_arrived",
    )(target_row, span_len, in_vmem(keep), got)
    answer_width = query_width + STATS
    keep, send = pl.pallas_call(
        attend_arrived,
        in_specs=[RESIDENT] * (4 + len(mine)),
        out_specs=[RESIDENT] * 2,
        out_shape=block_pair(answer_width),
        compiler_params=compiler_params(24),
        name="attend_arrived",
    )(*map(in_vmem, prepared), other, *mine)

    shares = []
    bounds = [row_count * i // (16 * len(steps)) * 16 for i in range(len(steps))] + [row_count]
    for done, at in enumerate(spans(bounds)):
        got = swapped(send, done)
        share = pl.pallas_call(
            functools.partial(attend_cache, rows_at=at),
            in_specs=[RESIDENT] * 6 + [REMAINS],
            out_specs=[RESIDENT] * 3,
            out_shape=[
                pltpu.VMEM((at.stop - at.start, query_width), BF16),
                pltpu.VMEM((slots, query_width), F32),
                pltpu.VMEM((slots, STATS), F32),
            ],
            compiler_params=compiler_params(24),
            name="attend_cache",
        )(queries_here, kv_here, lengths, mine[-1], other, in_vmem(pick), in_vmem(keep))
        shares += share
        if done + 1 < len(steps):
            keep, send = regrouped(keep, got, done + 1, share[2])

    return pl.pallas_call(
        merge,
        in_specs=[RESIDENT] * (3 + len(shares)),
        out_specs=RESIDENT,
        out_shape=jax.ShapeDtypeStruct((row_count, query_width), BF16),
        compiler_params=compiler_params(24),
        name="merge",
    )(*map(in_vmem, (pick, *shares, keep)), got)


def solution(mesh):
    in_specs = (
        P(("groups", "section"), "tp"),
        P(("groups", "section"), "tp"),
        P(("groups", "section"), "tp"),
        P(("groups", "section"), None, "tp"),
        P(("groups", "section")),
        P("groups", None),
        P("groups", None),
        P("tp", None),
        P(),
    )
    out_specs = P(("groups", "section"), "tp")
    return jax.shard_map(shards, mesh=mesh, in_specs=in_specs, out_specs=out_specs, check_vma=False)
```

```python
import functools
import math

import jax
import jax.numpy as jnp
from jax import lax
from jax.experimental import pallas as pl
from jax.experimental.pallas import tpu as pltpu
from jax.sharding import PartitionSpec as P

HD = 128
CAP = 2
STATS = 128
MASKED = -1e30
LSE_PITCH = 40
PITCH = 8
LOG2_SCALE = HD ** (-0.5) * math.log2(math.e)
F32 = jnp.float32
BF16 = jnp.bfloat16
TRANSPOSED = (((0,), (0,)), ((), ()))


def iota(shape, dim):
    return lax.broadcasted_iota(jnp.int32, shape, dim)


def one_hot(shape, dim, index):
    return (iota(shape, dim) == index).astype(F32).astype(BF16)


def pick_rows(target_ref, row_count):
    sections, requests = target_ref.shape
    shape = (sections * CAP, requests)
    position = lax.axis_index("section")
    slot_id = iota(shape, 0)
    table = jnp.zeros(shape, jnp.int32)
    for k in range(sections):
        mine = (slot_id >= k * CAP) & (slot_id < (k + 1) * CAP)
        section = position ^ distance(k, lax.axis_index("tp"), sections)
        table = jnp.where(mine, target_ref[pl.ds(section, 1), :], table)
    local = table - position * row_count
    here = (local >= 0) & (local < row_count)
    square = (requests, requests)
    earlier = jnp.dot(
        here.astype(F32).astype(BF16),
        (iota(square, 0) < iota(square, 1)).astype(F32).astype(BF16),
        preferred_element_type=F32,
    )
    chosen = here & (earlier == lax.rem(slot_id, CAP).astype(F32))
    row = jnp.max(jnp.where(chosen, local.astype(F32), -1.0), axis=1, keepdims=True)
    return one_hot((shape[0], row_count), 1, row.astype(jnp.int32))


def steps_of(sections):
    steps = []
    bit = sections // 2
    while bit:
        sent = [k for k in range(sections) if k & bit]
        steps.append((bit, sent, [k for k in range(sections) if not k & bit]))
        bit //= 2
    return steps


def distance(block, tp, sections):
    turned = (block << 1) & (sections - 1) | block // (sections // 2)
    return jnp.where(tp == 0, block, turned)


def block_at(distances, tp, sections):
    turned = (distances >> 1) | (distances & 1) * (sections // 2)
    return jnp.where(tp == 0, distances, turned)


def regroup(kept_ref, got_ref, after_ref, keep_ref, send_ref, *, steps, done):
    where = {k: (got_ref, i) for i, k in enumerate(steps[done - 1][1])}
    where |= {k: (kept_ref, i) for i, k in enumerate(steps[done - 1][2])}
    for out_ref, blocks in ((send_ref, steps[done][1]), (keep_ref, steps[done][2])):
        for i, k in enumerate(blocks):
            ref, at = where[k]
            out_ref[i] = ref[at]


def all_blocks(steps, kept_ref, got_ref):
    where = {k: got_ref[i] for i, k in enumerate(steps[-1][1])}
    where |= {k: kept_ref[i] for i, k in enumerate(steps[-1][2])}
    return jnp.concatenate([where[k].astype(F32) for k in range(len(where))], axis=0)


def select_queries(target_ref, queries_ref, pick_ref, keep_ref, send_ref):
    _, sent, kept = steps_of(target_ref.shape[0])[0]
    pick = pick_rows(target_ref, queries_ref.shape[0])
    pick_ref[...] = pick
    asked = jnp.dot(pick, queries_ref[...], preferred_element_type=F32)
    for ref, blocks in ((send_ref, sent), (keep_ref, kept)):
        for i, k in enumerate(blocks):
            ref[i] = asked[k * CAP : (k + 1) * CAP].astype(BF16)


def spans(edges):
    return [slice(a, b) for a, b in zip(edges[:-1], edges[1:])]


def load_rows(prompts_ref, hidden_ref, there, rows_ref, here, sems):
    prompt_rows = prompts_ref.shape[0]
    return [
        pltpu.make_async_copy(
            prompts_ref.at[:, there], rows_ref.at[:prompt_rows, here], sems.at[0]
        ),
        pltpu.make_async_copy(
            hidden_ref.at[:, there], rows_ref.at[prompt_rows:, here], sems.at[1]
        ),
    ]


def channels(offset, width):
    tp = lax.axis_index("tp")
    return pl.ds(pl.multiple_of(((tp + offset) & 1) * width, width), width)


def project_first(
    prompts_ref, hidden_ref, w_ref, rows_ref, w_tail_ref, total_ref, w_head_ref, sems, *, edges
):
    theirs = channels(1, total_ref.shape[1])
    chunks = spans(edges)
    head = edges[-2]
    waits = []
    for c, at in enumerate(chunks):
        here = at if at.stop <= head else slice(0, at.stop - head)
        w_here_ref = w_head_ref if at.stop <= head else w_tail_ref
        copies = load_rows(prompts_ref, hidden_ref, at, rows_ref, at, sems.at[c])
        copies.append(
            pltpu.make_async_copy(w_ref.at[at, theirs], w_here_ref.at[here, :], sems.at[c, 2])
        )
        for copy in copies:
            copy.start()
        waits.append(copies)
    for c, at in enumerate(chunks):
        for copy in waits[c]:
            copy.wait()
        if at.stop <= head:
            part = jnp.dot(rows_ref[:, at], w_head_ref[at, :], preferred_element_type=F32)
            if c == 0:
                total_ref[...] = part
            else:
                total_ref[...] += part


def project_rest(
    prompts_ref,
    hidden_ref,
    w_ref,
    scale_ref,
    rows_ref,
    w_tail_ref,
    total_ref,
    after_ref,
    theirs_ref,
    rows_rest_ref,
    w_mine_ref,
    w_rest_ref,
    scale_here_ref,
    sems,
):
    width = theirs_ref.shape[1]
    theirs, mine = channels(1, width), channels(0, width)
    depth = rows_ref.shape[1]
    head = depth - w_tail_ref.shape[0]
    rest = slice(depth, depth + rows_rest_ref.shape[1])
    copies = load_rows(prompts_ref, hidden_ref, rest, rows_rest_ref, slice(None), sems)
    copies += [
        pltpu.make_async_copy(w_ref.at[rest, theirs], w_rest_ref, sems.at[2]),
        pltpu.make_async_copy(scale_ref.at[:, theirs], scale_here_ref, sems.at[3]),
        pltpu.make_async_copy(w_ref.at[:, mine], w_mine_ref, sems.at[4]),
    ]
    for copy in copies:
        copy.start()
    total = total_ref[...] + jnp.dot(
        rows_ref[:, head:], w_tail_ref[...], preferred_element_type=F32
    )
    for copy in copies[:-1]:
        copy.wait()
    total += jnp.dot(rows_rest_ref[...], w_rest_ref[...], preferred_element_type=F32)
    theirs_ref[...] = (total * scale_here_ref[...]).astype(BF16)
    copies[-1].wait()


def project_mine(rows_ref, rows_rest_ref, w_mine_ref, scale_ref, after_ref, *refs, at, last):
    refs, (scale_here_ref, sems) = refs[:-2], refs[-2:]
    if last:
        cache_ref, queries_ref, out_ref, cache_here_ref, queries_here_ref = refs
    else:
        (out_ref,) = refs
    mine = channels(0, out_ref.shape[1])
    copies = [pltpu.make_async_copy(scale_ref.at[:, mine], scale_here_ref, sems.at[0])]
    if last:
        copies.append(pltpu.make_async_copy(queries_ref, queries_here_ref, sems.at[1]))
        copies.append(pltpu.make_async_copy(cache_ref, cache_here_ref, sems.at[2]))
    for copy in copies:
        copy.start()
    depth = rows_ref.shape[1]
    count = at.stop - at.start
    block = count // 2 if count % 32 == 0 else count
    for m in spans(range(0, count + 1, block)):
        there = slice(at.start + m.start, at.start + m.stop)
        total = jnp.dot(rows_ref[there, :], w_mine_ref[:depth, :], preferred_element_type=F32)
        total += jnp.dot(
            rows_rest_ref[there, :], w_mine_ref[depth:, :], preferred_element_type=F32
        )
        if m.start == 0:
            copies[0].wait()
        out_ref[m, :] = (total * scale_here_ref[...]).astype(BF16)
    for copy in copies[1:]:
        copy.wait()


def split_bf16(x):
    high = x.astype(BF16).astype(F32)
    middle = (x - high).astype(BF16).astype(F32)
    return high, middle, (x - high - middle).astype(BF16).astype(F32)


def request_slots(target_ref, span_ref, row_count, padded):
    sections, requests = target_ref.shape
    position = lax.axis_index("section")
    target = target_ref[pl.ds(position, 1), :].astype(F32)
    span = span_ref[pl.ds(position, 1), :].astype(F32)
    diagonal = iota((padded, requests), 0) == iota((padded, requests), 1)
    target_col = jnp.sum(jnp.where(diagonal, target, 0.0), axis=1, keepdims=True)
    span_col = jnp.sum(jnp.where(diagonal, span, 0.0), axis=1, keepdims=True)
    section_row = jnp.zeros_like(target)
    section_col = jnp.zeros_like(target_col)
    for s in range(1, sections):
        section_row = section_row + (target >= s * row_count).astype(F32)
        section_col = section_col + (target_col >= s * row_count).astype(F32)
    before = (section_row == section_col) & (
        iota((padded, requests), 1) < iota((padded, requests), 0)
    )
    rank_col = jnp.sum(before.astype(F32), axis=1, keepdims=True).astype(jnp.int32)
    real = iota((padded, 1), 0) < requests
    section_col = jnp.where(real, section_col.astype(jnp.int32), -1)
    return section_col, rank_col, span_col.astype(jnp.int32)


def prepare_arrived(
    target_ref, span_ref, kept_ref, got_ref, rows_ref, slot_of_ref, bias_ref, *, row_count
):
    sections, requests = target_ref.shape
    padded, prompt_rows = bias_ref.shape
    span_rows = prompt_rows // requests
    section_col, rank_col, span_col = request_slots(target_ref, span_ref, row_count, padded)
    block = block_at(
        section_col ^ lax.axis_index("section"), lax.axis_index("tp"), sections
    )
    slot = jnp.where(section_col >= 0, block * PITCH + rank_col, -1)
    slot_of_ref[...] = one_hot((padded, sections * PITCH), 1, slot)
    slot = jnp.where(section_col >= 0, block * CAP + rank_col, -1)
    rows_ref[...] = jnp.dot(
        one_hot((padded, sections * CAP), 1, slot),
        all_blocks(steps_of(sections), kept_ref, got_ref).astype(BF16),
        preferred_element_type=F32,
    ).astype(BF16)
    key = iota((padded, prompt_rows), 1) - iota((padded, prompt_rows), 0) * span_rows
    bias_ref[...] = jnp.where((key >= 0) & (key < span_col), 0.0, MASKED)


def attend_arrived(rows_ref, slot_of_ref, bias_ref, other_ref, *refs):
    mine_refs, (keep_ref, send_ref) = refs[:-2], refs[-2:]
    padded, prompt_rows = bias_ref.shape
    kv_heads = other_ref.shape[1] // (2 * HD)
    group = rows_ref.shape[1] // (kv_heads * HD)
    rows = rows_ref[...]
    slot_of = slot_of_ref[...]
    bias = bias_ref[...]
    mine = jnp.concatenate([ref[...] for ref in mine_refs], axis=0)
    kv = (mine[:prompt_rows].astype(F32) + other_ref[:prompt_rows, :].astype(F32)).astype(BF16)
    scores = []
    for h in range(kv_heads):
        stacked = jnp.concatenate(
            [rows[:, (h * group + i) * HD : (h * group + i + 1) * HD] for i in range(group)],
            axis=0,
        )
        keys = kv[:, h * 2 * HD : (h * 2 + 1) * HD]
        scores.append(
            lax.dot_general(
                stacked, keys, (((1,), (1,)), ((), ())), preferred_element_type=F32
            )
        )
    scores = [
        x.reshape(group, padded, prompt_rows) * LOG2_SCALE + bias[None] for x in scores
    ]
    largest = [jnp.max(x, axis=2, keepdims=True) for x in scores]
    weights = [jnp.exp2(x - y) for x, y in zip(scores, largest)]
    totals = [jnp.sum(x, axis=2, keepdims=True) for x in weights]
    lane = iota((padded, STATS), 1)
    lse = jnp.zeros((padded, STATS), F32)
    pieces = []
    for h in range(kv_heads):
        values = jnp.dot(
            weights[h].reshape(group * padded, prompt_rows).astype(BF16),
            kv[:, (h * 2 + 1) * HD : (h * 2 + 2) * HD],
            preferred_element_type=F32,
        ).reshape(group, padded, HD)
        values = values / totals[h]
        head_lse = largest[h] + jnp.log2(totals[h])
        for i in range(group):
            pieces.append(values[i])
            lse = jnp.where(lane == h * group + i, head_lse[i], lse)
    high, middle, low = split_bf16(lse)
    stats = high + pltpu.roll(middle, LSE_PITCH, 1) + pltpu.roll(low, 2 * LSE_PITCH, 1)
    result = jnp.concatenate(pieces + [stats], axis=1).astype(BF16)
    answers = lax.dot_general(slot_of, result, TRANSPOSED, preferred_element_type=F32)
    _, sent, kept = steps_of(2 * keep_ref.shape[0])[0]
    for ref, blocks in ((send_ref, sent), (keep_ref, kept)):
        for i, k in enumerate(blocks):
            ref[i] = answers[k * PITCH : k * PITCH + CAP].astype(BF16)


def attend_cache(
    queries_ref,
    cache_ref,
    len_ref,
    mine_ref,
    other_ref,
    pick_ref,
    after_ref,
    out_ref,
    slot_out_ref,
    slot_lse_ref,
    *,
    rows_at,
):
    row_count, cache_rows, width = cache_ref.shape
    first_row, block_rows = rows_at.start, rows_at.stop - rows_at.start
    kv_heads = width // (2 * HD)
    group = queries_ref.shape[1] // (kv_heads * HD)
    unit = 8
    keys_of = unit * cache_rows
    queries = queries_ref[rows_at, :].astype(F32)
    own = sum(
        ref[pl.ds(ref.shape[0] - row_count + first_row, block_rows), :].astype(F32)
        for ref in (mine_ref, other_ref)
    )
    own = own.astype(BF16).astype(F32)
    key = iota((unit, keys_of), 1) - iota((unit, keys_of), 0) * cache_rows
    lengths = len_ref[...].astype(F32)
    lane = iota((unit, STATS), 1)
    ones = jnp.ones((keys_of, HD), BF16)
    units = range(block_rows // unit)

    def rows_of(u):
        return slice(first_row + u * unit, first_row + (u + 1) * unit)

    pairs = [(u, h) for u in units for h in range(kv_heads)]
    bias = []
    for u in units:
        row = iota((unit, row_count), 0) + (first_row + u * unit)
        length = jnp.sum(
            jnp.where(iota((unit, row_count), 1) == row, lengths, 0.0), axis=1, keepdims=True
        ).astype(jnp.int32)
        bias.append(jnp.where((key >= 0) & (key < length), 0.0, MASKED))
    q, scores, own_scores = [], [], []
    for u, h in pairs:
        at = slice(u * unit, (u + 1) * unit)
        q.append(
            jnp.stack(
                [
                    queries[at, (h * group + i) * HD : (h * group + i + 1) * HD]
                    for i in range(group)
                ],
                axis=0,
            )
        )
        keys = cache_ref[rows_of(u), :, h * 2 * HD : (h * 2 + 1) * HD].reshape(keys_of, HD)
        scores.append(
            lax.dot_general(
                q[-1].reshape(group * unit, HD).astype(BF16),
                keys,
                (((1,), (1,)), ((), ())),
                preferred_element_type=F32,
            ).reshape(group, unit, keys_of)
        )
    for n, (u, h) in enumerate(pairs):
        at = slice(u * unit, (u + 1) * unit)
        own_key = own[at, h * 2 * HD : (h * 2 + 1) * HD]
        own_scores.append(jnp.sum(q[n] * own_key[None], axis=2, keepdims=True) * LOG2_SCALE)
    scores = [scores[n] * LOG2_SCALE + bias[u][None] for n, (u, h) in enumerate(pairs)]
    largest = [
        jnp.maximum(jnp.max(x, axis=2, keepdims=True), y) for x, y in zip(scores, own_scores)
    ]
    weights = [jnp.exp2(x - y).astype(BF16) for x, y in zip(scores, largest)]
    own_weights = [jnp.exp2(x - y) for x, y in zip(own_scores, largest)]
    sums = []
    for n, (u, h) in enumerate(pairs):
        at = slice(u * unit, (u + 1) * unit)
        values = cache_ref[rows_of(u), :, (h * 2 + 1) * HD : (h * 2 + 2) * HD].reshape(keys_of, HD)
        sums.append(
            jnp.dot(
                weights[n].reshape(group * unit, keys_of),
                jnp.concatenate([values, ones], axis=1),
                preferred_element_type=F32,
            ).reshape(group, unit, 2 * HD)
        )
    pieces = [[] for _ in units]
    stats = [jnp.zeros((unit, STATS), F32) for _ in units]
    for n, (u, h) in enumerate(pairs):
        at = slice(u * unit, (u + 1) * unit)
        own_value = own[at, (h * 2 + 1) * HD : (h * 2 + 2) * HD]
        total = sums[n][:, :, HD:] + own_weights[n]
        result = (sums[n][:, :, :HD] + own_weights[n] * own_value[None]) / total
        lse = largest[n] + jnp.log2(total)
        for i in range(group):
            pieces[u].append(result[i])
            stats[u] = jnp.where(lane == h * group + i, lse[i], stats[u])
    out = jnp.concatenate([jnp.concatenate(x, axis=1) for x in pieces], axis=0).astype(BF16)
    out_ref[...] = out
    here = iota((row_count, block_rows), 0) == iota((row_count, block_rows), 1) + first_row
    pick = jnp.dot(
        pick_ref[...], here.astype(F32).astype(BF16), preferred_element_type=F32
    ).astype(BF16)
    slot_out_ref[...] = jnp.dot(pick, out, preferred_element_type=F32)
    lse = jnp.concatenate(stats, axis=0)
    slot_lse_ref[...] = sum(
        jnp.dot(pick, part.astype(BF16), preferred_element_type=F32) for part in split_bf16(lse)
    )


def merge(pick_ref, *refs):
    parts, (kept_ref, got_ref, out_ref) = refs[:-3], refs[-3:]
    cached_refs, slot_out_refs, slot_lse_refs = parts[0::3], parts[1::3], parts[2::3]
    width = out_ref.shape[1]
    pick = pick_ref[...]
    arrived = all_blocks(steps_of(2 * kept_ref.shape[0]), kept_ref, got_ref)
    stats = arrived[:, width:]
    arrived_lse = (
        stats
        + pltpu.roll(stats, STATS - LSE_PITCH, 1)
        + pltpu.roll(stats, STATS - 2 * LSE_PITCH, 1)
    )
    cached_lse = sum(ref[...] for ref in slot_lse_refs)
    largest = jnp.maximum(cached_lse, arrived_lse)
    cached_weight = jnp.exp2(cached_lse - largest)
    arrived_weight = jnp.exp2(arrived_lse - largest)
    total = cached_weight + arrived_weight
    cached_weight = cached_weight / total
    arrived_weight = arrived_weight / total
    has = lax.dot_general(
        pick, jnp.ones((pick.shape[0], HD), BF16), TRANSPOSED, preferred_element_type=F32
    )
    for i in range(width // HD):
        at = slice(i * HD, (i + 1) * HD)
        merged = (
            sum(ref[:, at] for ref in slot_out_refs) * cached_weight[:, i : i + 1]
            + arrived[:, at] * arrived_weight[:, i : i + 1]
        )
        placed = lax.dot_general(
            pick, merged.astype(BF16), TRANSPOSED, preferred_element_type=F32
        )
        row = 0
        for ref in cached_refs:
            rows = slice(row, row + ref.shape[0])
            kept = ref[:, at].astype(F32)
            out_ref[rows, at] = jnp.where(has[rows] > 0.5, placed[rows], kept).astype(BF16)
            row += ref.shape[0]


def compiler_params(megabytes):
    return pltpu.CompilerParams(vmem_limit_bytes=megabytes * 1024 * 1024)


RESIDENT = pl.BlockSpec(memory_space=pltpu.VMEM)
REMAINS = pl.BlockSpec(memory_space=pl.ANY)


def in_vmem(x):
    return pltpu.with_memory_space_constraint(x, pltpu.VMEM)


def in_hbm(x):
    return pltpu.with_memory_space_constraint(x, pltpu.HBM)


def shards(
    prompts, decode_hidden, queries, kv_cache, cache_len, span_len, target_row, w_kv, kv_scale
):
    row_count = decode_hidden.shape[0]
    prompt_rows, features = prompts.shape
    sections = lax.axis_size("section")
    tensor_parts = lax.axis_size("tp")
    local_width = kv_cache.shape[2]
    query_width = queries.shape[1]
    slots = sections * CAP
    all_rows = prompt_rows + row_count
    scale = kv_scale.reshape(1, -1)
    lengths = cache_len.reshape(1, -1)

    steps = steps_of(sections)
    half = sections // 2
    prompts, decode_hidden, w_kv, scale = map(in_hbm, (prompts, decode_hidden, w_kv, scale))
    target_row, span_len, queries = map(in_hbm, (target_row, span_len, queries))
    kv_cache, lengths = map(in_hbm, (kv_cache, lengths))

    def block_pair(width):
        return [pltpu.VMEM((half, CAP, width), BF16)] * 2

    def swapped(blocks, done):
        bit = steps[done][0]
        turned = (bit << 1) & (sections - 1) or 1
        pairs = []
        for section in range(sections):
            for tp in range(tensor_parts):
                partner = section ^ (turned if tp else bit)
                pairs.append((section * tensor_parts + tp, partner * tensor_parts + tp))
        return in_vmem(lax.ppermute(blocks, ("section", "tp"), pairs))

    pick, keep, send = pl.pallas_call(
        select_queries,
        in_specs=[RESIDENT, RESIDENT],
        out_specs=[RESIDENT] * 3,
        out_shape=[pltpu.VMEM((slots, row_count), BF16)] + block_pair(query_width),
        compiler_params=compiler_params(16),
        name="select_queries",
    )(target_row, queries)
    got = swapped(send, 0)

    def regrouped(blocks, got, done, after):
        return pl.pallas_call(
            functools.partial(regroup, steps=steps, done=done),
            in_specs=[RESIDENT] * 2 + [REMAINS],
            out_specs=[RESIDENT] * 2,
            out_shape=block_pair(blocks.shape[2]),
            compiler_params=compiler_params(16),
            name="regroup",
        )(in_vmem(blocks), got, in_vmem(after))

    edges = (0, 256, 768, 1536, 2560, 4096)
    depth, head = edges[-1], edges[-2]
    rows, w_tail, total = pl.pallas_call(
        functools.partial(project_first, edges=edges),
        in_specs=[REMAINS] * 3,
        out_specs=[RESIDENT] * 3,
        out_shape=[
            pltpu.VMEM((all_rows, depth), BF16),
            pltpu.VMEM((depth - head, local_width), BF16),
            pltpu.VMEM((all_rows, local_width), F32),
        ],
        scratch_shapes=[
            pltpu.VMEM((head, local_width), BF16),
            pltpu.SemaphoreType.DMA((len(edges) - 1, 3)),
        ],
        compiler_params=compiler_params(12),
        name="project_first",
    )(prompts, decode_hidden, w_kv)
    keep, send = regrouped(keep, got, 1, total)
    got = swapped(send, 1)
    theirs, rows_rest, w_mine = pl.pallas_call(
        project_rest,
        in_specs=[REMAINS] * 4 + [RESIDENT] * 3 + [REMAINS],
        out_specs=[RESIDENT] * 3,
        out_shape=[
            pltpu.VMEM((all_rows, local_width), BF16),
            pltpu.VMEM((all_rows, features - depth), BF16),
            pltpu.VMEM((features, local_width), BF16),
        ],
        scratch_shapes=[
            pltpu.VMEM((features - depth, local_width), BF16),
            pltpu.VMEM((1, local_width), F32),
            pltpu.SemaphoreType.DMA((5,)),
        ],
        compiler_params=compiler_params(16),
        name="project_rest",
    )(prompts, decode_hidden, w_kv, scale, *map(in_vmem, (rows, w_tail, total, keep)))
    theirs, got = lax.optimization_barrier((theirs, got))
    got = in_vmem(got)
    other = in_vmem(lax.ppermute(theirs, "tp", [(0, 1), (1, 0)]))

    mine = []
    pieces = max(len(steps) - 2, 1)
    bounds = [all_rows * i // (16 * pieces) * 16 for i in range(pieces)] + [all_rows]
    after = theirs
    for piece, at in enumerate(spans(bounds)):
        if piece + 2 < len(steps):
            keep, send = regrouped(keep, got, piece + 2, after)
            got = swapped(send, piece + 2)
        last = piece == pieces - 1
        extra = [kv_cache, queries] if last else []
        part, *here = pl.pallas_call(
            functools.partial(project_mine, at=at, last=last),
            in_specs=[RESIDENT] * 3 + [REMAINS] * (2 + len(extra)),
            out_specs=[RESIDENT] * (1 + len(extra)),
            out_shape=[pltpu.VMEM((at.stop - at.start, local_width), BF16)]
            + [pltpu.VMEM(x.shape, BF16) for x in extra],
            scratch_shapes=[pltpu.VMEM((1, local_width), F32), pltpu.SemaphoreType.DMA((3,))],
            compiler_params=compiler_params(16),
            name="project_mine",
        )(*map(in_vmem, (rows, rows_rest, w_mine)), scale, in_vmem(keep), *extra)
        after = part
        mine.append(in_vmem(part))
    kv_here, queries_here = map(in_vmem, here)

    padded = -(-span_len.shape[1] // 16) * 16
    prepared = pl.pallas_call(
        functools.partial(prepare_arrived, row_count=row_count),
        in_specs=[RESIDENT] * 4,
        out_specs=[RESIDENT] * 3,
        out_shape=[
            pltpu.VMEM((padded, query_width), BF16),
            pltpu.VMEM((padded, sections * PITCH), BF16),
            pltpu.VMEM((padded, prompt_rows), F32),
        ],
        compiler_params=compiler_params(16),
        name="prepare_arrived",
    )(target_row, span_len, in_vmem(keep), got)
    answer_width = query_width + STATS
    keep, send = pl.pallas_call(
        attend_arrived,
        in_specs=[RESIDENT] * (4 + len(mine)),
        out_specs=[RESIDENT] * 2,
        out_shape=block_pair(answer_width),
        compiler_params=compiler_params(24),
        name="attend_arrived",
    )(*map(in_vmem, prepared), other, *mine)

    shares = []
    bounds = [row_count * i // (16 * len(steps)) * 16 for i in range(len(steps))] + [row_count]
    for done, at in enumerate(spans(bounds)):
        got = swapped(send, done)
        share = pl.pallas_call(
            functools.partial(attend_cache, rows_at=at),
            in_specs=[RESIDENT] * 6 + [REMAINS],
            out_specs=[RESIDENT] * 3,
            out_shape=[
                pltpu.VMEM((at.stop - at.start, query_width), BF16),
                pltpu.VMEM((slots, query_width), F32),
                pltpu.VMEM((slots, STATS), F32),
            ],
            compiler_params=compiler_params(24),
            name="attend_cache",
        )(queries_here, kv_here, lengths, mine[-1], other, in_vmem(pick), in_vmem(keep))
        shares += share
        if done + 1 < len(steps):
            keep, send = regrouped(keep, got, done + 1, share[2])

    return pl.pallas_call(
        merge,
        in_specs=[RESIDENT] * (3 + len(shares)),
        out_specs=RESIDENT,
        out_shape=jax.ShapeDtypeStruct((row_count, query_width), BF16),
        compiler_params=compiler_params(24),
        name="merge",
    )(*map(in_vmem, (pick, *shares, keep)), got)


def solution(mesh):
    in_specs = (
        P(("groups", "section"), "tp"),
        P(("groups", "section"), "tp"),
        P(("groups", "section"), "tp"),
        P(("groups", "section"), None, "tp"),
        P(("groups", "section")),
        P("groups", None),
        P("groups", None),
        P("tp", None),
        P(),
    )
    out_specs = P(("groups", "section"), "tp")
    return jax.shard_map(shards, mesh=mesh, in_specs=in_specs, out_specs=out_specs, check_vma=False)
```

```python
import functools
import math

import jax
import jax.numpy as jnp
from jax import lax
from jax.experimental import pallas as pl
from jax.experimental.pallas import tpu as pltpu
from jax.sharding import PartitionSpec as P

HD = 128
CAP = 2
STATS = 128
MASKED = -1e30
LSE_PITCH = 40
PITCH = 8
LOG2_SCALE = HD ** (-0.5) * math.log2(math.e)
F32 = jnp.float32
BF16 = jnp.bfloat16
TRANSPOSED = (((0,), (0,)), ((), ()))


def iota(shape, dim):
    return lax.broadcasted_iota(jnp.int32, shape, dim)


def one_hot(shape, dim, index):
    return (iota(shape, dim) == index).astype(F32).astype(BF16)


def pick_rows(target_ref, row_count):
    sections, requests = target_ref.shape
    shape = (sections * CAP, requests)
    position = lax.axis_index("section")
    slot_id = iota(shape, 0)
    table = jnp.zeros(shape, jnp.int32)
    for k in range(sections):
        mine = (slot_id >= k * CAP) & (slot_id < (k + 1) * CAP)
        table = jnp.where(mine, target_ref[pl.ds(position ^ k, 1), :], table)
    local = table - position * row_count
    here = (local >= 0) & (local < row_count)
    square = (requests, requests)
    earlier = jnp.dot(
        here.astype(F32).astype(BF16),
        (iota(square, 0) < iota(square, 1)).astype(F32).astype(BF16),
        preferred_element_type=F32,
    )
    chosen = here & (earlier == lax.rem(slot_id, CAP).astype(F32))
    row = jnp.max(jnp.where(chosen, local.astype(F32), -1.0), axis=1, keepdims=True)
    return one_hot((shape[0], row_count), 1, row.astype(jnp.int32))


def steps_of(sections):
    steps = []
    bit = sections // 2
    while bit:
        sent = [k for k in range(sections) if k & bit]
        steps.append((bit, sent, [k for k in range(sections) if not k & bit]))
        bit //= 2
    return steps


def answer_steps_of(sections):
    steps = []
    bit = 1
    while 4 * bit < sections:
        sent = [k for k in range(sections) if k & bit]
        steps.append((bit, sent, [k for k in range(sections) if not k & bit]))
        bit *= 2
    return steps


def rearrange(step, kept_ref, got_ref, *out):
    where = {k: (got_ref, i) for i, k in enumerate(step[1])}
    where |= {k: (kept_ref, i) for i, k in enumerate(step[2])}
    for out_ref, blocks in out:
        for i, k in enumerate(blocks):
            ref, at = where[k]
            out_ref[i] = ref[at]


def regroup(kept_ref, got_ref, after_ref, keep_ref, send_ref, *, steps, done):
    _, sent, kept = steps[done]
    rearrange(steps[done - 1], kept_ref, got_ref, (send_ref, sent), (keep_ref, kept))


def fan_out(kept_ref, got_ref, after_ref, *out_refs, step):
    size = out_refs[0].shape[0]
    groups = [range(m * size, (m + 1) * size) for m in range(len(out_refs))]
    rearrange(step, kept_ref, got_ref, *zip(out_refs, groups))


def all_blocks(steps, kept_ref, got_ref):
    where = {k: got_ref[i] for i, k in enumerate(steps[-1][1])}
    where |= {k: kept_ref[i] for i, k in enumerate(steps[-1][2])}
    return jnp.concatenate([where[k].astype(F32) for k in range(len(where))], axis=0)


def select_queries(target_ref, queries_ref, pick_ref, keep_ref, send_ref):
    _, sent, kept = steps_of(target_ref.shape[0])[0]
    pick = pick_rows(target_ref, queries_ref.shape[0])
    pick_ref[...] = pick
    asked = jnp.dot(pick, queries_ref[...], preferred_element_type=F32)
    for ref, blocks in ((send_ref, sent), (keep_ref, kept)):
        for i, k in enumerate(blocks):
            ref[i] = asked[k * CAP : (k + 1) * CAP].astype(BF16)


def spans(edges):
    return [slice(a, b) for a, b in zip(edges[:-1], edges[1:])]


def load_rows(prompts_ref, hidden_ref, there, rows_ref, here, sems):
    prompt_rows = prompts_ref.shape[0]
    return [
        pltpu.make_async_copy(
            prompts_ref.at[:, there], rows_ref.at[:prompt_rows, here], sems.at[0]
        ),
        pltpu.make_async_copy(
            hidden_ref.at[:, there], rows_ref.at[prompt_rows:, here], sems.at[1]
        ),
    ]


def channels(offset, width):
    tp = lax.axis_index("tp")
    return pl.ds(pl.multiple_of(((tp + offset) & 1) * width, width), width)


def project_first(
    prompts_ref, hidden_ref, w_ref, rows_ref, w_tail_ref, total_ref, w_head_ref, sems, *, edges
):
    theirs = channels(1, total_ref.shape[1])
    chunks = spans(edges)
    head = edges[-2]
    waits = []
    for c, at in enumerate(chunks):
        here = at if at.stop <= head else slice(0, at.stop - head)
        w_here_ref = w_head_ref if at.stop <= head else w_tail_ref
        copies = load_rows(prompts_ref, hidden_ref, at, rows_ref, at, sems.at[c])
        copies.append(
            pltpu.make_async_copy(w_ref.at[at, theirs], w_here_ref.at[here, :], sems.at[c, 2])
        )
        for copy in copies:
            copy.start()
        waits.append(copies)
    for c, at in enumerate(chunks):
        for copy in waits[c]:
            copy.wait()
        if at.stop <= head:
            part = jnp.dot(rows_ref[:, at], w_head_ref[at, :], preferred_element_type=F32)
            if c == 0:
                total_ref[...] = part
            else:
                total_ref[...] += part


def project_rest(
    prompts_ref,
    hidden_ref,
    w_ref,
    scale_ref,
    rows_ref,
    w_tail_ref,
    total_ref,
    after_ref,
    theirs_ref,
    rows_rest_ref,
    w_mine_ref,
    w_rest_ref,
    scale_here_ref,
    sems,
):
    width = theirs_ref.shape[1]
    theirs, mine = channels(1, width), channels(0, width)
    depth = rows_ref.shape[1]
    head = depth - w_tail_ref.shape[0]
    rest = slice(depth, depth + rows_rest_ref.shape[1])
    copies = load_rows(prompts_ref, hidden_ref, rest, rows_rest_ref, slice(None), sems)
    copies += [
        pltpu.make_async_copy(w_ref.at[rest, theirs], w_rest_ref, sems.at[2]),
        pltpu.make_async_copy(scale_ref.at[:, theirs], scale_here_ref, sems.at[3]),
        pltpu.make_async_copy(w_ref.at[:, mine], w_mine_ref, sems.at[4]),
    ]
    for copy in copies:
        copy.start()
    total = total_ref[...] + jnp.dot(
        rows_ref[:, head:], w_tail_ref[...], preferred_element_type=F32
    )
    for copy in copies[:-1]:
        copy.wait()
    total += jnp.dot(rows_rest_ref[...], w_rest_ref[...], preferred_element_type=F32)
    theirs_ref[...] = (total * scale_here_ref[...]).astype(BF16)
    copies[-1].wait()


def project_mine(rows_ref, rows_rest_ref, w_mine_ref, scale_ref, after_ref, *refs, at, last):
    refs, (scale_here_ref, sems) = refs[:-2], refs[-2:]
    if last:
        cache_ref, queries_ref, out_ref, cache_here_ref, queries_here_ref = refs
    else:
        (out_ref,) = refs
    mine = channels(0, out_ref.shape[1])
    copies = [pltpu.make_async_copy(scale_ref.at[:, mine], scale_here_ref, sems.at[0])]
    if last:
        copies.append(pltpu.make_async_copy(queries_ref, queries_here_ref, sems.at[1]))
        copies.append(pltpu.make_async_copy(cache_ref, cache_here_ref, sems.at[2]))
    for copy in copies:
        copy.start()
    depth = rows_ref.shape[1]
    count = at.stop - at.start
    block = count // 2 if count % 32 == 0 else count
    for m in spans(range(0, count + 1, block)):
        there = slice(at.start + m.start, at.start + m.stop)
        total = jnp.dot(rows_ref[there, :], w_mine_ref[:depth, :], preferred_element_type=F32)
        total += jnp.dot(
            rows_rest_ref[there, :], w_mine_ref[depth:, :], preferred_element_type=F32
        )
        if m.start == 0:
            copies[0].wait()
        out_ref[m, :] = (total * scale_here_ref[...]).astype(BF16)
    for copy in copies[1:]:
        copy.wait()


def split_bf16(x):
    high = x.astype(BF16).astype(F32)
    middle = (x - high).astype(BF16).astype(F32)
    return high, middle, (x - high - middle).astype(BF16).astype(F32)


def request_slots(target_ref, span_ref, row_count, padded):
    sections, requests = target_ref.shape
    position = lax.axis_index("section")
    target = target_ref[pl.ds(position, 1), :].astype(F32)
    span = span_ref[pl.ds(position, 1), :].astype(F32)
    diagonal = iota((padded, requests), 0) == iota((padded, requests), 1)
    target_col = jnp.sum(jnp.where(diagonal, target, 0.0), axis=1, keepdims=True)
    span_col = jnp.sum(jnp.where(diagonal, span, 0.0), axis=1, keepdims=True)
    section_row = jnp.zeros_like(target)
    section_col = jnp.zeros_like(target_col)
    for s in range(1, sections):
        section_row = section_row + (target >= s * row_count).astype(F32)
        section_col = section_col + (target_col >= s * row_count).astype(F32)
    before = (section_row == section_col) & (
        iota((padded, requests), 1) < iota((padded, requests), 0)
    )
    rank_col = jnp.sum(before.astype(F32), axis=1, keepdims=True).astype(jnp.int32)
    real = iota((padded, 1), 0) < requests
    section_col = jnp.where(real, section_col.astype(jnp.int32), -1)
    return section_col, rank_col, span_col.astype(jnp.int32)


def prepare_arrived(
    target_ref, span_ref, kept_ref, got_ref, rows_ref, slot_of_ref, bias_ref, *, row_count
):
    sections, requests = target_ref.shape
    padded, prompt_rows = bias_ref.shape
    span_rows = prompt_rows // requests
    section_col, rank_col, span_col = request_slots(target_ref, span_ref, row_count, padded)
    block = section_col ^ lax.axis_index("section")
    slot = jnp.where(section_col >= 0, block * PITCH + rank_col, -1)
    slot_of_ref[...] = one_hot((padded, sections * PITCH), 1, slot)
    slot = jnp.where(section_col >= 0, block * CAP + rank_col, -1)
    rows_ref[...] = jnp.dot(
        one_hot((padded, sections * CAP), 1, slot),
        all_blocks(steps_of(sections), kept_ref, got_ref).astype(BF16),
        preferred_element_type=F32,
    ).astype(BF16)
    key = iota((padded, prompt_rows), 1) - iota((padded, prompt_rows), 0) * span_rows
    bias_ref[...] = jnp.where((key >= 0) & (key < span_col), 0.0, MASKED)


def attend_arrived(rows_ref, slot_of_ref, bias_ref, other_ref, *refs):
    mine_refs, (keep_ref, send_ref) = refs[:-2], refs[-2:]
    padded, prompt_rows = bias_ref.shape
    kv_heads = other_ref.shape[1] // (2 * HD)
    group = rows_ref.shape[1] // (kv_heads * HD)
    rows = rows_ref[...]
    slot_of = slot_of_ref[...]
    bias = bias_ref[...]
    mine = jnp.concatenate([ref[...] for ref in mine_refs], axis=0)
    kv = (mine[:prompt_rows].astype(F32) + other_ref[:prompt_rows, :].astype(F32)).astype(BF16)
    scores = []
    for h in range(kv_heads):
        stacked = jnp.concatenate(
            [rows[:, (h * group + i) * HD : (h * group + i + 1) * HD] for i in range(group)],
            axis=0,
        )
        keys = kv[:, h * 2 * HD : (h * 2 + 1) * HD]
        scores.append(
            lax.dot_general(
                stacked, keys, (((1,), (1,)), ((), ())), preferred_element_type=F32
            )
        )
    scores = [
        x.reshape(group, padded, prompt_rows) * LOG2_SCALE + bias[None] for x in scores
    ]
    largest = [jnp.max(x, axis=2, keepdims=True) for x in scores]
    weights = [jnp.exp2(x - y) for x, y in zip(scores, largest)]
    totals = [jnp.sum(x, axis=2, keepdims=True) for x in weights]
    lane = iota((padded, STATS), 1)
    lse = jnp.zeros((padded, STATS), F32)
    pieces = []
    for h in range(kv_heads):
        values = jnp.dot(
            weights[h].reshape(group * padded, prompt_rows).astype(BF16),
            kv[:, (h * 2 + 1) * HD : (h * 2 + 2) * HD],
            preferred_element_type=F32,
        ).reshape(group, padded, HD)
        values = values / totals[h]
        head_lse = largest[h] + jnp.log2(totals[h])
        for i in range(group):
            pieces.append(values[i])
            lse = jnp.where(lane == h * group + i, head_lse[i], lse)
    high, middle, low = split_bf16(lse)
    stats = high + pltpu.roll(middle, LSE_PITCH, 1) + pltpu.roll(low, 2 * LSE_PITCH, 1)
    result = jnp.concatenate(pieces + [stats], axis=1).astype(BF16)
    answers = lax.dot_general(slot_of, result, TRANSPOSED, preferred_element_type=F32)
    _, sent, kept = answer_steps_of(2 * keep_ref.shape[0])[0]
    for ref, blocks in ((send_ref, sent), (keep_ref, kept)):
        for i, k in enumerate(blocks):
            ref[i] = answers[k * PITCH : k * PITCH + CAP].astype(BF16)


def attend_cache(
    queries_ref,
    cache_ref,
    len_ref,
    mine_ref,
    other_ref,
    pick_ref,
    after_ref,
    out_ref,
    slot_out_ref,
    slot_lse_ref,
    *,
    rows_at,
):
    row_count, cache_rows, width = cache_ref.shape
    first_row, block_rows = rows_at.start, rows_at.stop - rows_at.start
    kv_heads = width // (2 * HD)
    group = queries_ref.shape[1] // (kv_heads * HD)
    unit = 8
    keys_of = unit * cache_rows
    queries = queries_ref[rows_at, :].astype(F32)
    own = sum(
        ref[pl.ds(ref.shape[0] - row_count + first_row, block_rows), :].astype(F32)
        for ref in (mine_ref, other_ref)
    )
    own = own.astype(BF16).astype(F32)
    key = iota((unit, keys_of), 1) - iota((unit, keys_of), 0) * cache_rows
    lengths = len_ref[...].astype(F32)
    lane = iota((unit, STATS), 1)
    ones = jnp.ones((keys_of, HD), BF16)
    units = range(block_rows // unit)

    def rows_of(u):
        return slice(first_row + u * unit, first_row + (u + 1) * unit)

    pairs = [(u, h) for u in units for h in range(kv_heads)]
    bias = []
    for u in units:
        row = iota((unit, row_count), 0) + (first_row + u * unit)
        length = jnp.sum(
            jnp.where(iota((unit, row_count), 1) == row, lengths, 0.0), axis=1, keepdims=True
        ).astype(jnp.int32)
        bias.append(jnp.where((key >= 0) & (key < length), 0.0, MASKED))
    q, scores, own_scores = [], [], []
    for u, h in pairs:
        at = slice(u * unit, (u + 1) * unit)
        q.append(
            jnp.stack(
                [
                    queries[at, (h * group + i) * HD : (h * group + i + 1) * HD]
                    for i in range(group)
                ],
                axis=0,
            )
        )
        keys = cache_ref[rows_of(u), :, h * 2 * HD : (h * 2 + 1) * HD].reshape(keys_of, HD)
        scores.append(
            lax.dot_general(
                q[-1].reshape(group * unit, HD).astype(BF16),
                keys,
                (((1,), (1,)), ((), ())),
                preferred_element_type=F32,
            ).reshape(group, unit, keys_of)
        )
    for n, (u, h) in enumerate(pairs):
        at = slice(u * unit, (u + 1) * unit)
        own_key = own[at, h * 2 * HD : (h * 2 + 1) * HD]
        own_scores.append(jnp.sum(q[n] * own_key[None], axis=2, keepdims=True) * LOG2_SCALE)
    scores = [scores[n] * LOG2_SCALE + bias[u][None] for n, (u, h) in enumerate(pairs)]
    largest = [
        jnp.maximum(jnp.max(x, axis=2, keepdims=True), y) for x, y in zip(scores, own_scores)
    ]
    weights = [jnp.exp2(x - y).astype(BF16) for x, y in zip(scores, largest)]
    own_weights = [jnp.exp2(x - y) for x, y in zip(own_scores, largest)]
    sums = []
    for n, (u, h) in enumerate(pairs):
        at = slice(u * unit, (u + 1) * unit)
        values = cache_ref[rows_of(u), :, (h * 2 + 1) * HD : (h * 2 + 2) * HD].reshape(keys_of, HD)
        sums.append(
            jnp.dot(
                weights[n].reshape(group * unit, keys_of),
                jnp.concatenate([values, ones], axis=1),
                preferred_element_type=F32,
            ).reshape(group, unit, 2 * HD)
        )
    pieces = [[] for _ in units]
    stats = [jnp.zeros((unit, STATS), F32) for _ in units]
    for n, (u, h) in enumerate(pairs):
        at = slice(u * unit, (u + 1) * unit)
        own_value = own[at, (h * 2 + 1) * HD : (h * 2 + 2) * HD]
        total = sums[n][:, :, HD:] + own_weights[n]
        result = (sums[n][:, :, :HD] + own_weights[n] * own_value[None]) / total
        lse = largest[n] + jnp.log2(total)
        for i in range(group):
            pieces[u].append(result[i])
            stats[u] = jnp.where(lane == h * group + i, lse[i], stats[u])
    out = jnp.concatenate([jnp.concatenate(x, axis=1) for x in pieces], axis=0).astype(BF16)
    out_ref[...] = out
    here = iota((row_count, block_rows), 0) == iota((row_count, block_rows), 1) + first_row
    pick = jnp.dot(
        pick_ref[...], here.astype(F32).astype(BF16), preferred_element_type=F32
    ).astype(BF16)
    slot_out_ref[...] = jnp.dot(pick, out, preferred_element_type=F32)
    lse = jnp.concatenate(stats, axis=0)
    slot_lse_ref[...] = sum(
        jnp.dot(pick, part.astype(BF16), preferred_element_type=F32) for part in split_bf16(lse)
    )


def merge(pick_ref, *refs):
    parts, group_refs, out_ref = refs[:-5], refs[-5:-1], refs[-1]
    cached_refs, slot_out_refs, slot_lse_refs = parts[0::3], parts[1::3], parts[2::3]
    width = out_ref.shape[1]
    pick = pick_ref[...]
    arrived = jnp.concatenate(
        [ref[i].astype(F32) for ref in group_refs for i in range(ref.shape[0])], axis=0
    )
    stats = arrived[:, width:]
    arrived_lse = (
        stats
        + pltpu.roll(stats, STATS - LSE_PITCH, 1)
        + pltpu.roll(stats, STATS - 2 * LSE_PITCH, 1)
    )
    cached_lse = sum(ref[...] for ref in slot_lse_refs)
    largest = jnp.maximum(cached_lse, arrived_lse)
    cached_weight = jnp.exp2(cached_lse - largest)
    arrived_weight = jnp.exp2(arrived_lse - largest)
    total = cached_weight + arrived_weight
    cached_weight = cached_weight / total
    arrived_weight = arrived_weight / total
    has = lax.dot_general(
        pick, jnp.ones((pick.shape[0], HD), BF16), TRANSPOSED, preferred_element_type=F32
    )
    for i in range(width // HD):
        at = slice(i * HD, (i + 1) * HD)
        merged = (
            sum(ref[:, at] for ref in slot_out_refs) * cached_weight[:, i : i + 1]
            + arrived[:, at] * arrived_weight[:, i : i + 1]
        )
        placed = lax.dot_general(
            pick, merged.astype(BF16), TRANSPOSED, preferred_element_type=F32
        )
        row = 0
        for ref in cached_refs:
            rows = slice(row, row + ref.shape[0])
            kept = ref[:, at].astype(F32)
            out_ref[rows, at] = jnp.where(has[rows] > 0.5, placed[rows], kept).astype(BF16)
            row += ref.shape[0]


def compiler_params(megabytes):
    return pltpu.CompilerParams(vmem_limit_bytes=megabytes * 1024 * 1024)


RESIDENT = pl.BlockSpec(memory_space=pltpu.VMEM)
REMAINS = pl.BlockSpec(memory_space=pl.ANY)


def in_vmem(x):
    return pltpu.with_memory_space_constraint(x, pltpu.VMEM)


def in_hbm(x):
    return pltpu.with_memory_space_constraint(x, pltpu.HBM)


def shards(
    prompts, decode_hidden, queries, kv_cache, cache_len, span_len, target_row, w_kv, kv_scale
):
    row_count = decode_hidden.shape[0]
    prompt_rows, features = prompts.shape
    sections = lax.axis_size("section")
    local_width = kv_cache.shape[2]
    query_width = queries.shape[1]
    slots = sections * CAP
    all_rows = prompt_rows + row_count
    scale = kv_scale.reshape(1, -1)
    lengths = cache_len.reshape(1, -1)

    steps = steps_of(sections)
    half = sections // 2
    prompts, decode_hidden, w_kv, scale = map(in_hbm, (prompts, decode_hidden, w_kv, scale))
    target_row, span_len, queries = map(in_hbm, (target_row, span_len, queries))
    kv_cache, lengths = map(in_hbm, (kv_cache, lengths))

    def block_pair(width):
        return [pltpu.VMEM((half, CAP, width), BF16)] * 2

    def swapped(blocks, distance):
        pairs = [(i, i ^ distance) for i in range(sections)]
        return in_vmem(lax.ppermute(blocks, "section", pairs))

    pick, keep, send = pl.pallas_call(
        select_queries,
        in_specs=[RESIDENT, RESIDENT],
        out_specs=[RESIDENT] * 3,
        out_shape=[pltpu.VMEM((slots, row_count), BF16)] + block_pair(query_width),
        compiler_params=compiler_params(16),
        name="select_queries",
    )(target_row, queries)
    got = swapped(send, steps[0][0])

    def regrouped(blocks, got, steps, done, after):
        return pl.pallas_call(
            functools.partial(regroup, steps=steps, done=done),
            in_specs=[RESIDENT] * 2 + [REMAINS],
            out_specs=[RESIDENT] * 2,
            out_shape=block_pair(blocks.shape[2]),
            compiler_params=compiler_params(16),
            name="regroup",
        )(in_vmem(blocks), got, in_vmem(after))

    edges = (0, 256, 768, 1536, 2560, 4096)
    depth, head = edges[-1], edges[-2]
    rows, w_tail, total = pl.pallas_call(
        functools.partial(project_first, edges=edges),
        in_specs=[REMAINS] * 3,
        out_specs=[RESIDENT] * 3,
        out_shape=[
            pltpu.VMEM((all_rows, depth), BF16),
            pltpu.VMEM((depth - head, local_width), BF16),
            pltpu.VMEM((all_rows, local_width), F32),
        ],
        scratch_shapes=[
            pltpu.VMEM((head, local_width), BF16),
            pltpu.SemaphoreType.DMA((len(edges) - 1, 3)),
        ],
        compiler_params=compiler_params(12),
        name="project_first",
    )(prompts, decode_hidden, w_kv)
    keep, send = regrouped(keep, got, steps, 1, total)
    got = swapped(send, steps[1][0])
    theirs, rows_rest, w_mine = pl.pallas_call(
        project_rest,
        in_specs=[REMAINS] * 4 + [RESIDENT] * 3 + [REMAINS],
        out_specs=[RESIDENT] * 3,
        out_shape=[
            pltpu.VMEM((all_rows, local_width), BF16),
            pltpu.VMEM((all_rows, features - depth), BF16),
            pltpu.VMEM((features, local_width), BF16),
        ],
        scratch_shapes=[
            pltpu.VMEM((features - depth, local_width), BF16),
            pltpu.VMEM((1, local_width), F32),
            pltpu.SemaphoreType.DMA((5,)),
        ],
        compiler_params=compiler_params(16),
        name="project_rest",
    )(prompts, decode_hidden, w_kv, scale, *map(in_vmem, (rows, w_tail, total, keep)))
    theirs, got = lax.optimization_barrier((theirs, got))
    got = in_vmem(got)
    other = in_vmem(lax.ppermute(theirs, "tp", [(0, 1), (1, 0)]))

    mine = []
    pieces = max(len(steps) - 2, 1)
    bounds = [all_rows * i // (16 * pieces) * 16 for i in range(pieces)] + [all_rows]
    after = theirs
    for piece, at in enumerate(spans(bounds)):
        if piece + 2 < len(steps):
            keep, send = regrouped(keep, got, steps, piece + 2, after)
            got = swapped(send, steps[piece + 2][0])
        last = piece == pieces - 1
        extra = [kv_cache, queries] if last else []
        part, *here = pl.pallas_call(
            functools.partial(project_mine, at=at, last=last),
            in_specs=[RESIDENT] * 3 + [REMAINS] * (2 + len(extra)),
            out_specs=[RESIDENT] * (1 + len(extra)),
            out_shape=[pltpu.VMEM((at.stop - at.start, local_width), BF16)]
            + [pltpu.VMEM(x.shape, BF16) for x in extra],
            scratch_shapes=[pltpu.VMEM((1, local_width), F32), pltpu.SemaphoreType.DMA((3,))],
            compiler_params=compiler_params(16),
            name="project_mine",
        )(*map(in_vmem, (rows, rows_rest, w_mine)), scale, in_vmem(keep), *extra)
        after = part
        mine.append(in_vmem(part))
    kv_here, queries_here = map(in_vmem, here)

    padded = -(-span_len.shape[1] // 16) * 16
    prepared = pl.pallas_call(
        functools.partial(prepare_arrived, row_count=row_count),
        in_specs=[RESIDENT] * 4,
        out_specs=[RESIDENT] * 3,
        out_shape=[
            pltpu.VMEM((padded, query_width), BF16),
            pltpu.VMEM((padded, sections * PITCH), BF16),
            pltpu.VMEM((padded, prompt_rows), F32),
        ],
        compiler_params=compiler_params(16),
        name="prepare_arrived",
    )(target_row, span_len, in_vmem(keep), got)
    answer_width = query_width + STATS
    keep, send = pl.pallas_call(
        attend_arrived,
        in_specs=[RESIDENT] * (4 + len(mine)),
        out_specs=[RESIDENT] * 2,
        out_shape=block_pair(answer_width),
        compiler_params=compiler_params(24),
        name="attend_arrived",
    )(*map(in_vmem, prepared), other, *mine)

    steps = answer_steps_of(sections)
    shares = []
    calls = len(steps) + 1
    bounds = [row_count * i // (16 * calls) * 16 for i in range(calls)] + [row_count]
    for done, at in enumerate(spans(bounds)):
        last = done == len(steps)
        if not last:
            got = swapped(send, steps[done][0])
        share = pl.pallas_call(
            functools.partial(attend_cache, rows_at=at),
            in_specs=[RESIDENT] * 6 + [REMAINS],
            out_specs=[RESIDENT] * 3,
            out_shape=[
                pltpu.VMEM((at.stop - at.start, query_width), BF16),
                pltpu.VMEM((slots, query_width), F32),
                pltpu.VMEM((slots, STATS), F32),
            ],
            compiler_params=compiler_params(24),
            name="attend_cache",
        )(queries_here, kv_here, lengths, mine[-1], other, in_vmem(pick), in_vmem(keep))
        shares += share
        if done + 1 < len(steps):
            keep, send = regrouped(keep, got, steps, done + 1, share[2])
        elif not last:
            size = sections // 4
            keep, *sent = pl.pallas_call(
                functools.partial(fan_out, step=steps[-1]),
                in_specs=[RESIDENT] * 2 + [REMAINS],
                out_specs=[RESIDENT] * 4,
                out_shape=[pltpu.VMEM((size, CAP, answer_width), BF16)] * 4,
                compiler_params=compiler_params(16),
                name="fan_out",
            )(in_vmem(keep), got, in_vmem(share[2]))
            groups = [in_vmem(keep)]
            groups += [swapped(blocks, (i + 1) * size) for i, blocks in enumerate(sent)]

    return pl.pallas_call(
        merge,
        in_specs=[RESIDENT] * (5 + len(shares)),
        out_specs=RESIDENT,
        out_shape=jax.ShapeDtypeStruct((row_count, query_width), BF16),
        compiler_params=compiler_params(24),
        name="merge",
    )(*map(in_vmem, (pick, *shares)), *groups)


def solution(mesh):
    in_specs = (
        P(("groups", "section"), "tp"),
        P(("groups", "section"), "tp"),
        P(("groups", "section"), "tp"),
        P(("groups", "section"), None, "tp"),
        P(("groups", "section")),
        P("groups", None),
        P("groups", None),
        P("tp", None),
        P(),
    )
    out_specs = P(("groups", "section"), "tp")
    return jax.shard_map(shards, mesh=mesh, in_specs=in_specs, out_specs=out_specs, check_vma=False)
```

```python
import functools
import math

import jax
import jax.numpy as jnp
from jax import lax
from jax.experimental import pallas as pl
from jax.experimental.pallas import tpu as pltpu
from jax.sharding import PartitionSpec as P

HD = 128
CAP = 2
STATS = 128
MASKED = -1e30
LSE_PITCH = 40
PITCH = 8
LOG2_SCALE = HD ** (-0.5) * math.log2(math.e)
F32 = jnp.float32
BF16 = jnp.bfloat16
TRANSPOSED = (((0,), (0,)), ((), ()))


def iota(shape, dim):
    return lax.broadcasted_iota(jnp.int32, shape, dim)


def one_hot(shape, dim, index):
    return (iota(shape, dim) == index).astype(F32).astype(BF16)


def pick_rows(target_ref, row_count):
    sections, requests = target_ref.shape
    shape = (sections * CAP, requests)
    position = lax.axis_index("section")
    slot_id = iota(shape, 0)
    table = jnp.zeros(shape, jnp.int32)
    for k in range(sections):
        mine = (slot_id >= k * CAP) & (slot_id < (k + 1) * CAP)
        table = jnp.where(mine, target_ref[pl.ds(position ^ k, 1), :], table)
    local = table - position * row_count
    here = (local >= 0) & (local < row_count)
    square = (requests, requests)
    earlier = jnp.dot(
        here.astype(F32).astype(BF16),
        (iota(square, 0) < iota(square, 1)).astype(F32).astype(BF16),
        preferred_element_type=F32,
    )
    chosen = here & (earlier == lax.rem(slot_id, CAP).astype(F32))
    row = jnp.max(jnp.where(chosen, local.astype(F32), -1.0), axis=1, keepdims=True)
    return one_hot((shape[0], row_count), 1, row.astype(jnp.int32))


def steps_of(sections):
    steps = []
    bit = sections // 2
    while bit:
        sent = [k for k in range(sections) if k & bit]
        steps.append((bit, sent, [k for k in range(sections) if not k & bit]))
        bit //= 2
    return steps


def answer_steps_of(sections):
    steps = []
    bit = 1
    while 4 * bit < sections:
        sent = [k for k in range(sections) if k & bit]
        steps.append((bit, sent, [k for k in range(sections) if not k & bit]))
        bit *= 2
    return steps


def rearrange(step, kept_ref, got_ref, *out):
    where = {k: (got_ref, i) for i, k in enumerate(step[1])}
    where |= {k: (kept_ref, i) for i, k in enumerate(step[2])}
    for out_ref, blocks in out:
        for i, k in enumerate(blocks):
            ref, at = where[k]
            out_ref[i] = ref[at]


def regroup(kept_ref, got_ref, after_ref, keep_ref, send_ref, *, steps, done):
    _, sent, kept = steps[done]
    rearrange(steps[done - 1], kept_ref, got_ref, (send_ref, sent), (keep_ref, kept))


def fan_out(kept_ref, got_ref, after_ref, *out_refs, step):
    size = out_refs[0].shape[0]
    groups = [range(m * size, (m + 1) * size) for m in range(len(out_refs))]
    rearrange(step, kept_ref, got_ref, *zip(out_refs, groups))


def all_blocks(steps, kept_ref, got_ref):
    where = {k: got_ref[i] for i, k in enumerate(steps[-1][1])}
    where |= {k: kept_ref[i] for i, k in enumerate(steps[-1][2])}
    return jnp.concatenate([where[k].astype(F32) for k in range(len(where))], axis=0)


def select_queries(target_ref, queries_ref, pick_ref, keep_ref, send_ref):
    _, sent, kept = steps_of(target_ref.shape[0])[0]
    pick = pick_rows(target_ref, queries_ref.shape[0])
    pick_ref[...] = pick
    asked = jnp.dot(pick, queries_ref[...], preferred_element_type=F32)
    for ref, blocks in ((send_ref, sent), (keep_ref, kept)):
        for i, k in enumerate(blocks):
            ref[i] = asked[k * CAP : (k + 1) * CAP].astype(BF16)


def spans(edges):
    return [slice(a, b) for a, b in zip(edges[:-1], edges[1:])]


def load_rows(prompts_ref, hidden_ref, there, rows_ref, here, sems):
    prompt_rows = prompts_ref.shape[0]
    return [
        pltpu.make_async_copy(
            prompts_ref.at[:, there], rows_ref.at[:prompt_rows, here], sems.at[0]
        ),
        pltpu.make_async_copy(
            hidden_ref.at[:, there], rows_ref.at[prompt_rows:, here], sems.at[1]
        ),
    ]


def channels(offset, width):
    tp = lax.axis_index("tp")
    return pl.ds(pl.multiple_of(((tp + offset) & 1) * width, width), width)


def project_first(
    prompts_ref,
    hidden_ref,
    w_ref,
    target_ref,
    span_ref,
    len_ref,
    rows_ref,
    w_tail_ref,
    total_ref,
    target_here_ref,
    span_here_ref,
    len_here_ref,
    w_head_ref,
    sems,
    small_sems,
    *,
    edges,
):
    theirs = channels(1, total_ref.shape[1])
    chunks = spans(edges)
    head = edges[-2]
    waits = []
    for c, at in enumerate(chunks):
        here = at if at.stop <= head else slice(0, at.stop - head)
        w_here_ref = w_head_ref if at.stop <= head else w_tail_ref
        copies = load_rows(prompts_ref, hidden_ref, at, rows_ref, at, sems.at[c])
        copies.append(
            pltpu.make_async_copy(w_ref.at[at, theirs], w_here_ref.at[here, :], sems.at[c, 2])
        )
        for copy in copies:
            copy.start()
        waits.append(copies)
    small = [
        pltpu.make_async_copy(target_ref, target_here_ref, small_sems.at[0]),
        pltpu.make_async_copy(span_ref, span_here_ref, small_sems.at[1]),
        pltpu.make_async_copy(len_ref, len_here_ref, small_sems.at[2]),
    ]
    for copy in small:
        copy.start()
    for c, at in enumerate(chunks):
        for copy in waits[c]:
            copy.wait()
        if at.stop <= head:
            part = jnp.dot(rows_ref[:, at], w_head_ref[at, :], preferred_element_type=F32)
            if c == 0:
                total_ref[...] = part
            else:
                total_ref[...] += part
    for copy in small:
        copy.wait()


def project_rest(
    prompts_ref,
    hidden_ref,
    w_ref,
    scale_ref,
    rows_ref,
    w_tail_ref,
    total_ref,
    after_ref,
    theirs_ref,
    rows_rest_ref,
    w_mine_ref,
    w_rest_ref,
    scale_here_ref,
    sems,
):
    width = theirs_ref.shape[1]
    theirs, mine = channels(1, width), channels(0, width)
    depth = rows_ref.shape[1]
    head = depth - w_tail_ref.shape[0]
    rest = slice(depth, depth + rows_rest_ref.shape[1])
    copies = load_rows(prompts_ref, hidden_ref, rest, rows_rest_ref, slice(None), sems)
    copies += [
        pltpu.make_async_copy(w_ref.at[rest, theirs], w_rest_ref, sems.at[2]),
        pltpu.make_async_copy(scale_ref.at[:, theirs], scale_here_ref, sems.at[3]),
        pltpu.make_async_copy(w_ref.at[:depth, mine], w_mine_ref, sems.at[4]),
    ]
    for copy in copies:
        copy.start()
    total = total_ref[...] + jnp.dot(
        rows_ref[:, head:], w_tail_ref[...], preferred_element_type=F32
    )
    for copy in copies[:-1]:
        copy.wait()
    total += jnp.dot(rows_rest_ref[...], w_rest_ref[...], preferred_element_type=F32)
    theirs_ref[...] = (total * scale_here_ref[...]).astype(BF16)
    copies[-1].wait()


def project_mine(
    rows_ref, rows_rest_ref, w_mine_ref, w_ref, scale_ref, after_ref, *refs, at, last, row_count
):
    refs, (w_rest_ref, scale_here_ref, sems) = refs[:-3], refs[-3:]
    if last:
        cache_ref, queries_ref, target_ref, span_ref = refs[:4]
        out_ref, cache_here_ref, queries_here_ref, *table_refs = refs[4:]
    else:
        (out_ref,) = refs
    mine = channels(0, out_ref.shape[1])
    depth = rows_ref.shape[1]
    rest = pl.ds(depth, w_rest_ref.shape[0])
    copies = [
        pltpu.make_async_copy(w_ref.at[rest, mine], w_rest_ref, sems.at[0]),
        pltpu.make_async_copy(scale_ref.at[:, mine], scale_here_ref, sems.at[1]),
    ]
    if last:
        copies.append(pltpu.make_async_copy(queries_ref, queries_here_ref, sems.at[2]))
        copies.append(pltpu.make_async_copy(cache_ref, cache_here_ref, sems.at[3]))
    for copy in copies:
        copy.start()
    if last:
        arrived_tables(target_ref, span_ref, *table_refs, row_count=row_count)
    count = at.stop - at.start
    block = count // 2 if count % 32 == 0 else count
    for m in spans(range(0, count + 1, block)):
        there = slice(at.start + m.start, at.start + m.stop)
        total = jnp.dot(rows_ref[there, :], w_mine_ref[...], preferred_element_type=F32)
        if m.start == 0:
            copies[0].wait()
            copies[1].wait()
        total += jnp.dot(rows_rest_ref[there, :], w_rest_ref[...], preferred_element_type=F32)
        out_ref[m, :] = (total * scale_here_ref[...]).astype(BF16)
    for copy in copies[2:]:
        copy.wait()


def split_bf16(x):
    high = x.astype(BF16).astype(F32)
    middle = (x - high).astype(BF16).astype(F32)
    return high, middle, (x - high - middle).astype(BF16).astype(F32)


def request_slots(target_ref, span_ref, row_count, padded):
    sections, requests = target_ref.shape
    position = lax.axis_index("section")
    target = target_ref[pl.ds(position, 1), :].astype(F32)
    span = span_ref[pl.ds(position, 1), :].astype(F32)
    diagonal = iota((padded, requests), 0) == iota((padded, requests), 1)
    target_col = jnp.sum(jnp.where(diagonal, target, 0.0), axis=1, keepdims=True)
    span_col = jnp.sum(jnp.where(diagonal, span, 0.0), axis=1, keepdims=True)
    section_row = jnp.zeros_like(target)
    section_col = jnp.zeros_like(target_col)
    for s in range(1, sections):
        section_row = section_row + (target >= s * row_count).astype(F32)
        section_col = section_col + (target_col >= s * row_count).astype(F32)
    before = (section_row == section_col) & (
        iota((padded, requests), 1) < iota((padded, requests), 0)
    )
    rank_col = jnp.sum(before.astype(F32), axis=1, keepdims=True).astype(jnp.int32)
    real = iota((padded, 1), 0) < requests
    section_col = jnp.where(real, section_col.astype(jnp.int32), -1)
    return section_col, rank_col, span_col.astype(jnp.int32)


def arrived_tables(target_ref, span_ref, from_slot_ref, slot_of_ref, bias_ref, *, row_count):
    sections, requests = target_ref.shape
    padded, prompt_rows = bias_ref.shape
    span_rows = prompt_rows // requests
    section_col, rank_col, span_col = request_slots(target_ref, span_ref, row_count, padded)
    block = section_col ^ lax.axis_index("section")
    slot = jnp.where(section_col >= 0, block * PITCH + rank_col, -1)
    slot_of_ref[...] = one_hot(slot_of_ref.shape, 1, slot)
    slot = jnp.where(section_col >= 0, block * CAP + rank_col, -1)
    from_slot_ref[...] = one_hot(from_slot_ref.shape, 1, slot)
    key = iota((padded, prompt_rows), 1) - iota((padded, prompt_rows), 0) * span_rows
    bias_ref[...] = jnp.where((key >= 0) & (key < span_col), 0.0, MASKED)


def attend_arrived(from_slot_ref, slot_of_ref, bias_ref, kept_ref, got_ref, other_ref, *refs):
    mine_refs, (keep_ref, send_ref) = refs[:-2], refs[-2:]
    padded, prompt_rows = bias_ref.shape
    kv_heads = other_ref.shape[1] // (2 * HD)
    group = kept_ref.shape[2] // (kv_heads * HD)
    asked = all_blocks(steps_of(2 * kept_ref.shape[0]), kept_ref, got_ref).astype(BF16)
    rows = jnp.dot(from_slot_ref[...], asked, preferred_element_type=F32).astype(BF16)
    slot_of = slot_of_ref[...]
    bias = bias_ref[...]
    mine = jnp.concatenate([ref[...] for ref in mine_refs], axis=0)
    kv = (mine[:prompt_rows].astype(F32) + other_ref[:prompt_rows, :].astype(F32)).astype(BF16)
    scores = []
    for h in range(kv_heads):
        stacked = jnp.concatenate(
            [rows[:, (h * group + i) * HD : (h * group + i + 1) * HD] for i in range(group)],
            axis=0,
        )
        keys = kv[:, h * 2 * HD : (h * 2 + 1) * HD]
        scores.append(
            lax.dot_general(
                stacked, keys, (((1,), (1,)), ((), ())), preferred_element_type=F32
            )
        )
    scores = [
        x.reshape(group, padded, prompt_rows) * LOG2_SCALE + bias[None] for x in scores
    ]
    largest = [jnp.max(x, axis=2, keepdims=True) for x in scores]
    weights = [jnp.exp2(x - y) for x, y in zip(scores, largest)]
    totals = [jnp.sum(x, axis=2, keepdims=True) for x in weights]
    lane = iota((padded, STATS), 1)
    lse = jnp.zeros((padded, STATS), F32)
    pieces = []
    for h in range(kv_heads):
        values = jnp.dot(
            weights[h].reshape(group * padded, prompt_rows).astype(BF16),
            kv[:, (h * 2 + 1) * HD : (h * 2 + 2) * HD],
            preferred_element_type=F32,
        ).reshape(group, padded, HD)
        values = values / totals[h]
        head_lse = largest[h] + jnp.log2(totals[h])
        for i in range(group):
            pieces.append(values[i])
            lse = jnp.where(lane == h * group + i, head_lse[i], lse)
    high, middle, low = split_bf16(lse)
    stats = high + pltpu.roll(middle, LSE_PITCH, 1) + pltpu.roll(low, 2 * LSE_PITCH, 1)
    result = jnp.concatenate(pieces + [stats], axis=1).astype(BF16)
    answers = lax.dot_general(slot_of, result, TRANSPOSED, preferred_element_type=F32)
    _, sent, kept = answer_steps_of(2 * keep_ref.shape[0])[0]
    for ref, blocks in ((send_ref, sent), (keep_ref, kept)):
        for i, k in enumerate(blocks):
            ref[i] = answers[k * PITCH : k * PITCH + CAP].astype(BF16)


def attend_cache(
    queries_ref,
    cache_ref,
    len_ref,
    mine_ref,
    other_ref,
    pick_ref,
    after_ref,
    out_ref,
    slot_out_ref,
    slot_lse_ref,
    *,
    rows_at,
):
    row_count, cache_rows, width = cache_ref.shape
    first_row, block_rows = rows_at.start, rows_at.stop - rows_at.start
    kv_heads = width // (2 * HD)
    group = queries_ref.shape[1] // (kv_heads * HD)
    unit = 8
    keys_of = unit * cache_rows
    queries = queries_ref[rows_at, :].astype(F32)
    own = sum(
        ref[pl.ds(ref.shape[0] - row_count + first_row, block_rows), :].astype(F32)
        for ref in (mine_ref, other_ref)
    )
    own = own.astype(BF16).astype(F32)
    key = iota((unit, keys_of), 1) - iota((unit, keys_of), 0) * cache_rows
    lengths = len_ref[...].astype(F32)
    lane = iota((unit, STATS), 1)
    ones = jnp.ones((keys_of, HD), BF16)
    units = range(block_rows // unit)

    def rows_of(u):
        return slice(first_row + u * unit, first_row + (u + 1) * unit)

    pairs = [(u, h) for u in units for h in range(kv_heads)]
    bias = []
    for u in units:
        row = iota((unit, row_count), 0) + (first_row + u * unit)
        length = jnp.sum(
            jnp.where(iota((unit, row_count), 1) == row, lengths, 0.0), axis=1, keepdims=True
        ).astype(jnp.int32)
        bias.append(jnp.where((key >= 0) & (key < length), 0.0, MASKED))
    q, scores, own_scores = [], [], []
    for u, h in pairs:
        at = slice(u * unit, (u + 1) * unit)
        q.append(
            jnp.stack(
                [
                    queries[at, (h * group + i) * HD : (h * group + i + 1) * HD]
                    for i in range(group)
                ],
                axis=0,
            )
        )
        keys = cache_ref[rows_of(u), :, h * 2 * HD : (h * 2 + 1) * HD].reshape(keys_of, HD)
        scores.append(
            lax.dot_general(
                q[-1].reshape(group * unit, HD).astype(BF16),
                keys,
                (((1,), (1,)), ((), ())),
                preferred_element_type=F32,
            ).reshape(group, unit, keys_of)
        )
    for n, (u, h) in enumerate(pairs):
        at = slice(u * unit, (u + 1) * unit)
        own_key = own[at, h * 2 * HD : (h * 2 + 1) * HD]
        own_scores.append(jnp.sum(q[n] * own_key[None], axis=2, keepdims=True) * LOG2_SCALE)
    scores = [scores[n] * LOG2_SCALE + bias[u][None] for n, (u, h) in enumerate(pairs)]
    largest = [
        jnp.maximum(jnp.max(x, axis=2, keepdims=True), y) for x, y in zip(scores, own_scores)
    ]
    weights = [jnp.exp2(x - y).astype(BF16) for x, y in zip(scores, largest)]
    own_weights = [jnp.exp2(x - y) for x, y in zip(own_scores, largest)]
    sums = []
    for n, (u, h) in enumerate(pairs):
        at = slice(u * unit, (u + 1) * unit)
        values = cache_ref[rows_of(u), :, (h * 2 + 1) * HD : (h * 2 + 2) * HD].reshape(keys_of, HD)
        sums.append(
            jnp.dot(
                weights[n].reshape(group * unit, keys_of),
                jnp.concatenate([values, ones], axis=1),
                preferred_element_type=F32,
            ).reshape(group, unit, 2 * HD)
        )
    pieces = [[] for _ in units]
    stats = [jnp.zeros((unit, STATS), F32) for _ in units]
    for n, (u, h) in enumerate(pairs):
        at = slice(u * unit, (u + 1) * unit)
        own_value = own[at, (h * 2 + 1) * HD : (h * 2 + 2) * HD]
        total = sums[n][:, :, HD:] + own_weights[n]
        result = (sums[n][:, :, :HD] + own_weights[n] * own_value[None]) / total
        lse = largest[n] + jnp.log2(total)
        for i in range(group):
            pieces[u].append(result[i])
            stats[u] = jnp.where(lane == h * group + i, lse[i], stats[u])
    out = jnp.concatenate([jnp.concatenate(x, axis=1) for x in pieces], axis=0).astype(BF16)
    out_ref[...] = out
    here = iota((row_count, block_rows), 0) == iota((row_count, block_rows), 1) + first_row
    pick = jnp.dot(
        pick_ref[...], here.astype(F32).astype(BF16), preferred_element_type=F32
    ).astype(BF16)
    slot_out_ref[...] = jnp.dot(pick, out, preferred_element_type=F32)
    lse = jnp.concatenate(stats, axis=0)
    slot_lse_ref[...] = sum(
        jnp.dot(pick, part.astype(BF16), preferred_element_type=F32) for part in split_bf16(lse)
    )


def merge(pick_ref, *refs):
    refs, (out_ref, out_here_ref, sems) = refs[:-3], refs[-3:]
    parts, group_refs = refs[:-4], refs[-4:]
    cached_refs, slot_out_refs, slot_lse_refs = parts[0::3], parts[1::3], parts[2::3]
    width = out_ref.shape[1]
    pick = pick_ref[...]
    arrived = jnp.concatenate(
        [ref[i].astype(F32) for ref in group_refs for i in range(ref.shape[0])], axis=0
    )
    stats = arrived[:, width:]
    arrived_lse = (
        stats
        + pltpu.roll(stats, STATS - LSE_PITCH, 1)
        + pltpu.roll(stats, STATS - 2 * LSE_PITCH, 1)
    )
    cached_lse = sum(ref[...] for ref in slot_lse_refs)
    largest = jnp.maximum(cached_lse, arrived_lse)
    cached_weight = jnp.exp2(cached_lse - largest)
    arrived_weight = jnp.exp2(arrived_lse - largest)
    total = cached_weight + arrived_weight
    cached_weight = cached_weight / total
    arrived_weight = arrived_weight / total
    has = lax.dot_general(
        pick, jnp.ones((pick.shape[0], HD), BF16), TRANSPOSED, preferred_element_type=F32
    )
    copies = []
    for i in range(width // HD):
        at = slice(i * HD, (i + 1) * HD)
        merged = (
            sum(ref[:, at] for ref in slot_out_refs) * cached_weight[:, i : i + 1]
            + arrived[:, at] * arrived_weight[:, i : i + 1]
        )
        placed = lax.dot_general(
            pick, merged.astype(BF16), TRANSPOSED, preferred_element_type=F32
        )
        row = 0
        for ref in cached_refs:
            rows = slice(row, row + ref.shape[0])
            kept = ref[:, at].astype(F32)
            out_here_ref[rows, at] = jnp.where(has[rows] > 0.5, placed[rows], kept).astype(BF16)
            row += ref.shape[0]
        ready = width * (len(copies) + 1) // sems.shape[0]
        if at.stop == ready:
            there = slice(width * len(copies) // sems.shape[0], ready)
            copies.append(
                pltpu.make_async_copy(
                    out_here_ref.at[:, there], out_ref.at[:, there], sems.at[len(copies)]
                )
            )
            copies[-1].start()
    for copy in copies:
        copy.wait()


def compiler_params(megabytes):
    return pltpu.CompilerParams(vmem_limit_bytes=megabytes * 1024 * 1024)


RESIDENT = pl.BlockSpec(memory_space=pltpu.VMEM)
REMAINS = pl.BlockSpec(memory_space=pl.ANY)


def in_vmem(x):
    return pltpu.with_memory_space_constraint(x, pltpu.VMEM)


def in_hbm(x):
    return pltpu.with_memory_space_constraint(x, pltpu.HBM)


def shards(
    prompts, decode_hidden, queries, kv_cache, cache_len, span_len, target_row, w_kv, kv_scale
):
    row_count = decode_hidden.shape[0]
    prompt_rows, features = prompts.shape
    sections = lax.axis_size("section")
    local_width = kv_cache.shape[2]
    query_width = queries.shape[1]
    slots = sections * CAP
    all_rows = prompt_rows + row_count
    scale = kv_scale.reshape(1, -1)
    lengths = cache_len.reshape(1, -1)

    steps = steps_of(sections)
    half = sections // 2
    prompts, decode_hidden, w_kv, scale = map(in_hbm, (prompts, decode_hidden, w_kv, scale))
    target_row, span_len, queries = map(in_hbm, (target_row, span_len, queries))
    kv_cache, lengths = map(in_hbm, (kv_cache, lengths))

    def block_pair(width):
        return [pltpu.VMEM((half, CAP, width), BF16)] * 2

    def swapped(blocks, distance):
        pairs = [(i, i ^ distance) for i in range(sections)]
        return in_vmem(lax.ppermute(blocks, "section", pairs))

    pick, keep, send = pl.pallas_call(
        select_queries,
        in_specs=[RESIDENT, RESIDENT],
        out_specs=[RESIDENT] * 3,
        out_shape=[pltpu.VMEM((slots, row_count), BF16)] + block_pair(query_width),
        compiler_params=compiler_params(16),
        name="select_queries",
    )(target_row, queries)
    got = swapped(send, steps[0][0])

    def regrouped(blocks, got, steps, done, after):
        return pl.pallas_call(
            functools.partial(regroup, steps=steps, done=done),
            in_specs=[RESIDENT] * 2 + [REMAINS],
            out_specs=[RESIDENT] * 2,
            out_shape=block_pair(blocks.shape[2]),
            compiler_params=compiler_params(16),
            name="regroup",
        )(in_vmem(blocks), got, in_vmem(after))

    edges = (0, 256, 768, 1536, 2560, 3584)
    depth, head = edges[-1], edges[-2]
    rows, w_tail, total, target_here, span_here, lengths = pl.pallas_call(
        functools.partial(project_first, edges=edges),
        in_specs=[REMAINS] * 6,
        out_specs=[RESIDENT] * 6,
        out_shape=[
            pltpu.VMEM((all_rows, depth), BF16),
            pltpu.VMEM((depth - head, local_width), BF16),
            pltpu.VMEM((all_rows, local_width), F32),
            pltpu.VMEM(target_row.shape, jnp.int32),
            pltpu.VMEM(span_len.shape, jnp.int32),
            pltpu.VMEM(lengths.shape, jnp.int32),
        ],
        scratch_shapes=[
            pltpu.VMEM((head, local_width), BF16),
            pltpu.SemaphoreType.DMA((len(edges) - 1, 3)),
            pltpu.SemaphoreType.DMA((3,)),
        ],
        compiler_params=compiler_params(12),
        name="project_first",
    )(prompts, decode_hidden, w_kv, target_row, span_len, lengths)
    keep, send = regrouped(keep, got, steps, 1, total)
    got = swapped(send, steps[1][0])
    theirs, rows_rest, w_mine = pl.pallas_call(
        project_rest,
        in_specs=[REMAINS] * 4 + [RESIDENT] * 3 + [REMAINS],
        out_specs=[RESIDENT] * 3,
        out_shape=[
            pltpu.VMEM((all_rows, local_width), BF16),
            pltpu.VMEM((all_rows, features - depth), BF16),
            pltpu.VMEM((depth, local_width), BF16),
        ],
        scratch_shapes=[
            pltpu.VMEM((features - depth, local_width), BF16),
            pltpu.VMEM((1, local_width), F32),
            pltpu.SemaphoreType.DMA((5,)),
        ],
        compiler_params=compiler_params(16),
        name="project_rest",
    )(prompts, decode_hidden, w_kv, scale, *map(in_vmem, (rows, w_tail, total, keep)))
    theirs, got = lax.optimization_barrier((theirs, got))
    got = in_vmem(got)
    other = in_vmem(lax.ppermute(theirs, "tp", [(0, 1), (1, 0)]))

    mine = []
    pieces = max(len(steps) - 2, 1)
    bounds = [all_rows * i // (16 * pieces) * 16 for i in range(pieces)] + [all_rows]
    after = theirs
    for piece, at in enumerate(spans(bounds)):
        if piece + 2 < len(steps):
            keep, send = regrouped(keep, got, steps, piece + 2, after)
            got = swapped(send, steps[piece + 2][0])
        last = piece == pieces - 1
        padded = -(-span_len.shape[1] // 16) * 16
        extra = [kv_cache, queries, in_vmem(target_here), in_vmem(span_here)] if last else []
        extra_out = [
            pltpu.VMEM(kv_cache.shape, BF16),
            pltpu.VMEM(queries.shape, BF16),
            pltpu.VMEM((padded, slots), BF16),
            pltpu.VMEM((padded, sections * PITCH), BF16),
            pltpu.VMEM((padded, prompt_rows), F32),
        ]
        extra_out = extra_out if last else []
        part, *extra_out = pl.pallas_call(
            functools.partial(project_mine, at=at, last=last, row_count=row_count),
            in_specs=[RESIDENT] * 3
            + [REMAINS] * 3
            + ([REMAINS] * 2 + [RESIDENT] * 2 if last else []),
            out_specs=[RESIDENT] * (1 + len(extra_out)),
            out_shape=[pltpu.VMEM((at.stop - at.start, local_width), BF16)] + extra_out,
            scratch_shapes=[
                pltpu.VMEM((features - depth, local_width), BF16),
                pltpu.VMEM((1, local_width), F32),
                pltpu.SemaphoreType.DMA((4,)),
            ],
            compiler_params=compiler_params(16),
            name="project_mine",
        )(*map(in_vmem, (rows, rows_rest, w_mine)), w_kv, scale, in_vmem(keep), *extra)
        after = part
        mine.append(in_vmem(part))
    kv_here, queries_here, *tables = map(in_vmem, extra_out)

    answer_width = query_width + STATS
    keep, send = pl.pallas_call(
        attend_arrived,
        in_specs=[RESIDENT] * (6 + len(mine)),
        out_specs=[RESIDENT] * 2,
        out_shape=block_pair(answer_width),
        compiler_params=compiler_params(24),
        name="attend_arrived",
    )(*tables, in_vmem(keep), got, other, *mine)

    steps = answer_steps_of(sections)
    shares = []
    calls = len(steps) + 1
    bounds = [row_count * i // (16 * calls) * 16 for i in range(calls)] + [row_count]
    for done, at in enumerate(spans(bounds)):
        last = done == len(steps)
        if not last:
            got = swapped(send, steps[done][0])
        share = pl.pallas_call(
            functools.partial(attend_cache, rows_at=at),
            in_specs=[RESIDENT] * 6 + [REMAINS],
            out_specs=[RESIDENT] * 3,
            out_shape=[
                pltpu.VMEM((at.stop - at.start, query_width), BF16),
                pltpu.VMEM((slots, query_width), F32),
                pltpu.VMEM((slots, STATS), F32),
            ],
            compiler_params=compiler_params(24),
            name="attend_cache",
        )(queries_here, kv_here, in_vmem(lengths), mine[-1], other, in_vmem(pick), in_vmem(keep))
        shares += share
        if done + 1 < len(steps):
            keep, send = regrouped(keep, got, steps, done + 1, share[2])
        elif not last:
            size = sections // 4
            keep, *sent = pl.pallas_call(
                functools.partial(fan_out, step=steps[-1]),
                in_specs=[RESIDENT] * 2 + [REMAINS],
                out_specs=[RESIDENT] * 4,
                out_shape=[pltpu.VMEM((size, CAP, answer_width), BF16)] * 4,
                compiler_params=compiler_params(16),
                name="fan_out",
            )(in_vmem(keep), got, in_vmem(share[2]))
            groups = [in_vmem(keep)]
            groups += [swapped(blocks, (i + 1) * size) for i, blocks in enumerate(sent)]

    return pl.pallas_call(
        merge,
        in_specs=[RESIDENT] * (5 + len(shares)),
        out_specs=REMAINS,
        out_shape=jax.ShapeDtypeStruct((row_count, query_width), BF16),
        scratch_shapes=[pltpu.VMEM((row_count, query_width), BF16), pltpu.SemaphoreType.DMA((4,))],
        compiler_params=compiler_params(24),
        name="merge",
    )(*map(in_vmem, (pick, *shares)), *groups)


def solution(mesh):
    in_specs = (
        P(("groups", "section"), "tp"),
        P(("groups", "section"), "tp"),
        P(("groups", "section"), "tp"),
        P(("groups", "section"), None, "tp"),
        P(("groups", "section")),
        P("groups", None),
        P("groups", None),
        P("tp", None),
        P(),
    )
    out_specs = P(("groups", "section"), "tp")
    return jax.shard_map(shards, mesh=mesh, in_specs=in_specs, out_specs=out_specs, check_vma=False)
```

```python
import functools
import math

import jax
import jax.numpy as jnp
from jax import lax
from jax.experimental import pallas as pl
from jax.experimental.pallas import tpu as pltpu
from jax.sharding import PartitionSpec as P

HD = 128
CAP = 2
STATS = 128
MASKED = -1e30
LSE_PITCH = 40
PITCH = 8
LOG2_SCALE = HD ** (-0.5) * math.log2(math.e)
F32 = jnp.float32
BF16 = jnp.bfloat16
TRANSPOSED = (((0,), (0,)), ((), ()))


def iota(shape, dim):
    return lax.broadcasted_iota(jnp.int32, shape, dim)


def one_hot(shape, dim, index):
    return (iota(shape, dim) == index).astype(F32).astype(BF16)


def pick_rows(target_ref, row_count):
    sections, requests = target_ref.shape
    shape = (sections * CAP, requests)
    position = lax.axis_index("section")
    slot_id = iota(shape, 0)
    table = jnp.zeros(shape, jnp.int32)
    for k in range(sections):
        mine = (slot_id >= k * CAP) & (slot_id < (k + 1) * CAP)
        table = jnp.where(mine, target_ref[pl.ds(position ^ k, 1), :], table)
    local = table - position * row_count
    here = (local >= 0) & (local < row_count)
    square = (requests, requests)
    earlier = jnp.dot(
        here.astype(F32).astype(BF16),
        (iota(square, 0) < iota(square, 1)).astype(F32).astype(BF16),
        preferred_element_type=F32,
    )
    chosen = here & (earlier == lax.rem(slot_id, CAP).astype(F32))
    row = jnp.max(jnp.where(chosen, local.astype(F32), -1.0), axis=1, keepdims=True)
    return one_hot((shape[0], row_count), 1, row.astype(jnp.int32))


def steps_of(sections):
    steps = []
    bit = sections // 2
    while bit:
        sent = [k for k in range(sections) if k & bit]
        steps.append((bit, sent, [k for k in range(sections) if not k & bit]))
        bit //= 2
    return steps


def answer_steps_of(sections):
    steps = []
    bit = 1
    while 4 * bit < sections:
        sent = [k for k in range(sections) if k & bit]
        steps.append((bit, sent, [k for k in range(sections) if not k & bit]))
        bit *= 2
    return steps


def rearrange(step, kept_ref, got_ref, *out):
    where = {k: (got_ref, i) for i, k in enumerate(step[1])}
    where |= {k: (kept_ref, i) for i, k in enumerate(step[2])}
    for out_ref, blocks in out:
        for i, k in enumerate(blocks):
            ref, at = where[k]
            out_ref[i] = ref[at]


def regroup(kept_ref, got_ref, after_ref, keep_ref, send_ref, *, steps, done):
    _, sent, kept = steps[done]
    rearrange(steps[done - 1], kept_ref, got_ref, (send_ref, sent), (keep_ref, kept))


def fan_out(kept_ref, got_ref, after_ref, *out_refs, step):
    size = out_refs[0].shape[0]
    groups = [range(m * size, (m + 1) * size) for m in range(len(out_refs))]
    rearrange(step, kept_ref, got_ref, *zip(out_refs, groups))


def all_blocks(steps, kept_ref, got_ref):
    where = {k: got_ref[i] for i, k in enumerate(steps[-1][1])}
    where |= {k: kept_ref[i] for i, k in enumerate(steps[-1][2])}
    return jnp.concatenate([where[k].astype(F32) for k in range(len(where))], axis=0)


def select_queries(target_ref, queries_ref, pick_ref, keep_ref, send_ref):
    _, sent, kept = steps_of(target_ref.shape[0])[0]
    pick = pick_rows(target_ref, queries_ref.shape[0])
    pick_ref[...] = pick
    asked = jnp.dot(pick, queries_ref[...], preferred_element_type=F32)
    for ref, blocks in ((send_ref, sent), (keep_ref, kept)):
        for i, k in enumerate(blocks):
            ref[i] = asked[k * CAP : (k + 1) * CAP].astype(BF16)


def spans(edges):
    return [slice(a, b) for a, b in zip(edges[:-1], edges[1:])]


def load_rows(prompts_ref, hidden_ref, there, rows_ref, here, sems):
    prompt_rows = prompts_ref.shape[0]
    return [
        pltpu.make_async_copy(
            prompts_ref.at[:, there], rows_ref.at[:prompt_rows, here], sems.at[0]
        ),
        pltpu.make_async_copy(
            hidden_ref.at[:, there], rows_ref.at[prompt_rows:, here], sems.at[1]
        ),
    ]


def channels(offset, width):
    tp = lax.axis_index("tp")
    return pl.ds(pl.multiple_of(((tp + offset) & 1) * width, width), width)


def project_first(
    prompts_ref,
    hidden_ref,
    w_ref,
    target_ref,
    span_ref,
    len_ref,
    rows_ref,
    w_tail_ref,
    total_ref,
    target_here_ref,
    span_here_ref,
    len_here_ref,
    w_head_ref,
    sems,
    small_sems,
    *,
    edges,
):
    theirs = channels(1, total_ref.shape[1])
    chunks = spans(edges)
    head = edges[-2]
    waits = []
    for c, at in enumerate(chunks):
        here = at if at.stop <= head else slice(0, at.stop - head)
        w_here_ref = w_head_ref if at.stop <= head else w_tail_ref
        copies = load_rows(prompts_ref, hidden_ref, at, rows_ref, at, sems.at[c])
        copies.append(
            pltpu.make_async_copy(w_ref.at[at, theirs], w_here_ref.at[here, :], sems.at[c, 2])
        )
        for copy in copies:
            copy.start()
        waits.append(copies)
    small = [
        pltpu.make_async_copy(target_ref, target_here_ref, small_sems.at[0]),
        pltpu.make_async_copy(span_ref, span_here_ref, small_sems.at[1]),
        pltpu.make_async_copy(len_ref, len_here_ref, small_sems.at[2]),
    ]
    for copy in small:
        copy.start()
    for c, at in enumerate(chunks):
        for copy in waits[c]:
            copy.wait()
        if at.stop <= head:
            part = jnp.dot(rows_ref[:, at], w_head_ref[at, :], preferred_element_type=F32)
            if c == 0:
                total_ref[...] = part
            else:
                total_ref[...] += part
    for copy in small:
        copy.wait()


def project_rest(
    prompts_ref,
    hidden_ref,
    w_ref,
    scale_ref,
    rows_ref,
    w_tail_ref,
    total_in_ref,
    after_ref,
    theirs_ref,
    rows_rest_ref,
    w_mine_ref,
    w_rest_ref,
    total_ref,
    scale_here_ref,
    sems,
):
    width = theirs_ref.shape[1]
    theirs, mine = channels(1, width), channels(0, width)
    depth = rows_ref.shape[1]
    head = depth - w_tail_ref.shape[0]
    rest = slice(depth, depth + rows_rest_ref.shape[1])
    size = rest.stop - rest.start
    chunks = spans((0, size // 2, size))
    waits = []
    for c, at in enumerate(chunks):
        there = slice(depth + at.start, depth + at.stop)
        copies = load_rows(prompts_ref, hidden_ref, there, rows_rest_ref, at, sems.at[c])
        copies.append(
            pltpu.make_async_copy(w_ref.at[there, theirs], w_rest_ref.at[at, :], sems.at[c, 2])
        )
        for copy in copies:
            copy.start()
        waits.append(copies)
    later = [
        pltpu.make_async_copy(scale_ref.at[:, theirs], scale_here_ref, sems.at[2, 0]),
        pltpu.make_async_copy(w_ref.at[:, mine], w_mine_ref, sems.at[2, 1]),
    ]
    for copy in later:
        copy.start()
    total_ref[...] = total_in_ref[...] + jnp.dot(
        rows_ref[:, head:], w_tail_ref[...], preferred_element_type=F32
    )
    for c, at in enumerate(chunks):
        for copy in waits[c]:
            copy.wait()
        part = jnp.dot(rows_rest_ref[:, at], w_rest_ref[at, :], preferred_element_type=F32)
        if c < len(chunks) - 1:
            total_ref[...] += part
        else:
            later[0].wait()
            theirs_ref[...] = ((total_ref[...] + part) * scale_here_ref[...]).astype(BF16)
    later[1].wait()


def project_mine(rows_ref, rows_rest_ref, w_mine_ref, scale_ref, after_ref, *refs, at, last):
    refs, (scale_here_ref, sems) = refs[:-2], refs[-2:]
    if last:
        cache_ref, queries_ref, out_ref, cache_here_ref, queries_here_ref = refs
    else:
        (out_ref,) = refs
    mine = channels(0, out_ref.shape[1])
    copies = [pltpu.make_async_copy(scale_ref.at[:, mine], scale_here_ref, sems.at[0])]
    if last:
        copies.append(pltpu.make_async_copy(queries_ref, queries_here_ref, sems.at[1]))
        copies.append(pltpu.make_async_copy(cache_ref, cache_here_ref, sems.at[2]))
    for copy in copies:
        copy.start()
    depth = rows_ref.shape[1]
    count = at.stop - at.start
    block = count // 2 if count % 32 == 0 else count
    for m in spans(range(0, count + 1, block)):
        there = slice(at.start + m.start, at.start + m.stop)
        total = jnp.dot(rows_ref[there, :], w_mine_ref[:depth, :], preferred_element_type=F32)
        total += jnp.dot(
            rows_rest_ref[there, :], w_mine_ref[depth:, :], preferred_element_type=F32
        )
        if m.start == 0:
            copies[0].wait()
        out_ref[m, :] = (total * scale_here_ref[...]).astype(BF16)
    for copy in copies[1:]:
        copy.wait()


def split_bf16(x):
    high = x.astype(BF16).astype(F32)
    middle = (x - high).astype(BF16).astype(F32)
    return high, middle, (x - high - middle).astype(BF16).astype(F32)


def request_slots(target_ref, span_ref, row_count, padded):
    sections, requests = target_ref.shape
    position = lax.axis_index("section")
    target = target_ref[pl.ds(position, 1), :].astype(F32)
    span = span_ref[pl.ds(position, 1), :].astype(F32)
    diagonal = iota((padded, requests), 0) == iota((padded, requests), 1)
    target_col = jnp.sum(jnp.where(diagonal, target, 0.0), axis=1, keepdims=True)
    span_col = jnp.sum(jnp.where(diagonal, span, 0.0), axis=1, keepdims=True)
    section_row = jnp.zeros_like(target)
    section_col = jnp.zeros_like(target_col)
    for s in range(1, sections):
        section_row = section_row + (target >= s * row_count).astype(F32)
        section_col = section_col + (target_col >= s * row_count).astype(F32)
    before = (section_row == section_col) & (
        iota((padded, requests), 1) < iota((padded, requests), 0)
    )
    rank_col = jnp.sum(before.astype(F32), axis=1, keepdims=True).astype(jnp.int32)
    real = iota((padded, 1), 0) < requests
    section_col = jnp.where(real, section_col.astype(jnp.int32), -1)
    return section_col, rank_col, span_col.astype(jnp.int32)


def prepare_arrived(
    target_ref, span_ref, kept_ref, got_ref, rows_ref, slot_of_ref, bias_ref, *, row_count
):
    sections, requests = target_ref.shape
    padded, prompt_rows = bias_ref.shape
    span_rows = prompt_rows // requests
    section_col, rank_col, span_col = request_slots(target_ref, span_ref, row_count, padded)
    block = section_col ^ lax.axis_index("section")
    slot = jnp.where(section_col >= 0, block * PITCH + rank_col, -1)
    slot_of_ref[...] = one_hot((padded, sections * PITCH), 1, slot)
    slot = jnp.where(section_col >= 0, block * CAP + rank_col, -1)
    rows_ref[...] = jnp.dot(
        one_hot((padded, sections * CAP), 1, slot),
        all_blocks(steps_of(sections), kept_ref, got_ref).astype(BF16),
        preferred_element_type=F32,
    ).astype(BF16)
    key = iota((padded, prompt_rows), 1) - iota((padded, prompt_rows), 0) * span_rows
    bias_ref[...] = jnp.where((key >= 0) & (key < span_col), 0.0, MASKED)


def attend_arrived(rows_ref, slot_of_ref, bias_ref, other_ref, *refs):
    mine_refs, (keep_ref, send_ref) = refs[:-2], refs[-2:]
    padded, prompt_rows = bias_ref.shape
    kv_heads = other_ref.shape[1] // (2 * HD)
    group = rows_ref.shape[1] // (kv_heads * HD)
    rows = rows_ref[...]
    slot_of = slot_of_ref[...]
    bias = bias_ref[...]
    mine = jnp.concatenate([ref[...] for ref in mine_refs], axis=0)
    kv = (mine[:prompt_rows].astype(F32) + other_ref[:prompt_rows, :].astype(F32)).astype(BF16)
    scores = []
    for h in range(kv_heads):
        stacked = jnp.concatenate(
            [rows[:, (h * group + i) * HD : (h * group + i + 1) * HD] for i in range(group)],
            axis=0,
        )
        keys = kv[:, h * 2 * HD : (h * 2 + 1) * HD]
        scores.append(
            lax.dot_general(
                stacked, keys, (((1,), (1,)), ((), ())), preferred_element_type=F32
            )
        )
    scores = [
        x.reshape(group, padded, prompt_rows) * LOG2_SCALE + bias[None] for x in scores
    ]
    largest = [jnp.max(x, axis=2, keepdims=True) for x in scores]
    weights = [jnp.exp2(x - y) for x, y in zip(scores, largest)]
    totals = [jnp.sum(x, axis=2, keepdims=True) for x in weights]
    lane = iota((padded, STATS), 1)
    lse = jnp.zeros((padded, STATS), F32)
    pieces = []
    for h in range(kv_heads):
        values = jnp.dot(
            weights[h].reshape(group * padded, prompt_rows).astype(BF16),
            kv[:, (h * 2 + 1) * HD : (h * 2 + 2) * HD],
            preferred_element_type=F32,
        ).reshape(group, padded, HD)
        values = values / totals[h]
        head_lse = largest[h] + jnp.log2(totals[h])
        for i in range(group):
            pieces.append(values[i])
            lse = jnp.where(lane == h * group + i, head_lse[i], lse)
    high, middle, low = split_bf16(lse)
    stats = high + pltpu.roll(middle, LSE_PITCH, 1) + pltpu.roll(low, 2 * LSE_PITCH, 1)
    result = jnp.concatenate(pieces + [stats], axis=1).astype(BF16)
    answers = lax.dot_general(slot_of, result, TRANSPOSED, preferred_element_type=F32)
    _, sent, kept = answer_steps_of(2 * keep_ref.shape[0])[0]
    for ref, blocks in ((send_ref, sent), (keep_ref, kept)):
        for i, k in enumerate(blocks):
            ref[i] = answers[k * PITCH : k * PITCH + CAP].astype(BF16)


def attend_cache(
    queries_ref,
    cache_ref,
    len_ref,
    mine_ref,
    other_ref,
    pick_ref,
    after_ref,
    out_ref,
    slot_out_ref,
    slot_lse_ref,
    *,
    rows_at,
):
    row_count, cache_rows, width = cache_ref.shape
    first_row, block_rows = rows_at.start, rows_at.stop - rows_at.start
    kv_heads = width // (2 * HD)
    group = queries_ref.shape[1] // (kv_heads * HD)
    unit = 8
    keys_of = unit * cache_rows
    queries = queries_ref[rows_at, :].astype(F32)
    own = sum(
        ref[pl.ds(ref.shape[0] - row_count + first_row, block_rows), :].astype(F32)
        for ref in (mine_ref, other_ref)
    )
    own = own.astype(BF16).astype(F32)
    key = iota((unit, keys_of), 1) - iota((unit, keys_of), 0) * cache_rows
    lengths = len_ref[...].astype(F32)
    lane = iota((unit, STATS), 1)
    ones = jnp.ones((keys_of, HD), BF16)
    units = range(block_rows // unit)

    def rows_of(u):
        return slice(first_row + u * unit, first_row + (u + 1) * unit)

    pairs = [(u, h) for u in units for h in range(kv_heads)]
    bias = []
    for u in units:
        row = iota((unit, row_count), 0) + (first_row + u * unit)
        length = jnp.sum(
            jnp.where(iota((unit, row_count), 1) == row, lengths, 0.0), axis=1, keepdims=True
        ).astype(jnp.int32)
        bias.append(jnp.where((key >= 0) & (key < length), 0.0, MASKED))
    q, scores, own_scores = [], [], []
    for u, h in pairs:
        at = slice(u * unit, (u + 1) * unit)
        q.append(
            jnp.stack(
                [
                    queries[at, (h * group + i) * HD : (h * group + i + 1) * HD]
                    for i in range(group)
                ],
                axis=0,
            )
        )
        keys = cache_ref[rows_of(u), :, h * 2 * HD : (h * 2 + 1) * HD].reshape(keys_of, HD)
        scores.append(
            lax.dot_general(
                q[-1].reshape(group * unit, HD).astype(BF16),
                keys,
                (((1,), (1,)), ((), ())),
                preferred_element_type=F32,
            ).reshape(group, unit, keys_of)
        )
    for n, (u, h) in enumerate(pairs):
        at = slice(u * unit, (u + 1) * unit)
        own_key = own[at, h * 2 * HD : (h * 2 + 1) * HD]
        own_scores.append(jnp.sum(q[n] * own_key[None], axis=2, keepdims=True) * LOG2_SCALE)
    scores = [scores[n] * LOG2_SCALE + bias[u][None] for n, (u, h) in enumerate(pairs)]
    largest = [
        jnp.maximum(jnp.max(x, axis=2, keepdims=True), y) for x, y in zip(scores, own_scores)
    ]
    weights = [jnp.exp2(x - y).astype(BF16) for x, y in zip(scores, largest)]
    own_weights = [jnp.exp2(x - y) for x, y in zip(own_scores, largest)]
    sums = []
    for n, (u, h) in enumerate(pairs):
        at = slice(u * unit, (u + 1) * unit)
        values = cache_ref[rows_of(u), :, (h * 2 + 1) * HD : (h * 2 + 2) * HD].reshape(keys_of, HD)
        sums.append(
            jnp.dot(
                weights[n].reshape(group * unit, keys_of),
                jnp.concatenate([values, ones], axis=1),
                preferred_element_type=F32,
            ).reshape(group, unit, 2 * HD)
        )
    pieces = [[] for _ in units]
    stats = [jnp.zeros((unit, STATS), F32) for _ in units]
    for n, (u, h) in enumerate(pairs):
        at = slice(u * unit, (u + 1) * unit)
        own_value = own[at, (h * 2 + 1) * HD : (h * 2 + 2) * HD]
        total = sums[n][:, :, HD:] + own_weights[n]
        result = (sums[n][:, :, :HD] + own_weights[n] * own_value[None]) / total
        lse = largest[n] + jnp.log2(total)
        for i in range(group):
            pieces[u].append(result[i])
            stats[u] = jnp.where(lane == h * group + i, lse[i], stats[u])
    out = jnp.concatenate([jnp.concatenate(x, axis=1) for x in pieces], axis=0).astype(BF16)
    out_ref[...] = out
    here = iota((row_count, block_rows), 0) == iota((row_count, block_rows), 1) + first_row
    pick = jnp.dot(
        pick_ref[...], here.astype(F32).astype(BF16), preferred_element_type=F32
    ).astype(BF16)
    slot_out_ref[...] = jnp.dot(pick, out, preferred_element_type=F32)
    lse = jnp.concatenate(stats, axis=0)
    slot_lse_ref[...] = sum(
        jnp.dot(pick, part.astype(BF16), preferred_element_type=F32) for part in split_bf16(lse)
    )


def merge(pick_ref, *refs):
    refs, (out_ref, out_here_ref, sems) = refs[:-3], refs[-3:]
    parts, group_refs = refs[:-4], refs[-4:]
    cached_refs, slot_out_refs, slot_lse_refs = parts[0::3], parts[1::3], parts[2::3]
    width = out_ref.shape[1]
    pick = pick_ref[...]
    arrived = jnp.concatenate(
        [ref[i].astype(F32) for ref in group_refs for i in range(ref.shape[0])], axis=0
    )
    stats = arrived[:, width:]
    arrived_lse = (
        stats
        + pltpu.roll(stats, STATS - LSE_PITCH, 1)
        + pltpu.roll(stats, STATS - 2 * LSE_PITCH, 1)
    )
    cached_lse = sum(ref[...] for ref in slot_lse_refs)
    largest = jnp.maximum(cached_lse, arrived_lse)
    cached_weight = jnp.exp2(cached_lse - largest)
    arrived_weight = jnp.exp2(arrived_lse - largest)
    total = cached_weight + arrived_weight
    cached_weight = cached_weight / total
    arrived_weight = arrived_weight / total
    has = lax.dot_general(
        pick, jnp.ones((pick.shape[0], HD), BF16), TRANSPOSED, preferred_element_type=F32
    )
    copies = []
    for i in range(width // HD):
        at = slice(i * HD, (i + 1) * HD)
        merged = (
            sum(ref[:, at] for ref in slot_out_refs) * cached_weight[:, i : i + 1]
            + arrived[:, at] * arrived_weight[:, i : i + 1]
        )
        placed = lax.dot_general(
            pick, merged.astype(BF16), TRANSPOSED, preferred_element_type=F32
        )
        row = 0
        for ref in cached_refs:
            rows = slice(row, row + ref.shape[0])
            kept = ref[:, at].astype(F32)
            out_here_ref[rows, at] = jnp.where(has[rows] > 0.5, placed[rows], kept).astype(BF16)
            row += ref.shape[0]
        ready = width * (len(copies) + 1) // sems.shape[0]
        if at.stop == ready:
            there = slice(width * len(copies) // sems.shape[0], ready)
            copies.append(
                pltpu.make_async_copy(
                    out_here_ref.at[:, there], out_ref.at[:, there], sems.at[len(copies)]
                )
            )
            copies[-1].start()
    for copy in copies:
        copy.wait()


def compiler_params(megabytes):
    return pltpu.CompilerParams(vmem_limit_bytes=megabytes * 1024 * 1024)


RESIDENT = pl.BlockSpec(memory_space=pltpu.VMEM)
REMAINS = pl.BlockSpec(memory_space=pl.ANY)


def in_vmem(x):
    return pltpu.with_memory_space_constraint(x, pltpu.VMEM)


def in_hbm(x):
    return pltpu.with_memory_space_constraint(x, pltpu.HBM)


def shards(
    prompts, decode_hidden, queries, kv_cache, cache_len, span_len, target_row, w_kv, kv_scale
):
    row_count = decode_hidden.shape[0]
    prompt_rows, features = prompts.shape
    sections = lax.axis_size("section")
    local_width = kv_cache.shape[2]
    query_width = queries.shape[1]
    slots = sections * CAP
    all_rows = prompt_rows + row_count
    scale = kv_scale.reshape(1, -1)
    lengths = cache_len.reshape(1, -1)

    steps = steps_of(sections)
    half = sections // 2
    prompts, decode_hidden, w_kv, scale = map(in_hbm, (prompts, decode_hidden, w_kv, scale))
    target_row, span_len, queries = map(in_hbm, (target_row, span_len, queries))
    kv_cache, lengths = map(in_hbm, (kv_cache, lengths))

    def block_pair(width):
        return [pltpu.VMEM((half, CAP, width), BF16)] * 2

    def swapped(blocks, distance):
        pairs = [(i, i ^ distance) for i in range(sections)]
        return in_vmem(lax.ppermute(blocks, "section", pairs))

    pick, keep, send = pl.pallas_call(
        select_queries,
        in_specs=[RESIDENT, RESIDENT],
        out_specs=[RESIDENT] * 3,
        out_shape=[pltpu.VMEM((slots, row_count), BF16)] + block_pair(query_width),
        compiler_params=compiler_params(16),
        name="select_queries",
    )(target_row, queries)
    got = swapped(send, steps[0][0])

    def regrouped(blocks, got, steps, done, after):
        return pl.pallas_call(
            functools.partial(regroup, steps=steps, done=done),
            in_specs=[RESIDENT] * 2 + [REMAINS],
            out_specs=[RESIDENT] * 2,
            out_shape=block_pair(blocks.shape[2]),
            compiler_params=compiler_params(16),
            name="regroup",
        )(in_vmem(blocks), got, in_vmem(after))

    edges = (0, 256, 768, 1536, 2560, 4096)
    depth, head = edges[-1], edges[-2]
    rows, w_tail, total, target_here, span_here, lengths = pl.pallas_call(
        functools.partial(project_first, edges=edges),
        in_specs=[REMAINS] * 6,
        out_specs=[RESIDENT] * 6,
        out_shape=[
            pltpu.VMEM((all_rows, depth), BF16),
            pltpu.VMEM((depth - head, local_width), BF16),
            pltpu.VMEM((all_rows, local_width), F32),
            pltpu.VMEM(target_row.shape, jnp.int32),
            pltpu.VMEM(span_len.shape, jnp.int32),
            pltpu.VMEM(lengths.shape, jnp.int32),
        ],
        scratch_shapes=[
            pltpu.VMEM((head, local_width), BF16),
            pltpu.SemaphoreType.DMA((len(edges) - 1, 3)),
            pltpu.SemaphoreType.DMA((3,)),
        ],
        compiler_params=compiler_params(12),
        name="project_first",
    )(prompts, decode_hidden, w_kv, target_row, span_len, lengths)
    keep, send = regrouped(keep, got, steps, 1, total)
    got = swapped(send, steps[1][0])
    theirs, rows_rest, w_mine = pl.pallas_call(
        project_rest,
        in_specs=[REMAINS] * 4 + [RESIDENT] * 3 + [REMAINS],
        out_specs=[RESIDENT] * 3,
        out_shape=[
            pltpu.VMEM((all_rows, local_width), BF16),
            pltpu.VMEM((all_rows, features - depth), BF16),
            pltpu.VMEM((features, local_width), BF16),
        ],
        scratch_shapes=[
            pltpu.VMEM((features - depth, local_width), BF16),
            pltpu.VMEM((all_rows, local_width), F32),
            pltpu.VMEM((1, local_width), F32),
            pltpu.SemaphoreType.DMA((3, 3)),
        ],
        compiler_params=compiler_params(16),
        name="project_rest",
    )(prompts, decode_hidden, w_kv, scale, *map(in_vmem, (rows, w_tail, total, keep)))
    theirs, got = lax.optimization_barrier((theirs, got))
    got = in_vmem(got)
    other = in_vmem(lax.ppermute(theirs, "tp", [(0, 1), (1, 0)]))

    mine = []
    pieces = max(len(steps) - 2, 1)
    bounds = [all_rows * i // (16 * pieces) * 16 for i in range(pieces)] + [all_rows]
    after = theirs
    for piece, at in enumerate(spans(bounds)):
        if piece + 2 < len(steps):
            keep, send = regrouped(keep, got, steps, piece + 2, after)
            got = swapped(send, steps[piece + 2][0])
        last = piece == pieces - 1
        extra = [kv_cache, queries] if last else []
        part, *here = pl.pallas_call(
            functools.partial(project_mine, at=at, last=last),
            in_specs=[RESIDENT] * 3 + [REMAINS] * (2 + len(extra)),
            out_specs=[RESIDENT] * (1 + len(extra)),
            out_shape=[pltpu.VMEM((at.stop - at.start, local_width), BF16)]
            + [pltpu.VMEM(x.shape, BF16) for x in extra],
            scratch_shapes=[pltpu.VMEM((1, local_width), F32), pltpu.SemaphoreType.DMA((3,))],
            compiler_params=compiler_params(16),
            name="project_mine",
        )(*map(in_vmem, (rows, rows_rest, w_mine)), scale, in_vmem(keep), *extra)
        after = part
        mine.append(in_vmem(part))
    kv_here, queries_here = map(in_vmem, here)

    padded = -(-span_len.shape[1] // 16) * 16
    prepared = pl.pallas_call(
        functools.partial(prepare_arrived, row_count=row_count),
        in_specs=[RESIDENT] * 4,
        out_specs=[RESIDENT] * 3,
        out_shape=[
            pltpu.VMEM((padded, query_width), BF16),
            pltpu.VMEM((padded, sections * PITCH), BF16),
            pltpu.VMEM((padded, prompt_rows), F32),
        ],
        compiler_params=compiler_params(16),
        name="prepare_arrived",
    )(in_vmem(target_here), in_vmem(span_here), in_vmem(keep), got)
    answer_width = query_width + STATS
    keep, send = pl.pallas_call(
        attend_arrived,
        in_specs=[RESIDENT] * (4 + len(mine)),
        out_specs=[RESIDENT] * 2,
        out_shape=block_pair(answer_width),
        compiler_params=compiler_params(24),
        name="attend_arrived",
    )(*map(in_vmem, prepared), other, *mine)

    steps = answer_steps_of(sections)
    shares = []
    calls = len(steps) + 1
    bounds = [row_count * i // (16 * calls) * 16 for i in range(calls)] + [row_count]
    for done, at in enumerate(spans(bounds)):
        last = done == len(steps)
        if not last:
            got = swapped(send, steps[done][0])
        share = pl.pallas_call(
            functools.partial(attend_cache, rows_at=at),
            in_specs=[RESIDENT] * 6 + [REMAINS],
            out_specs=[RESIDENT] * 3,
            out_shape=[
                pltpu.VMEM((at.stop - at.start, query_width), BF16),
                pltpu.VMEM((slots, query_width), F32),
                pltpu.VMEM((slots, STATS), F32),
            ],
            compiler_params=compiler_params(24),
            name="attend_cache",
        )(queries_here, kv_here, in_vmem(lengths), mine[-1], other, in_vmem(pick), in_vmem(keep))
        shares += share
        if done + 1 < len(steps):
            keep, send = regrouped(keep, got, steps, done + 1, share[2])
        elif not last:
            size = sections // 4
            keep, *sent = pl.pallas_call(
                functools.partial(fan_out, step=steps[-1]),
                in_specs=[RESIDENT] * 2 + [REMAINS],
                out_specs=[RESIDENT] * 4,
                out_shape=[pltpu.VMEM((size, CAP, answer_width), BF16)] * 4,
                compiler_params=compiler_params(16),
                name="fan_out",
            )(in_vmem(keep), got, in_vmem(share[2]))
            groups = [in_vmem(keep)]
            groups += [swapped(blocks, (i + 1) * size) for i, blocks in enumerate(sent)]

    return pl.pallas_call(
        merge,
        in_specs=[RESIDENT] * (5 + len(shares)),
        out_specs=REMAINS,
        out_shape=jax.ShapeDtypeStruct((row_count, query_width), BF16),
        scratch_shapes=[pltpu.VMEM((row_count, query_width), BF16), pltpu.SemaphoreType.DMA((4,))],
        compiler_params=compiler_params(24),
        name="merge",
    )(*map(in_vmem, (pick, *shares)), *groups)


def solution(mesh):
    in_specs = (
        P(("groups", "section"), "tp"),
        P(("groups", "section"), "tp"),
        P(("groups", "section"), "tp"),
        P(("groups", "section"), None, "tp"),
        P(("groups", "section")),
        P("groups", None),
        P("groups", None),
        P("tp", None),
        P(),
    )
    out_specs = P(("groups", "section"), "tp")
    return jax.shard_map(shards, mesh=mesh, in_specs=in_specs, out_specs=out_specs, check_vma=False)
```

```python
import functools
import math

import jax
import jax.numpy as jnp
from jax import lax
from jax.experimental import pallas as pl
from jax.experimental.pallas import tpu as pltpu
from jax.sharding import PartitionSpec as P

HD = 128
CAP = 2
STATS = 128
MASKED = -1e30
LSE_PITCH = 40
PITCH = 8
LOG2_SCALE = HD ** (-0.5) * math.log2(math.e)
F32 = jnp.float32
BF16 = jnp.bfloat16
TRANSPOSED = (((0,), (0,)), ((), ()))


def iota(shape, dim):
    return lax.broadcasted_iota(jnp.int32, shape, dim)


def one_hot(shape, dim, index):
    return (iota(shape, dim) == index).astype(F32).astype(BF16)


def pick_rows(target_ref, row_count):
    sections, requests = target_ref.shape
    shape = (sections * CAP, requests)
    position = lax.axis_index("section")
    slot_id = iota(shape, 0)
    table = jnp.zeros(shape, jnp.int32)
    for k in range(sections):
        mine = (slot_id >= k * CAP) & (slot_id < (k + 1) * CAP)
        table = jnp.where(mine, target_ref[pl.ds(position ^ k, 1), :], table)
    local = table - position * row_count
    here = (local >= 0) & (local < row_count)
    square = (requests, requests)
    earlier = jnp.dot(
        here.astype(F32).astype(BF16),
        (iota(square, 0) < iota(square, 1)).astype(F32).astype(BF16),
        preferred_element_type=F32,
    )
    chosen = here & (earlier == lax.rem(slot_id, CAP).astype(F32))
    row = jnp.max(jnp.where(chosen, local.astype(F32), -1.0), axis=1, keepdims=True)
    return one_hot((shape[0], row_count), 1, row.astype(jnp.int32))


def steps_of(sections):
    steps = []
    bit = sections // 2
    while bit:
        sent = [k for k in range(sections) if k & bit]
        steps.append((bit, sent, [k for k in range(sections) if not k & bit]))
        bit //= 2
    return steps


def answer_steps_of(sections):
    return steps_of(sections)[:-2]


def rearrange(step, kept_ref, got_ref, *out):
    where = {k: (got_ref, i) for i, k in enumerate(step[1])}
    where |= {k: (kept_ref, i) for i, k in enumerate(step[2])}
    for out_ref, blocks in out:
        for i, k in enumerate(blocks):
            ref, at = where[k]
            out_ref[i] = ref[at]


def regroup(kept_ref, got_ref, after_ref, keep_ref, send_ref, *, steps, done):
    _, sent, kept = steps[done]
    rearrange(steps[done - 1], kept_ref, got_ref, (send_ref, sent), (keep_ref, kept))


def fan_out(kept_ref, got_ref, after_ref, *out_refs, step):
    groups = [range(m, 4 * out_refs[m].shape[0], 4) for m in range(len(out_refs))]
    rearrange(step, kept_ref, got_ref, *zip(out_refs, groups))


def all_blocks(steps, kept_ref, got_ref):
    where = {k: got_ref[i] for i, k in enumerate(steps[-1][1])}
    where |= {k: kept_ref[i] for i, k in enumerate(steps[-1][2])}
    return jnp.concatenate([where[k].astype(F32) for k in range(len(where))], axis=0)


def select_queries(target_ref, queries_ref, pick_ref, keep_ref, send_ref):
    _, sent, kept = steps_of(target_ref.shape[0])[0]
    pick = pick_rows(target_ref, queries_ref.shape[0])
    pick_ref[...] = pick
    asked = jnp.dot(pick, queries_ref[...], preferred_element_type=F32)
    for ref, blocks in ((send_ref, sent), (keep_ref, kept)):
        for i, k in enumerate(blocks):
            ref[i] = asked[k * CAP : (k + 1) * CAP].astype(BF16)


def spans(edges):
    return [slice(a, b) for a, b in zip(edges[:-1], edges[1:])]


def load_rows(prompts_ref, hidden_ref, there, rows_ref, here, sems):
    prompt_rows = prompts_ref.shape[0]
    return [
        pltpu.make_async_copy(
            prompts_ref.at[:, there], rows_ref.at[:prompt_rows, here], sems.at[0]
        ),
        pltpu.make_async_copy(
            hidden_ref.at[:, there], rows_ref.at[prompt_rows:, here], sems.at[1]
        ),
    ]


def channels(offset, width):
    tp = lax.axis_index("tp")
    return pl.ds(pl.multiple_of(((tp + offset) & 1) * width, width), width)


def project_first(
    prompts_ref,
    hidden_ref,
    w_ref,
    target_ref,
    span_ref,
    len_ref,
    rows_ref,
    w_tail_ref,
    total_ref,
    target_here_ref,
    span_here_ref,
    len_here_ref,
    w_head_ref,
    sems,
    small_sems,
    *,
    edges,
):
    theirs = channels(1, total_ref.shape[1])
    chunks = spans(edges)
    head = edges[-2]
    waits = []
    for c, at in enumerate(chunks):
        here = at if at.stop <= head else slice(0, at.stop - head)
        w_here_ref = w_head_ref if at.stop <= head else w_tail_ref
        copies = load_rows(prompts_ref, hidden_ref, at, rows_ref, at, sems.at[c])
        copies.append(
            pltpu.make_async_copy(w_ref.at[at, theirs], w_here_ref.at[here, :], sems.at[c, 2])
        )
        for copy in copies:
            copy.start()
        waits.append(copies)
    small = [
        pltpu.make_async_copy(target_ref, target_here_ref, small_sems.at[0]),
        pltpu.make_async_copy(span_ref, span_here_ref, small_sems.at[1]),
        pltpu.make_async_copy(len_ref, len_here_ref, small_sems.at[2]),
    ]
    for copy in small:
        copy.start()
    for c, at in enumerate(chunks):
        for copy in waits[c]:
            copy.wait()
        if at.stop <= head:
            part = jnp.dot(rows_ref[:, at], w_head_ref[at, :], preferred_element_type=F32)
            if c == 0:
                total_ref[...] = part
            else:
                total_ref[...] += part
    for copy in small:
        copy.wait()


def project_rest(
    prompts_ref,
    hidden_ref,
    w_ref,
    scale_ref,
    rows_ref,
    w_tail_ref,
    total_ref,
    after_ref,
    theirs_ref,
    rows_rest_ref,
    w_mine_ref,
    w_rest_ref,
    scale_here_ref,
    sems,
):
    width = theirs_ref.shape[1]
    theirs, mine = channels(1, width), channels(0, width)
    depth = rows_ref.shape[1]
    head = depth - w_tail_ref.shape[0]
    rest = slice(depth, depth + rows_rest_ref.shape[1])
    copies = load_rows(prompts_ref, hidden_ref, rest, rows_rest_ref, slice(None), sems)
    copies += [
        pltpu.make_async_copy(w_ref.at[rest, theirs], w_rest_ref, sems.at[2]),
        pltpu.make_async_copy(scale_ref.at[:, theirs], scale_here_ref, sems.at[3]),
        pltpu.make_async_copy(w_ref.at[:, mine], w_mine_ref, sems.at[4]),
    ]
    for copy in copies:
        copy.start()
    total = total_ref[...] + jnp.dot(
        rows_ref[:, head:], w_tail_ref[...], preferred_element_type=F32
    )
    for copy in copies[:-1]:
        copy.wait()
    total += jnp.dot(rows_rest_ref[...], w_rest_ref[...], preferred_element_type=F32)
    theirs_ref[...] = (total * scale_here_ref[...]).astype(BF16)
    copies[-1].wait()


def project_mine(rows_ref, rows_rest_ref, w_mine_ref, scale_ref, after_ref, *refs, at, last):
    refs, (scale_here_ref, sems) = refs[:-2], refs[-2:]
    if last:
        cache_ref, queries_ref, out_ref, cache_here_ref, queries_here_ref = refs
    else:
        (out_ref,) = refs
    mine = channels(0, out_ref.shape[1])
    copies = [pltpu.make_async_copy(scale_ref.at[:, mine], scale_here_ref, sems.at[0])]
    if last:
        copies.append(pltpu.make_async_copy(queries_ref, queries_here_ref, sems.at[1]))
        copies.append(pltpu.make_async_copy(cache_ref, cache_here_ref, sems.at[2]))
    for copy in copies:
        copy.start()
    depth = rows_ref.shape[1]
    count = at.stop - at.start
    block = count // 2 if count % 32 == 0 else count
    for m in spans(range(0, count + 1, block)):
        there = slice(at.start + m.start, at.start + m.stop)
        total = jnp.dot(rows_ref[there, :], w_mine_ref[:depth, :], preferred_element_type=F32)
        total += jnp.dot(
            rows_rest_ref[there, :], w_mine_ref[depth:, :], preferred_element_type=F32
        )
        if m.start == 0:
            copies[0].wait()
        out_ref[m, :] = (total * scale_here_ref[...]).astype(BF16)
    for copy in copies[1:]:
        copy.wait()


def split_bf16(x):
    high = x.astype(BF16).astype(F32)
    middle = (x - high).astype(BF16).astype(F32)
    return high, middle, (x - high - middle).astype(BF16).astype(F32)


def request_slots(target_ref, span_ref, row_count, padded):
    sections, requests = target_ref.shape
    position = lax.axis_index("section")
    target = target_ref[pl.ds(position, 1), :].astype(F32)
    span = span_ref[pl.ds(position, 1), :].astype(F32)
    diagonal = iota((padded, requests), 0) == iota((padded, requests), 1)
    target_col = jnp.sum(jnp.where(diagonal, target, 0.0), axis=1, keepdims=True)
    span_col = jnp.sum(jnp.where(diagonal, span, 0.0), axis=1, keepdims=True)
    section_row = jnp.zeros_like(target)
    section_col = jnp.zeros_like(target_col)
    for s in range(1, sections):
        section_row = section_row + (target >= s * row_count).astype(F32)
        section_col = section_col + (target_col >= s * row_count).astype(F32)
    before = (section_row == section_col) & (
        iota((padded, requests), 1) < iota((padded, requests), 0)
    )
    rank_col = jnp.sum(before.astype(F32), axis=1, keepdims=True).astype(jnp.int32)
    real = iota((padded, 1), 0) < requests
    section_col = jnp.where(real, section_col.astype(jnp.int32), -1)
    return section_col, rank_col, span_col.astype(jnp.int32)


def prepare_arrived(
    target_ref, span_ref, kept_ref, got_ref, rows_ref, slot_of_ref, bias_ref, *, row_count
):
    sections, requests = target_ref.shape
    padded, prompt_rows = bias_ref.shape
    span_rows = prompt_rows // requests
    section_col, rank_col, span_col = request_slots(target_ref, span_ref, row_count, padded)
    block = section_col ^ lax.axis_index("section")
    slot = jnp.where(section_col >= 0, block * PITCH + rank_col, -1)
    slot_of_ref[...] = one_hot((padded, sections * PITCH), 1, slot)
    slot = jnp.where(section_col >= 0, block * CAP + rank_col, -1)
    rows_ref[...] = jnp.dot(
        one_hot((padded, sections * CAP), 1, slot),
        all_blocks(steps_of(sections), kept_ref, got_ref).astype(BF16),
        preferred_element_type=F32,
    ).astype(BF16)
    key = iota((padded, prompt_rows), 1) - iota((padded, prompt_rows), 0) * span_rows
    bias_ref[...] = jnp.where((key >= 0) & (key < span_col), 0.0, MASKED)


def attend_arrived(rows_ref, slot_of_ref, bias_ref, other_ref, *refs):
    mine_refs, (keep_ref, send_ref) = refs[:-2], refs[-2:]
    padded, prompt_rows = bias_ref.shape
    kv_heads = other_ref.shape[1] // (2 * HD)
    group = rows_ref.shape[1] // (kv_heads * HD)
    rows = rows_ref[...]
    slot_of = slot_of_ref[...]
    bias = bias_ref[...]
    mine = jnp.concatenate([ref[...] for ref in mine_refs], axis=0)
    kv = (mine[:prompt_rows].astype(F32) + other_ref[:prompt_rows, :].astype(F32)).astype(BF16)
    scores = []
    for h in range(kv_heads):
        stacked = jnp.concatenate(
            [rows[:, (h * group + i) * HD : (h * group + i + 1) * HD] for i in range(group)],
            axis=0,
        )
        keys = kv[:, h * 2 * HD : (h * 2 + 1) * HD]
        scores.append(
            lax.dot_general(
                stacked, keys, (((1,), (1,)), ((), ())), preferred_element_type=F32
            )
        )
    scores = [
        x.reshape(group, padded, prompt_rows) * LOG2_SCALE + bias[None] for x in scores
    ]
    largest = [jnp.max(x, axis=2, keepdims=True) for x in scores]
    weights = [jnp.exp2(x - y) for x, y in zip(scores, largest)]
    totals = [jnp.sum(x, axis=2, keepdims=True) for x in weights]
    lane = iota((padded, STATS), 1)
    lse = jnp.zeros((padded, STATS), F32)
    pieces = []
    for h in range(kv_heads):
        values = jnp.dot(
            weights[h].reshape(group * padded, prompt_rows).astype(BF16),
            kv[:, (h * 2 + 1) * HD : (h * 2 + 2) * HD],
            preferred_element_type=F32,
        ).reshape(group, padded, HD)
        values = values / totals[h]
        head_lse = largest[h] + jnp.log2(totals[h])
        for i in range(group):
            pieces.append(values[i])
            lse = jnp.where(lane == h * group + i, head_lse[i], lse)
    high, middle, low = split_bf16(lse)
    stats = high + pltpu.roll(middle, LSE_PITCH, 1) + pltpu.roll(low, 2 * LSE_PITCH, 1)
    result = jnp.concatenate(pieces + [stats], axis=1).astype(BF16)
    answers = lax.dot_general(slot_of, result, TRANSPOSED, preferred_element_type=F32)
    _, sent, kept = answer_steps_of(2 * keep_ref.shape[0])[0]
    for ref, blocks in ((send_ref, sent), (keep_ref, kept)):
        for i, k in enumerate(blocks):
            ref[i] = answers[k * PITCH : k * PITCH + CAP].astype(BF16)


def attend_cache(
    queries_ref,
    cache_ref,
    len_ref,
    mine_ref,
    other_ref,
    pick_ref,
    after_ref,
    out_ref,
    slot_out_ref,
    slot_lse_ref,
    *,
    rows_at,
):
    row_count, cache_rows, width = cache_ref.shape
    first_row, block_rows = rows_at.start, rows_at.stop - rows_at.start
    kv_heads = width // (2 * HD)
    group = queries_ref.shape[1] // (kv_heads * HD)
    unit = 8
    keys_of = unit * cache_rows
    queries = queries_ref[rows_at, :].astype(F32)
    own = sum(
        ref[pl.ds(ref.shape[0] - row_count + first_row, block_rows), :].astype(F32)
        for ref in (mine_ref, other_ref)
    )
    own = own.astype(BF16).astype(F32)
    key = iota((unit, keys_of), 1) - iota((unit, keys_of), 0) * cache_rows
    lengths = len_ref[...].astype(F32)
    lane = iota((unit, STATS), 1)
    ones = jnp.ones((keys_of, HD), BF16)
    units = range(block_rows // unit)

    def rows_of(u):
        return slice(first_row + u * unit, first_row + (u + 1) * unit)

    pairs = [(u, h) for u in units for h in range(kv_heads)]
    bias = []
    for u in units:
        row = iota((unit, row_count), 0) + (first_row + u * unit)
        length = jnp.sum(
            jnp.where(iota((unit, row_count), 1) == row, lengths, 0.0), axis=1, keepdims=True
        ).astype(jnp.int32)
        bias.append(jnp.where((key >= 0) & (key < length), 0.0, MASKED))
    q, scores, own_scores = [], [], []
    for u, h in pairs:
        at = slice(u * unit, (u + 1) * unit)
        q.append(
            jnp.stack(
                [
                    queries[at, (h * group + i) * HD : (h * group + i + 1) * HD]
                    for i in range(group)
                ],
                axis=0,
            )
        )
        keys = cache_ref[rows_of(u), :, h * 2 * HD : (h * 2 + 1) * HD].reshape(keys_of, HD)
        scores.append(
            lax.dot_general(
                q[-1].reshape(group * unit, HD).astype(BF16),
                keys,
                (((1,), (1,)), ((), ())),
                preferred_element_type=F32,
            ).reshape(group, unit, keys_of)
        )
    for n, (u, h) in enumerate(pairs):
        at = slice(u * unit, (u + 1) * unit)
        own_key = own[at, h * 2 * HD : (h * 2 + 1) * HD]
        own_scores.append(jnp.sum(q[n] * own_key[None], axis=2, keepdims=True) * LOG2_SCALE)
    scores = [scores[n] * LOG2_SCALE + bias[u][None] for n, (u, h) in enumerate(pairs)]
    largest = [
        jnp.maximum(jnp.max(x, axis=2, keepdims=True), y) for x, y in zip(scores, own_scores)
    ]
    weights = [jnp.exp2(x - y).astype(BF16) for x, y in zip(scores, largest)]
    own_weights = [jnp.exp2(x - y) for x, y in zip(own_scores, largest)]
    sums = []
    for n, (u, h) in enumerate(pairs):
        at = slice(u * unit, (u + 1) * unit)
        values = cache_ref[rows_of(u), :, (h * 2 + 1) * HD : (h * 2 + 2) * HD].reshape(keys_of, HD)
        sums.append(
            jnp.dot(
                weights[n].reshape(group * unit, keys_of),
                jnp.concatenate([values, ones], axis=1),
                preferred_element_type=F32,
            ).reshape(group, unit, 2 * HD)
        )
    pieces = [[] for _ in units]
    stats = [jnp.zeros((unit, STATS), F32) for _ in units]
    for n, (u, h) in enumerate(pairs):
        at = slice(u * unit, (u + 1) * unit)
        own_value = own[at, (h * 2 + 1) * HD : (h * 2 + 2) * HD]
        total = sums[n][:, :, HD:] + own_weights[n]
        result = (sums[n][:, :, :HD] + own_weights[n] * own_value[None]) / total
        lse = largest[n] + jnp.log2(total)
        for i in range(group):
            pieces[u].append(result[i])
            stats[u] = jnp.where(lane == h * group + i, lse[i], stats[u])
    out = jnp.concatenate([jnp.concatenate(x, axis=1) for x in pieces], axis=0).astype(BF16)
    out_ref[...] = out
    here = iota((row_count, block_rows), 0) == iota((row_count, block_rows), 1) + first_row
    pick = jnp.dot(
        pick_ref[...], here.astype(F32).astype(BF16), preferred_element_type=F32
    ).astype(BF16)
    slot_out_ref[...] = jnp.dot(pick, out, preferred_element_type=F32)
    lse = jnp.concatenate(stats, axis=0)
    slot_lse_ref[...] = sum(
        jnp.dot(pick, part.astype(BF16), preferred_element_type=F32) for part in split_bf16(lse)
    )


def merge(pick_ref, *refs):
    refs, (out_ref, out_here_ref, sems) = refs[:-3], refs[-3:]
    parts, group_refs = refs[:-4], refs[-4:]
    cached_refs, slot_out_refs, slot_lse_refs = parts[0::3], parts[1::3], parts[2::3]
    width = out_ref.shape[1]
    pick = pick_ref[...]
    arrived = jnp.concatenate(
        [ref[i].astype(F32) for i in range(group_refs[0].shape[0]) for ref in group_refs], axis=0
    )
    stats = arrived[:, width:]
    arrived_lse = (
        stats
        + pltpu.roll(stats, STATS - LSE_PITCH, 1)
        + pltpu.roll(stats, STATS - 2 * LSE_PITCH, 1)
    )
    cached_lse = sum(ref[...] for ref in slot_lse_refs)
    largest = jnp.maximum(cached_lse, arrived_lse)
    cached_weight = jnp.exp2(cached_lse - largest)
    arrived_weight = jnp.exp2(arrived_lse - largest)
    total = cached_weight + arrived_weight
    cached_weight = cached_weight / total
    arrived_weight = arrived_weight / total
    has = lax.dot_general(
        pick, jnp.ones((pick.shape[0], HD), BF16), TRANSPOSED, preferred_element_type=F32
    )
    copies = []
    for i in range(width // HD):
        at = slice(i * HD, (i + 1) * HD)
        merged = (
            sum(ref[:, at] for ref in slot_out_refs) * cached_weight[:, i : i + 1]
            + arrived[:, at] * arrived_weight[:, i : i + 1]
        )
        placed = lax.dot_general(
            pick, merged.astype(BF16), TRANSPOSED, preferred_element_type=F32
        )
        row = 0
        for ref in cached_refs:
            rows = slice(row, row + ref.shape[0])
            kept = ref[:, at].astype(F32)
            out_here_ref[rows, at] = jnp.where(has[rows] > 0.5, placed[rows], kept).astype(BF16)
            row += ref.shape[0]
        ready = width * (len(copies) + 1) // sems.shape[0]
        if at.stop == ready:
            there = slice(width * len(copies) // sems.shape[0], ready)
            copies.append(
                pltpu.make_async_copy(
                    out_here_ref.at[:, there], out_ref.at[:, there], sems.at[len(copies)]
                )
            )
            copies[-1].start()
    for copy in copies:
        copy.wait()


def compiler_params(megabytes):
    return pltpu.CompilerParams(vmem_limit_bytes=megabytes * 1024 * 1024)


RESIDENT = pl.BlockSpec(memory_space=pltpu.VMEM)
REMAINS = pl.BlockSpec(memory_space=pl.ANY)


def in_vmem(x):
    return pltpu.with_memory_space_constraint(x, pltpu.VMEM)


def in_hbm(x):
    return pltpu.with_memory_space_constraint(x, pltpu.HBM)


def shards(
    prompts, decode_hidden, queries, kv_cache, cache_len, span_len, target_row, w_kv, kv_scale
):
    row_count = decode_hidden.shape[0]
    prompt_rows, features = prompts.shape
    sections = lax.axis_size("section")
    local_width = kv_cache.shape[2]
    query_width = queries.shape[1]
    slots = sections * CAP
    all_rows = prompt_rows + row_count
    scale = kv_scale.reshape(1, -1)
    lengths = cache_len.reshape(1, -1)

    steps = steps_of(sections)
    half = sections // 2
    prompts, decode_hidden, w_kv, scale = map(in_hbm, (prompts, decode_hidden, w_kv, scale))
    target_row, span_len, queries = map(in_hbm, (target_row, span_len, queries))
    kv_cache, lengths = map(in_hbm, (kv_cache, lengths))

    def block_pair(width):
        return [pltpu.VMEM((half, CAP, width), BF16)] * 2

    def swapped(blocks, distance):
        pairs = [(i, i ^ distance) for i in range(sections)]
        return in_vmem(lax.ppermute(blocks, "section", pairs))

    pick, keep, send = pl.pallas_call(
        select_queries,
        in_specs=[RESIDENT, RESIDENT],
        out_specs=[RESIDENT] * 3,
        out_shape=[pltpu.VMEM((slots, row_count), BF16)] + block_pair(query_width),
        compiler_params=compiler_params(16),
        name="select_queries",
    )(target_row, queries)
    got = swapped(send, steps[0][0])

    def regrouped(blocks, got, steps, done, after):
        return pl.pallas_call(
            functools.partial(regroup, steps=steps, done=done),
            in_specs=[RESIDENT] * 2 + [REMAINS],
            out_specs=[RESIDENT] * 2,
            out_shape=block_pair(blocks.shape[2]),
            compiler_params=compiler_params(16),
            name="regroup",
        )(in_vmem(blocks), got, in_vmem(after))

    edges = (0, 256, 768, 1536, 2560, 4096)
    depth, head = edges[-1], edges[-2]
    rows, w_tail, total, target_here, span_here, lengths = pl.pallas_call(
        functools.partial(project_first, edges=edges),
        in_specs=[REMAINS] * 6,
        out_specs=[RESIDENT] * 6,
        out_shape=[
            pltpu.VMEM((all_rows, depth), BF16),
            pltpu.VMEM((depth - head, local_width), BF16),
            pltpu.VMEM((all_rows, local_width), F32),
            pltpu.VMEM(target_row.shape, jnp.int32),
            pltpu.VMEM(span_len.shape, jnp.int32),
            pltpu.VMEM(lengths.shape, jnp.int32),
        ],
        scratch_shapes=[
            pltpu.VMEM((head, local_width), BF16),
            pltpu.SemaphoreType.DMA((len(edges) - 1, 3)),
            pltpu.SemaphoreType.DMA((3,)),
        ],
        compiler_params=compiler_params(12),
        name="project_first",
    )(prompts, decode_hidden, w_kv, target_row, span_len, lengths)
    keep, send = regrouped(keep, got, steps, 1, total)
    got = swapped(send, steps[1][0])
    theirs, rows_rest, w_mine = pl.pallas_call(
        project_rest,
        in_specs=[REMAINS] * 4 + [RESIDENT] * 3 + [REMAINS],
        out_specs=[RESIDENT] * 3,
        out_shape=[
            pltpu.VMEM((all_rows, local_width), BF16),
            pltpu.VMEM((all_rows, features - depth), BF16),
            pltpu.VMEM((features, local_width), BF16),
        ],
        scratch_shapes=[
            pltpu.VMEM((features - depth, local_width), BF16),
            pltpu.VMEM((1, local_width), F32),
            pltpu.SemaphoreType.DMA((5,)),
        ],
        compiler_params=compiler_params(16),
        name="project_rest",
    )(prompts, decode_hidden, w_kv, scale, *map(in_vmem, (rows, w_tail, total, keep)))
    theirs, got = lax.optimization_barrier((theirs, got))
    got = in_vmem(got)
    other = in_vmem(lax.ppermute(theirs, "tp", [(0, 1), (1, 0)]))

    mine = []
    pieces = max(len(steps) - 2, 1)
    bounds = [all_rows * i // (16 * pieces) * 16 for i in range(pieces)] + [all_rows]
    after = theirs
    for piece, at in enumerate(spans(bounds)):
        if piece + 2 < len(steps):
            keep, send = regrouped(keep, got, steps, piece + 2, after)
            got = swapped(send, steps[piece + 2][0])
        last = piece == pieces - 1
        extra = [kv_cache, queries] if last else []
        part, *here = pl.pallas_call(
            functools.partial(project_mine, at=at, last=last),
            in_specs=[RESIDENT] * 3 + [REMAINS] * (2 + len(extra)),
            out_specs=[RESIDENT] * (1 + len(extra)),
            out_shape=[pltpu.VMEM((at.stop - at.start, local_width), BF16)]
            + [pltpu.VMEM(x.shape, BF16) for x in extra],
            scratch_shapes=[pltpu.VMEM((1, local_width), F32), pltpu.SemaphoreType.DMA((3,))],
            compiler_params=compiler_params(16),
            name="project_mine",
        )(*map(in_vmem, (rows, rows_rest, w_mine)), scale, in_vmem(keep), *extra)
        after = part
        mine.append(in_vmem(part))
    kv_here, queries_here = map(in_vmem, here)

    padded = -(-span_len.shape[1] // 16) * 16
    prepared = pl.pallas_call(
        functools.partial(prepare_arrived, row_count=row_count),
        in_specs=[RESIDENT] * 4,
        out_specs=[RESIDENT] * 3,
        out_shape=[
            pltpu.VMEM((padded, query_width), BF16),
            pltpu.VMEM((padded, sections * PITCH), BF16),
            pltpu.VMEM((padded, prompt_rows), F32),
        ],
        compiler_params=compiler_params(16),
        name="prepare_arrived",
    )(in_vmem(target_here), in_vmem(span_here), in_vmem(keep), got)
    answer_width = query_width + STATS
    keep, send = pl.pallas_call(
        attend_arrived,
        in_specs=[RESIDENT] * (4 + len(mine)),
        out_specs=[RESIDENT] * 2,
        out_shape=block_pair(answer_width),
        compiler_params=compiler_params(24),
        name="attend_arrived",
    )(*map(in_vmem, prepared), other, *mine)

    steps = answer_steps_of(sections)
    shares = []
    calls = len(steps) + 1
    bounds = [row_count * i // (16 * calls) * 16 for i in range(calls)] + [row_count]
    for done, at in enumerate(spans(bounds)):
        last = done == len(steps)
        if not last:
            got = swapped(send, steps[done][0])
        share = pl.pallas_call(
            functools.partial(attend_cache, rows_at=at),
            in_specs=[RESIDENT] * 6 + [REMAINS],
            out_specs=[RESIDENT] * 3,
            out_shape=[
                pltpu.VMEM((at.stop - at.start, query_width), BF16),
                pltpu.VMEM((slots, query_width), F32),
                pltpu.VMEM((slots, STATS), F32),
            ],
            compiler_params=compiler_params(24),
            name="attend_cache",
        )(queries_here, kv_here, in_vmem(lengths), mine[-1], other, in_vmem(pick), in_vmem(keep))
        shares += share
        if done + 1 < len(steps):
            keep, send = regrouped(keep, got, steps, done + 1, share[2])
        elif not last:
            size = sections // 4
            keep, *sent = pl.pallas_call(
                functools.partial(fan_out, step=steps[-1]),
                in_specs=[RESIDENT] * 2 + [REMAINS],
                out_specs=[RESIDENT] * 4,
                out_shape=[pltpu.VMEM((size, CAP, answer_width), BF16)] * 4,
                compiler_params=compiler_params(16),
                name="fan_out",
            )(in_vmem(keep), got, in_vmem(share[2]))
            groups = [in_vmem(keep)]
            groups += [swapped(blocks, i + 1) for i, blocks in enumerate(sent)]

    return pl.pallas_call(
        merge,
        in_specs=[RESIDENT] * (5 + len(shares)),
        out_specs=REMAINS,
        out_shape=jax.ShapeDtypeStruct((row_count, query_width), BF16),
        scratch_shapes=[pltpu.VMEM((row_count, query_width), BF16), pltpu.SemaphoreType.DMA((4,))],
        compiler_params=compiler_params(24),
        name="merge",
    )(*map(in_vmem, (pick, *shares)), *groups)


def solution(mesh):
    in_specs = (
        P(("groups", "section"), "tp"),
        P(("groups", "section"), "tp"),
        P(("groups", "section"), "tp"),
        P(("groups", "section"), None, "tp"),
        P(("groups", "section")),
        P("groups", None),
        P("groups", None),
        P("tp", None),
        P(),
    )
    out_specs = P(("groups", "section"), "tp")
    return jax.shard_map(shards, mesh=mesh, in_specs=in_specs, out_specs=out_specs, check_vma=False)
```

```python
import functools
import math

import jax
import jax.numpy as jnp
from jax import lax
from jax.experimental import pallas as pl
from jax.experimental.pallas import tpu as pltpu
from jax.sharding import PartitionSpec as P

HD = 128
CAP = 2
STATS = 128
MASKED = -1e30
LSE_PITCH = 40
PITCH = 8
LOG2_SCALE = HD ** (-0.5) * math.log2(math.e)
F32 = jnp.float32
BF16 = jnp.bfloat16
TRANSPOSED = (((0,), (0,)), ((), ()))


def iota(shape, dim):
    return lax.broadcasted_iota(jnp.int32, shape, dim)


def one_hot(shape, dim, index):
    return (iota(shape, dim) == index).astype(F32).astype(BF16)


def pick_rows(target_ref, row_count):
    sections, requests = target_ref.shape
    shape = (sections * CAP, requests)
    position = lax.axis_index("section")
    slot_id = iota(shape, 0)
    table = jnp.zeros(shape, jnp.int32)
    for k in range(sections):
        mine = (slot_id >= k * CAP) & (slot_id < (k + 1) * CAP)
        table = jnp.where(mine, target_ref[pl.ds(position ^ k, 1), :], table)
    local = table - position * row_count
    here = (local >= 0) & (local < row_count)
    square = (requests, requests)
    earlier = jnp.dot(
        here.astype(F32).astype(BF16),
        (iota(square, 0) < iota(square, 1)).astype(F32).astype(BF16),
        preferred_element_type=F32,
    )
    chosen = here & (earlier == lax.rem(slot_id, CAP).astype(F32))
    row = jnp.max(jnp.where(chosen, local.astype(F32), -1.0), axis=1, keepdims=True)
    return one_hot((shape[0], row_count), 1, row.astype(jnp.int32))


def steps_of(sections):
    steps = []
    bit = sections // 2
    while bit:
        sent = [k for k in range(sections) if k & bit]
        steps.append((bit, sent, [k for k in range(sections) if not k & bit]))
        bit //= 2
    return steps


def answer_steps_of(sections):
    steps = []
    bit = 1
    while 4 * bit < sections:
        sent = [k for k in range(sections) if k & bit]
        steps.append((bit, sent, [k for k in range(sections) if not k & bit]))
        bit *= 2
    return steps


def rearrange(step, kept_ref, got_ref, *out):
    where = {k: (got_ref, i) for i, k in enumerate(step[1])}
    where |= {k: (kept_ref, i) for i, k in enumerate(step[2])}
    for out_ref, blocks in out:
        for i, k in enumerate(blocks):
            ref, at = where[k]
            out_ref[i] = ref[at]


def regroup(kept_ref, got_ref, after_ref, keep_ref, send_ref, *, steps, done):
    _, sent, kept = steps[done]
    rearrange(steps[done - 1], kept_ref, got_ref, (send_ref, sent), (keep_ref, kept))


def fan_out(kept_ref, got_ref, after_ref, *out_refs, step):
    size = out_refs[0].shape[0]
    groups = [range(m * size, (m + 1) * size) for m in range(len(out_refs))]
    rearrange(step, kept_ref, got_ref, *zip(out_refs, groups))


def all_blocks(steps, kept_ref, got_ref):
    where = {k: got_ref[i] for i, k in enumerate(steps[-1][1])}
    where |= {k: kept_ref[i] for i, k in enumerate(steps[-1][2])}
    return jnp.concatenate([where[k].astype(F32) for k in range(len(where))], axis=0)


def select_queries(
    target_ref, queries_ref, pick_ref, keep_ref, send_ref, queries_here_ref, sem
):
    copy = pltpu.make_async_copy(queries_ref, queries_here_ref, sem)
    copy.start()
    _, sent, kept = steps_of(target_ref.shape[0])[0]
    pick = pick_rows(target_ref, queries_ref.shape[0])
    pick_ref[...] = pick
    copy.wait()
    asked = jnp.dot(pick, queries_here_ref[...], preferred_element_type=F32)
    for ref, blocks in ((send_ref, sent), (keep_ref, kept)):
        for i, k in enumerate(blocks):
            ref[i] = asked[k * CAP : (k + 1) * CAP].astype(BF16)


def spans(edges):
    return [slice(a, b) for a, b in zip(edges[:-1], edges[1:])]


def load_rows(prompts_ref, hidden_ref, there, rows_ref, here, sems):
    prompt_rows = prompts_ref.shape[0]
    return [
        pltpu.make_async_copy(
            prompts_ref.at[:, there], rows_ref.at[:prompt_rows, here], sems.at[0]
        ),
        pltpu.make_async_copy(
            hidden_ref.at[:, there], rows_ref.at[prompt_rows:, here], sems.at[1]
        ),
    ]


def channels(offset, width):
    tp = lax.axis_index("tp")
    return pl.ds(pl.multiple_of(((tp + offset) & 1) * width, width), width)


def project_first(
    prompts_ref,
    hidden_ref,
    w_ref,
    target_ref,
    span_ref,
    len_ref,
    rows_ref,
    w_tail_ref,
    total_ref,
    target_here_ref,
    span_here_ref,
    len_here_ref,
    w_head_ref,
    sems,
    small_sems,
    *,
    edges,
):
    theirs = channels(1, total_ref.shape[1])
    chunks = spans(edges)
    head = edges[-2]
    waits = []
    for c, at in enumerate(chunks):
        here = at if at.stop <= head else slice(0, at.stop - head)
        w_here_ref = w_head_ref if at.stop <= head else w_tail_ref
        copies = load_rows(prompts_ref, hidden_ref, at, rows_ref, at, sems.at[c])
        copies.append(
            pltpu.make_async_copy(w_ref.at[at, theirs], w_here_ref.at[here, :], sems.at[c, 2])
        )
        for copy in copies:
            copy.start()
        waits.append(copies)
    small = [
        pltpu.make_async_copy(target_ref, target_here_ref, small_sems.at[0]),
        pltpu.make_async_copy(span_ref, span_here_ref, small_sems.at[1]),
        pltpu.make_async_copy(len_ref, len_here_ref, small_sems.at[2]),
    ]
    for copy in small:
        copy.start()
    for c, at in enumerate(chunks):
        for copy in waits[c]:
            copy.wait()
        if at.stop <= head:
            part = jnp.dot(rows_ref[:, at], w_head_ref[at, :], preferred_element_type=F32)
            if c == 0:
                total_ref[...] = part
            else:
                total_ref[...] += part
    for copy in small:
        copy.wait()


def project_rest(
    prompts_ref,
    hidden_ref,
    w_ref,
    scale_ref,
    rows_ref,
    w_tail_ref,
    total_ref,
    after_ref,
    theirs_ref,
    rows_rest_ref,
    w_mine_ref,
    w_rest_ref,
    scale_here_ref,
    sems,
):
    width = theirs_ref.shape[1]
    theirs, mine = channels(1, width), channels(0, width)
    depth = rows_ref.shape[1]
    head = depth - w_tail_ref.shape[0]
    rest = slice(depth, depth + rows_rest_ref.shape[1])
    copies = load_rows(prompts_ref, hidden_ref, rest, rows_rest_ref, slice(None), sems)
    copies += [
        pltpu.make_async_copy(w_ref.at[rest, theirs], w_rest_ref, sems.at[2]),
        pltpu.make_async_copy(scale_ref.at[:, theirs], scale_here_ref, sems.at[3]),
        pltpu.make_async_copy(w_ref.at[:, mine], w_mine_ref, sems.at[4]),
    ]
    for copy in copies:
        copy.start()
    total = total_ref[...] + jnp.dot(
        rows_ref[:, head:], w_tail_ref[...], preferred_element_type=F32
    )
    for copy in copies[:-1]:
        copy.wait()
    total += jnp.dot(rows_rest_ref[...], w_rest_ref[...], preferred_element_type=F32)
    theirs_ref[...] = (total * scale_here_ref[...]).astype(BF16)
    copies[-1].wait()


def project_mine(rows_ref, rows_rest_ref, w_mine_ref, scale_ref, after_ref, *refs, at, last):
    refs, (scale_here_ref, sems) = refs[:-2], refs[-2:]
    if last:
        cache_ref, queries_ref, out_ref, cache_here_ref, queries_here_ref = refs
    else:
        (out_ref,) = refs
    mine = channels(0, out_ref.shape[1])
    copies = [pltpu.make_async_copy(scale_ref.at[:, mine], scale_here_ref, sems.at[0])]
    if last:
        copies.append(pltpu.make_async_copy(queries_ref, queries_here_ref, sems.at[1]))
        copies.append(pltpu.make_async_copy(cache_ref, cache_here_ref, sems.at[2]))
    for copy in copies:
        copy.start()
    depth = rows_ref.shape[1]
    count = at.stop - at.start
    block = count // 2 if count % 32 == 0 else count
    for m in spans(range(0, count + 1, block)):
        there = slice(at.start + m.start, at.start + m.stop)
        total = jnp.dot(rows_ref[there, :], w_mine_ref[:depth, :], preferred_element_type=F32)
        total += jnp.dot(
            rows_rest_ref[there, :], w_mine_ref[depth:, :], preferred_element_type=F32
        )
        if m.start == 0:
            copies[0].wait()
        out_ref[m, :] = (total * scale_here_ref[...]).astype(BF16)
    for copy in copies[1:]:
        copy.wait()


def split_bf16(x):
    high = x.astype(BF16).astype(F32)
    middle = (x - high).astype(BF16).astype(F32)
    return high, middle, (x - high - middle).astype(BF16).astype(F32)


def request_slots(target_ref, span_ref, row_count, padded):
    sections, requests = target_ref.shape
    position = lax.axis_index("section")
    target = target_ref[pl.ds(position, 1), :].astype(F32)
    span = span_ref[pl.ds(position, 1), :].astype(F32)
    diagonal = iota((padded, requests), 0) == iota((padded, requests), 1)
    target_col = jnp.sum(jnp.where(diagonal, target, 0.0), axis=1, keepdims=True)
    span_col = jnp.sum(jnp.where(diagonal, span, 0.0), axis=1, keepdims=True)
    section_row = jnp.zeros_like(target)
    section_col = jnp.zeros_like(target_col)
    for s in range(1, sections):
        section_row = section_row + (target >= s * row_count).astype(F32)
        section_col = section_col + (target_col >= s * row_count).astype(F32)
    before = (section_row == section_col) & (
        iota((padded, requests), 1) < iota((padded, requests), 0)
    )
    rank_col = jnp.sum(before.astype(F32), axis=1, keepdims=True).astype(jnp.int32)
    real = iota((padded, 1), 0) < requests
    section_col = jnp.where(real, section_col.astype(jnp.int32), -1)
    return section_col, rank_col, span_col.astype(jnp.int32)


def prepare_arrived(
    target_ref, span_ref, kept_ref, got_ref, rows_ref, slot_of_ref, bias_ref, *, row_count
):
    sections, requests = target_ref.shape
    padded, prompt_rows = bias_ref.shape
    span_rows = prompt_rows // requests
    section_col, rank_col, span_col = request_slots(target_ref, span_ref, row_count, padded)
    block = section_col ^ lax.axis_index("section")
    slot = jnp.where(section_col >= 0, block * PITCH + rank_col, -1)
    slot_of_ref[...] = one_hot((padded, sections * PITCH), 1, slot)
    slot = jnp.where(section_col >= 0, block * CAP + rank_col, -1)
    rows_ref[...] = jnp.dot(
        one_hot((padded, sections * CAP), 1, slot),
        all_blocks(steps_of(sections), kept_ref, got_ref).astype(BF16),
        preferred_element_type=F32,
    ).astype(BF16)
    key = iota((padded, prompt_rows), 1) - iota((padded, prompt_rows), 0) * span_rows
    bias_ref[...] = jnp.where((key >= 0) & (key < span_col), 0.0, MASKED)


def attend_arrived(rows_ref, slot_of_ref, bias_ref, other_ref, *refs):
    mine_refs, (keep_ref, send_ref) = refs[:-2], refs[-2:]
    padded, prompt_rows = bias_ref.shape
    kv_heads = other_ref.shape[1] // (2 * HD)
    group = rows_ref.shape[1] // (kv_heads * HD)
    rows = rows_ref[...]
    slot_of = slot_of_ref[...]
    bias = bias_ref[...]
    mine = jnp.concatenate([ref[...] for ref in mine_refs], axis=0)
    kv = (mine[:prompt_rows].astype(F32) + other_ref[:prompt_rows, :].astype(F32)).astype(BF16)
    scores = []
    for h in range(kv_heads):
        stacked = jnp.concatenate(
            [rows[:, (h * group + i) * HD : (h * group + i + 1) * HD] for i in range(group)],
            axis=0,
        )
        keys = kv[:, h * 2 * HD : (h * 2 + 1) * HD]
        scores.append(
            lax.dot_general(
                stacked, keys, (((1,), (1,)), ((), ())), preferred_element_type=F32
            )
        )
    scores = [
        x.reshape(group, padded, prompt_rows) * LOG2_SCALE + bias[None] for x in scores
    ]
    largest = [jnp.max(x, axis=2, keepdims=True) for x in scores]
    weights = [jnp.exp2(x - y) for x, y in zip(scores, largest)]
    totals = [jnp.sum(x, axis=2, keepdims=True) for x in weights]
    lane = iota((padded, STATS), 1)
    lse = jnp.zeros((padded, STATS), F32)
    pieces = []
    for h in range(kv_heads):
        values = jnp.dot(
            weights[h].reshape(group * padded, prompt_rows).astype(BF16),
            kv[:, (h * 2 + 1) * HD : (h * 2 + 2) * HD],
            preferred_element_type=F32,
        ).reshape(group, padded, HD)
        values = values / totals[h]
        head_lse = largest[h] + jnp.log2(totals[h])
        for i in range(group):
            pieces.append(values[i])
            lse = jnp.where(lane == h * group + i, head_lse[i], lse)
    high, middle, low = split_bf16(lse)
    stats = high + pltpu.roll(middle, LSE_PITCH, 1) + pltpu.roll(low, 2 * LSE_PITCH, 1)
    result = jnp.concatenate(pieces + [stats], axis=1).astype(BF16)
    answers = lax.dot_general(slot_of, result, TRANSPOSED, preferred_element_type=F32)
    _, sent, kept = answer_steps_of(2 * keep_ref.shape[0])[0]
    for ref, blocks in ((send_ref, sent), (keep_ref, kept)):
        for i, k in enumerate(blocks):
            ref[i] = answers[k * PITCH : k * PITCH + CAP].astype(BF16)


def attend_cache(
    queries_ref,
    cache_ref,
    len_ref,
    mine_ref,
    other_ref,
    pick_ref,
    after_ref,
    out_ref,
    slot_out_ref,
    slot_lse_ref,
    *,
    rows_at,
):
    row_count, cache_rows, width = cache_ref.shape
    first_row, block_rows = rows_at.start, rows_at.stop - rows_at.start
    kv_heads = width // (2 * HD)
    group = queries_ref.shape[1] // (kv_heads * HD)
    unit = 8
    keys_of = unit * cache_rows
    queries = queries_ref[rows_at, :].astype(F32)
    own = sum(
        ref[pl.ds(ref.shape[0] - row_count + first_row, block_rows), :].astype(F32)
        for ref in (mine_ref, other_ref)
    )
    own = own.astype(BF16).astype(F32)
    key = iota((unit, keys_of), 1) - iota((unit, keys_of), 0) * cache_rows
    lengths = len_ref[...].astype(F32)
    lane = iota((unit, STATS), 1)
    ones = jnp.ones((keys_of, HD), BF16)
    units = range(block_rows // unit)

    def rows_of(u):
        return slice(first_row + u * unit, first_row + (u + 1) * unit)

    pairs = [(u, h) for u in units for h in range(kv_heads)]
    bias = []
    for u in units:
        row = iota((unit, row_count), 0) + (first_row + u * unit)
        length = jnp.sum(
            jnp.where(iota((unit, row_count), 1) == row, lengths, 0.0), axis=1, keepdims=True
        ).astype(jnp.int32)
        bias.append(jnp.where((key >= 0) & (key < length), 0.0, MASKED))
    q, scores, own_scores = [], [], []
    for u, h in pairs:
        at = slice(u * unit, (u + 1) * unit)
        q.append(
            jnp.stack(
                [
                    queries[at, (h * group + i) * HD : (h * group + i + 1) * HD]
                    for i in range(group)
                ],
                axis=0,
            )
        )
        keys = cache_ref[rows_of(u), :, h * 2 * HD : (h * 2 + 1) * HD].reshape(keys_of, HD)
        scores.append(
            lax.dot_general(
                q[-1].reshape(group * unit, HD).astype(BF16),
                keys,
                (((1,), (1,)), ((), ())),
                preferred_element_type=F32,
            ).reshape(group, unit, keys_of)
        )
    for n, (u, h) in enumerate(pairs):
        at = slice(u * unit, (u + 1) * unit)
        own_key = own[at, h * 2 * HD : (h * 2 + 1) * HD]
        own_scores.append(jnp.sum(q[n] * own_key[None], axis=2, keepdims=True) * LOG2_SCALE)
    scores = [scores[n] * LOG2_SCALE + bias[u][None] for n, (u, h) in enumerate(pairs)]
    largest = [
        jnp.maximum(jnp.max(x, axis=2, keepdims=True), y) for x, y in zip(scores, own_scores)
    ]
    weights = [jnp.exp2(x - y).astype(BF16) for x, y in zip(scores, largest)]
    own_weights = [jnp.exp2(x - y) for x, y in zip(own_scores, largest)]
    sums = []
    for n, (u, h) in enumerate(pairs):
        at = slice(u * unit, (u + 1) * unit)
        values = cache_ref[rows_of(u), :, (h * 2 + 1) * HD : (h * 2 + 2) * HD].reshape(keys_of, HD)
        sums.append(
            jnp.dot(
                weights[n].reshape(group * unit, keys_of),
                jnp.concatenate([values, ones], axis=1),
                preferred_element_type=F32,
            ).reshape(group, unit, 2 * HD)
        )
    pieces = [[] for _ in units]
    stats = [jnp.zeros((unit, STATS), F32) for _ in units]
    for n, (u, h) in enumerate(pairs):
        at = slice(u * unit, (u + 1) * unit)
        own_value = own[at, (h * 2 + 1) * HD : (h * 2 + 2) * HD]
        total = sums[n][:, :, HD:] + own_weights[n]
        result = (sums[n][:, :, :HD] + own_weights[n] * own_value[None]) / total
        lse = largest[n] + jnp.log2(total)
        for i in range(group):
            pieces[u].append(result[i])
            stats[u] = jnp.where(lane == h * group + i, lse[i], stats[u])
    out = jnp.concatenate([jnp.concatenate(x, axis=1) for x in pieces], axis=0).astype(BF16)
    out_ref[...] = out
    here = iota((row_count, block_rows), 0) == iota((row_count, block_rows), 1) + first_row
    pick = jnp.dot(
        pick_ref[...], here.astype(F32).astype(BF16), preferred_element_type=F32
    ).astype(BF16)
    slot_out_ref[...] = jnp.dot(pick, out, preferred_element_type=F32)
    lse = jnp.concatenate(stats, axis=0)
    slot_lse_ref[...] = sum(
        jnp.dot(pick, part.astype(BF16), preferred_element_type=F32) for part in split_bf16(lse)
    )


def merge(pick_ref, *refs):
    refs, (out_ref, out_here_ref, sems) = refs[:-3], refs[-3:]
    parts, group_refs = refs[:-4], refs[-4:]
    cached_refs, slot_out_refs, slot_lse_refs = parts[0::3], parts[1::3], parts[2::3]
    width = out_ref.shape[1]
    pick = pick_ref[...]
    arrived = jnp.concatenate(
        [ref[i].astype(F32) for ref in group_refs for i in range(ref.shape[0])], axis=0
    )
    stats = arrived[:, width:]
    arrived_lse = (
        stats
        + pltpu.roll(stats, STATS - LSE_PITCH, 1)
        + pltpu.roll(stats, STATS - 2 * LSE_PITCH, 1)
    )
    cached_lse = sum(ref[...] for ref in slot_lse_refs)
    largest = jnp.maximum(cached_lse, arrived_lse)
    cached_weight = jnp.exp2(cached_lse - largest)
    arrived_weight = jnp.exp2(arrived_lse - largest)
    total = cached_weight + arrived_weight
    cached_weight = cached_weight / total
    arrived_weight = arrived_weight / total
    has = lax.dot_general(
        pick, jnp.ones((pick.shape[0], HD), BF16), TRANSPOSED, preferred_element_type=F32
    )
    copies = []
    for i in range(width // HD):
        at = slice(i * HD, (i + 1) * HD)
        merged = (
            sum(ref[:, at] for ref in slot_out_refs) * cached_weight[:, i : i + 1]
            + arrived[:, at] * arrived_weight[:, i : i + 1]
        )
        placed = lax.dot_general(
            pick, merged.astype(BF16), TRANSPOSED, preferred_element_type=F32
        )
        row = 0
        for ref in cached_refs:
            rows = slice(row, row + ref.shape[0])
            kept = ref[:, at].astype(F32)
            out_here_ref[rows, at] = jnp.where(has[rows] > 0.5, placed[rows], kept).astype(BF16)
            row += ref.shape[0]
        ready = width * (len(copies) + 1) // sems.shape[0]
        if at.stop == ready:
            there = slice(width * len(copies) // sems.shape[0], ready)
            copies.append(
                pltpu.make_async_copy(
                    out_here_ref.at[:, there], out_ref.at[:, there], sems.at[len(copies)]
                )
            )
            copies[-1].start()
    for copy in copies:
        copy.wait()


def compiler_params(megabytes):
    return pltpu.CompilerParams(vmem_limit_bytes=megabytes * 1024 * 1024)


RESIDENT = pl.BlockSpec(memory_space=pltpu.VMEM)
REMAINS = pl.BlockSpec(memory_space=pl.ANY)


def in_vmem(x):
    return pltpu.with_memory_space_constraint(x, pltpu.VMEM)


def in_hbm(x):
    return pltpu.with_memory_space_constraint(x, pltpu.HBM)


def shards(
    prompts, decode_hidden, queries, kv_cache, cache_len, span_len, target_row, w_kv, kv_scale
):
    row_count = decode_hidden.shape[0]
    prompt_rows, features = prompts.shape
    sections = lax.axis_size("section")
    local_width = kv_cache.shape[2]
    query_width = queries.shape[1]
    slots = sections * CAP
    all_rows = prompt_rows + row_count
    scale = kv_scale.reshape(1, -1)
    lengths = cache_len.reshape(1, -1)

    steps = steps_of(sections)
    half = sections // 2
    prompts, decode_hidden, w_kv, scale = map(in_hbm, (prompts, decode_hidden, w_kv, scale))
    target_row, span_len, queries = map(in_hbm, (target_row, span_len, queries))
    kv_cache, lengths = map(in_hbm, (kv_cache, lengths))

    def block_pair(width):
        return [pltpu.VMEM((half, CAP, width), BF16)] * 2

    def swapped(blocks, distance):
        pairs = [(i, i ^ distance) for i in range(sections)]
        return in_vmem(lax.ppermute(blocks, "section", pairs))

    pick, keep, send = pl.pallas_call(
        select_queries,
        in_specs=[RESIDENT, REMAINS],
        out_specs=[RESIDENT] * 3,
        scratch_shapes=[pltpu.VMEM(queries.shape, BF16), pltpu.SemaphoreType.DMA(())],
        out_shape=[pltpu.VMEM((slots, row_count), BF16)] + block_pair(query_width),
        compiler_params=compiler_params(16),
        name="select_queries",
    )(target_row, queries)
    got = swapped(send, steps[0][0])

    def regrouped(blocks, got, steps, done, after):
        return pl.pallas_call(
            functools.partial(regroup, steps=steps, done=done),
            in_specs=[RESIDENT] * 2 + [REMAINS],
            out_specs=[RESIDENT] * 2,
            out_shape=block_pair(blocks.shape[2]),
            compiler_params=compiler_params(16),
            name="regroup",
        )(in_vmem(blocks), got, in_vmem(after))

    edges = (0, 256, 768, 1536, 3072, 5120)
    depth, head = edges[-1], edges[-2]
    rows, w_tail, total, target_here, span_here, lengths = pl.pallas_call(
        functools.partial(project_first, edges=edges),
        in_specs=[REMAINS] * 6,
        out_specs=[RESIDENT] * 6,
        out_shape=[
            pltpu.VMEM((all_rows, depth), BF16),
            pltpu.VMEM((depth - head, local_width), BF16),
            pltpu.VMEM((all_rows, local_width), F32),
            pltpu.VMEM(target_row.shape, jnp.int32),
            pltpu.VMEM(span_len.shape, jnp.int32),
            pltpu.VMEM(lengths.shape, jnp.int32),
        ],
        scratch_shapes=[
            pltpu.VMEM((head, local_width), BF16),
            pltpu.SemaphoreType.DMA((len(edges) - 1, 3)),
            pltpu.SemaphoreType.DMA((3,)),
        ],
        compiler_params=compiler_params(12),
        name="project_first",
    )(prompts, decode_hidden, w_kv, target_row, span_len, lengths)
    keep, send = regrouped(keep, got, steps, 1, total)
    got = swapped(send, steps[1][0])
    theirs, rows_rest, w_mine = pl.pallas_call(
        project_rest,
        in_specs=[REMAINS] * 4 + [RESIDENT] * 3 + [REMAINS],
        out_specs=[RESIDENT] * 3,
        out_shape=[
            pltpu.VMEM((all_rows, local_width), BF16),
            pltpu.VMEM((all_rows, features - depth), BF16),
            pltpu.VMEM((features, local_width), BF16),
        ],
        scratch_shapes=[
            pltpu.VMEM((features - depth, local_width), BF16),
            pltpu.VMEM((1, local_width), F32),
            pltpu.SemaphoreType.DMA((5,)),
        ],
        compiler_params=compiler_params(16),
        name="project_rest",
    )(prompts, decode_hidden, w_kv, scale, *map(in_vmem, (rows, w_tail, total, keep)))
    theirs, got = lax.optimization_barrier((theirs, got))
    got = in_vmem(got)
    other = in_vmem(lax.ppermute(theirs, "tp", [(0, 1), (1, 0)]))

    mine = []
    pieces = max(len(steps) - 2, 1)
    bounds = [all_rows * i // (16 * pieces) * 16 for i in range(pieces)] + [all_rows]
    after = theirs
    for piece, at in enumerate(spans(bounds)):
        if piece + 2 < len(steps):
            keep, send = regrouped(keep, got, steps, piece + 2, after)
            got = swapped(send, steps[piece + 2][0])
        last = piece == pieces - 1
        extra = [kv_cache, queries] if last else []
        part, *here = pl.pallas_call(
            functools.partial(project_mine, at=at, last=last),
            in_specs=[RESIDENT] * 3 + [REMAINS] * (2 + len(extra)),
            out_specs=[RESIDENT] * (1 + len(extra)),
            out_shape=[pltpu.VMEM((at.stop - at.start, local_width), BF16)]
            + [pltpu.VMEM(x.shape, BF16) for x in extra],
            scratch_shapes=[pltpu.VMEM((1, local_width), F32), pltpu.SemaphoreType.DMA((3,))],
            compiler_params=compiler_params(16),
            name="project_mine",
        )(*map(in_vmem, (rows, rows_rest, w_mine)), scale, in_vmem(keep), *extra)
        after = part
        mine.append(in_vmem(part))
    kv_here, queries_here = map(in_vmem, here)

    padded = -(-span_len.shape[1] // 16) * 16
    prepared = pl.pallas_call(
        functools.partial(prepare_arrived, row_count=row_count),
        in_specs=[RESIDENT] * 4,
        out_specs=[RESIDENT] * 3,
        out_shape=[
            pltpu.VMEM((padded, query_width), BF16),
            pltpu.VMEM((padded, sections * PITCH), BF16),
            pltpu.VMEM((padded, prompt_rows), F32),
        ],
        compiler_params=compiler_params(16),
        name="prepare_arrived",
    )(in_vmem(target_here), in_vmem(span_here), in_vmem(keep), got)
    answer_width = query_width + STATS
    keep, send = pl.pallas_call(
        attend_arrived,
        in_specs=[RESIDENT] * (4 + len(mine)),
        out_specs=[RESIDENT] * 2,
        out_shape=block_pair(answer_width),
        compiler_params=compiler_params(24),
        name="attend_arrived",
    )(*map(in_vmem, prepared), other, *mine)

    steps = answer_steps_of(sections)
    shares = []
    calls = len(steps) + 1
    bounds = [row_count * i // (16 * calls) * 16 for i in range(calls)] + [row_count]
    for done, at in enumerate(spans(bounds)):
        last = done == len(steps)
        if not last:
            got = swapped(send, steps[done][0])
        share = pl.pallas_call(
            functools.partial(attend_cache, rows_at=at),
            in_specs=[RESIDENT] * 6 + [REMAINS],
            out_specs=[RESIDENT] * 3,
            out_shape=[
                pltpu.VMEM((at.stop - at.start, query_width), BF16),
                pltpu.VMEM((slots, query_width), F32),
                pltpu.VMEM((slots, STATS), F32),
            ],
            compiler_params=compiler_params(24),
            name="attend_cache",
        )(queries_here, kv_here, in_vmem(lengths), mine[-1], other, in_vmem(pick), in_vmem(keep))
        shares += share
        if done + 1 < len(steps):
            keep, send = regrouped(keep, got, steps, done + 1, share[2])
        elif not last:
            size = sections // 4
            keep, *sent = pl.pallas_call(
                functools.partial(fan_out, step=steps[-1]),
                in_specs=[RESIDENT] * 2 + [REMAINS],
                out_specs=[RESIDENT] * 4,
                out_shape=[pltpu.VMEM((size, CAP, answer_width), BF16)] * 4,
                compiler_params=compiler_params(16),
                name="fan_out",
            )(in_vmem(keep), got, in_vmem(share[2]))
            groups = [in_vmem(keep)]
            groups += [swapped(blocks, (i + 1) * size) for i, blocks in enumerate(sent)]

    return pl.pallas_call(
        merge,
        in_specs=[RESIDENT] * (5 + len(shares)),
        out_specs=REMAINS,
        out_shape=jax.ShapeDtypeStruct((row_count, query_width), BF16),
        scratch_shapes=[pltpu.VMEM((row_count, query_width), BF16), pltpu.SemaphoreType.DMA((4,))],
        compiler_params=compiler_params(24),
        name="merge",
    )(*map(in_vmem, (pick, *shares)), *groups)


def solution(mesh):
    in_specs = (
        P(("groups", "section"), "tp"),
        P(("groups", "section"), "tp"),
        P(("groups", "section"), "tp"),
        P(("groups", "section"), None, "tp"),
        P(("groups", "section")),
        P("groups", None),
        P("groups", None),
        P("tp", None),
        P(),
    )
    out_specs = P(("groups", "section"), "tp")
    return jax.shard_map(shards, mesh=mesh, in_specs=in_specs, out_specs=out_specs, check_vma=False)
```

```python
import functools
import math

import jax
import jax.numpy as jnp
from jax import lax
from jax.experimental import pallas as pl
from jax.experimental.pallas import tpu as pltpu
from jax.sharding import PartitionSpec as P

HD = 128
CAP = 2
STATS = 128
MASKED = -1e30
LSE_PITCH = 40
PITCH = 8
LOG2_SCALE = HD ** (-0.5) * math.log2(math.e)
F32 = jnp.float32
BF16 = jnp.bfloat16
TRANSPOSED = (((0,), (0,)), ((), ()))


def iota(shape, dim):
    return lax.broadcasted_iota(jnp.int32, shape, dim)


def one_hot(shape, dim, index):
    return (iota(shape, dim) == index).astype(F32).astype(BF16)


def pick_rows(target_ref, row_count):
    sections, requests = target_ref.shape
    shape = (sections * CAP, requests)
    position = lax.axis_index("section")
    slot_id = iota(shape, 0)
    table = jnp.zeros(shape, jnp.int32)
    for k in range(sections):
        mine = (slot_id >= k * CAP) & (slot_id < (k + 1) * CAP)
        table = jnp.where(mine, target_ref[pl.ds(position ^ k, 1), :], table)
    local = table - position * row_count
    here = (local >= 0) & (local < row_count)
    square = (requests, requests)
    earlier = jnp.dot(
        here.astype(F32).astype(BF16),
        (iota(square, 0) < iota(square, 1)).astype(F32).astype(BF16),
        preferred_element_type=F32,
    )
    chosen = here & (earlier == lax.rem(slot_id, CAP).astype(F32))
    row = jnp.max(jnp.where(chosen, local.astype(F32), -1.0), axis=1, keepdims=True)
    return one_hot((shape[0], row_count), 1, row.astype(jnp.int32))


def steps_of(sections):
    steps = []
    bit = sections // 2
    while bit:
        sent = [k for k in range(sections) if k & bit]
        steps.append((bit, sent, [k for k in range(sections) if not k & bit]))
        bit //= 2
    return steps


def answer_steps_of(sections):
    steps = []
    bit = 1
    while 4 * bit < sections:
        sent = [k for k in range(sections) if k & bit]
        steps.append((bit, sent, [k for k in range(sections) if not k & bit]))
        bit *= 2
    return steps


def rearrange(step, kept_ref, got_ref, *out):
    where = {k: (got_ref, i) for i, k in enumerate(step[1])}
    where |= {k: (kept_ref, i) for i, k in enumerate(step[2])}
    for out_ref, blocks in out:
        for i, k in enumerate(blocks):
            ref, at = where[k]
            out_ref[i] = ref[at]


def regroup(kept_ref, got_ref, after_ref, keep_ref, send_ref, *, steps, done):
    _, sent, kept = steps[done]
    rearrange(steps[done - 1], kept_ref, got_ref, (send_ref, sent), (keep_ref, kept))


def fan_out(kept_ref, got_ref, after_ref, *out_refs, step):
    size = out_refs[0].shape[0]
    groups = [range(m * size, (m + 1) * size) for m in range(len(out_refs))]
    rearrange(step, kept_ref, got_ref, *zip(out_refs, groups))


def all_blocks(steps, kept_ref, got_ref):
    where = {k: got_ref[i] for i, k in enumerate(steps[-1][1])}
    where |= {k: kept_ref[i] for i, k in enumerate(steps[-1][2])}
    return jnp.concatenate([where[k].astype(F32) for k in range(len(where))], axis=0)


def select_queries(target_ref, queries_ref, pick_ref, keep_ref, send_ref):
    _, sent, kept = steps_of(target_ref.shape[0])[0]
    pick = pick_rows(target_ref, queries_ref.shape[0])
    pick_ref[...] = pick
    asked = jnp.dot(pick, queries_ref[...], preferred_element_type=F32)
    for ref, blocks in ((send_ref, sent), (keep_ref, kept)):
        for i, k in enumerate(blocks):
            ref[i] = asked[k * CAP : (k + 1) * CAP].astype(BF16)


def spans(edges):
    return [slice(a, b) for a, b in zip(edges[:-1], edges[1:])]


def load_rows(prompts_ref, hidden_ref, there, rows_ref, here, sems):
    prompt_rows = prompts_ref.shape[0]
    return [
        pltpu.make_async_copy(
            prompts_ref.at[:, there], rows_ref.at[:prompt_rows, here], sems.at[0]
        ),
        pltpu.make_async_copy(
            hidden_ref.at[:, there], rows_ref.at[prompt_rows:, here], sems.at[1]
        ),
    ]


def channels(offset, width):
    tp = lax.axis_index("tp")
    return pl.ds(pl.multiple_of(((tp + offset) & 1) * width, width), width)


def project_first(
    prompts_ref,
    hidden_ref,
    w_ref,
    target_ref,
    span_ref,
    len_ref,
    rows_ref,
    w_tail_ref,
    total_ref,
    target_here_ref,
    span_here_ref,
    len_here_ref,
    w_head_ref,
    sems,
    small_sems,
    *,
    edges,
):
    theirs = channels(1, total_ref.shape[1])
    chunks = spans(edges)
    head = edges[-2]
    waits = []
    for c, at in enumerate(chunks):
        here = at if at.stop <= head else slice(0, at.stop - head)
        w_here_ref = w_head_ref if at.stop <= head else w_tail_ref
        copies = load_rows(prompts_ref, hidden_ref, at, rows_ref, at, sems.at[c])
        copies.append(
            pltpu.make_async_copy(w_ref.at[at, theirs], w_here_ref.at[here, :], sems.at[c, 2])
        )
        for copy in copies:
            copy.start()
        waits.append(copies)
    small = [
        pltpu.make_async_copy(target_ref, target_here_ref, small_sems.at[0]),
        pltpu.make_async_copy(span_ref, span_here_ref, small_sems.at[1]),
        pltpu.make_async_copy(len_ref, len_here_ref, small_sems.at[2]),
    ]
    for copy in small:
        copy.start()
    for c, at in enumerate(chunks):
        for copy in waits[c]:
            copy.wait()
        if at.stop <= head:
            part = jnp.dot(rows_ref[:, at], w_head_ref[at, :], preferred_element_type=F32)
            if c == 0:
                total_ref[...] = part
            else:
                total_ref[...] += part
    for copy in small:
        copy.wait()


def project_rest(
    prompts_ref,
    hidden_ref,
    w_ref,
    scale_ref,
    rows_ref,
    w_tail_ref,
    total_ref,
    after_ref,
    theirs_ref,
    rows_rest_ref,
    w_mine_ref,
    w_rest_ref,
    scale_here_ref,
    sems,
):
    width = theirs_ref.shape[1]
    theirs, mine = channels(1, width), channels(0, width)
    depth = rows_ref.shape[1]
    head = depth - w_tail_ref.shape[0]
    rest = slice(depth, depth + rows_rest_ref.shape[1])
    copies = load_rows(prompts_ref, hidden_ref, rest, rows_rest_ref, slice(None), sems)
    copies += [
        pltpu.make_async_copy(w_ref.at[rest, theirs], w_rest_ref, sems.at[2]),
        pltpu.make_async_copy(scale_ref.at[:, theirs], scale_here_ref, sems.at[3]),
        pltpu.make_async_copy(w_ref.at[:, mine], w_mine_ref, sems.at[4]),
    ]
    for copy in copies:
        copy.start()
    total = total_ref[...] + jnp.dot(
        rows_ref[:, head:], w_tail_ref[...], preferred_element_type=F32
    )
    for copy in copies[:-1]:
        copy.wait()
    total += jnp.dot(rows_rest_ref[...], w_rest_ref[...], preferred_element_type=F32)
    theirs_ref[...] = (total * scale_here_ref[...]).astype(BF16)
    copies[-1].wait()


def project_mine(rows_ref, rows_rest_ref, w_mine_ref, scale_ref, after_ref, *refs, at, last):
    refs, (scale_here_ref, sems) = refs[:-2], refs[-2:]
    if last:
        cache_ref, queries_ref, out_ref, cache_here_ref, queries_here_ref = refs
    else:
        (out_ref,) = refs
    mine = channels(0, out_ref.shape[1])
    copies = [pltpu.make_async_copy(scale_ref.at[:, mine], scale_here_ref, sems.at[0])]
    if last:
        copies.append(pltpu.make_async_copy(queries_ref, queries_here_ref, sems.at[1]))
        copies.append(pltpu.make_async_copy(cache_ref, cache_here_ref, sems.at[2]))
    for copy in copies:
        copy.start()
    depth = rows_ref.shape[1]
    count = at.stop - at.start
    block = count // 2 if count % 32 == 0 else count
    for m in spans(range(0, count + 1, block)):
        there = slice(at.start + m.start, at.start + m.stop)
        total = jnp.dot(rows_ref[there, :], w_mine_ref[:depth, :], preferred_element_type=F32)
        total += jnp.dot(
            rows_rest_ref[there, :], w_mine_ref[depth:, :], preferred_element_type=F32
        )
        if m.start == 0:
            copies[0].wait()
        out_ref[m, :] = (total * scale_here_ref[...]).astype(BF16)
    for copy in copies[1:]:
        copy.wait()


def split_bf16(x):
    high = x.astype(BF16).astype(F32)
    middle = (x - high).astype(BF16).astype(F32)
    return high, middle, (x - high - middle).astype(BF16).astype(F32)


def request_slots(target_ref, span_ref, row_count, padded):
    sections, requests = target_ref.shape
    position = lax.axis_index("section")
    target = target_ref[pl.ds(position, 1), :].astype(F32)
    span = span_ref[pl.ds(position, 1), :].astype(F32)
    diagonal = iota((padded, requests), 0) == iota((padded, requests), 1)
    target_col = jnp.sum(jnp.where(diagonal, target, 0.0), axis=1, keepdims=True)
    span_col = jnp.sum(jnp.where(diagonal, span, 0.0), axis=1, keepdims=True)
    section_row = jnp.zeros_like(target)
    section_col = jnp.zeros_like(target_col)
    for s in range(1, sections):
        section_row = section_row + (target >= s * row_count).astype(F32)
        section_col = section_col + (target_col >= s * row_count).astype(F32)
    before = (section_row == section_col) & (
        iota((padded, requests), 1) < iota((padded, requests), 0)
    )
    rank_col = jnp.sum(before.astype(F32), axis=1, keepdims=True).astype(jnp.int32)
    real = iota((padded, 1), 0) < requests
    section_col = jnp.where(real, section_col.astype(jnp.int32), -1)
    return section_col, rank_col, span_col.astype(jnp.int32)


def prepare_arrived(
    target_ref, span_ref, kept_ref, got_ref, rows_ref, slot_of_ref, bias_ref, *, row_count
):
    sections, requests = target_ref.shape
    padded, prompt_rows = bias_ref.shape
    span_rows = prompt_rows // requests
    section_col, rank_col, span_col = request_slots(target_ref, span_ref, row_count, padded)
    block = section_col ^ lax.axis_index("section")
    slot = jnp.where(section_col >= 0, block * PITCH + rank_col, -1)
    slot_of_ref[...] = one_hot((padded, sections * PITCH), 1, slot)
    slot = jnp.where(section_col >= 0, block * CAP + rank_col, -1)
    rows_ref[...] = jnp.dot(
        one_hot((padded, sections * CAP), 1, slot),
        all_blocks(steps_of(sections), kept_ref, got_ref).astype(BF16),
        preferred_element_type=F32,
    ).astype(BF16)
    key = iota((padded, prompt_rows), 1) - iota((padded, prompt_rows), 0) * span_rows
    bias_ref[...] = jnp.where((key >= 0) & (key < span_col), 0.0, MASKED)


def attend_arrived(rows_ref, slot_of_ref, bias_ref, other_ref, *refs):
    mine_refs, (keep_ref, send_ref) = refs[:-2], refs[-2:]
    padded, prompt_rows = bias_ref.shape
    kv_heads = other_ref.shape[1] // (2 * HD)
    group = rows_ref.shape[1] // (kv_heads * HD)
    rows = rows_ref[...]
    slot_of = slot_of_ref[...]
    bias = bias_ref[...]
    mine = jnp.concatenate([ref[...] for ref in mine_refs], axis=0)
    kv = (mine[:prompt_rows].astype(F32) + other_ref[:prompt_rows, :].astype(F32)).astype(BF16)
    scores = []
    for h in range(kv_heads):
        stacked = jnp.concatenate(
            [rows[:, (h * group + i) * HD : (h * group + i + 1) * HD] for i in range(group)],
            axis=0,
        )
        keys = kv[:, h * 2 * HD : (h * 2 + 1) * HD]
        scores.append(
            lax.dot_general(
                stacked, keys, (((1,), (1,)), ((), ())), preferred_element_type=F32
            )
        )
    scores = [
        x.reshape(group, padded, prompt_rows) * LOG2_SCALE + bias[None] for x in scores
    ]
    largest = [jnp.max(x, axis=2, keepdims=True) for x in scores]
    weights = [jnp.exp2(x - y) for x, y in zip(scores, largest)]
    totals = [jnp.sum(x, axis=2, keepdims=True) for x in weights]
    lane = iota((padded, STATS), 1)
    lse = jnp.zeros((padded, STATS), F32)
    pieces = []
    for h in range(kv_heads):
        values = jnp.dot(
            weights[h].reshape(group * padded, prompt_rows).astype(BF16),
            kv[:, (h * 2 + 1) * HD : (h * 2 + 2) * HD],
            preferred_element_type=F32,
        ).reshape(group, padded, HD)
        values = values / totals[h]
        head_lse = largest[h] + jnp.log2(totals[h])
        for i in range(group):
            pieces.append(values[i])
            lse = jnp.where(lane == h * group + i, head_lse[i], lse)
    high, middle, low = split_bf16(lse)
    stats = high + pltpu.roll(middle, LSE_PITCH, 1) + pltpu.roll(low, 2 * LSE_PITCH, 1)
    result = jnp.concatenate(pieces + [stats], axis=1).astype(BF16)
    answers = lax.dot_general(slot_of, result, TRANSPOSED, preferred_element_type=F32)
    _, sent, kept = answer_steps_of(2 * keep_ref.shape[0])[0]
    for ref, blocks in ((send_ref, sent), (keep_ref, kept)):
        for i, k in enumerate(blocks):
            ref[i] = answers[k * PITCH : k * PITCH + CAP].astype(BF16)


def attend_cache(
    queries_ref,
    cache_ref,
    len_ref,
    mine_ref,
    other_ref,
    pick_ref,
    after_ref,
    out_ref,
    slot_out_ref,
    slot_lse_ref,
    *,
    rows_at,
):
    row_count, cache_rows, width = cache_ref.shape
    first_row, block_rows = rows_at.start, rows_at.stop - rows_at.start
    kv_heads = width // (2 * HD)
    group = queries_ref.shape[1] // (kv_heads * HD)
    unit = 8
    keys_of = unit * cache_rows
    queries = queries_ref[rows_at, :].astype(F32)
    own = sum(
        ref[pl.ds(ref.shape[0] - row_count + first_row, block_rows), :].astype(F32)
        for ref in (mine_ref, other_ref)
    )
    own = own.astype(BF16).astype(F32)
    key = iota((unit, keys_of), 1) - iota((unit, keys_of), 0) * cache_rows
    lengths = len_ref[...].astype(F32)
    lane = iota((unit, STATS), 1)
    ones = jnp.ones((keys_of, HD), BF16)
    units = range(block_rows // unit)

    def rows_of(u):
        return slice(first_row + u * unit, first_row + (u + 1) * unit)

    pairs = [(u, h) for u in units for h in range(kv_heads)]
    bias = []
    for u in units:
        row = iota((unit, row_count), 0) + (first_row + u * unit)
        length = jnp.sum(
            jnp.where(iota((unit, row_count), 1) == row, lengths, 0.0), axis=1, keepdims=True
        ).astype(jnp.int32)
        bias.append(jnp.where((key >= 0) & (key < length), 0.0, MASKED))
    q, scores, own_scores = [], [], []
    for u, h in pairs:
        at = slice(u * unit, (u + 1) * unit)
        q.append(
            jnp.stack(
                [
                    queries[at, (h * group + i) * HD : (h * group + i + 1) * HD]
                    for i in range(group)
                ],
                axis=0,
            )
        )
        keys = cache_ref[rows_of(u), :, h * 2 * HD : (h * 2 + 1) * HD].reshape(keys_of, HD)
        scores.append(
            lax.dot_general(
                q[-1].reshape(group * unit, HD).astype(BF16),
                keys,
                (((1,), (1,)), ((), ())),
                preferred_element_type=F32,
            ).reshape(group, unit, keys_of)
        )
    for n, (u, h) in enumerate(pairs):
        at = slice(u * unit, (u + 1) * unit)
        own_key = own[at, h * 2 * HD : (h * 2 + 1) * HD]
        own_scores.append(jnp.sum(q[n] * own_key[None], axis=2, keepdims=True) * LOG2_SCALE)
    scores = [scores[n] * LOG2_SCALE + bias[u][None] for n, (u, h) in enumerate(pairs)]
    largest = [
        jnp.maximum(jnp.max(x, axis=2, keepdims=True), y) for x, y in zip(scores, own_scores)
    ]
    weights = [jnp.exp2(x - y).astype(BF16) for x, y in zip(scores, largest)]
    own_weights = [jnp.exp2(x - y) for x, y in zip(own_scores, largest)]
    sums = []
    for n, (u, h) in enumerate(pairs):
        at = slice(u * unit, (u + 1) * unit)
        values = cache_ref[rows_of(u), :, (h * 2 + 1) * HD : (h * 2 + 2) * HD].reshape(keys_of, HD)
        sums.append(
            jnp.dot(
                weights[n].reshape(group * unit, keys_of),
                jnp.concatenate([values, ones], axis=1),
                preferred_element_type=F32,
            ).reshape(group, unit, 2 * HD)
        )
    pieces = [[] for _ in units]
    stats = [jnp.zeros((unit, STATS), F32) for _ in units]
    for n, (u, h) in enumerate(pairs):
        at = slice(u * unit, (u + 1) * unit)
        own_value = own[at, (h * 2 + 1) * HD : (h * 2 + 2) * HD]
        total = sums[n][:, :, HD:] + own_weights[n]
        result = (sums[n][:, :, :HD] + own_weights[n] * own_value[None]) / total
        lse = largest[n] + jnp.log2(total)
        for i in range(group):
            pieces[u].append(result[i])
            stats[u] = jnp.where(lane == h * group + i, lse[i], stats[u])
    out = jnp.concatenate([jnp.concatenate(x, axis=1) for x in pieces], axis=0).astype(BF16)
    out_ref[...] = out
    here = iota((row_count, block_rows), 0) == iota((row_count, block_rows), 1) + first_row
    pick = jnp.dot(
        pick_ref[...], here.astype(F32).astype(BF16), preferred_element_type=F32
    ).astype(BF16)
    slot_out_ref[...] = jnp.dot(pick, out, preferred_element_type=F32)
    lse = jnp.concatenate(stats, axis=0)
    slot_lse_ref[...] = sum(
        jnp.dot(pick, part.astype(BF16), preferred_element_type=F32) for part in split_bf16(lse)
    )


def merge(pick_ref, *refs):
    refs, (out_ref, out_here_ref, sems) = refs[:-3], refs[-3:]
    parts, group_refs = refs[:-4], refs[-4:]
    cached_refs, slot_out_refs, slot_lse_refs = parts[0::3], parts[1::3], parts[2::3]
    width = out_ref.shape[1]
    pick = pick_ref[...]
    arrived = jnp.concatenate(
        [ref[i].astype(F32) for ref in group_refs for i in range(ref.shape[0])], axis=0
    )
    stats = arrived[:, width:]
    arrived_lse = (
        stats
        + pltpu.roll(stats, STATS - LSE_PITCH, 1)
        + pltpu.roll(stats, STATS - 2 * LSE_PITCH, 1)
    )
    cached_lse = sum(ref[...] for ref in slot_lse_refs)
    largest = jnp.maximum(cached_lse, arrived_lse)
    cached_weight = jnp.exp2(cached_lse - largest)
    arrived_weight = jnp.exp2(arrived_lse - largest)
    total = cached_weight + arrived_weight
    cached_weight = cached_weight / total
    arrived_weight = arrived_weight / total
    has = lax.dot_general(
        pick, jnp.ones((pick.shape[0], HD), BF16), TRANSPOSED, preferred_element_type=F32
    )
    copies = []
    for i in range(width // HD):
        at = slice(i * HD, (i + 1) * HD)
        merged = (
            sum(ref[:, at] for ref in slot_out_refs) * cached_weight[:, i : i + 1]
            + arrived[:, at] * arrived_weight[:, i : i + 1]
        )
        placed = lax.dot_general(
            pick, merged.astype(BF16), TRANSPOSED, preferred_element_type=F32
        )
        row = 0
        for ref in cached_refs:
            rows = slice(row, row + ref.shape[0])
            kept = ref[:, at].astype(F32)
            out_here_ref[rows, at] = jnp.where(has[rows] > 0.5, placed[rows], kept).astype(BF16)
            row += ref.shape[0]
        ready = width * (len(copies) + 1) // sems.shape[0]
        if at.stop == ready:
            there = slice(width * len(copies) // sems.shape[0], ready)
            copies.append(
                pltpu.make_async_copy(
                    out_here_ref.at[:, there], out_ref.at[:, there], sems.at[len(copies)]
                )
            )
            copies[-1].start()
    for copy in copies:
        copy.wait()


def compiler_params(megabytes):
    return pltpu.CompilerParams(vmem_limit_bytes=megabytes * 1024 * 1024)


RESIDENT = pl.BlockSpec(memory_space=pltpu.VMEM)
REMAINS = pl.BlockSpec(memory_space=pl.ANY)


def in_vmem(x):
    return pltpu.with_memory_space_constraint(x, pltpu.VMEM)


def in_hbm(x):
    return pltpu.with_memory_space_constraint(x, pltpu.HBM)


def shards(
    prompts, decode_hidden, queries, kv_cache, cache_len, span_len, target_row, w_kv, kv_scale
):
    row_count = decode_hidden.shape[0]
    prompt_rows, features = prompts.shape
    sections = lax.axis_size("section")
    local_width = kv_cache.shape[2]
    query_width = queries.shape[1]
    slots = sections * CAP
    all_rows = prompt_rows + row_count
    scale = kv_scale.reshape(1, -1)
    lengths = cache_len.reshape(1, -1)

    steps = steps_of(sections)
    half = sections // 2
    prompts, decode_hidden, w_kv, scale = map(in_hbm, (prompts, decode_hidden, w_kv, scale))
    target_row, span_len, queries = map(in_hbm, (target_row, span_len, queries))
    kv_cache, lengths = map(in_hbm, (kv_cache, lengths))

    def block_pair(width):
        return [pltpu.VMEM((half, CAP, width), BF16)] * 2

    def swapped(blocks, distance):
        pairs = [(i, i ^ distance) for i in range(sections)]
        return in_vmem(lax.ppermute(blocks, "section", pairs))

    pick, keep, send = pl.pallas_call(
        select_queries,
        in_specs=[RESIDENT, RESIDENT],
        out_specs=[RESIDENT] * 3,
        out_shape=[pltpu.VMEM((slots, row_count), BF16)] + block_pair(query_width),
        compiler_params=compiler_params(16),
        name="select_queries",
    )(target_row, queries)
    got = swapped(send, steps[0][0])

    def regrouped(blocks, got, steps, done, after):
        return pl.pallas_call(
            functools.partial(regroup, steps=steps, done=done),
            in_specs=[RESIDENT] * 2 + [REMAINS],
            out_specs=[RESIDENT] * 2,
            out_shape=block_pair(blocks.shape[2]),
            compiler_params=compiler_params(16),
            name="regroup",
        )(in_vmem(blocks), got, in_vmem(after))

    edges = (0, 256, 768, 1536, 2560, 4096)
    depth, head = edges[-1], edges[-2]
    rows, w_tail, total, target_here, span_here, lengths = pl.pallas_call(
        functools.partial(project_first, edges=edges),
        in_specs=[REMAINS] * 6,
        out_specs=[RESIDENT] * 6,
        out_shape=[
            pltpu.VMEM((all_rows, depth), BF16),
            pltpu.VMEM((depth - head, local_width), BF16),
            pltpu.VMEM((all_rows, local_width), F32),
            pltpu.VMEM(target_row.shape, jnp.int32),
            pltpu.VMEM(span_len.shape, jnp.int32),
            pltpu.VMEM(lengths.shape, jnp.int32),
        ],
        scratch_shapes=[
            pltpu.VMEM((head, local_width), BF16),
            pltpu.SemaphoreType.DMA((len(edges) - 1, 3)),
            pltpu.SemaphoreType.DMA((3,)),
        ],
        compiler_params=compiler_params(12),
        name="project_first",
    )(prompts, decode_hidden, w_kv, target_row, span_len, lengths)
    keep, send = regrouped(keep, got, steps, 1, total)
    got = swapped(send, steps[1][0])
    theirs, rows_rest, w_mine = pl.pallas_call(
        project_rest,
        in_specs=[REMAINS] * 4 + [RESIDENT] * 3 + [REMAINS],
        out_specs=[RESIDENT] * 3,
        out_shape=[
            pltpu.VMEM((all_rows, local_width), BF16),
            pltpu.VMEM((all_rows, features - depth), BF16),
            pltpu.VMEM((features, local_width), BF16),
        ],
        scratch_shapes=[
            pltpu.VMEM((features - depth, local_width), BF16),
            pltpu.VMEM((1, local_width), F32),
            pltpu.SemaphoreType.DMA((5,)),
        ],
        compiler_params=compiler_params(16),
        name="project_rest",
    )(prompts, decode_hidden, w_kv, scale, *map(in_vmem, (rows, w_tail, total, keep)))
    theirs, got = lax.optimization_barrier((theirs, got))
    got = in_vmem(got)
    other = in_vmem(lax.ppermute(theirs, "tp", [(0, 1), (1, 0)]))

    mine = []
    pieces = max(len(steps) - 2, 1)
    bounds = [all_rows * i // (16 * pieces) * 16 for i in range(pieces)] + [all_rows]
    after = theirs
    for piece, at in enumerate(spans(bounds)):
        if piece + 2 < len(steps):
            keep, send = regrouped(keep, got, steps, piece + 2, after)
            got = swapped(send, steps[piece + 2][0])
        last = piece == pieces - 1
        extra = [kv_cache, queries] if last else []
        part, *here = pl.pallas_call(
            functools.partial(project_mine, at=at, last=last),
            in_specs=[RESIDENT] * 3 + [REMAINS] * (2 + len(extra)),
            out_specs=[RESIDENT] * (1 + len(extra)),
            out_shape=[pltpu.VMEM((at.stop - at.start, local_width), BF16)]
            + [pltpu.VMEM(x.shape, BF16) for x in extra],
            scratch_shapes=[pltpu.VMEM((1, local_width), F32), pltpu.SemaphoreType.DMA((3,))],
            compiler_params=compiler_params(16),
            name="project_mine",
        )(*map(in_vmem, (rows, rows_rest, w_mine)), scale, in_vmem(keep), *extra)
        after = part
        mine.append(in_vmem(part))
    kv_here, queries_here = map(in_vmem, here)

    padded = -(-span_len.shape[1] // 16) * 16
    prepared = pl.pallas_call(
        functools.partial(prepare_arrived, row_count=row_count),
        in_specs=[RESIDENT] * 4,
        out_specs=[RESIDENT] * 3,
        out_shape=[
            pltpu.VMEM((padded, query_width), BF16),
            pltpu.VMEM((padded, sections * PITCH), BF16),
            pltpu.VMEM((padded, prompt_rows), F32),
        ],
        compiler_params=compiler_params(16),
        name="prepare_arrived",
    )(in_vmem(target_here), in_vmem(span_here), in_vmem(keep), got)
    answer_width = query_width + STATS
    keep, send = pl.pallas_call(
        attend_arrived,
        in_specs=[RESIDENT] * (4 + len(mine)),
        out_specs=[RESIDENT] * 2,
        out_shape=block_pair(answer_width),
        compiler_params=compiler_params(24),
        name="attend_arrived",
    )(*map(in_vmem, prepared), other, *mine)

    steps = answer_steps_of(sections)
    shares = []
    calls = len(steps) + 1
    bounds = [row_count * i // (16 * calls) * 16 for i in range(calls)] + [row_count]
    for done, at in enumerate(spans(bounds)):
        last = done == len(steps)
        if not last:
            got = swapped(send, steps[done][0])
        share = pl.pallas_call(
            functools.partial(attend_cache, rows_at=at),
            in_specs=[RESIDENT] * 6 + [REMAINS],
            out_specs=[RESIDENT] * 3,
            out_shape=[
                pltpu.VMEM((at.stop - at.start, query_width), BF16),
                pltpu.VMEM((slots, query_width), F32),
                pltpu.VMEM((slots, STATS), F32),
            ],
            compiler_params=compiler_params(24),
            name="attend_cache",
        )(queries_here, kv_here, in_vmem(lengths), mine[-1], other, in_vmem(pick), in_vmem(keep))
        shares += share
        if done + 1 < len(steps):
            keep, send = regrouped(keep, got, steps, done + 1, share[2])
        elif not last:
            size = sections // 4
            keep, *sent = pl.pallas_call(
                functools.partial(fan_out, step=steps[-1]),
                in_specs=[RESIDENT] * 2 + [REMAINS],
                out_specs=[RESIDENT] * 4,
                out_shape=[pltpu.VMEM((size, CAP, answer_width), BF16)] * 4,
                compiler_params=compiler_params(16),
                name="fan_out",
            )(in_vmem(keep), got, in_vmem(share[2]))
            groups = [in_vmem(keep)]
            groups += [swapped(blocks, (i + 1) * size) for i, blocks in enumerate(sent)]

    return pl.pallas_call(
        merge,
        in_specs=[RESIDENT] * (5 + len(shares)),
        out_specs=REMAINS,
        out_shape=jax.ShapeDtypeStruct((row_count, query_width), BF16),
        scratch_shapes=[pltpu.VMEM((row_count, query_width), BF16), pltpu.SemaphoreType.DMA((4,))],
        compiler_params=compiler_params(24),
        name="merge",
    )(*map(in_vmem, (pick, *shares)), *groups)


def solution(mesh):
    in_specs = (
        P(("groups", "section"), "tp"),
        P(("groups", "section"), "tp"),
        P(("groups", "section"), "tp"),
        P(("groups", "section"), None, "tp"),
        P(("groups", "section")),
        P("groups", None),
        P("groups", None),
        P("tp", None),
        P(),
    )
    out_specs = P(("groups", "section"), "tp")
    return jax.shard_map(shards, mesh=mesh, in_specs=in_specs, out_specs=out_specs, check_vma=False)
```

```python
import functools
import math

import jax
import jax.numpy as jnp
from jax import lax
from jax.experimental import pallas as pl
from jax.experimental.pallas import tpu as pltpu
from jax.sharding import PartitionSpec as P

HD = 128
CAP = 2
STATS = 128
MASKED = -1e30
LSE_PITCH = 40
PITCH = 8
LOG2_SCALE = HD ** (-0.5) * math.log2(math.e)
F32 = jnp.float32
BF16 = jnp.bfloat16
TRANSPOSED = (((0,), (0,)), ((), ()))


def iota(shape, dim):
    return lax.broadcasted_iota(jnp.int32, shape, dim)


def one_hot(shape, dim, index):
    return (iota(shape, dim) == index).astype(F32).astype(BF16)


def pick_rows(target_ref, row_count):
    sections, requests = target_ref.shape
    shape = (sections * CAP, requests)
    position = lax.axis_index("section")
    slot_id = iota(shape, 0)
    table = jnp.zeros(shape, jnp.int32)
    for k in range(sections):
        mine = (slot_id >= k * CAP) & (slot_id < (k + 1) * CAP)
        table = jnp.where(mine, target_ref[pl.ds(position ^ k, 1), :], table)
    local = table - position * row_count
    here = (local >= 0) & (local < row_count)
    square = (requests, requests)
    earlier = jnp.dot(
        here.astype(F32).astype(BF16),
        (iota(square, 0) < iota(square, 1)).astype(F32).astype(BF16),
        preferred_element_type=F32,
    )
    chosen = here & (earlier == lax.rem(slot_id, CAP).astype(F32))
    row = jnp.max(jnp.where(chosen, local.astype(F32), -1.0), axis=1, keepdims=True)
    return one_hot((shape[0], row_count), 1, row.astype(jnp.int32))


def steps_of(sections):
    steps = []
    bit = sections // 2
    while bit:
        sent = [k for k in range(sections) if k & bit]
        steps.append((bit, sent, [k for k in range(sections) if not k & bit]))
        bit //= 2
    return steps


def answer_steps_of(sections):
    steps = []
    bit = 1
    while 4 * bit < sections:
        sent = [k for k in range(sections) if k & bit]
        steps.append((bit, sent, [k for k in range(sections) if not k & bit]))
        bit *= 2
    return steps


def rearrange(step, kept_ref, got_ref, *out):
    where = {k: (got_ref, i) for i, k in enumerate(step[1])}
    where |= {k: (kept_ref, i) for i, k in enumerate(step[2])}
    for out_ref, blocks in out:
        for i, k in enumerate(blocks):
            ref, at = where[k]
            out_ref[i] = ref[at]


def regroup(kept_ref, got_ref, after_ref, keep_ref, send_ref, *, steps, done):
    _, sent, kept = steps[done]
    rearrange(steps[done - 1], kept_ref, got_ref, (send_ref, sent), (keep_ref, kept))


def fan_out(kept_ref, got_ref, after_ref, *out_refs, step):
    size = out_refs[0].shape[0]
    groups = [range(m * size, (m + 1) * size) for m in range(len(out_refs))]
    rearrange(step, kept_ref, got_ref, *zip(out_refs, groups))


def all_blocks(steps, kept_ref, got_ref):
    where = {k: got_ref[i] for i, k in enumerate(steps[-1][1])}
    where |= {k: kept_ref[i] for i, k in enumerate(steps[-1][2])}
    return jnp.concatenate([where[k].astype(F32) for k in range(len(where))], axis=0)


def select_queries(target_ref, queries_ref, pick_ref, keep_ref, send_ref):
    _, sent, kept = steps_of(target_ref.shape[0])[0]
    pick = pick_rows(target_ref, queries_ref.shape[0])
    pick_ref[...] = pick
    asked = jnp.dot(pick, queries_ref[...], preferred_element_type=F32)
    for ref, blocks in ((send_ref, sent), (keep_ref, kept)):
        for i, k in enumerate(blocks):
            ref[i] = asked[k * CAP : (k + 1) * CAP].astype(BF16)


def spans(edges):
    return [slice(a, b) for a, b in zip(edges[:-1], edges[1:])]


def load_rows(prompts_ref, hidden_ref, there, rows_ref, here, sems):
    prompt_rows = prompts_ref.shape[0]
    return [
        pltpu.make_async_copy(
            prompts_ref.at[:, there], rows_ref.at[:prompt_rows, here], sems.at[0]
        ),
        pltpu.make_async_copy(
            hidden_ref.at[:, there], rows_ref.at[prompt_rows:, here], sems.at[1]
        ),
    ]


def channels(offset, width):
    tp = lax.axis_index("tp")
    return pl.ds(pl.multiple_of(((tp + offset) & 1) * width, width), width)


def project_first(
    prompts_ref,
    hidden_ref,
    w_ref,
    target_ref,
    span_ref,
    len_ref,
    rows_ref,
    w_tail_ref,
    total_ref,
    target_here_ref,
    span_here_ref,
    len_here_ref,
    w_head_ref,
    sems,
    small_sems,
    *,
    edges,
):
    theirs = channels(1, total_ref.shape[1])
    chunks = spans(edges)
    head = edges[-2]
    waits = []
    for c, at in enumerate(chunks):
        here = at if at.stop <= head else slice(0, at.stop - head)
        w_here_ref = w_head_ref if at.stop <= head else w_tail_ref
        copies = load_rows(prompts_ref, hidden_ref, at, rows_ref, at, sems.at[c])
        copies.append(
            pltpu.make_async_copy(w_ref.at[at, theirs], w_here_ref.at[here, :], sems.at[c, 2])
        )
        for copy in copies:
            copy.start()
        waits.append(copies)
    small = [
        pltpu.make_async_copy(target_ref, target_here_ref, small_sems.at[0]),
        pltpu.make_async_copy(span_ref, span_here_ref, small_sems.at[1]),
        pltpu.make_async_copy(len_ref, len_here_ref, small_sems.at[2]),
    ]
    for copy in small:
        copy.start()
    for c, at in enumerate(chunks):
        for copy in waits[c]:
            copy.wait()
        if at.stop <= head:
            part = jnp.dot(rows_ref[:, at], w_head_ref[at, :], preferred_element_type=F32)
            if c == 0:
                total_ref[...] = part
            else:
                total_ref[...] += part
    for copy in small:
        copy.wait()


def project_rest(
    prompts_ref,
    hidden_ref,
    w_ref,
    scale_ref,
    rows_ref,
    w_tail_ref,
    total_ref,
    after_ref,
    theirs_ref,
    rows_rest_ref,
    w_mine_ref,
    w_rest_ref,
    scale_here_ref,
    sems,
):
    width = theirs_ref.shape[1]
    theirs, mine = channels(1, width), channels(0, width)
    depth = rows_ref.shape[1]
    head = depth - w_tail_ref.shape[0]
    rest = slice(depth, depth + rows_rest_ref.shape[1])
    copies = load_rows(prompts_ref, hidden_ref, rest, rows_rest_ref, slice(None), sems)
    copies += [
        pltpu.make_async_copy(w_ref.at[rest, theirs], w_rest_ref, sems.at[2]),
        pltpu.make_async_copy(scale_ref.at[:, theirs], scale_here_ref, sems.at[3]),
        pltpu.make_async_copy(w_ref.at[:, mine], w_mine_ref, sems.at[4]),
    ]
    for copy in copies:
        copy.start()
    total = total_ref[...] + jnp.dot(
        rows_ref[:, head:], w_tail_ref[...], preferred_element_type=F32
    )
    for copy in copies[:-1]:
        copy.wait()
    total += jnp.dot(rows_rest_ref[...], w_rest_ref[...], preferred_element_type=F32)
    theirs_ref[...] = (total * scale_here_ref[...]).astype(BF16)
    copies[-1].wait()


def project_mine(rows_ref, rows_rest_ref, w_mine_ref, scale_ref, after_ref, *refs, at, last):
    refs, (scale_here_ref, sems) = refs[:-2], refs[-2:]
    if last:
        cache_ref, queries_ref, out_ref, cache_here_ref, queries_here_ref = refs
    else:
        (out_ref,) = refs
    mine = channels(0, out_ref.shape[1])
    copies = [pltpu.make_async_copy(scale_ref.at[:, mine], scale_here_ref, sems.at[0])]
    if last:
        copies.append(pltpu.make_async_copy(queries_ref, queries_here_ref, sems.at[1]))
        copies.append(pltpu.make_async_copy(cache_ref, cache_here_ref, sems.at[2]))
    for copy in copies:
        copy.start()
    depth = rows_ref.shape[1]
    count = at.stop - at.start
    block = count // 2 if count % 32 == 0 and count > 256 else count
    for m in spans(range(0, count + 1, block)):
        there = slice(at.start + m.start, at.start + m.stop)
        total = jnp.dot(rows_ref[there, :], w_mine_ref[:depth, :], preferred_element_type=F32)
        total += jnp.dot(
            rows_rest_ref[there, :], w_mine_ref[depth:, :], preferred_element_type=F32
        )
        if m.start == 0:
            copies[0].wait()
        out_ref[m, :] = (total * scale_here_ref[...]).astype(BF16)
    for copy in copies[1:]:
        copy.wait()


def split_bf16(x):
    high = x.astype(BF16).astype(F32)
    middle = (x - high).astype(BF16).astype(F32)
    return high, middle, (x - high - middle).astype(BF16).astype(F32)


def request_slots(target_ref, span_ref, row_count, padded):
    sections, requests = target_ref.shape
    position = lax.axis_index("section")
    target = target_ref[pl.ds(position, 1), :].astype(F32)
    span = span_ref[pl.ds(position, 1), :].astype(F32)
    diagonal = iota((padded, requests), 0) == iota((padded, requests), 1)
    target_col = jnp.sum(jnp.where(diagonal, target, 0.0), axis=1, keepdims=True)
    span_col = jnp.sum(jnp.where(diagonal, span, 0.0), axis=1, keepdims=True)
    section_row = jnp.zeros_like(target)
    section_col = jnp.zeros_like(target_col)
    for s in range(1, sections):
        section_row = section_row + (target >= s * row_count).astype(F32)
        section_col = section_col + (target_col >= s * row_count).astype(F32)
    before = (section_row == section_col) & (
        iota((padded, requests), 1) < iota((padded, requests), 0)
    )
    rank_col = jnp.sum(before.astype(F32), axis=1, keepdims=True).astype(jnp.int32)
    real = iota((padded, 1), 0) < requests
    section_col = jnp.where(real, section_col.astype(jnp.int32), -1)
    return section_col, rank_col, span_col.astype(jnp.int32)


def prepare_arrived(
    target_ref, span_ref, kept_ref, got_ref, rows_ref, slot_of_ref, bias_ref, *, row_count
):
    sections, requests = target_ref.shape
    padded, prompt_rows = bias_ref.shape
    span_rows = prompt_rows // requests
    section_col, rank_col, span_col = request_slots(target_ref, span_ref, row_count, padded)
    block = section_col ^ lax.axis_index("section")
    slot = jnp.where(section_col >= 0, block * PITCH + rank_col, -1)
    slot_of_ref[...] = one_hot((padded, sections * PITCH), 1, slot)
    slot = jnp.where(section_col >= 0, block * CAP + rank_col, -1)
    rows_ref[...] = jnp.dot(
        one_hot((padded, sections * CAP), 1, slot),
        all_blocks(steps_of(sections), kept_ref, got_ref).astype(BF16),
        preferred_element_type=F32,
    ).astype(BF16)
    key = iota((padded, prompt_rows), 1) - iota((padded, prompt_rows), 0) * span_rows
    bias_ref[...] = jnp.where((key >= 0) & (key < span_col), 0.0, MASKED)


def attend_arrived(rows_ref, slot_of_ref, bias_ref, other_ref, *refs):
    mine_refs, (keep_ref, send_ref) = refs[:-2], refs[-2:]
    padded, prompt_rows = bias_ref.shape
    kv_heads = other_ref.shape[1] // (2 * HD)
    group = rows_ref.shape[1] // (kv_heads * HD)
    rows = rows_ref[...]
    slot_of = slot_of_ref[...]
    bias = bias_ref[...]
    mine = jnp.concatenate([ref[...] for ref in mine_refs], axis=0)
    kv = (mine[:prompt_rows].astype(F32) + other_ref[:prompt_rows, :].astype(F32)).astype(BF16)
    scores = []
    for h in range(kv_heads):
        stacked = jnp.concatenate(
            [rows[:, (h * group + i) * HD : (h * group + i + 1) * HD] for i in range(group)],
            axis=0,
        )
        keys = kv[:, h * 2 * HD : (h * 2 + 1) * HD]
        scores.append(
            lax.dot_general(
                stacked, keys, (((1,), (1,)), ((), ())), preferred_element_type=F32
            )
        )
    scores = [
        x.reshape(group, padded, prompt_rows) * LOG2_SCALE + bias[None] for x in scores
    ]
    largest = [jnp.max(x, axis=2, keepdims=True) for x in scores]
    weights = [jnp.exp2(x - y) for x, y in zip(scores, largest)]
    totals = [jnp.sum(x, axis=2, keepdims=True) for x in weights]
    lane = iota((padded, STATS), 1)
    lse = jnp.zeros((padded, STATS), F32)
    pieces = []
    for h in range(kv_heads):
        values = jnp.dot(
            weights[h].reshape(group * padded, prompt_rows).astype(BF16),
            kv[:, (h * 2 + 1) * HD : (h * 2 + 2) * HD],
            preferred_element_type=F32,
        ).reshape(group, padded, HD)
        values = values / totals[h]
        head_lse = largest[h] + jnp.log2(totals[h])
        for i in range(group):
            pieces.append(values[i])
            lse = jnp.where(lane == h * group + i, head_lse[i], lse)
    high, middle, low = split_bf16(lse)
    stats = high + pltpu.roll(middle, LSE_PITCH, 1) + pltpu.roll(low, 2 * LSE_PITCH, 1)
    result = jnp.concatenate(pieces + [stats], axis=1).astype(BF16)
    answers = lax.dot_general(slot_of, result, TRANSPOSED, preferred_element_type=F32)
    _, sent, kept = answer_steps_of(2 * keep_ref.shape[0])[0]
    for ref, blocks in ((send_ref, sent), (keep_ref, kept)):
        for i, k in enumerate(blocks):
            ref[i] = answers[k * PITCH : k * PITCH + CAP].astype(BF16)


def attend_cache(
    queries_ref,
    cache_ref,
    len_ref,
    mine_ref,
    other_ref,
    pick_ref,
    after_ref,
    out_ref,
    slot_out_ref,
    slot_lse_ref,
    *,
    rows_at,
):
    row_count, cache_rows, width = cache_ref.shape
    first_row, block_rows = rows_at.start, rows_at.stop - rows_at.start
    kv_heads = width // (2 * HD)
    group = queries_ref.shape[1] // (kv_heads * HD)
    unit = 8
    keys_of = unit * cache_rows
    queries = queries_ref[rows_at, :].astype(F32)
    own = sum(
        ref[pl.ds(ref.shape[0] - row_count + first_row, block_rows), :].astype(F32)
        for ref in (mine_ref, other_ref)
    )
    own = own.astype(BF16).astype(F32)
    key = iota((unit, keys_of), 1) - iota((unit, keys_of), 0) * cache_rows
    lengths = len_ref[...].astype(F32)
    lane = iota((unit, STATS), 1)
    ones = jnp.ones((keys_of, HD), BF16)
    units = range(block_rows // unit)

    def rows_of(u):
        return slice(first_row + u * unit, first_row + (u + 1) * unit)

    pairs = [(u, h) for u in units for h in range(kv_heads)]
    bias = []
    for u in units:
        row = iota((unit, row_count), 0) + (first_row + u * unit)
        length = jnp.sum(
            jnp.where(iota((unit, row_count), 1) == row, lengths, 0.0), axis=1, keepdims=True
        ).astype(jnp.int32)
        bias.append(jnp.where((key >= 0) & (key < length), 0.0, MASKED))
    q, scores, own_scores = [], [], []
    for u, h in pairs:
        at = slice(u * unit, (u + 1) * unit)
        q.append(
            jnp.stack(
                [
                    queries[at, (h * group + i) * HD : (h * group + i + 1) * HD]
                    for i in range(group)
                ],
                axis=0,
            )
        )
        keys = cache_ref[rows_of(u), :, h * 2 * HD : (h * 2 + 1) * HD].reshape(keys_of, HD)
        scores.append(
            lax.dot_general(
                q[-1].reshape(group * unit, HD).astype(BF16),
                keys,
                (((1,), (1,)), ((), ())),
                preferred_element_type=F32,
            ).reshape(group, unit, keys_of)
        )
    for n, (u, h) in enumerate(pairs):
        at = slice(u * unit, (u + 1) * unit)
        own_key = own[at, h * 2 * HD : (h * 2 + 1) * HD]
        own_scores.append(jnp.sum(q[n] * own_key[None], axis=2, keepdims=True) * LOG2_SCALE)
    scores = [scores[n] * LOG2_SCALE + bias[u][None] for n, (u, h) in enumerate(pairs)]
    largest = [
        jnp.maximum(jnp.max(x, axis=2, keepdims=True), y) for x, y in zip(scores, own_scores)
    ]
    weights = [jnp.exp2(x - y).astype(BF16) for x, y in zip(scores, largest)]
    own_weights = [jnp.exp2(x - y) for x, y in zip(own_scores, largest)]
    sums = []
    for n, (u, h) in enumerate(pairs):
        at = slice(u * unit, (u + 1) * unit)
        values = cache_ref[rows_of(u), :, (h * 2 + 1) * HD : (h * 2 + 2) * HD].reshape(keys_of, HD)
        sums.append(
            jnp.dot(
                weights[n].reshape(group * unit, keys_of),
                jnp.concatenate([values, ones], axis=1),
                preferred_element_type=F32,
            ).reshape(group, unit, 2 * HD)
        )
    pieces = [[] for _ in units]
    stats = [jnp.zeros((unit, STATS), F32) for _ in units]
    for n, (u, h) in enumerate(pairs):
        at = slice(u * unit, (u + 1) * unit)
        own_value = own[at, (h * 2 + 1) * HD : (h * 2 + 2) * HD]
        total = sums[n][:, :, HD:] + own_weights[n]
        result = (sums[n][:, :, :HD] + own_weights[n] * own_value[None]) / total
        lse = largest[n] + jnp.log2(total)
        for i in range(group):
            pieces[u].append(result[i])
            stats[u] = jnp.where(lane == h * group + i, lse[i], stats[u])
    out = jnp.concatenate([jnp.concatenate(x, axis=1) for x in pieces], axis=0).astype(BF16)
    out_ref[...] = out
    here = iota((row_count, block_rows), 0) == iota((row_count, block_rows), 1) + first_row
    pick = jnp.dot(
        pick_ref[...], here.astype(F32).astype(BF16), preferred_element_type=F32
    ).astype(BF16)
    slot_out_ref[...] = jnp.dot(pick, out, preferred_element_type=F32)
    lse = jnp.concatenate(stats, axis=0)
    slot_lse_ref[...] = sum(
        jnp.dot(pick, part.astype(BF16), preferred_element_type=F32) for part in split_bf16(lse)
    )


def merge(pick_ref, *refs):
    refs, (out_ref, out_here_ref, sems) = refs[:-3], refs[-3:]
    parts, group_refs = refs[:-4], refs[-4:]
    cached_refs, slot_out_refs, slot_lse_refs = parts[0::3], parts[1::3], parts[2::3]
    width = out_ref.shape[1]
    pick = pick_ref[...]
    arrived = jnp.concatenate(
        [ref[i].astype(F32) for ref in group_refs for i in range(ref.shape[0])], axis=0
    )
    stats = arrived[:, width:]
    arrived_lse = (
        stats
        + pltpu.roll(stats, STATS - LSE_PITCH, 1)
        + pltpu.roll(stats, STATS - 2 * LSE_PITCH, 1)
    )
    cached_lse = sum(ref[...] for ref in slot_lse_refs)
    largest = jnp.maximum(cached_lse, arrived_lse)
    cached_weight = jnp.exp2(cached_lse - largest)
    arrived_weight = jnp.exp2(arrived_lse - largest)
    total = cached_weight + arrived_weight
    cached_weight = cached_weight / total
    arrived_weight = arrived_weight / total
    has = lax.dot_general(
        pick, jnp.ones((pick.shape[0], HD), BF16), TRANSPOSED, preferred_element_type=F32
    )
    copies = []
    for i in range(width // HD):
        at = slice(i * HD, (i + 1) * HD)
        merged = (
            sum(ref[:, at] for ref in slot_out_refs) * cached_weight[:, i : i + 1]
            + arrived[:, at] * arrived_weight[:, i : i + 1]
        )
        placed = lax.dot_general(
            pick, merged.astype(BF16), TRANSPOSED, preferred_element_type=F32
        )
        row = 0
        for ref in cached_refs:
            rows = slice(row, row + ref.shape[0])
            kept = ref[:, at].astype(F32)
            out_here_ref[rows, at] = jnp.where(has[rows] > 0.5, placed[rows], kept).astype(BF16)
            row += ref.shape[0]
        ready = width * (len(copies) + 1) // sems.shape[0]
        if at.stop == ready:
            there = slice(width * len(copies) // sems.shape[0], ready)
            copies.append(
                pltpu.make_async_copy(
                    out_here_ref.at[:, there], out_ref.at[:, there], sems.at[len(copies)]
                )
            )
            copies[-1].start()
    for copy in copies:
        copy.wait()


def compiler_params(megabytes):
    return pltpu.CompilerParams(vmem_limit_bytes=megabytes * 1024 * 1024)


RESIDENT = pl.BlockSpec(memory_space=pltpu.VMEM)
REMAINS = pl.BlockSpec(memory_space=pl.ANY)


def in_vmem(x):
    return pltpu.with_memory_space_constraint(x, pltpu.VMEM)


def in_hbm(x):
    return pltpu.with_memory_space_constraint(x, pltpu.HBM)


def shards(
    prompts, decode_hidden, queries, kv_cache, cache_len, span_len, target_row, w_kv, kv_scale
):
    row_count = decode_hidden.shape[0]
    prompt_rows, features = prompts.shape
    sections = lax.axis_size("section")
    local_width = kv_cache.shape[2]
    query_width = queries.shape[1]
    slots = sections * CAP
    all_rows = prompt_rows + row_count
    scale = kv_scale.reshape(1, -1)
    lengths = cache_len.reshape(1, -1)

    steps = steps_of(sections)
    half = sections // 2
    prompts, decode_hidden, w_kv, scale = map(in_hbm, (prompts, decode_hidden, w_kv, scale))
    target_row, span_len, queries = map(in_hbm, (target_row, span_len, queries))
    kv_cache, lengths = map(in_hbm, (kv_cache, lengths))

    def block_pair(width):
        return [pltpu.VMEM((half, CAP, width), BF16)] * 2

    def swapped(blocks, distance):
        pairs = [(i, i ^ distance) for i in range(sections)]
        return in_vmem(lax.ppermute(blocks, "section", pairs))

    pick, keep, send = pl.pallas_call(
        select_queries,
        in_specs=[RESIDENT, RESIDENT],
        out_specs=[RESIDENT] * 3,
        out_shape=[pltpu.VMEM((slots, row_count), BF16)] + block_pair(query_width),
        compiler_params=compiler_params(16),
        name="select_queries",
    )(target_row, queries)
    got = swapped(send, steps[0][0])

    def regrouped(blocks, got, steps, done, after):
        return pl.pallas_call(
            functools.partial(regroup, steps=steps, done=done),
            in_specs=[RESIDENT] * 2 + [REMAINS],
            out_specs=[RESIDENT] * 2,
            out_shape=block_pair(blocks.shape[2]),
            compiler_params=compiler_params(16),
            name="regroup",
        )(in_vmem(blocks), got, in_vmem(after))

    edges = (0, 256, 768, 1536, 2560, 4096)
    depth, head = edges[-1], edges[-2]
    rows, w_tail, total, target_here, span_here, lengths = pl.pallas_call(
        functools.partial(project_first, edges=edges),
        in_specs=[REMAINS] * 6,
        out_specs=[RESIDENT] * 6,
        out_shape=[
            pltpu.VMEM((all_rows, depth), BF16),
            pltpu.VMEM((depth - head, local_width), BF16),
            pltpu.VMEM((all_rows, local_width), F32),
            pltpu.VMEM(target_row.shape, jnp.int32),
            pltpu.VMEM(span_len.shape, jnp.int32),
            pltpu.VMEM(lengths.shape, jnp.int32),
        ],
        scratch_shapes=[
            pltpu.VMEM((head, local_width), BF16),
            pltpu.SemaphoreType.DMA((len(edges) - 1, 3)),
            pltpu.SemaphoreType.DMA((3,)),
        ],
        compiler_params=compiler_params(12),
        name="project_first",
    )(prompts, decode_hidden, w_kv, target_row, span_len, lengths)
    keep, send = regrouped(keep, got, steps, 1, total)
    got = swapped(send, steps[1][0])
    theirs, rows_rest, w_mine = pl.pallas_call(
        project_rest,
        in_specs=[REMAINS] * 4 + [RESIDENT] * 3 + [REMAINS],
        out_specs=[RESIDENT] * 3,
        out_shape=[
            pltpu.VMEM((all_rows, local_width), BF16),
            pltpu.VMEM((all_rows, features - depth), BF16),
            pltpu.VMEM((features, local_width), BF16),
        ],
        scratch_shapes=[
            pltpu.VMEM((features - depth, local_width), BF16),
            pltpu.VMEM((1, local_width), F32),
            pltpu.SemaphoreType.DMA((5,)),
        ],
        compiler_params=compiler_params(16),
        name="project_rest",
    )(prompts, decode_hidden, w_kv, scale, *map(in_vmem, (rows, w_tail, total, keep)))
    theirs, got = lax.optimization_barrier((theirs, got))
    got = in_vmem(got)
    other = in_vmem(lax.ppermute(theirs, "tp", [(0, 1), (1, 0)]))

    def own_channels(at, after, extra):
        return pl.pallas_call(
            functools.partial(project_mine, at=at, last=len(extra) > 0),
            in_specs=[RESIDENT] * 3 + [REMAINS] * (2 + len(extra)),
            out_specs=[RESIDENT] * (1 + len(extra)),
            out_shape=[pltpu.VMEM((at.stop - at.start, local_width), BF16)]
            + [pltpu.VMEM(x.shape, BF16) for x in extra],
            scratch_shapes=[pltpu.VMEM((1, local_width), F32), pltpu.SemaphoreType.DMA((3,))],
            compiler_params=compiler_params(16),
            name="project_mine",
        )(*map(in_vmem, (rows, rows_rest, w_mine)), scale, in_vmem(after), *extra)

    mine = []
    pieces = max(len(steps) - 2, 1)
    bounds = [prompt_rows * i // (16 * pieces) * 16 for i in range(pieces)] + [prompt_rows]
    after = theirs
    for piece, at in enumerate(spans(bounds)):
        if piece + 2 < len(steps):
            keep, send = regrouped(keep, got, steps, piece + 2, after)
            got = swapped(send, steps[piece + 2][0])
        last = piece == pieces - 1
        extra = [kv_cache, queries] if last else []
        part, *here = own_channels(at, keep, extra)
        after = part
        mine.append(in_vmem(part))
    kv_here, queries_here = map(in_vmem, here)

    padded = -(-span_len.shape[1] // 16) * 16
    prepared = pl.pallas_call(
        functools.partial(prepare_arrived, row_count=row_count),
        in_specs=[RESIDENT] * 4,
        out_specs=[RESIDENT] * 3,
        out_shape=[
            pltpu.VMEM((padded, query_width), BF16),
            pltpu.VMEM((padded, sections * PITCH), BF16),
            pltpu.VMEM((padded, prompt_rows), F32),
        ],
        compiler_params=compiler_params(16),
        name="prepare_arrived",
    )(in_vmem(target_here), in_vmem(span_here), in_vmem(keep), got)
    answer_width = query_width + STATS
    keep, send = pl.pallas_call(
        attend_arrived,
        in_specs=[RESIDENT] * (4 + len(mine)),
        out_specs=[RESIDENT] * 2,
        out_shape=block_pair(answer_width),
        compiler_params=compiler_params(24),
        name="attend_arrived",
    )(*map(in_vmem, prepared), other, *mine)

    (own_part,) = own_channels(slice(prompt_rows, all_rows), keep, [])
    steps = answer_steps_of(sections)
    shares = []
    calls = len(steps) + 1
    bounds = [row_count * i // (16 * calls) * 16 for i in range(calls)] + [row_count]
    for done, at in enumerate(spans(bounds)):
        last = done == len(steps)
        if not last:
            got = swapped(send, steps[done][0])
        share = pl.pallas_call(
            functools.partial(attend_cache, rows_at=at),
            in_specs=[RESIDENT] * 6 + [REMAINS],
            out_specs=[RESIDENT] * 3,
            out_shape=[
                pltpu.VMEM((at.stop - at.start, query_width), BF16),
                pltpu.VMEM((slots, query_width), F32),
                pltpu.VMEM((slots, STATS), F32),
            ],
            compiler_params=compiler_params(24),
            name="attend_cache",
        )(queries_here, kv_here, in_vmem(lengths), in_vmem(own_part), other, in_vmem(pick), in_vmem(keep))
        shares += share
        if done + 1 < len(steps):
            keep, send = regrouped(keep, got, steps, done + 1, share[2])
        elif not last:
            size = sections // 4
            keep, *sent = pl.pallas_call(
                functools.partial(fan_out, step=steps[-1]),
                in_specs=[RESIDENT] * 2 + [REMAINS],
                out_specs=[RESIDENT] * 4,
                out_shape=[pltpu.VMEM((size, CAP, answer_width), BF16)] * 4,
                compiler_params=compiler_params(16),
                name="fan_out",
            )(in_vmem(keep), got, in_vmem(share[2]))
            groups = [in_vmem(keep)]
            groups += [swapped(blocks, (i + 1) * size) for i, blocks in enumerate(sent)]

    return pl.pallas_call(
        merge,
        in_specs=[RESIDENT] * (5 + len(shares)),
        out_specs=REMAINS,
        out_shape=jax.ShapeDtypeStruct((row_count, query_width), BF16),
        scratch_shapes=[pltpu.VMEM((row_count, query_width), BF16), pltpu.SemaphoreType.DMA((4,))],
        compiler_params=compiler_params(24),
        name="merge",
    )(*map(in_vmem, (pick, *shares)), *groups)


def solution(mesh):
    in_specs = (
        P(("groups", "section"), "tp"),
        P(("groups", "section"), "tp"),
        P(("groups", "section"), "tp"),
        P(("groups", "section"), None, "tp"),
        P(("groups", "section")),
        P("groups", None),
        P("groups", None),
        P("tp", None),
        P(),
    )
    out_specs = P(("groups", "section"), "tp")
    return jax.shard_map(shards, mesh=mesh, in_specs=in_specs, out_specs=out_specs, check_vma=False)
```

```python
import functools
import math

import jax
import jax.numpy as jnp
from jax import lax
from jax.experimental import pallas as pl
from jax.experimental.pallas import tpu as pltpu
from jax.sharding import PartitionSpec as P

HD = 128
CAP = 2
STATS = 128
MASKED = -1e30
LSE_PITCH = 40
PITCH = 8
LOG2_SCALE = HD ** (-0.5) * math.log2(math.e)
F32 = jnp.float32
BF16 = jnp.bfloat16
TRANSPOSED = (((0,), (0,)), ((), ()))


def iota(shape, dim):
    return lax.broadcasted_iota(jnp.int32, shape, dim)


def one_hot(shape, dim, index):
    return (iota(shape, dim) == index).astype(F32).astype(BF16)


def pick_rows(target_ref, row_count):
    sections, requests = target_ref.shape
    shape = (sections * CAP, requests)
    position = lax.axis_index("section")
    slot_id = iota(shape, 0)
    table = jnp.zeros(shape, jnp.int32)
    for k in range(sections):
        mine = (slot_id >= k * CAP) & (slot_id < (k + 1) * CAP)
        table = jnp.where(mine, target_ref[pl.ds(position ^ k, 1), :], table)
    local = table - position * row_count
    here = (local >= 0) & (local < row_count)
    square = (requests, requests)
    earlier = jnp.dot(
        here.astype(F32).astype(BF16),
        (iota(square, 0) < iota(square, 1)).astype(F32).astype(BF16),
        preferred_element_type=F32,
    )
    chosen = here & (earlier == lax.rem(slot_id, CAP).astype(F32))
    row = jnp.max(jnp.where(chosen, local.astype(F32), -1.0), axis=1, keepdims=True)
    return one_hot((shape[0], row_count), 1, row.astype(jnp.int32))


def steps_of(sections):
    steps = []
    bit = sections // 2
    while bit:
        sent = [k for k in range(sections) if k & bit]
        steps.append((bit, sent, [k for k in range(sections) if not k & bit]))
        bit //= 2
    return steps


def answer_steps_of(sections):
    steps = []
    bit = 1
    while 4 * bit < sections:
        sent = [k for k in range(sections) if k & bit]
        steps.append((bit, sent, [k for k in range(sections) if not k & bit]))
        bit *= 2
    return steps


def rearrange(step, kept_ref, got_ref, *out):
    where = {k: (got_ref, i) for i, k in enumerate(step[1])}
    where |= {k: (kept_ref, i) for i, k in enumerate(step[2])}
    for out_ref, blocks in out:
        for i, k in enumerate(blocks):
            ref, at = where[k]
            out_ref[i] = ref[at]


def regroup(kept_ref, got_ref, after_ref, keep_ref, send_ref, *, steps, done):
    _, sent, kept = steps[done]
    rearrange(steps[done - 1], kept_ref, got_ref, (send_ref, sent), (keep_ref, kept))


def fan_out(kept_ref, got_ref, after_ref, *out_refs, step):
    size = out_refs[0].shape[0]
    groups = [range(m * size, (m + 1) * size) for m in range(len(out_refs))]
    rearrange(step, kept_ref, got_ref, *zip(out_refs, groups))


def all_blocks(steps, kept_ref, got_ref):
    where = {k: got_ref[i] for i, k in enumerate(steps[-1][1])}
    where |= {k: kept_ref[i] for i, k in enumerate(steps[-1][2])}
    return jnp.concatenate([where[k].astype(F32) for k in range(len(where))], axis=0)


def select_queries(target_ref, queries_ref, pick_ref, keep_ref, send_ref):
    _, sent, kept = steps_of(target_ref.shape[0])[0]
    pick = pick_rows(target_ref, queries_ref.shape[0])
    pick_ref[...] = pick
    asked = jnp.dot(pick, queries_ref[...], preferred_element_type=F32)
    for ref, blocks in ((send_ref, sent), (keep_ref, kept)):
        for i, k in enumerate(blocks):
            ref[i] = asked[k * CAP : (k + 1) * CAP].astype(BF16)


def spans(edges):
    return [slice(a, b) for a, b in zip(edges[:-1], edges[1:])]


def load_rows(prompts_ref, hidden_ref, there, rows_ref, here, sems):
    prompt_rows = prompts_ref.shape[0]
    return [
        pltpu.make_async_copy(
            prompts_ref.at[:, there], rows_ref.at[:prompt_rows, here], sems.at[0]
        ),
        pltpu.make_async_copy(
            hidden_ref.at[:, there], rows_ref.at[prompt_rows:, here], sems.at[1]
        ),
    ]


def channels(offset, width):
    tp = lax.axis_index("tp")
    return pl.ds(pl.multiple_of(((tp + offset) & 1) * width, width), width)


def project_first(
    prompts_ref,
    hidden_ref,
    w_ref,
    target_ref,
    span_ref,
    len_ref,
    rows_ref,
    w_tail_ref,
    total_ref,
    target_here_ref,
    span_here_ref,
    len_here_ref,
    w_head_ref,
    sems,
    small_sems,
    *,
    edges,
):
    theirs = channels(1, total_ref.shape[1])
    chunks = spans(edges)
    head = edges[-2]
    waits = []
    for c, at in enumerate(chunks):
        here = at if at.stop <= head else slice(0, at.stop - head)
        w_here_ref = w_head_ref if at.stop <= head else w_tail_ref
        copies = load_rows(prompts_ref, hidden_ref, at, rows_ref, at, sems.at[c])
        copies.append(
            pltpu.make_async_copy(w_ref.at[at, theirs], w_here_ref.at[here, :], sems.at[c, 2])
        )
        for copy in copies:
            copy.start()
        waits.append(copies)
    small = [
        pltpu.make_async_copy(target_ref, target_here_ref, small_sems.at[0]),
        pltpu.make_async_copy(span_ref, span_here_ref, small_sems.at[1]),
        pltpu.make_async_copy(len_ref, len_here_ref, small_sems.at[2]),
    ]
    for copy in small:
        copy.start()
    for c, at in enumerate(chunks):
        for copy in waits[c]:
            copy.wait()
        if at.stop <= head:
            part = jnp.dot(rows_ref[:, at], w_head_ref[at, :], preferred_element_type=F32)
            if c == 0:
                total_ref[...] = part
            else:
                total_ref[...] += part
    for copy in small:
        copy.wait()


def project_rest(
    prompts_ref,
    hidden_ref,
    w_ref,
    scale_ref,
    rows_ref,
    w_tail_ref,
    total_ref,
    after_ref,
    theirs_ref,
    rows_rest_ref,
    w_mine_ref,
    w_rest_ref,
    scale_here_ref,
    sems,
):
    width = theirs_ref.shape[1]
    theirs, mine = channels(1, width), channels(0, width)
    depth = rows_ref.shape[1]
    head = depth - w_tail_ref.shape[0]
    rest = slice(depth, depth + rows_rest_ref.shape[1])
    copies = load_rows(prompts_ref, hidden_ref, rest, rows_rest_ref, slice(None), sems)
    copies += [
        pltpu.make_async_copy(w_ref.at[rest, theirs], w_rest_ref, sems.at[2]),
        pltpu.make_async_copy(scale_ref.at[:, theirs], scale_here_ref, sems.at[3]),
        pltpu.make_async_copy(w_ref.at[:, mine], w_mine_ref, sems.at[4]),
    ]
    for copy in copies[:-1]:
        copy.start()
    total = total_ref[...] + jnp.dot(
        rows_ref[:, head:], w_tail_ref[...], preferred_element_type=F32
    )
    copies[-1].start()
    for copy in copies[:-1]:
        copy.wait()
    total += jnp.dot(rows_rest_ref[...], w_rest_ref[...], preferred_element_type=F32)
    theirs_ref[...] = (total * scale_here_ref[...]).astype(BF16)
    copies[-1].wait()


def project_mine(rows_ref, rows_rest_ref, w_mine_ref, scale_ref, after_ref, *refs, at, last):
    refs, (scale_here_ref, sems) = refs[:-2], refs[-2:]
    if last:
        cache_ref, queries_ref, out_ref, cache_here_ref, queries_here_ref = refs
    else:
        (out_ref,) = refs
    mine = channels(0, out_ref.shape[1])
    copies = [pltpu.make_async_copy(scale_ref.at[:, mine], scale_here_ref, sems.at[0])]
    if last:
        copies.append(pltpu.make_async_copy(queries_ref, queries_here_ref, sems.at[1]))
        copies.append(pltpu.make_async_copy(cache_ref, cache_here_ref, sems.at[2]))
    for copy in copies:
        copy.start()
    depth = rows_ref.shape[1]
    count = at.stop - at.start
    block = count // 2 if count % 32 == 0 and count > 256 else count
    for m in spans(range(0, count + 1, block)):
        there = slice(at.start + m.start, at.start + m.stop)
        total = jnp.dot(rows_ref[there, :], w_mine_ref[:depth, :], preferred_element_type=F32)
        total += jnp.dot(
            rows_rest_ref[there, :], w_mine_ref[depth:, :], preferred_element_type=F32
        )
        if m.start == 0:
            copies[0].wait()
        out_ref[m, :] = (total * scale_here_ref[...]).astype(BF16)
    for copy in copies[1:]:
        copy.wait()


def split_bf16(x):
    high = x.astype(BF16).astype(F32)
    middle = (x - high).astype(BF16).astype(F32)
    return high, middle, (x - high - middle).astype(BF16).astype(F32)


def request_slots(target_ref, span_ref, row_count, padded):
    sections, requests = target_ref.shape
    position = lax.axis_index("section")
    target = target_ref[pl.ds(position, 1), :].astype(F32)
    span = span_ref[pl.ds(position, 1), :].astype(F32)
    diagonal = iota((padded, requests), 0) == iota((padded, requests), 1)
    target_col = jnp.sum(jnp.where(diagonal, target, 0.0), axis=1, keepdims=True)
    span_col = jnp.sum(jnp.where(diagonal, span, 0.0), axis=1, keepdims=True)
    section_row = jnp.zeros_like(target)
    section_col = jnp.zeros_like(target_col)
    for s in range(1, sections):
        section_row = section_row + (target >= s * row_count).astype(F32)
        section_col = section_col + (target_col >= s * row_count).astype(F32)
    before = (section_row == section_col) & (
        iota((padded, requests), 1) < iota((padded, requests), 0)
    )
    rank_col = jnp.sum(before.astype(F32), axis=1, keepdims=True).astype(jnp.int32)
    real = iota((padded, 1), 0) < requests
    section_col = jnp.where(real, section_col.astype(jnp.int32), -1)
    return section_col, rank_col, span_col.astype(jnp.int32)


def prepare_arrived(
    target_ref, span_ref, kept_ref, got_ref, rows_ref, slot_of_ref, bias_ref, *, row_count
):
    sections, requests = target_ref.shape
    padded, prompt_rows = bias_ref.shape
    span_rows = prompt_rows // requests
    section_col, rank_col, span_col = request_slots(target_ref, span_ref, row_count, padded)
    block = section_col ^ lax.axis_index("section")
    slot = jnp.where(section_col >= 0, block * PITCH + rank_col, -1)
    slot_of_ref[...] = one_hot((padded, sections * PITCH), 1, slot)
    slot = jnp.where(section_col >= 0, block * CAP + rank_col, -1)
    rows_ref[...] = jnp.dot(
        one_hot((padded, sections * CAP), 1, slot),
        all_blocks(steps_of(sections), kept_ref, got_ref).astype(BF16),
        preferred_element_type=F32,
    ).astype(BF16)
    key = iota((padded, prompt_rows), 1) - iota((padded, prompt_rows), 0) * span_rows
    bias_ref[...] = jnp.where((key >= 0) & (key < span_col), 0.0, MASKED)


def attend_arrived(target_ref, span_ref, kept_ref, got_ref, other_ref, *refs, row_count):
    rows_ref, slot_of_ref, bias_ref = refs[-3:]
    mine_refs, (keep_ref, send_ref) = refs[:-5], refs[-5:-3]
    prepare_arrived(
        target_ref,
        span_ref,
        kept_ref,
        got_ref,
        rows_ref,
        slot_of_ref,
        bias_ref,
        row_count=row_count,
    )
    padded, prompt_rows = bias_ref.shape
    kv_heads = other_ref.shape[1] // (2 * HD)
    group = rows_ref.shape[1] // (kv_heads * HD)
    rows = rows_ref[...]
    slot_of = slot_of_ref[...]
    bias = bias_ref[...]
    mine = jnp.concatenate([ref[...] for ref in mine_refs], axis=0)
    kv = (mine[:prompt_rows].astype(F32) + other_ref[:prompt_rows, :].astype(F32)).astype(BF16)
    scores = []
    for h in range(kv_heads):
        stacked = jnp.concatenate(
            [rows[:, (h * group + i) * HD : (h * group + i + 1) * HD] for i in range(group)],
            axis=0,
        )
        keys = kv[:, h * 2 * HD : (h * 2 + 1) * HD]
        scores.append(
            lax.dot_general(
                stacked, keys, (((1,), (1,)), ((), ())), preferred_element_type=F32
            )
        )
    scores = [
        x.reshape(group, padded, prompt_rows) * LOG2_SCALE + bias[None] for x in scores
    ]
    largest = [jnp.max(x, axis=2, keepdims=True) for x in scores]
    weights = [jnp.exp2(x - y) for x, y in zip(scores, largest)]
    totals = [jnp.sum(x, axis=2, keepdims=True) for x in weights]
    lane = iota((padded, STATS), 1)
    lse = jnp.zeros((padded, STATS), F32)
    pieces = []
    for h in range(kv_heads):
        values = jnp.dot(
            weights[h].reshape(group * padded, prompt_rows).astype(BF16),
            kv[:, (h * 2 + 1) * HD : (h * 2 + 2) * HD],
            preferred_element_type=F32,
        ).reshape(group, padded, HD)
        values = values / totals[h]
        head_lse = largest[h] + jnp.log2(totals[h])
        for i in range(group):
            pieces.append(values[i])
            lse = jnp.where(lane == h * group + i, head_lse[i], lse)
    high, middle, low = split_bf16(lse)
    stats = high + pltpu.roll(middle, LSE_PITCH, 1) + pltpu.roll(low, 2 * LSE_PITCH, 1)
    result = jnp.concatenate(pieces + [stats], axis=1).astype(BF16)
    answers = lax.dot_general(slot_of, result, TRANSPOSED, preferred_element_type=F32)
    _, sent, kept = answer_steps_of(2 * keep_ref.shape[0])[0]
    for ref, blocks in ((send_ref, sent), (keep_ref, kept)):
        for i, k in enumerate(blocks):
            ref[i] = answers[k * PITCH : k * PITCH + CAP].astype(BF16)


def attend_cache(
    queries_ref,
    cache_ref,
    len_ref,
    mine_ref,
    other_ref,
    pick_ref,
    after_ref,
    out_ref,
    slot_out_ref,
    slot_lse_ref,
    *,
    rows_at,
):
    row_count, cache_rows, width = cache_ref.shape
    first_row, block_rows = rows_at.start, rows_at.stop - rows_at.start
    kv_heads = width // (2 * HD)
    group = queries_ref.shape[1] // (kv_heads * HD)
    unit = 8
    keys_of = unit * cache_rows
    queries = queries_ref[rows_at, :].astype(F32)
    own = sum(
        ref[pl.ds(ref.shape[0] - row_count + first_row, block_rows), :].astype(F32)
        for ref in (mine_ref, other_ref)
    )
    own = own.astype(BF16).astype(F32)
    key = iota((unit, keys_of), 1) - iota((unit, keys_of), 0) * cache_rows
    lengths = len_ref[...].astype(F32)
    lane = iota((unit, STATS), 1)
    ones = jnp.ones((keys_of, HD), BF16)
    units = range(block_rows // unit)

    def rows_of(u):
        return slice(first_row + u * unit, first_row + (u + 1) * unit)

    pairs = [(u, h) for u in units for h in range(kv_heads)]
    bias = []
    for u in units:
        row = iota((unit, row_count), 0) + (first_row + u * unit)
        length = jnp.sum(
            jnp.where(iota((unit, row_count), 1) == row, lengths, 0.0), axis=1, keepdims=True
        ).astype(jnp.int32)
        bias.append(jnp.where((key >= 0) & (key < length), 0.0, MASKED))
    q, scores, own_scores = [], [], []
    for u, h in pairs:
        at = slice(u * unit, (u + 1) * unit)
        q.append(
            jnp.stack(
                [
                    queries[at, (h * group + i) * HD : (h * group + i + 1) * HD]
                    for i in range(group)
                ],
                axis=0,
            )
        )
        keys = cache_ref[rows_of(u), :, h * 2 * HD : (h * 2 + 1) * HD].reshape(keys_of, HD)
        scores.append(
            lax.dot_general(
                q[-1].reshape(group * unit, HD).astype(BF16),
                keys,
                (((1,), (1,)), ((), ())),
                preferred_element_type=F32,
            ).reshape(group, unit, keys_of)
        )
    for n, (u, h) in enumerate(pairs):
        at = slice(u * unit, (u + 1) * unit)
        own_key = own[at, h * 2 * HD : (h * 2 + 1) * HD]
        own_scores.append(jnp.sum(q[n] * own_key[None], axis=2, keepdims=True) * LOG2_SCALE)
    scores = [scores[n] * LOG2_SCALE + bias[u][None] for n, (u, h) in enumerate(pairs)]
    largest = [
        jnp.maximum(jnp.max(x, axis=2, keepdims=True), y) for x, y in zip(scores, own_scores)
    ]
    weights = [jnp.exp2(x - y).astype(BF16) for x, y in zip(scores, largest)]
    own_weights = [jnp.exp2(x - y) for x, y in zip(own_scores, largest)]
    sums = []
    for n, (u, h) in enumerate(pairs):
        at = slice(u * unit, (u + 1) * unit)
        values = cache_ref[rows_of(u), :, (h * 2 + 1) * HD : (h * 2 + 2) * HD].reshape(keys_of, HD)
        sums.append(
            jnp.dot(
                weights[n].reshape(group * unit, keys_of),
                jnp.concatenate([values, ones], axis=1),
                preferred_element_type=F32,
            ).reshape(group, unit, 2 * HD)
        )
    pieces = [[] for _ in units]
    stats = [jnp.zeros((unit, STATS), F32) for _ in units]
    for n, (u, h) in enumerate(pairs):
        at = slice(u * unit, (u + 1) * unit)
        own_value = own[at, (h * 2 + 1) * HD : (h * 2 + 2) * HD]
        total = sums[n][:, :, HD:] + own_weights[n]
        result = (sums[n][:, :, :HD] + own_weights[n] * own_value[None]) / total
        lse = largest[n] + jnp.log2(total)
        for i in range(group):
            pieces[u].append(result[i])
            stats[u] = jnp.where(lane == h * group + i, lse[i], stats[u])
    out = jnp.concatenate([jnp.concatenate(x, axis=1) for x in pieces], axis=0).astype(BF16)
    out_ref[...] = out
    here = iota((row_count, block_rows), 0) == iota((row_count, block_rows), 1) + first_row
    pick = jnp.dot(
        pick_ref[...], here.astype(F32).astype(BF16), preferred_element_type=F32
    ).astype(BF16)
    slot_out_ref[...] = jnp.dot(pick, out, preferred_element_type=F32)
    lse = jnp.concatenate(stats, axis=0)
    slot_lse_ref[...] = sum(
        jnp.dot(pick, part.astype(BF16), preferred_element_type=F32) for part in split_bf16(lse)
    )


def merge(pick_ref, *refs):
    refs, (out_ref, out_here_ref, sems) = refs[:-3], refs[-3:]
    parts, group_refs = refs[:-4], refs[-4:]
    cached_refs, slot_out_refs, slot_lse_refs = parts[0::3], parts[1::3], parts[2::3]
    width = out_ref.shape[1]
    pick = pick_ref[...]
    arrived = jnp.concatenate(
        [ref[i].astype(F32) for ref in group_refs for i in range(ref.shape[0])], axis=0
    )
    stats = arrived[:, width:]
    arrived_lse = (
        stats
        + pltpu.roll(stats, STATS - LSE_PITCH, 1)
        + pltpu.roll(stats, STATS - 2 * LSE_PITCH, 1)
    )
    cached_lse = sum(ref[...] for ref in slot_lse_refs)
    largest = jnp.maximum(cached_lse, arrived_lse)
    cached_weight = jnp.exp2(cached_lse - largest)
    arrived_weight = jnp.exp2(arrived_lse - largest)
    total = cached_weight + arrived_weight
    cached_weight = cached_weight / total
    arrived_weight = arrived_weight / total
    has = lax.dot_general(
        pick, jnp.ones((pick.shape[0], HD), BF16), TRANSPOSED, preferred_element_type=F32
    )
    copies = []
    for i in range(width // HD):
        at = slice(i * HD, (i + 1) * HD)
        merged = (
            sum(ref[:, at] for ref in slot_out_refs) * cached_weight[:, i : i + 1]
            + arrived[:, at] * arrived_weight[:, i : i + 1]
        )
        placed = lax.dot_general(
            pick, merged.astype(BF16), TRANSPOSED, preferred_element_type=F32
        )
        row = 0
        for ref in cached_refs:
            rows = slice(row, row + ref.shape[0])
            kept = ref[:, at].astype(F32)
            out_here_ref[rows, at] = jnp.where(has[rows] > 0.5, placed[rows], kept).astype(BF16)
            row += ref.shape[0]
        ready = width * (len(copies) + 1) // sems.shape[0]
        if at.stop == ready:
            there = slice(width * len(copies) // sems.shape[0], ready)
            copies.append(
                pltpu.make_async_copy(
                    out_here_ref.at[:, there], out_ref.at[:, there], sems.at[len(copies)]
                )
            )
            copies[-1].start()
    for copy in copies:
        copy.wait()


def compiler_params(megabytes):
    return pltpu.CompilerParams(vmem_limit_bytes=megabytes * 1024 * 1024)


RESIDENT = pl.BlockSpec(memory_space=pltpu.VMEM)
REMAINS = pl.BlockSpec(memory_space=pl.ANY)


def in_vmem(x):
    return pltpu.with_memory_space_constraint(x, pltpu.VMEM)


def in_hbm(x):
    return pltpu.with_memory_space_constraint(x, pltpu.HBM)


def shards(
    prompts, decode_hidden, queries, kv_cache, cache_len, span_len, target_row, w_kv, kv_scale
):
    row_count = decode_hidden.shape[0]
    prompt_rows, features = prompts.shape
    sections = lax.axis_size("section")
    local_width = kv_cache.shape[2]
    query_width = queries.shape[1]
    slots = sections * CAP
    all_rows = prompt_rows + row_count
    scale = kv_scale.reshape(1, -1)
    lengths = cache_len.reshape(1, -1)

    steps = steps_of(sections)
    half = sections // 2
    prompts, decode_hidden, w_kv, scale = map(in_hbm, (prompts, decode_hidden, w_kv, scale))
    target_row, span_len, queries = map(in_hbm, (target_row, span_len, queries))
    kv_cache, lengths = map(in_hbm, (kv_cache, lengths))

    def block_pair(width):
        return [pltpu.VMEM((half, CAP, width), BF16)] * 2

    def swapped(blocks, distance):
        pairs = [(i, i ^ distance) for i in range(sections)]
        return in_vmem(lax.ppermute(blocks, "section", pairs))

    pick, keep, send = pl.pallas_call(
        select_queries,
        in_specs=[RESIDENT, RESIDENT],
        out_specs=[RESIDENT] * 3,
        out_shape=[pltpu.VMEM((slots, row_count), BF16)] + block_pair(query_width),
        compiler_params=compiler_params(16),
        name="select_queries",
    )(target_row, queries)
    got = swapped(send, steps[0][0])

    def regrouped(blocks, got, steps, done, after):
        return pl.pallas_call(
            functools.partial(regroup, steps=steps, done=done),
            in_specs=[RESIDENT] * 2 + [REMAINS],
            out_specs=[RESIDENT] * 2,
            out_shape=block_pair(blocks.shape[2]),
            compiler_params=compiler_params(16),
            name="regroup",
        )(in_vmem(blocks), got, in_vmem(after))

    edges = (0, 256, 768, 1536, 2560, 4096)
    depth, head = edges[-1], edges[-2]
    rows, w_tail, total, target_here, span_here, lengths = pl.pallas_call(
        functools.partial(project_first, edges=edges),
        in_specs=[REMAINS] * 6,
        out_specs=[RESIDENT] * 6,
        out_shape=[
            pltpu.VMEM((all_rows, depth), BF16),
            pltpu.VMEM((depth - head, local_width), BF16),
            pltpu.VMEM((all_rows, local_width), F32),
            pltpu.VMEM(target_row.shape, jnp.int32),
            pltpu.VMEM(span_len.shape, jnp.int32),
            pltpu.VMEM(lengths.shape, jnp.int32),
        ],
        scratch_shapes=[
            pltpu.VMEM((head, local_width), BF16),
            pltpu.SemaphoreType.DMA((len(edges) - 1, 3)),
            pltpu.SemaphoreType.DMA((3,)),
        ],
        compiler_params=compiler_params(12),
        name="project_first",
    )(prompts, decode_hidden, w_kv, target_row, span_len, lengths)
    keep, send = regrouped(keep, got, steps, 1, total)
    got = swapped(send, steps[1][0])
    theirs, rows_rest, w_mine = pl.pallas_call(
        project_rest,
        in_specs=[REMAINS] * 4 + [RESIDENT] * 3 + [REMAINS],
        out_specs=[RESIDENT] * 3,
        out_shape=[
            pltpu.VMEM((all_rows, local_width), BF16),
            pltpu.VMEM((all_rows, features - depth), BF16),
            pltpu.VMEM((features, local_width), BF16),
        ],
        scratch_shapes=[
            pltpu.VMEM((features - depth, local_width), BF16),
            pltpu.VMEM((1, local_width), F32),
            pltpu.SemaphoreType.DMA((5,)),
        ],
        compiler_params=compiler_params(16),
        name="project_rest",
    )(prompts, decode_hidden, w_kv, scale, *map(in_vmem, (rows, w_tail, total, keep)))
    theirs, got = lax.optimization_barrier((theirs, got))
    got = in_vmem(got)
    other = in_vmem(lax.ppermute(theirs, "tp", [(0, 1), (1, 0)]))

    def own_channels(at, after, extra):
        return pl.pallas_call(
            functools.partial(project_mine, at=at, last=len(extra) > 0),
            in_specs=[RESIDENT] * 3 + [REMAINS] * (2 + len(extra)),
            out_specs=[RESIDENT] * (1 + len(extra)),
            out_shape=[pltpu.VMEM((at.stop - at.start, local_width), BF16)]
            + [pltpu.VMEM(x.shape, BF16) for x in extra],
            scratch_shapes=[pltpu.VMEM((1, local_width), F32), pltpu.SemaphoreType.DMA((3,))],
            compiler_params=compiler_params(16),
            name="project_mine",
        )(*map(in_vmem, (rows, rows_rest, w_mine)), scale, in_vmem(after), *extra)

    mine = []
    pieces = max(len(steps) - 2, 1)
    bounds = [prompt_rows * i // (16 * pieces) * 16 for i in range(pieces)] + [prompt_rows]
    after = theirs
    for piece, at in enumerate(spans(bounds)):
        if piece + 2 < len(steps):
            keep, send = regrouped(keep, got, steps, piece + 2, after)
            got = swapped(send, steps[piece + 2][0])
        last = piece == pieces - 1
        extra = [kv_cache, queries] if last else []
        part, *here = own_channels(at, keep, extra)
        after = part
        mine.append(in_vmem(part))
    kv_here, queries_here = map(in_vmem, here)

    padded = -(-span_len.shape[1] // 16) * 16
    answer_width = query_width + STATS
    keep, send = pl.pallas_call(
        functools.partial(attend_arrived, row_count=row_count),
        in_specs=[RESIDENT] * (5 + len(mine)),
        out_specs=[RESIDENT] * 2,
        out_shape=block_pair(answer_width),
        scratch_shapes=[
            pltpu.VMEM((padded, query_width), BF16),
            pltpu.VMEM((padded, sections * PITCH), BF16),
            pltpu.VMEM((padded, prompt_rows), F32),
        ],
        compiler_params=compiler_params(24),
        name="attend_arrived",
    )(in_vmem(target_here), in_vmem(span_here), in_vmem(keep), got, other, *mine)

    (own_part,) = own_channels(slice(prompt_rows, all_rows), keep, [])
    steps = answer_steps_of(sections)
    shares = []
    calls = len(steps) + 1
    bounds = [row_count * i // (16 * calls) * 16 for i in range(calls)] + [row_count]
    for done, at in enumerate(spans(bounds)):
        last = done == len(steps)
        if not last:
            got = swapped(send, steps[done][0])
        share = pl.pallas_call(
            functools.partial(attend_cache, rows_at=at),
            in_specs=[RESIDENT] * 6 + [REMAINS],
            out_specs=[RESIDENT] * 3,
            out_shape=[
                pltpu.VMEM((at.stop - at.start, query_width), BF16),
                pltpu.VMEM((slots, query_width), F32),
                pltpu.VMEM((slots, STATS), F32),
            ],
            compiler_params=compiler_params(24),
            name="attend_cache",
        )(queries_here, kv_here, in_vmem(lengths), in_vmem(own_part), other, in_vmem(pick), in_vmem(keep))
        shares += share
        if done + 1 < len(steps):
            keep, send = regrouped(keep, got, steps, done + 1, share[2])
        elif not last:
            size = sections // 4
            keep, *sent = pl.pallas_call(
                functools.partial(fan_out, step=steps[-1]),
                in_specs=[RESIDENT] * 2 + [REMAINS],
                out_specs=[RESIDENT] * 4,
                out_shape=[pltpu.VMEM((size, CAP, answer_width), BF16)] * 4,
                compiler_params=compiler_params(16),
                name="fan_out",
            )(in_vmem(keep), got, in_vmem(share[2]))
            groups = [in_vmem(keep)]
            groups += [swapped(blocks, (i + 1) * size) for i, blocks in enumerate(sent)]

    return pl.pallas_call(
        merge,
        in_specs=[RESIDENT] * (5 + len(shares)),
        out_specs=REMAINS,
        out_shape=jax.ShapeDtypeStruct((row_count, query_width), BF16),
        scratch_shapes=[pltpu.VMEM((row_count, query_width), BF16), pltpu.SemaphoreType.DMA((4,))],
        compiler_params=compiler_params(24),
        name="merge",
    )(*map(in_vmem, (pick, *shares)), *groups)


def solution(mesh):
    in_specs = (
        P(("groups", "section"), "tp"),
        P(("groups", "section"), "tp"),
        P(("groups", "section"), "tp"),
        P(("groups", "section"), None, "tp"),
        P(("groups", "section")),
        P("groups", None),
        P("groups", None),
        P("tp", None),
        P(),
    )
    out_specs = P(("groups", "section"), "tp")
    return jax.shard_map(shards, mesh=mesh, in_specs=in_specs, out_specs=out_specs, check_vma=False)
```
